32 devices in a mesh: rows: 16 (over z, y, x), cols: 2 (over core).
Axes of the slice: x: 2, y: 2, z: 4, core: 2. Of those that a mesh axis runs over, the one named last changes fastest.
Arguments:
- features: bfloat16 [64, 512, 2048], P('rows', 'cols'), may hold values from -6 to 6
- reduce_weight: bfloat16 [2048, 512], replicated, may hold values from -0.125 to 0.125
- dilated_weight: bfloat16 [9, 512, 512], replicated, may hold values from -0.09375 to 0.09375
- expand_weight: bfloat16 [512, 2048], replicated, may hold values from -0.25 to 0.25
- mid_gain: float32 [2, 512], replicated, may hold values from 0.5 to 1.5
- mid_shift: float32 [2, 512], replicated, may hold values from -2 to 2
- out_gain: float32 [2048], replicated, may hold values from 0.5 to 1.5
- out_shift: float32 [2048], replicated, may hold values from -2 to 2
- aspp_point: bfloat16 [2048, 256], replicated, may hold values from -0.125 to 0.125
- sep_depth: bfloat16 [3, 9, 2048], replicated, may hold values from -2 to 2
- sep_point: bfloat16 [3, 2048, 256], replicated, may hold values from -0.125 to 0.125
- pool_weight: bfloat16 [2048, 256], replicated, may hold values from -0.125 to 0.125
- proj_weight: bfloat16 [1280, 256], replicated, may hold values from -0.15625 to 0.15625
- aspp_gain: float32 [5, 256], replicated, may hold values from 0.5 to 1.5
- aspp_shift: float32 [5, 256], replicated, may hold values from -2 to 2
- head_weight: bfloat16 [256, 17], replicated, may hold values from -0.75 to 0.75
- head_bias: float32 [17], replicated, may hold values from -3 to 3
- task_scales: float32 [3], replicated, may hold values from -1 to 1
- crop_ids: int32 [64, 512], P('rows', 'cols'), may hold values from 0 to 15, as said below
- labels: int32 [64, 512], P('rows', 'cols'), may hold values from 0 to 12
- boundary_mask: int32 [64, 512], P('rows', 'cols'), may hold values from 0 to 1, as said below
- valid_mask: int32 [64, 512], P('rows', 'cols'), may hold values from 0 to 1
- geometry_target: float32 [4, 64, 512], P(None, 'rows', 'cols'), may hold values from -6 to 6
Outputs:
- objective: float32 [], replicated
- grad_features: bfloat16 [64, 512, 2048], P('rows', 'cols')
- grad_reduce_weight: float32 [2048, 512], replicated
- grad_dilated_weight: float32 [9, 512, 512], replicated
- grad_expand_weight: float32 [512, 2048], replicated
- grad_mid_gain: float32 [2, 512], replicated
- grad_mid_shift: float32 [2, 512], replicated
- grad_out_gain: float32 [2048], replicated
- grad_out_shift: float32 [2048], replicated
- grad_aspp_point: float32 [2048, 256], replicated
- grad_sep_depth: float32 [3, 9, 2048], replicated
- grad_sep_point: float32 [3, 2048, 256], replicated
- grad_pool_weight: float32 [2048, 256], replicated
- grad_proj_weight: float32 [1280, 256], replicated
- grad_aspp_gain: float32 [5, 256], replicated
- grad_aspp_shift: float32 [5, 256], replicated
- grad_head_weight: float32 [256, 17], replicated
- grad_head_bias: float32 [17], replicated
- grad_task_scales: float32 [3], replicated
The draws below stay inside these ranges and needn't reach their ends.
Inputs may be any that keep to these rules, and one draw needn't show every extreme that they name: `crop_ids`: each crop covers a rectangle of the canvas and has pixels; crop 0 covers all 64 rows. `boundary_mask`: the first canvas row has no ones, so the semantic loss always has pixels.
All inputs are finite; a program needn't handle non-finite values.
Results may differ from the reference program's by a relative error of at most 0.03.
Values may be sent and summed in bfloat16 or wider, within the bound.
A program may use at most 448 MiB of HBM per device.

```python
import jax
import jax.numpy as jnp
from jax import lax

C_IN = 2048
MID = 512
ASPP = 256
CLASSES = 13
CROPS = 16
MID_RATE = 4
BASE_RATE = 12
HEIGHT = 64
WIDTH = 512
OUTS = 17


def draw_crop_ids(key, part):
    key = jax.random.fold_in(key, 11)
    key_split, key_rows = jax.random.split(key)
    split = jax.random.randint(key_split, (), WIDTH // 4, 3 * WIDTH // 4 + 1)
    order = jax.random.permutation(key_rows, HEIGHT - 1) + 1
    cuts = jnp.sort(order[:CROPS - 2])
    row_index = jnp.arange(HEIGHT)
    band = jnp.sum((row_index[:, None] >= cuts[None, :]).astype(jnp.int32), axis=1) + 1
    col_index = jnp.arange(WIDTH)
    return jnp.where(col_index[None, :] < split, 0, band[:, None]).astype(jnp.int32)


def draw_boundary_mask(key, part):
    key = jax.random.fold_in(key, 31)
    row_index = jnp.arange(HEIGHT).astype(jnp.int32)
    limit = 750 * row_index // max(HEIGHT - 1, 1)
    ticket = jax.random.randint(key, (HEIGHT, WIDTH), 0, 1000)
    return (ticket < limit[:, None]).astype(jnp.int32)


def draw_valid_mask(key, part):
    key = jax.random.fold_in(key, 37)
    row_index = jnp.arange(HEIGHT).astype(jnp.int32)
    limit = 900 - 600 * row_index // max(HEIGHT - 1, 1)
    ticket = jax.random.randint(key, (HEIGHT, WIDTH), 0, 1000)
    return (ticket < limit[:, None]).astype(jnp.int32)


def draw_geometry_target(key, part):
    key = jax.random.fold_in(key, 23)
    place = jnp.arange(HEIGHT).astype(jnp.float32) / max(HEIGHT - 1, 1)
    scale = 0.5 + place
    base = jnp.clip(jax.random.normal(key, (4, HEIGHT, WIDTH), jnp.float32), -3.0, 3.0)
    return (base * scale[None, :, None]).astype(jnp.float32)


def with_ends(drawn, stream_key, low, top_value):
    dims = drawn.shape
    spot = [jax.random.randint(jax.random.fold_in(stream_key, axis), (), 0, dims[axis]) for axis in range(len(dims))]
    drawn = drawn.at[tuple(spot)].set(low)
    longest = dims.index(max(dims))
    spot[longest] = (spot[longest] + 1) % dims[longest]
    return drawn.at[tuple(spot)].set(top_value)


def block_levels(own_key, shape, shards, low, top_value):
    factor_of, own = 1.0, jax.random.fold_in(own_key, 6)
    for axis_at, parts in shards:
        draws = jnp.exp(jax.random.uniform(jax.random.fold_in(own, axis_at), (parts,), jnp.float32, low / len(shards), top_value / len(shards)))
        factor_of = factor_of * jnp.repeat(draws, shape[axis_at] // parts).reshape([-1 if axis == axis_at else 1 for axis in range(len(shape))])
    return factor_of


def normal_values(own_key, dims, scale, reach, cuts=(), held_as=jnp.bfloat16):
    result = jax.random.normal(own_key, dims, jnp.float32) * scale
    if len(cuts) > 0:
        result = block_levels(own_key, dims, cuts, -0.22, 0.18) * result
    return jnp.clip(result, min=-reach, max=reach).astype(held_as)


def setup_inputs(seed: int = 0) -> dict:
    seeds = jax.random.split(jax.random.key(seed), 24)
    features = normal_values(seeds[0], (HEIGHT, WIDTH, C_IN), 1.0, 6.0, ((0, 16), (1, 2)))
    reduce_weight = normal_values(seeds[1], (C_IN, MID), C_IN ** -0.5, 0.125)
    dilated_weight = normal_values(seeds[2], (9, MID, MID), (9 * MID) ** -0.5, 0.09375)
    expand_weight = normal_values(seeds[3], (MID, C_IN), MID ** -0.5, 0.25)
    mid_gain = jnp.clip(1.0 + 0.1 * jax.random.normal(seeds[4], (2, MID), jnp.float32), 0.5, 1.5)
    mid_shift = normal_values(seeds[5], (2, MID), 0.3, 2.0, (), jnp.float32)
    out_gain = jnp.clip(1.0 + 0.1 * jax.random.normal(seeds[6], (C_IN,), jnp.float32), 0.5, 1.5)
    out_shift = normal_values(seeds[7], (C_IN,), 0.3, 2.0, (), jnp.float32)
    aspp_point = normal_values(seeds[8], (C_IN, ASPP), C_IN ** -0.5, 0.125)
    sep_depth = normal_values(seeds[9], (3, 9, C_IN), 9 ** -0.5, 2.0)
    sep_point = normal_values(seeds[10], (3, C_IN, ASPP), C_IN ** -0.5, 0.125)
    pool_weight = normal_values(seeds[11], (C_IN, ASPP), C_IN ** -0.5, 0.125)
    proj_weight = normal_values(seeds[12], (5 * ASPP, ASPP), (5 * ASPP) ** -0.5, 0.15625)
    aspp_gain = jnp.clip(1.0 + 0.1 * jax.random.normal(seeds[13], (5, ASPP), jnp.float32), 0.5, 1.5)
    aspp_shift = normal_values(seeds[14], (5, ASPP), 0.3, 2.0, (), jnp.float32)
    head_weight = normal_values(seeds[15], (ASPP, OUTS), (ASPP // 4) ** -0.5, 0.75)
    head_bias = normal_values(seeds[16], (OUTS,), 0.5, 3.0, (), jnp.float32)
    task_scales = jnp.clip(jax.random.uniform(seeds[17], (3,), jnp.float32, -1.0, 1.0), -1.0, 1.0)
    crop_ids = draw_crop_ids(jax.random.fold_in(seeds[23], 71), 0)
    labels = with_ends(jax.random.randint(seeds[19], (HEIGHT, WIDTH), 0, CLASSES), jax.random.fold_in(seeds[19], 1), 0, CLASSES - 1).astype(jnp.int32)
    boundary_mask = draw_boundary_mask(jax.random.fold_in(seeds[23], 71), 0)
    valid_mask = draw_valid_mask(jax.random.fold_in(seeds[23], 71), 0)
    geometry_target = draw_geometry_target(jax.random.fold_in(seeds[23], 71), 0)
    return dict(features=features, reduce_weight=reduce_weight, dilated_weight=dilated_weight, expand_weight=expand_weight, mid_gain=mid_gain, mid_shift=mid_shift, out_gain=out_gain, out_shift=out_shift, aspp_point=aspp_point, sep_depth=sep_depth, sep_point=sep_point, pool_weight=pool_weight, proj_weight=proj_weight, aspp_gain=aspp_gain, aspp_shift=aspp_shift, head_weight=head_weight, head_bias=head_bias, task_scales=task_scales, crop_ids=crop_ids, labels=labels, boundary_mask=boundary_mask, valid_mask=valid_mask, geometry_target=geometry_target)


@jax.custom_vjp
def low(v):
    return lax.optimization_barrier(v.astype(jnp.bfloat16)).astype(jnp.float32)

@jax.custom_vjp
def low_back(v):
    return v

def low_keep(v):
    return (low(v), None)

def low_pass(kept, grad):
    return (grad,)

def back_keep(v):
    return (v, None)

def back_low(kept, grad):
    return (low(grad),)
low.defvjp(low_keep, low_pass)
low_back.defvjp(back_keep, back_low)
EPS = 1e-05

def product(left, right):
    return jnp.dot(left, right, precision=lax.Precision.HIGHEST, preferred_element_type=jnp.float32)

def sigmoid_linear(value):
    return value * jax.nn.sigmoid(value)

def batch_norm(value, gain, shift):
    center = lax.optimization_barrier(jnp.mean(value, axis=0))
    spread = lax.optimization_barrier(jnp.mean((value - center) ** 2, axis=0))
    return (value - center) * lax.rsqrt(spread + EPS) * gain + shift

def offsets(field, rate):
    height, width = (field.shape[0], field.shape[1])
    padded = jnp.pad(field, ((rate, rate), (rate, rate), (0, 0)))
    pieces = []
    for row_step in (-1, 0, 1):
        for col_step in (-1, 0, 1):
            top = rate + row_step * rate
            left = rate + col_step * rate
            pieces.append(padded[top:top + height, left:left + width, :])
    return pieces

def dilated_conv(field, weight, rate):
    pieces = offsets(field, rate)
    pixels = field.shape[0] * field.shape[1]
    total = jnp.zeros((pixels, weight.shape[2]), jnp.float32)
    for index in range(9):
        total = total + product(pieces[index].reshape(pixels, -1), weight[index])
    return total

def depthwise(field, weight, rate):
    pieces = offsets(field, rate)
    pixels = field.shape[0] * field.shape[1]
    total = jnp.zeros((pixels, field.shape[2]), jnp.float32)
    for index in range(9):
        total = total + pieces[index].reshape(pixels, -1) * weight[index]
    return total
conv_checked = jax.checkpoint(dilated_conv, static_argnums=(2,))
depth_checked = jax.checkpoint(depthwise, static_argnums=(2,))

def forward(features, reduce_weight, dilated_weight, expand_weight, mid_gain, mid_shift, out_gain, out_shift, aspp_point, sep_depth, sep_point, pool_weight, proj_weight, aspp_gain, aspp_shift, head_weight, head_bias, task_scales, crop_ids, labels, boundary_mask, valid_mask, geometry_target):
    height, width, channels = features.shape
    pixels = height * width
    flat = features.reshape(pixels, channels)
    reduced = low_back(product(flat, reduce_weight))
    first_act = low(sigmoid_linear(batch_norm(reduced, mid_gain[0], mid_shift[0])))
    dilated = low_back(conv_checked(first_act.reshape(height, width, -1), dilated_weight, MID_RATE))
    second_act = low(sigmoid_linear(batch_norm(dilated, mid_gain[1], mid_shift[1])))
    expanded = low_back(product(second_act, expand_weight))
    trunk = low(sigmoid_linear(batch_norm(expanded, out_gain, out_shift) + flat))
    field = trunk.reshape(height, width, channels)
    branch_list = [low(sigmoid_linear(batch_norm(low_back(product(trunk, aspp_point)), aspp_gain[0], aspp_shift[0])))]
    for index in range(3):
        separable = low(low_back(depth_checked(field, sep_depth[index], BASE_RATE * (index + 1))))
        branch_pre = low_back(product(separable, sep_point[index]))
        branch_list.append(low(sigmoid_linear(batch_norm(branch_pre, aspp_gain[index + 1], aspp_shift[index + 1]))))
    members = (crop_ids.reshape(pixels)[:, None] == jnp.arange(CROPS)[None, :]).astype(jnp.float32)
    crop_count = lax.optimization_barrier(jnp.sum(members, axis=0))
    pooled = low(product(members.T, trunk) / crop_count[:, None])
    crop_act = low(sigmoid_linear(low_back(product(pooled, pool_weight))))
    branch_list.append(product(members, crop_act))
    joined = jnp.concatenate(branch_list, axis=1)
    united = low(sigmoid_linear(batch_norm(low_back(product(joined, proj_weight)), aspp_gain[4], aspp_shift[4])))
    heads = low_back(product(united, head_weight)) + head_bias
    logits = heads[:, :CLASSES]
    top = lax.optimization_barrier(jnp.max(logits, axis=1, keepdims=True))
    log_total = top[:, 0] + jnp.log(lax.optimization_barrier(jnp.sum(jnp.exp(logits - top), axis=1)))
    label_hot = (labels.reshape(pixels)[:, None] == jnp.arange(CLASSES)[None, :]).astype(jnp.float32)
    picked = lax.optimization_barrier(jnp.sum(logits * label_hot, axis=1))
    keep = (1 - boundary_mask.reshape(pixels)).astype(jnp.float32)
    valid = valid_mask.reshape(pixels).astype(jnp.float32)
    target = geometry_target.reshape(4, pixels)
    depth_error = heads[:, CLASSES] - target[0]
    normal_error = heads[:, CLASSES + 1:] - target[1:].T
    semantic = jnp.sum(keep * (log_total - picked)) / jnp.sum(keep)
    depth_loss = jnp.sum(valid * (jnp.sqrt(depth_error * depth_error + 1.0) - 1.0)) / jnp.sum(valid)
    normal_loss = jnp.sum(valid * lax.optimization_barrier(jnp.sum(normal_error * normal_error, axis=1))) / jnp.sum(valid)
    losses = jnp.stack([semantic, depth_loss, normal_loss])
    return jnp.sum(jnp.exp(task_scales) * losses - task_scales)

def reference(features, reduce_weight, dilated_weight, expand_weight, mid_gain, mid_shift, out_gain, out_shift, aspp_point, sep_depth, sep_point, pool_weight, proj_weight, aspp_gain, aspp_shift, head_weight, head_bias, task_scales, crop_ids, labels, boundary_mask, valid_mask, geometry_target):
    floats = (features, reduce_weight, dilated_weight, expand_weight, mid_gain, mid_shift, out_gain, out_shift, aspp_point, sep_depth, sep_point, pool_weight, proj_weight, aspp_gain, aspp_shift, head_weight, head_bias, task_scales)
    floats = tuple((item.astype(jnp.float32) for item in floats))
    target = geometry_target.astype(jnp.float32)

    def objective_of(*params):
        return forward(*params, crop_ids, labels, boundary_mask, valid_mask, target)
    objective, pullback = jax.vjp(objective_of, *floats)
    grads = pullback(jnp.ones((), jnp.float32))
    return (objective, grads[0].astype(jnp.bfloat16), grads[1], grads[2], grads[3], grads[4], grads[5], grads[6], grads[7], grads[8], grads[9], grads[10], grads[11], grads[12], grads[13], grads[14], grads[15], grads[16], grads[17])
```

```python
import functools

import jax
import jax.numpy as jnp
from jax import lax
from jax.experimental import pallas as pl
from jax.experimental.pallas import tpu as pltpu
from jax.sharding import PartitionSpec as P

CLASSES = 13
CROPS = 16
MID_RATE = 4
BASE_RATE = 12
LANES = 128

EPS = 1e-05
MESH = pl.DeviceIdType.MESH


def gather_kernel(rows, cols, x_ref, out_ref, send, recv):
    devices = rows * cols
    me = lax.axis_index("rows") * cols + lax.axis_index("cols")
    barrier = pltpu.get_barrier_semaphore()

    def peer(step):
        other = lax.rem(me + step, devices)
        return (other // cols, lax.rem(other, cols))

    def greet(step, carry):
        pl.semaphore_signal(barrier, inc=1, device_id=peer(step), device_id_type=MESH)
        return carry

    lax.fori_loop(1, devices, greet, 0)
    out_ref[me] = x_ref[...]
    pl.semaphore_wait(barrier, devices - 1)

    def go(step, carry):
        pltpu.make_async_remote_copy(
            x_ref, out_ref.at[me], send, recv, device_id=peer(step), device_id_type=MESH
        ).start()
        return carry

    lax.fori_loop(1, devices, go, 0)
    others = out_ref.at[pl.ds(0, devices - 1)]
    pltpu.make_async_remote_copy(
        others, others, send, recv, device_id=peer(1), device_id_type=MESH
    ).wait()


def gather_all(value, collective):
    rows, cols = lax.axis_size("rows"), lax.axis_size("cols")
    flat = value.reshape(-1, LANES)
    gathered = pl.pallas_call(
        functools.partial(gather_kernel, rows, cols),
        out_shape=jax.ShapeDtypeStruct((rows * cols,) + flat.shape, flat.dtype),
        in_specs=[pl.BlockSpec(memory_space=pltpu.VMEM)],
        out_specs=pl.BlockSpec(memory_space=pltpu.VMEM),
        scratch_shapes=[pltpu.SemaphoreType.DMA, pltpu.SemaphoreType.DMA],
        compiler_params=pltpu.CompilerParams(collective_id=collective, has_side_effects=True),
        name="gather_all",
    )(flat)
    return gathered.reshape((rows * cols,) + value.shape)


def extended(block, sides, width):
    for axis, dim in sides:
        count = lax.axis_size(axis)
        forward = [(i, i + 1) for i in range(count - 1)]
        backward = [(target, source) for source, target in forward]
        low = lax.ppermute(
            lax.slice_in_dim(block, block.shape[dim] - width, None, axis=dim), axis, forward
        )
        high = lax.ppermute(lax.slice_in_dim(block, 0, width, axis=dim), axis, backward)
        block = jnp.concatenate([low, block, high], axis=dim)
    return block


def from_behind(value, axis, steps):
    count = lax.axis_size(axis)
    initial, last = (max(0, -steps), min(count, count - steps))
    return lax.ppermute(value, axis, [(source, source + steps) for source in range(initial, last)])


def sigmoid_linear(value):
    return value * jax.nn.sigmoid(value)


def gate_slope(value):
    sigma = jax.nn.sigmoid(value)
    return sigma * (1.0 + value * (1.0 - sigma))


def matmul(left, right):
    return jnp.dot(left, right, preferred_element_type=jnp.float32)


def fetch(block, rate):
    step = rate // block.shape[0]
    widened = extended(block, (("cols", 1),), rate)
    moved = {}
    for sign in (1, -1):
        moved[sign] = from_behind(widened, "rows", sign * step)
    return (moved[1], widened, moved[-1])


def offset_piece(near, index, rate, width):
    start = rate + (index % 3 - 1) * rate
    rows_part = near[index // 3]
    return rows_part[:, start : start + width, :].reshape(-1, rows_part.shape[2])


def local_stats(value):
    mean = jnp.mean(value, axis=1)
    centered = value - mean[:, None, :]
    return mean, jnp.sum(centered * centered, axis=1)


def merged_stats(means, squares, share, count):
    center = jnp.mean(means, axis=0)
    apart = means - center
    spread = (jnp.sum(squares, axis=0) + share * jnp.sum(apart * apart, axis=0)) / count
    return center, lax.rsqrt(spread + EPS)


def pack(*values):
    flat = jnp.concatenate([value.reshape(-1) for value in values])
    unit = 8 * LANES
    short = -flat.shape[0] % unit
    return jnp.pad(flat, (0, short)) if short else flat


def unpack(flat, *shapes):
    out, at = [], 0
    for shape in shapes:
        size = 1
        for extent in shape:
            size *= extent
        out.append(flat[..., at : at + size].reshape(flat.shape[:-1] + tuple(shape)))
        at += size
    return out


def shared_sums(collective, *values):
    flat = jnp.sum(gather_all(pack(*values), collective), axis=0)
    return unpack(flat, *[value.shape for value in values])


def normalize(value, center, scale):
    return (value - center[:, None, :]) * scale[:, None, :]


def norm_backward(upstream, normed, scale, gain, count, collective, *extra):
    shift_grad, gain_grad, *extra = shared_sums(
        collective, jnp.sum(upstream, axis=1), jnp.sum(upstream * normed, axis=1), *extra
    )
    inner = upstream - shift_grad[:, None, :] / count - normed * (gain_grad / count)[:, None, :]
    return (inner * (gain * scale)[:, None, :], gain_grad, shift_grad, *extra)


def on_device(
    features,
    reduce_weight,
    dilated_weight,
    expand_weight,
    mid_gain,
    mid_shift,
    out_gain,
    out_shift,
    aspp_point,
    sep_depth,
    sep_point,
    pool_weight,
    proj_weight,
    aspp_gain,
    aspp_shift,
    head_weight,
    head_bias,
    task_scales,
    crop_ids,
    labels,
    boundary_mask,
    valid_mask,
    geometry_target,
):
    height, width, channels = features.shape
    pixels = height * width
    share = float(pixels)
    count = float(pixels * lax.axis_size("rows") * lax.axis_size("cols"))
    highest = lax.Precision.HIGHEST
    low = jnp.bfloat16
    aspp_width = proj_weight.shape[1]
    crop_flat = crop_ids.reshape(pixels)
    members = (crop_flat[:, None] == jnp.arange(CROPS)[None, :]).astype(low)
    members_wide = members.astype(jnp.float32)
    keep = (1 - boundary_mask.reshape(pixels)).astype(jnp.float32)
    valid = valid_mask.reshape(pixels).astype(jnp.float32)
    flat = features.reshape(pixels, channels)
    reduced = matmul(flat, reduce_weight)[None]
    mean, square = local_stats(reduced)
    own_counts = (jnp.sum(members_wide, axis=0), jnp.sum(keep)[None], jnp.sum(valid)[None])
    gathered = gather_all(pack(mean, square, *own_counts), 0)
    means, squares, crop_counts, keeps, valids = unpack(
        gathered, mean.shape, square.shape, (CROPS,), (1,), (1,)
    )
    center, scale_one = merged_stats(means, squares, share, count)
    crop_count, keep_count, valid_count = (
        jnp.sum(crop_counts, axis=0), jnp.sum(keeps), jnp.sum(valids)
    )
    normed_one = normalize(reduced, center, scale_one)
    gated_one = normed_one[0] * mid_gain[0] + mid_shift[0]
    first_act = sigmoid_linear(gated_one).astype(low)
    first_field = first_act.reshape(height, width, -1)
    first_near = fetch(first_field, MID_RATE)
    dilated = jnp.zeros((pixels, dilated_weight.shape[2]), jnp.float32)
    for index in range(9):
        dilated = dilated + matmul(
            offset_piece(first_near, index, MID_RATE, width), dilated_weight[index]
        )
    dilated = dilated[None]
    mean, square = local_stats(dilated)
    means, squares = unpack(gather_all(pack(mean, square), 1), mean.shape, square.shape)
    center, scale_two = merged_stats(means, squares, share, count)
    normed_two = normalize(dilated, center, scale_two)
    gated_two = normed_two[0] * mid_gain[1] + mid_shift[1]
    second_act = sigmoid_linear(gated_two).astype(low)
    expanded = matmul(second_act, expand_weight)[None]
    mean, square = local_stats(expanded)
    means, squares = unpack(gather_all(pack(mean, square), 2), mean.shape, square.shape)
    center, scale_three = merged_stats(means, squares, share, count)
    normed_three = normalize(expanded, center, scale_three)
    pre_trunk = normed_three[0] * out_gain + out_shift + flat.astype(jnp.float32)
    trunk = sigmoid_linear(pre_trunk).astype(low)
    taps = sep_depth.astype(jnp.float32)[:, :, :, None] * sep_point.astype(jnp.float32)[:, None, :, :]
    taps = jnp.transpose(taps.astype(low), (0, 2, 1, 3)).reshape(3, channels, 9 * aspp_width)
    branch_pre = [matmul(trunk, aspp_point)]
    for index in range(3):
        rate = BASE_RATE * (index + 1)
        step = rate // height
        made = matmul(trunk, taps[index]).astype(low).reshape(height, width, 3, 3, aspp_width)
        side = lax.axis_size("cols")
        up = [(i, i + 1) for i in range(side - 1)]
        down = [(i + 1, i) for i in range(side - 1)]
        before = lax.ppermute(made[:, width - rate :, :, 0, :], "cols", up)
        after = lax.ppermute(made[:, :rate, :, 2, :], "cols", down)
        wide = jnp.float32
        rows_sum = (
            made[:, :, :, 1].astype(wide)
            + jnp.concatenate([before, made[:, : width - rate, :, 0]], axis=1).astype(wide)
            + jnp.concatenate([made[:, rate:, :, 2], after], axis=1).astype(wide)
        )
        above = from_behind(rows_sum[:, :, 0].astype(low), "rows", step).astype(wide)
        below = from_behind(rows_sum[:, :, 2].astype(low), "rows", -step).astype(wide)
        branch_pre.append((rows_sum[:, :, 1] + above + below).reshape(pixels, aspp_width))
    stacked = jnp.stack(branch_pre)
    local_sums = jnp.einsum("pk,pc->kc", members, trunk, preferred_element_type=jnp.float32)
    mean, square = local_stats(stacked)
    crop_part = jnp.dot(local_sums, pool_weight.astype(jnp.float32), precision=highest)
    means, squares, crop_parts = unpack(
        gather_all(pack(mean, square, crop_part), 3), mean.shape, square.shape, crop_part.shape
    )
    center, scale_branch = merged_stats(means, squares, share, count)
    normed_branch = normalize(stacked, center, scale_branch)
    gated_branch = normed_branch * aspp_gain[:4, None, :] + aspp_shift[:4, None, :]
    branch_act = sigmoid_linear(gated_branch).astype(low)
    crop_pre = jnp.sum(crop_parts, axis=0) / crop_count[:, None]
    crop_act = sigmoid_linear(crop_pre).astype(low)
    crop_spread = matmul(members, crop_act).astype(low)
    joined = jnp.concatenate(
        [branch_act[0], branch_act[1], branch_act[2], branch_act[3], crop_spread], axis=1
    )
    projected = matmul(joined, proj_weight)[None]
    mean, square = local_stats(projected)
    means, squares = unpack(gather_all(pack(mean, square), 4), mean.shape, square.shape)
    center, scale_proj = merged_stats(means, squares, share, count)
    normed_proj = normalize(projected, center, scale_proj)
    gated_proj = normed_proj[0] * aspp_gain[4] + aspp_shift[4]
    united = sigmoid_linear(gated_proj).astype(low)
    heads = matmul(united, head_weight) + head_bias
    logits = heads[:, :CLASSES]
    top = jnp.max(logits, axis=1, keepdims=True)
    exps = jnp.exp(logits - top)
    totals = jnp.sum(exps, axis=1)
    label_hot = (labels.reshape(pixels)[:, None] == jnp.arange(CLASSES)[None, :]).astype(
        jnp.float32
    )
    picked = jnp.sum(logits * label_hot, axis=1)
    target = geometry_target.reshape(4, pixels)
    depth_error = heads[:, CLASSES] - target[0]
    root = jnp.sqrt(depth_error * depth_error + 1.0)
    normal_error = heads[:, CLASSES + 1 :] - target[1:].T
    local_losses = jnp.stack(
        [
            jnp.sum(keep * (top[:, 0] + jnp.log(totals) - picked)),
            jnp.sum(valid * (root - 1.0)),
            jnp.sum(valid * jnp.sum(normal_error * normal_error, axis=1)),
        ]
    )
    counts = jnp.stack([keep_count, valid_count, valid_count])
    scale_exp = jnp.exp(task_scales)
    factor = scale_exp / counts
    logit_grad = factor[0] * keep[:, None] * (exps / totals[:, None] - label_hot)
    depth_grad = factor[1] * valid * depth_error / root
    normal_grad = factor[2] * valid[:, None] * 2.0 * normal_error
    head_grad = jnp.concatenate([logit_grad, depth_grad[:, None], normal_grad], axis=1)
    head_low = head_grad.astype(low)
    head_weight_part = jnp.einsum("pc,pk->ck", united, head_low, preferred_element_type=jnp.float32)
    united_grad = jnp.einsum("pk,ck->pc", head_low, head_weight, preferred_element_type=jnp.float32)
    proj_grad, proj_gain_grad, proj_shift_grad, loss_sums, grad_head_bias = norm_backward(
        (united_grad * gate_slope(gated_proj))[None], normed_proj, scale_proj, aspp_gain[4:5], count,
        5, local_losses, jnp.sum(head_grad, axis=0),
    )
    losses = loss_sums / counts
    objective = jnp.sum(scale_exp * losses - task_scales)
    grad_scales = scale_exp * losses - 1.0
    proj_low = proj_grad[0].astype(low)
    grad_proj_weight = jnp.einsum("pc,pd->cd", joined, proj_low, preferred_element_type=jnp.float32)
    joined_grad = jnp.einsum("pd,cd->pc", proj_low, proj_weight, preferred_element_type=jnp.float32)
    branch_up = jnp.stack(
        [joined_grad[:, branch * aspp_width : (branch + 1) * aspp_width] for branch in range(4)]
    )
    crop_local = jnp.einsum(
        "pk,pc->kc", members_wide, joined_grad[:, 4 * aspp_width :], precision=highest
    )
    branch_grad, branch_gain_grad, branch_shift_grad, crop_total = norm_backward(
        branch_up * gate_slope(gated_branch), normed_branch, scale_branch, aspp_gain[:4], count,
        6, crop_local,
    )
    branch_low = branch_grad.astype(low)
    crop_low = (crop_total * gate_slope(crop_pre)).astype(low)
    pooled = (lax.psum(local_sums, ("rows", "cols")) / crop_count[:, None]).astype(low)
    grad_pool_weight = jnp.einsum("kc,kd->cd", pooled, crop_low, preferred_element_type=jnp.float32)
    pooled_grad = (
        jnp.einsum("kd,cd->kc", crop_low, pool_weight, preferred_element_type=jnp.float32)
        / crop_count[:, None]
    )
    trunk_grad = jnp.einsum(
        "pd,cd->pc", branch_low[0], aspp_point, preferred_element_type=jnp.float32
    )
    trunk_grad = trunk_grad + jnp.dot(members_wide, pooled_grad, precision=highest)
    grad_aspp_point = jnp.einsum(
        "pc,pd->cd", trunk, branch_low[0], preferred_element_type=jnp.float32
    )
    point_grads = []
    depth_grads = []
    for index in range(3):
        rate = BASE_RATE * (index + 1)
        near = fetch(branch_low[index + 1].reshape(height, width, aspp_width), rate)
        moved = jnp.concatenate(
            [offset_piece(near, 8 - tap, rate, width) for tap in range(9)], axis=1
        )
        trunk_grad = trunk_grad + jnp.einsum(
            "pd,cd->pc", moved, taps[index], preferred_element_type=jnp.float32
        )
        whole = jnp.einsum("pc,pd->cd", trunk, moved, preferred_element_type=jnp.float32)
        whole = whole.reshape(channels, 9, aspp_width)
        point_grads.append(jnp.sum(whole * sep_depth[index].T.astype(jnp.float32)[:, :, None], axis=1))
        depth_grads.append(
            jnp.sum(whole * sep_point[index].astype(jnp.float32)[:, None, :], axis=2).T
        )
    pre_grad = trunk_grad * gate_slope(pre_trunk)
    expand_grad, out_gain_grad, out_shift_grad = norm_backward(
        pre_grad[None], normed_three, scale_three, out_gain[None], count, 7
    )
    expand_low = expand_grad[0].astype(low)
    grad_expand_weight = jnp.einsum(
        "pc,pd->cd", second_act, expand_low, preferred_element_type=jnp.float32
    )
    second_grad = jnp.einsum(
        "pd,cd->pc", expand_low, expand_weight, preferred_element_type=jnp.float32
    )
    dilated_grad, two_gain_grad, two_shift_grad = norm_backward(
        (second_grad * gate_slope(gated_two))[None], normed_two, scale_two, mid_gain[1:2], count, 8
    )
    dilated_low = dilated_grad[0].astype(low)
    dilated_near = fetch(dilated_low.reshape(height, width, -1), MID_RATE)
    first_grad = jnp.zeros((pixels, dilated_weight.shape[1]), jnp.float32)
    dilated_grads = []
    for tap in range(9):
        dilated_grads.append(
            jnp.einsum(
                "pc,pd->cd",
                offset_piece(first_near, tap, MID_RATE, width),
                dilated_low,
                preferred_element_type=jnp.float32,
            )
        )
        first_grad = first_grad + jnp.einsum(
            "pd,cd->pc",
            offset_piece(dilated_near, 8 - tap, MID_RATE, width),
            dilated_weight[tap],
            preferred_element_type=jnp.float32,
        )
    reduced_grad, one_gain_grad, one_shift_grad = norm_backward(
        (first_grad * gate_slope(gated_one))[None], normed_one, scale_one, mid_gain[0:1], count, 9
    )
    reduced_low = reduced_grad[0].astype(low)
    grad_reduce_weight = jnp.einsum(
        "pc,pd->cd", flat, reduced_low, preferred_element_type=jnp.float32
    )
    input_grad = (
        jnp.einsum("pd,cd->pc", reduced_low, reduce_weight, preferred_element_type=jnp.float32)
        + pre_grad
    )
    grad_features = input_grad.astype(low).reshape(height, width, channels)
    parts = (
        grad_reduce_weight,
        jnp.stack(dilated_grads),
        grad_expand_weight,
        grad_aspp_point,
        jnp.stack(depth_grads),
        jnp.stack(point_grads),
        grad_proj_weight,
        jnp.pad(head_weight_part, ((0, 0), (0, LANES - head_weight_part.shape[1]))),
    )
    summed = lax.psum(tuple(part.astype(low) for part in parts), ("rows", "cols"))
    summed = [part.astype(jnp.float32) for part in summed]
    grad_mid_gain = jnp.concatenate([one_gain_grad, two_gain_grad], axis=0)
    grad_mid_shift = jnp.concatenate([one_shift_grad, two_shift_grad], axis=0)
    grad_aspp_gain = jnp.concatenate([branch_gain_grad, proj_gain_grad], axis=0)
    grad_aspp_shift = jnp.concatenate([branch_shift_grad, proj_shift_grad], axis=0)
    return (
        objective,
        grad_features,
        summed[0],
        summed[1],
        summed[2],
        grad_mid_gain,
        grad_mid_shift,
        out_gain_grad[0],
        out_shift_grad[0],
        summed[3],
        summed[4],
        summed[5],
        grad_pool_weight,
        summed[6],
        grad_aspp_gain,
        grad_aspp_shift,
        summed[7][:, : head_weight.shape[1]],
        grad_head_bias,
        grad_scales,
    )


def solution(mesh):
    in_specs = (
        P("rows", "cols", None),
        P(),
        P(),
        P(),
        P(),
        P(),
        P(),
        P(),
        P(),
        P(),
        P(),
        P(),
        P(),
        P(),
        P(),
        P(),
        P(),
        P(),
        P("rows", "cols"),
        P("rows", "cols"),
        P("rows", "cols"),
        P("rows", "cols"),
        P(None, "rows", "cols"),
    )
    out_specs = (
        P(),
        P("rows", "cols", None),
        P(),
        P(),
        P(),
        P(),
        P(),
        P(),
        P(),
        P(),
        P(),
        P(),
        P(),
        P(),
        P(),
        P(),
        P(),
        P(),
        P(),
    )
    return jax.shard_map(
        on_device, mesh=mesh, in_specs=in_specs, out_specs=out_specs, check_vma=False
    )
```

```python
import functools

import jax
import jax.numpy as jnp
from jax import lax
from jax.experimental import pallas as pl
from jax.experimental.pallas import tpu as pltpu
from jax.sharding import PartitionSpec as P

CLASSES = 13
CROPS = 16
MID_RATE = 4
BASE_RATE = 12
LANES = 128

EPS = 1e-05
MESH = pl.DeviceIdType.MESH


def gather_kernel(rows, cols, x_ref, out_ref, send, recv):
    devices = rows * cols
    me = lax.axis_index("rows") * cols + lax.axis_index("cols")
    barrier = pltpu.get_barrier_semaphore()

    def peer(step):
        other = lax.rem(me + step, devices)
        return (other // cols, lax.rem(other, cols))

    def greet(step, carry):
        pl.semaphore_signal(barrier, inc=1, device_id=peer(step), device_id_type=MESH)
        return carry

    lax.fori_loop(1, devices, greet, 0)
    out_ref[me] = x_ref[...]
    pl.semaphore_wait(barrier, devices - 1)

    def go(step, carry):
        pltpu.make_async_remote_copy(
            x_ref, out_ref.at[me], send, recv, device_id=peer(step), device_id_type=MESH
        ).start()
        return carry

    lax.fori_loop(1, devices, go, 0)
    others = out_ref.at[pl.ds(0, devices - 1)]
    pltpu.make_async_remote_copy(
        others, others, send, recv, device_id=peer(1), device_id_type=MESH
    ).wait()


def gather_all(value, collective):
    rows, cols = lax.axis_size("rows"), lax.axis_size("cols")
    flat = value.reshape(-1, LANES)
    gathered = pl.pallas_call(
        functools.partial(gather_kernel, rows, cols),
        out_shape=jax.ShapeDtypeStruct((rows * cols,) + flat.shape, flat.dtype),
        in_specs=[pl.BlockSpec(memory_space=pltpu.VMEM)],
        out_specs=pl.BlockSpec(memory_space=pltpu.VMEM),
        scratch_shapes=[pltpu.SemaphoreType.DMA, pltpu.SemaphoreType.DMA],
        compiler_params=pltpu.CompilerParams(collective_id=collective, has_side_effects=True),
        name="gather_all",
    )(flat)
    return gathered.reshape((rows * cols,) + value.shape)


def extended(block, sides, width):
    for axis, dim in sides:
        count = lax.axis_size(axis)
        forward = [(i, i + 1) for i in range(count - 1)]
        backward = [(target, source) for source, target in forward]
        low = lax.ppermute(
            lax.slice_in_dim(block, block.shape[dim] - width, None, axis=dim), axis, forward
        )
        high = lax.ppermute(lax.slice_in_dim(block, 0, width, axis=dim), axis, backward)
        block = jnp.concatenate([low, block, high], axis=dim)
    return block


def from_behind(value, axis, steps):
    count = lax.axis_size(axis)
    initial, last = (max(0, -steps), min(count, count - steps))
    return lax.ppermute(value, axis, [(source, source + steps) for source in range(initial, last)])


def sigmoid_linear(value):
    return value * jax.nn.sigmoid(value)


def gate_slope(value):
    sigma = jax.nn.sigmoid(value)
    return sigma * (1.0 + value * (1.0 - sigma))


def matmul(left, right):
    return jnp.dot(left, right, preferred_element_type=jnp.float32)


def fetch(block, rate):
    step = rate // block.shape[0]
    widened = extended(block, (("cols", 1),), rate)
    moved = {}
    for sign in (1, -1):
        moved[sign] = from_behind(widened, "rows", sign * step)
    return (moved[1], widened, moved[-1])


def offset_piece(near, index, rate, width):
    start = rate + (index % 3 - 1) * rate
    rows_part = near[index // 3]
    return rows_part[:, start : start + width, :].reshape(-1, rows_part.shape[2])


def local_stats(value):
    mean = jnp.mean(value, axis=1)
    centered = value - mean[:, None, :]
    return mean, jnp.sum(centered * centered, axis=1)


def merged_stats(means, squares, share, count):
    center = jnp.mean(means, axis=0)
    apart = means - center
    spread = (jnp.sum(squares, axis=0) + share * jnp.sum(apart * apart, axis=0)) / count
    return center, lax.rsqrt(spread + EPS)


def pack(*values):
    flat = jnp.concatenate([value.reshape(-1) for value in values])
    unit = 8 * LANES
    short = -flat.shape[0] % unit
    return jnp.pad(flat, (0, short)) if short else flat


def unpack(flat, *shapes):
    out, at = [], 0
    for shape in shapes:
        size = 1
        for extent in shape:
            size *= extent
        out.append(flat[..., at : at + size].reshape(flat.shape[:-1] + tuple(shape)))
        at += size
    return out


def shared_sums(collective, *values):
    flat = jnp.sum(gather_all(pack(*values), collective), axis=0)
    return unpack(flat, *[value.shape for value in values])


def normalize(value, center, scale):
    return (value - center[:, None, :]) * scale[:, None, :]


def norm_backward(upstream, normed, scale, gain, count, collective, *extra):
    shift_grad, gain_grad, *extra = shared_sums(
        collective, jnp.sum(upstream, axis=1), jnp.sum(upstream * normed, axis=1), *extra
    )
    inner = upstream - shift_grad[:, None, :] / count - normed * (gain_grad / count)[:, None, :]
    return (inner * (gain * scale)[:, None, :], gain_grad, shift_grad, *extra)


PAD = 48
VMEM_BYTES = 60 * 1024 * 1024


def place():
    rows, cols = lax.axis_size("rows"), lax.axis_size("cols")
    row, col = lax.axis_index("rows"), lax.axis_index("cols")
    return rows, cols, row, col, row * cols + col


def greet_all():
    rows, cols, row, col, me = place()
    barrier = pltpu.get_barrier_semaphore()

    def greet(step, carry):
        other = lax.rem(me + step, rows * cols)
        pl.semaphore_signal(
            barrier, inc=1, device_id=(other // cols, lax.rem(other, cols)), device_id_type=MESH
        )
        return carry

    lax.fori_loop(1, rows * cols, greet, 0)


def await_all():
    rows, cols = lax.axis_size("rows"), lax.axis_size("cols")
    pl.semaphore_wait(pltpu.get_barrier_semaphore(), rows * cols - 1)


def share(slots, sems):
    rows, cols, row, col, me = place()

    def go(step, carry):
        other = lax.rem(me + step, rows * cols)
        pltpu.make_async_remote_copy(
            slots.at[me],
            slots.at[me],
            sems.at[0],
            sems.at[1],
            device_id=(other // cols, lax.rem(other, cols)),
            device_id_type=MESH,
        ).start()
        return carry

    lax.fori_loop(1, rows * cols, go, 0)


def shared(slots, sems):
    rows, cols, row, col, me = place()
    others = slots.at[pl.ds(0, rows * cols - 1)]
    pltpu.make_async_remote_copy(
        others,
        others,
        sems.at[0],
        sems.at[1],
        device_id=(row, lax.rem(col + 1, cols)),
        device_id_type=MESH,
    ).wait()


def put_row(slots, me, at, vector):
    for part in range(vector.shape[1] // LANES):
        slots[me, at + part : at + part + 1, :] = vector[:, part * LANES : (part + 1) * LANES]


def take_row(table, at, width):
    parts = [table[at + part : at + part + 1, :] for part in range(width // LANES)]
    return parts[0] if len(parts) == 1 else jnp.concatenate(parts, axis=1)


def merged(slots, half, share_size, count):
    center = jnp.mean(slots[:, :half, :], axis=0)
    apart = slots[:, :half, :] - center[None]
    spread = jnp.sum(slots[:, half : 2 * half, :], axis=0) + share_size * jnp.sum(apart * apart, axis=0)
    return center, lax.rsqrt(spread / count + EPS)


def sigmoid(value):
    return 1.0 / (1.0 + jnp.exp(-value))


def across(left, right):
    return lax.dot_general(left, right, (((1,), (1,)), ((), ())), preferred_element_type=jnp.float32)


def down(left, right):
    return lax.dot_general(left, right, (((0,), (0,)), ((), ())), preferred_element_type=jnp.float32)


def pyramid_kernel(
    height,
    trunk,
    depth,
    sep_point,
    aspp_point,
    crop_part,
    crop_count,
    members,
    proj_weight,
    gains,
    shifts,
    head_weight,
    head_bias,
    factors,
    info,
    branch_low,
    proj_part,
    head_part,
    crop_local,
    crop_pre,
    sums_five,
    sums_four,
    field,
    send_main,
    recv_main,
    send_side,
    recv_side,
    pre,
    joined,
    crop_act,
    projected,
    united,
    head_low,
    upstream,
    proj_low,
    branch_up,
    crop_slots,
    four_slots,
    five_slots,
    back_five,
    back_four,
    main_sems,
    side_sems,
    crop_sems,
    four_sems,
    five_sems,
    back_five_sems,
    back_four_sems,
):
    rows, cols, row, col, me = place()
    low, wide = jnp.bfloat16, jnp.float32
    pixels = trunk.shape[0]
    width = pixels // height
    share_size = float(pixels)
    count = float(pixels * rows * cols)
    aspp = sep_point.shape[2]
    greet_all()

    def exists(target):
        return jnp.logical_and(target >= 0, target < rows)

    for index in range(3):
        step = BASE_RATE * (index + 1) // height
        for way in (0, 2):

            @pl.when(jnp.logical_not(exists(row - (1 - way) * step)))
            def _():
                recv_main[index, way] = jnp.zeros(recv_main.shape[2:], low)
                recv_side[index, way] = jnp.zeros(recv_side.shape[2:], low)

    half = crop_part.shape[0]
    crop_slots[me, :half, :] = crop_part[:, :LANES]
    crop_slots[me, half:, :] = crop_part[:, LANES:]
    pre[0] = jnp.dot(trunk[...], aspp_point[...], preferred_element_type=wide)
    await_all()
    share(crop_slots, crop_sems)
    side_from = pl.multiple_of((1 - col) * (PAD + width), 16)
    side_to = pl.multiple_of((1 - col) * (width - PAD), 16)

    def main_copy(index, way, step):
        return pltpu.make_async_remote_copy(
            send_main.at[index, way],
            recv_main.at[index, way],
            main_sems.at[0, index, way],
            main_sems.at[1, index, way],
            device_id=(row + (1 - way) * step, col),
            device_id_type=MESH,
        )

    def side_copy(index, way, step):
        return pltpu.make_async_remote_copy(
            send_side.at[index, way],
            recv_side.at[index, way],
            side_sems.at[0, index, way],
            side_sems.at[1, index, way],
            device_id=(row + (1 - way) * step, 1 - col),
            device_id_type=MESH,
        )

    for index in (2, 1, 0):
        rate = BASE_RATE * (index + 1)
        step = rate // height

        def one_way(turn, carry):
            way = lax.rem(2 * turn, 3)
            for sign in (0, 1, -1):
                tap = depth[pl.ds(index * 9 + 3 * way + 1 - sign, 1), :].astype(low)
                made = jnp.dot(trunk[...] * tap, sep_point[index], preferred_element_type=wide)
                for line in range(height):
                    part = made[line * width : (line + 1) * width, :]
                    if sign == 0:
                        field[line, PAD : PAD + width, :] = part
                        field[line, :PAD, :] = jnp.zeros((PAD, aspp), wide)
                        field[line, PAD + width :, :] = jnp.zeros((PAD, aspp), wide)
                    else:
                        at = PAD + sign * rate
                        field[line, at : at + width, :] += part
            send_side[index, way] = field[:, pl.ds(side_from, PAD), :].astype(low)

            @pl.when(way == 1)
            def _():
                for line in range(height):
                    pre[index + 1, line * width : (line + 1) * width, :] = field[
                        line, PAD : PAD + width, :
                    ]

            @pl.when(way != 1)
            def _():
                send_main[index, way] = field[:, PAD : PAD + width, :].astype(low)

                @pl.when(exists(row + (1 - way) * step))
                def _():
                    main_copy(index, way, step).start()

            @pl.when(exists(row + (1 - way) * step))
            def _():
                side_copy(index, way, step).start()

            return carry

        lax.fori_loop(0, 3, one_way, 0)

    def lines(body, carry=0):
        def run(line, carry):
            return body(line, pl.ds(pl.multiple_of(line * width, width), width), carry)

        return lax.fori_loop(0, height, run, carry)

    zero_row = jnp.zeros((1, aspp), wide)

    def statistics(value_of, slots, at, half_rows):
        total = lines(
            lambda line, span, acc: acc + jnp.sum(value_of(span), axis=0, keepdims=True), zero_row
        )
        mean = total / share_size

        def squares(line, span, acc):
            apart = value_of(span) - mean
            return acc + jnp.sum(apart * apart, axis=0, keepdims=True)

        put_row(slots, me, at, mean)
        put_row(slots, me, half_rows + at, lines(squares, zero_row))

    per = aspp // LANES
    statistics(lambda span: pre[0, span, :], four_slots, 0, 4 * per)
    for index in (2, 1, 0):
        step = BASE_RATE * (index + 1) // height
        for way in (0, 2, 1):

            @pl.when(exists(row - (1 - way) * step))
            def _():
                if way != 1:
                    main_copy(index, way, step).wait_recv()
                side_copy(index, way, step).wait_recv()

        def assemble(line, span, carry):
            pre[index + 1, span, :] += recv_main[index, 0, line].astype(wide) + recv_main[
                index, 2, line
            ].astype(wide)
            edge = pl.ds(pl.multiple_of(line * width + side_to, 16), PAD)
            pre[index + 1, edge, :] += (
                recv_side[index, 0, line].astype(wide)
                + recv_side[index, 1, line].astype(wide)
                + recv_side[index, 2, line].astype(wide)
            )
            return carry

        lines(assemble)
        statistics(lambda span: pre[index + 1, span, :], four_slots, per * (index + 1), 4 * per)
    share(four_slots, four_sems)
    shared(crop_slots, crop_sems)
    crop_total = jnp.sum(crop_slots[...], axis=0)
    crop_value = jnp.concatenate([crop_total[:half], crop_total[half:]], axis=1) / crop_count[...]
    crop_pre[...] = crop_value
    crop_act[...] = jnp.zeros(crop_act.shape, low)
    crop_act[:half, :] = (crop_value * sigmoid(crop_value)).astype(low)

    def spread(line, span, carry):
        joined[span, 4 * aspp :] = jnp.dot(
            members[span, :], crop_act[...], preferred_element_type=wide
        ).astype(low)
        return carry

    lines(spread)
    shared(four_slots, four_sems)
    center_four, scale_four = merged(four_slots, 4 * per, share_size, count)
    centers = [take_row(center_four, per * part, aspp) for part in range(4)]
    scales = [take_row(scale_four, per * part, aspp) for part in range(4)]

    def activate(line, span, carry):
        for part in range(4):
            normed = (pre[part, span, :] - centers[part]) * scales[part]
            gated = normed * gains[part : part + 1, :] + shifts[part : part + 1, :]
            joined[span, part * aspp : (part + 1) * aspp] = (gated * sigmoid(gated)).astype(low)
        return carry

    lines(activate)
    projected[...] = jnp.dot(joined[...], proj_weight[...], preferred_element_type=wide)
    five_slots[me] = jnp.zeros(five_slots.shape[1:], wide)
    statistics(lambda span: projected[span, :], five_slots, 0, per)
    share(five_slots, five_sems)
    shared(five_slots, five_sems)
    center_five, scale_five = merged(five_slots, per, share_size, count)
    center_five, scale_five = take_row(center_five, 0, aspp), take_row(scale_five, 0, aspp)
    gain_five, shift_five = gains[4:5, :], shifts[4:5, :]
    lane = lax.broadcasted_iota(jnp.int32, (width, LANES), 1)

    def heads_of(line, span, carry):
        losses, bias_sum, shift_sum, gain_sum = carry
        normed = (projected[span, :] - center_five) * scale_five
        gated = normed * gain_five + shift_five
        sigma = sigmoid(gated)
        act = (gated * sigma).astype(low)
        united[span, :] = act
        heads = jnp.dot(act, head_weight[...], preferred_element_type=wide) + head_bias[0:1, :]
        facts = info[span, :]
        label, keep, valid = facts[:, 0:1], facts[:, 1:2], facts[:, 2:3]
        is_class = lane < CLASSES
        hot = jnp.where(lane.astype(wide) == label, 1.0, 0.0)
        target = jnp.zeros((width, LANES), wide)
        for part in range(4):
            target = jnp.where(lane == CLASSES + part, facts[:, 3 + part : 4 + part], target)
        top = jnp.max(jnp.where(is_class, heads, -jnp.inf), axis=1, keepdims=True)
        exps = jnp.where(is_class, jnp.exp(heads - top), 0.0)
        totals = jnp.sum(exps, axis=1, keepdims=True)
        picked = jnp.sum(jnp.where(is_class, heads, 0.0) * hot, axis=1, keepdims=True)
        error = jnp.where(is_class, 0.0, heads - target)
        root = jnp.sqrt(error * error + 1.0)
        is_depth, is_normal = lane == CLASSES, jnp.logical_and(lane > CLASSES, lane < CLASSES + 4)
        semantic = keep * (top + jnp.log(totals) - picked)
        terms = jnp.where(lane == 0, semantic, 0.0)
        terms = jnp.where(is_depth, valid * (root - 1.0), terms)
        terms = jnp.where(is_normal, valid * error * error, terms)
        grad = jnp.where(is_class, keep * (exps / totals - hot), 0.0)
        grad = jnp.where(is_depth, valid * error / root, grad)
        grad = jnp.where(is_normal, valid * error, grad)
        grad = grad * factors[0:1, :]
        grad_low = grad.astype(low)
        head_low[span, :] = grad_low
        up = across(grad_low, head_weight[...]) * (sigma * (1.0 + gated * (1.0 - sigma)))
        upstream[span, :] = up
        return (
            losses + jnp.sum(terms, axis=0, keepdims=True),
            bias_sum + jnp.sum(grad, axis=0, keepdims=True),
            shift_sum + jnp.sum(up, axis=0, keepdims=True),
            gain_sum + jnp.sum(up * normed, axis=0, keepdims=True),
        )

    zero_lane = jnp.zeros((1, LANES), wide)
    losses, bias_sum, shift_sum, gain_sum = lines(
        heads_of, (zero_lane, zero_lane, zero_row, zero_row)
    )
    back_five[me] = jnp.zeros(back_five.shape[1:], wide)
    put_row(back_five, me, 0, shift_sum)
    put_row(back_five, me, per, gain_sum)
    put_row(back_five, me, 2 * per, losses)
    put_row(back_five, me, 2 * per + 1, bias_sum)
    share(back_five, back_five_sems)
    head_part[...] = down(united[...], head_low[...]).astype(low)
    shared(back_five, back_five_sems)
    total_five = jnp.sum(back_five[...], axis=0)
    sums_five[...] = total_five
    shift_mean = take_row(total_five, 0, aspp) / count
    gain_mean = take_row(total_five, per, aspp) / count

    def project_back(line, span, carry):
        normed = (projected[span, :] - center_five) * scale_five
        inner = upstream[span, :] - shift_mean - normed * gain_mean
        proj_low[span, :] = (inner * (gain_five * scale_five)).astype(low)
        return carry

    lines(project_back)
    for part in range(4):
        branch_up[part] = across(
            proj_low[...], proj_weight[part * aspp : (part + 1) * aspp, :]
        )
    crop_up = across(proj_low[...], proj_weight[4 * aspp :, :])
    crop_high = crop_up.astype(low)
    crop_rest = (crop_up - crop_high.astype(wide)).astype(low)
    crop_sum = down(members[...], crop_high) + down(members[...], crop_rest)
    crop_local[...] = crop_sum[:half, :]

    for part in range(4):

        def branch_sums(line, span, carry):
            shift_sum, gain_sum = carry
            normed = (pre[part, span, :] - centers[part]) * scales[part]
            gated = normed * gains[part : part + 1, :] + shifts[part : part + 1, :]
            sigma = sigmoid(gated)
            up = branch_up[part, span, :] * (sigma * (1.0 + gated * (1.0 - sigma)))
            branch_up[part, span, :] = up
            return (
                shift_sum + jnp.sum(up, axis=0, keepdims=True),
                gain_sum + jnp.sum(up * normed, axis=0, keepdims=True),
            )

        shift_sum, gain_sum = lines(branch_sums, (zero_row, zero_row))
        put_row(back_four, me, per * part, shift_sum)
        put_row(back_four, me, per * (4 + part), gain_sum)
    share(back_four, back_four_sems)
    proj_part[...] = down(joined[...], proj_low[...]).astype(low)
    shared(back_four, back_four_sems)
    total_four = jnp.sum(back_four[...], axis=0)
    sums_four[...] = total_four
    for part in range(4):
        shift_mean = take_row(total_four, per * part, aspp) / count
        gain_mean = take_row(total_four, per * (4 + part), aspp) / count
        factor = gains[part : part + 1, :] * scales[part]

        def branch_back(line, span, carry):
            normed = (pre[part, span, :] - centers[part]) * scales[part]
            inner = branch_up[part, span, :] - shift_mean - normed * gain_mean
            branch_low[part, span, :] = (inner * factor).astype(low)
            return carry

        lines(branch_back)
    for index in range(3):
        step = BASE_RATE * (index + 1) // height
        for way in range(3):

            @pl.when(exists(row + (1 - way) * step))
            def _():
                if way != 1:
                    main_copy(index, way, step).wait_send()
                side_copy(index, way, step).wait_send()


def pyramid(height, trunk, depth, sep_point, aspp_point, crop_part, crop_count, members, proj_weight,
            gains, shifts, head_weight, head_bias, factors, info):
    devices = lax.axis_size("rows") * lax.axis_size("cols")
    pixels = trunk.shape[0]
    width = pixels // height
    aspp = sep_point.shape[2]
    crops = crop_part.shape[0]
    low, wide = jnp.bfloat16, jnp.float32
    shape = jax.ShapeDtypeStruct
    whole = pl.BlockSpec(memory_space=pltpu.VMEM)
    joined = proj_weight.shape[0]
    per = aspp // LANES
    outs = (
        shape((4, pixels, aspp), low),
        shape((joined, aspp), low),
        shape((aspp, LANES), low),
        shape((crops, aspp), wide),
        shape((crops, aspp), wide),
        shape((8, LANES), wide),
        shape((8 * per, LANES), wide),
    )
    sems = pltpu.SemaphoreType.DMA
    return pl.pallas_call(
        functools.partial(pyramid_kernel, height),
        out_shape=outs,
        in_specs=[whole] * 14,
        out_specs=(whole,) * len(outs),
        scratch_shapes=[
            pltpu.VMEM((height, width + 2 * PAD, aspp), wide),
            pltpu.VMEM((3, 3, height, width, aspp), low),
            pltpu.VMEM((3, 3, height, width, aspp), low),
            pltpu.VMEM((3, 3, height, PAD, aspp), low),
            pltpu.VMEM((3, 3, height, PAD, aspp), low),
            pltpu.VMEM((4, pixels, aspp), wide),
            pltpu.VMEM((pixels, joined), low),
            pltpu.VMEM((LANES, aspp), low),
            pltpu.VMEM((pixels, aspp), wide),
            pltpu.VMEM((pixels, aspp), low),
            pltpu.VMEM((pixels, LANES), low),
            pltpu.VMEM((pixels, aspp), wide),
            pltpu.VMEM((pixels, aspp), low),
            pltpu.VMEM((4, pixels, aspp), wide),
            pltpu.VMEM((devices, 2 * crops, LANES), wide),
            pltpu.VMEM((devices, 8 * per, LANES), wide),
            pltpu.VMEM((devices, 8, LANES), wide),
            pltpu.VMEM((devices, 8, LANES), wide),
            pltpu.VMEM((devices, 8 * per, LANES), wide),
            sems((2, 3, 3)),
            sems((2, 3, 3)),
            sems((2,)),
            sems((2,)),
            sems((2,)),
            sems((2,)),
            sems((2,)),
        ],
        compiler_params=pltpu.CompilerParams(
            collective_id=10, has_side_effects=True, vmem_limit_bytes=VMEM_BYTES
        ),
        name="pyramid",
    )(trunk, depth, sep_point, aspp_point, crop_part, crop_count, members, proj_weight, gains, shifts,
      head_weight, head_bias, factors, info)


def on_device(
    features,
    reduce_weight,
    dilated_weight,
    expand_weight,
    mid_gain,
    mid_shift,
    out_gain,
    out_shift,
    aspp_point,
    sep_depth,
    sep_point,
    pool_weight,
    proj_weight,
    aspp_gain,
    aspp_shift,
    head_weight,
    head_bias,
    task_scales,
    crop_ids,
    labels,
    boundary_mask,
    valid_mask,
    geometry_target,
):
    height, width, channels = features.shape
    pixels = height * width
    share = float(pixels)
    count = float(pixels * lax.axis_size("rows") * lax.axis_size("cols"))
    highest = lax.Precision.HIGHEST
    low = jnp.bfloat16
    aspp_width = proj_weight.shape[1]
    crop_flat = crop_ids.reshape(pixels)
    members = (crop_flat[:, None] == jnp.arange(CROPS)[None, :]).astype(low)
    members_wide = members.astype(jnp.float32)
    keep = (1 - boundary_mask.reshape(pixels)).astype(jnp.float32)
    valid = valid_mask.reshape(pixels).astype(jnp.float32)
    flat = features.reshape(pixels, channels)
    reduced = matmul(flat, reduce_weight)[None]
    mean, square = local_stats(reduced)
    own_counts = (jnp.sum(members_wide, axis=0), jnp.sum(keep)[None], jnp.sum(valid)[None])
    gathered = gather_all(pack(mean, square, *own_counts), 0)
    means, squares, crop_counts, keeps, valids = unpack(
        gathered, mean.shape, square.shape, (CROPS,), (1,), (1,)
    )
    center, scale_one = merged_stats(means, squares, share, count)
    crop_count, keep_count, valid_count = (
        jnp.sum(crop_counts, axis=0), jnp.sum(keeps), jnp.sum(valids)
    )
    normed_one = normalize(reduced, center, scale_one)
    gated_one = normed_one[0] * mid_gain[0] + mid_shift[0]
    first_act = sigmoid_linear(gated_one).astype(low)
    first_field = first_act.reshape(height, width, -1)
    first_near = fetch(first_field, MID_RATE)
    dilated = jnp.zeros((pixels, dilated_weight.shape[2]), jnp.float32)
    for index in range(9):
        dilated = dilated + matmul(
            offset_piece(first_near, index, MID_RATE, width), dilated_weight[index]
        )
    dilated = dilated[None]
    mean, square = local_stats(dilated)
    means, squares = unpack(gather_all(pack(mean, square), 1), mean.shape, square.shape)
    center, scale_two = merged_stats(means, squares, share, count)
    normed_two = normalize(dilated, center, scale_two)
    gated_two = normed_two[0] * mid_gain[1] + mid_shift[1]
    second_act = sigmoid_linear(gated_two).astype(low)
    expanded = matmul(second_act, expand_weight)[None]
    mean, square = local_stats(expanded)
    means, squares = unpack(gather_all(pack(mean, square), 2), mean.shape, square.shape)
    center, scale_three = merged_stats(means, squares, share, count)
    normed_three = normalize(expanded, center, scale_three)
    pre_trunk = normed_three[0] * out_gain + out_shift + flat.astype(jnp.float32)
    trunk = sigmoid_linear(pre_trunk).astype(low)
    local_sums = jnp.einsum("pk,pc->kc", members, trunk, preferred_element_type=jnp.float32)
    crop_part = jnp.dot(local_sums, pool_weight.astype(jnp.float32), precision=highest)
    scale_exp = jnp.exp(task_scales)
    counts = jnp.stack([keep_count, valid_count, valid_count])
    factor = scale_exp / counts
    lane = jnp.arange(LANES)
    factors = jnp.where(
        lane < CLASSES, factor[0], jnp.where(lane == CLASSES, factor[1], 2.0 * factor[2])
    )
    outs = head_weight.shape[1]
    wide_row = ((0, 0), (0, LANES - outs))
    info = jnp.stack(
        [labels.reshape(pixels).astype(jnp.float32), keep, valid, *geometry_target.reshape(4, pixels)],
        axis=1,
    )
    branch_low, proj_part, head_part, crop_local, crop_pre, sums_five, sums_four = pyramid(
        height,
        trunk,
        jnp.pad(sep_depth.reshape(27, channels).astype(jnp.float32), ((0, 5), (0, 0))),
        sep_point,
        aspp_point,
        crop_part,
        jnp.broadcast_to(crop_count[:, None], (CROPS, aspp_width)),
        jnp.pad(members, ((0, 0), (0, LANES - CROPS))),
        proj_weight,
        jnp.pad(aspp_gain, ((0, 3), (0, 0))),
        jnp.pad(aspp_shift, ((0, 3), (0, 0))),
        jnp.pad(head_weight, wide_row),
        jnp.pad(jnp.broadcast_to(head_bias, (8, outs)), wide_row),
        jnp.broadcast_to(factors, (8, LANES)),
        jnp.pad(info, ((0, 0), (0, 1))),
    )
    per = aspp_width // LANES
    proj_shift_grad = sums_five[:per].reshape(1, aspp_width)
    proj_gain_grad = sums_five[per : 2 * per].reshape(1, aspp_width)
    loss_row = sums_five[2 * per]
    grad_head_bias = sums_five[2 * per + 1, :outs]
    branch_shift_grad = sums_four[: 4 * per].reshape(4, aspp_width)
    branch_gain_grad = sums_four[4 * per :].reshape(4, aspp_width)
    loss_sums = jnp.stack(
        [loss_row[0], loss_row[CLASSES], jnp.sum(loss_row[CLASSES + 1 : CLASSES + 4])]
    )
    losses = loss_sums / counts
    objective = jnp.sum(scale_exp * losses - task_scales)
    grad_scales = scale_exp * losses - 1.0
    (crop_total,) = shared_sums(3, crop_local)
    taps = sep_depth.astype(jnp.float32)[:, :, :, None] * sep_point.astype(jnp.float32)[:, None, :, :]
    taps = jnp.transpose(taps.astype(low), (0, 2, 1, 3)).reshape(3, channels, 9 * aspp_width)
    crop_low = (crop_total * gate_slope(crop_pre)).astype(low)
    pooled = (lax.psum(local_sums, ("rows", "cols")) / crop_count[:, None]).astype(low)
    grad_pool_weight = jnp.einsum("kc,kd->cd", pooled, crop_low, preferred_element_type=jnp.float32)
    pooled_grad = (
        jnp.einsum("kd,cd->kc", crop_low, pool_weight, preferred_element_type=jnp.float32)
        / crop_count[:, None]
    )
    trunk_grad = jnp.einsum(
        "pd,cd->pc", branch_low[0], aspp_point, preferred_element_type=jnp.float32
    )
    trunk_grad = trunk_grad + jnp.dot(members_wide, pooled_grad, precision=highest)
    grad_aspp_point = jnp.einsum(
        "pc,pd->cd", trunk, branch_low[0], preferred_element_type=jnp.float32
    )
    point_grads = []
    depth_grads = []
    for index in range(3):
        rate = BASE_RATE * (index + 1)
        near = fetch(branch_low[index + 1].reshape(height, width, aspp_width), rate)
        moved = jnp.concatenate(
            [offset_piece(near, 8 - tap, rate, width) for tap in range(9)], axis=1
        )
        trunk_grad = trunk_grad + jnp.einsum(
            "pd,cd->pc", moved, taps[index], preferred_element_type=jnp.float32
        )
        whole = jnp.einsum("pc,pd->cd", trunk, moved, preferred_element_type=jnp.float32)
        whole = whole.reshape(channels, 9, aspp_width)
        point_grads.append(jnp.sum(whole * sep_depth[index].T.astype(jnp.float32)[:, :, None], axis=1))
        depth_grads.append(
            jnp.sum(whole * sep_point[index].astype(jnp.float32)[:, None, :], axis=2).T
        )
    pre_grad = trunk_grad * gate_slope(pre_trunk)
    expand_grad, out_gain_grad, out_shift_grad = norm_backward(
        pre_grad[None], normed_three, scale_three, out_gain[None], count, 7
    )
    expand_low = expand_grad[0].astype(low)
    grad_expand_weight = jnp.einsum(
        "pc,pd->cd", second_act, expand_low, preferred_element_type=jnp.float32
    )
    second_grad = jnp.einsum(
        "pd,cd->pc", expand_low, expand_weight, preferred_element_type=jnp.float32
    )
    dilated_grad, two_gain_grad, two_shift_grad = norm_backward(
        (second_grad * gate_slope(gated_two))[None], normed_two, scale_two, mid_gain[1:2], count, 8
    )
    dilated_low = dilated_grad[0].astype(low)
    dilated_near = fetch(dilated_low.reshape(height, width, -1), MID_RATE)
    first_grad = jnp.zeros((pixels, dilated_weight.shape[1]), jnp.float32)
    dilated_grads = []
    for tap in range(9):
        dilated_grads.append(
            jnp.einsum(
                "pc,pd->cd",
                offset_piece(first_near, tap, MID_RATE, width),
                dilated_low,
                preferred_element_type=jnp.float32,
            )
        )
        first_grad = first_grad + jnp.einsum(
            "pd,cd->pc",
            offset_piece(dilated_near, 8 - tap, MID_RATE, width),
            dilated_weight[tap],
            preferred_element_type=jnp.float32,
        )
    reduced_grad, one_gain_grad, one_shift_grad = norm_backward(
        (first_grad * gate_slope(gated_one))[None], normed_one, scale_one, mid_gain[0:1], count, 9
    )
    reduced_low = reduced_grad[0].astype(low)
    grad_reduce_weight = jnp.einsum(
        "pc,pd->cd", flat, reduced_low, preferred_element_type=jnp.float32
    )
    input_grad = (
        jnp.einsum("pd,cd->pc", reduced_low, reduce_weight, preferred_element_type=jnp.float32)
        + pre_grad
    )
    grad_features = input_grad.astype(low).reshape(height, width, channels)
    parts = (
        grad_reduce_weight,
        jnp.stack(dilated_grads),
        grad_expand_weight,
        grad_aspp_point,
        jnp.stack(depth_grads),
        jnp.stack(point_grads),
        proj_part,
        head_part,
    )
    summed = lax.psum(tuple(part.astype(low) for part in parts), ("rows", "cols"))
    summed = [part.astype(jnp.float32) for part in summed]
    grad_mid_gain = jnp.concatenate([one_gain_grad, two_gain_grad], axis=0)
    grad_mid_shift = jnp.concatenate([one_shift_grad, two_shift_grad], axis=0)
    grad_aspp_gain = jnp.concatenate([branch_gain_grad, proj_gain_grad], axis=0)
    grad_aspp_shift = jnp.concatenate([branch_shift_grad, proj_shift_grad], axis=0)
    return (
        objective,
        grad_features,
        summed[0],
        summed[1],
        summed[2],
        grad_mid_gain,
        grad_mid_shift,
        out_gain_grad[0],
        out_shift_grad[0],
        summed[3],
        summed[4],
        summed[5],
        grad_pool_weight,
        summed[6],
        grad_aspp_gain,
        grad_aspp_shift,
        summed[7][:, : head_weight.shape[1]],
        grad_head_bias,
        grad_scales,
    )


def solution(mesh):
    in_specs = (
        P("rows", "cols", None),
        P(),
        P(),
        P(),
        P(),
        P(),
        P(),
        P(),
        P(),
        P(),
        P(),
        P(),
        P(),
        P(),
        P(),
        P(),
        P(),
        P(),
        P("rows", "cols"),
        P("rows", "cols"),
        P("rows", "cols"),
        P("rows", "cols"),
        P(None, "rows", "cols"),
    )
    out_specs = (
        P(),
        P("rows", "cols", None),
        P(),
        P(),
        P(),
        P(),
        P(),
        P(),
        P(),
        P(),
        P(),
        P(),
        P(),
        P(),
        P(),
        P(),
        P(),
        P(),
        P(),
    )
    return jax.shard_map(
        on_device, mesh=mesh, in_specs=in_specs, out_specs=out_specs, check_vma=False
    )
```

```python
import functools

import jax
import jax.numpy as jnp
from jax import lax
from jax.experimental import pallas as pl
from jax.experimental.pallas import tpu as pltpu
from jax.sharding import PartitionSpec as P

CLASSES = 13
CROPS = 16
MID_RATE = 4
BASE_RATE = 12
LANES = 128

EPS = 1e-05
MESH = pl.DeviceIdType.MESH


def gather_kernel(rows, cols, x_ref, out_ref, send, recv):
    devices = rows * cols
    me = lax.axis_index("rows") * cols + lax.axis_index("cols")
    barrier = pltpu.get_barrier_semaphore()

    def peer(step):
        other = lax.rem(me + step, devices)
        return (other // cols, lax.rem(other, cols))

    def greet(step, carry):
        pl.semaphore_signal(barrier, inc=1, device_id=peer(step), device_id_type=MESH)
        return carry

    lax.fori_loop(1, devices, greet, 0)
    out_ref[me] = x_ref[...]
    pl.semaphore_wait(barrier, devices - 1)

    def go(step, carry):
        pltpu.make_async_remote_copy(
            x_ref, out_ref.at[me], send, recv, device_id=peer(step), device_id_type=MESH
        ).start()
        return carry

    lax.fori_loop(1, devices, go, 0)
    others = out_ref.at[pl.ds(0, devices - 1)]
    pltpu.make_async_remote_copy(
        others, others, send, recv, device_id=peer(1), device_id_type=MESH
    ).wait()


def gather_all(value, collective):
    rows, cols = lax.axis_size("rows"), lax.axis_size("cols")
    flat = value.reshape(-1, LANES)
    gathered = pl.pallas_call(
        functools.partial(gather_kernel, rows, cols),
        out_shape=jax.ShapeDtypeStruct((rows * cols,) + flat.shape, flat.dtype),
        in_specs=[pl.BlockSpec(memory_space=pltpu.VMEM)],
        out_specs=pl.BlockSpec(memory_space=pltpu.VMEM),
        scratch_shapes=[pltpu.SemaphoreType.DMA, pltpu.SemaphoreType.DMA],
        compiler_params=pltpu.CompilerParams(collective_id=collective, has_side_effects=True),
        name="gather_all",
    )(flat)
    return gathered.reshape((rows * cols,) + value.shape)


def extended(block, sides, width):
    for axis, dim in sides:
        count = lax.axis_size(axis)
        forward = [(i, i + 1) for i in range(count - 1)]
        backward = [(target, source) for source, target in forward]
        low = lax.ppermute(
            lax.slice_in_dim(block, block.shape[dim] - width, None, axis=dim), axis, forward
        )
        high = lax.ppermute(lax.slice_in_dim(block, 0, width, axis=dim), axis, backward)
        block = jnp.concatenate([low, block, high], axis=dim)
    return block


def from_behind(value, axis, steps):
    count = lax.axis_size(axis)
    initial, last = (max(0, -steps), min(count, count - steps))
    return lax.ppermute(value, axis, [(source, source + steps) for source in range(initial, last)])


def sigmoid_linear(value):
    return value * jax.nn.sigmoid(value)


def gate_slope(value):
    sigma = jax.nn.sigmoid(value)
    return sigma * (1.0 + value * (1.0 - sigma))


def matmul(left, right):
    return jnp.dot(left, right, preferred_element_type=jnp.float32)


def fetch(block, rate):
    step = rate // block.shape[0]
    widened = extended(block, (("cols", 1),), rate)
    moved = {}
    for sign in (1, -1):
        moved[sign] = from_behind(widened, "rows", sign * step)
    return (moved[1], widened, moved[-1])


def offset_piece(near, index, rate, width):
    start = rate + (index % 3 - 1) * rate
    rows_part = near[index // 3]
    return rows_part[:, start : start + width, :].reshape(-1, rows_part.shape[2])


def local_stats(value):
    mean = jnp.mean(value, axis=1)
    centered = value - mean[:, None, :]
    return mean, jnp.sum(centered * centered, axis=1)


def merged_stats(means, squares, share, count):
    center = jnp.mean(means, axis=0)
    apart = means - center
    spread = (jnp.sum(squares, axis=0) + share * jnp.sum(apart * apart, axis=0)) / count
    return center, lax.rsqrt(spread + EPS)


def pack(*values):
    flat = jnp.concatenate([value.reshape(-1) for value in values])
    unit = 8 * LANES
    short = -flat.shape[0] % unit
    return jnp.pad(flat, (0, short)) if short else flat


def unpack(flat, *shapes):
    out, at = [], 0
    for shape in shapes:
        size = 1
        for extent in shape:
            size *= extent
        out.append(flat[..., at : at + size].reshape(flat.shape[:-1] + tuple(shape)))
        at += size
    return out


def shared_sums(collective, *values):
    flat = jnp.sum(gather_all(pack(*values), collective), axis=0)
    return unpack(flat, *[value.shape for value in values])


def normalize(value, center, scale):
    return (value - center[:, None, :]) * scale[:, None, :]


def norm_backward(upstream, normed, scale, gain, count, collective, *extra):
    shift_grad, gain_grad, *extra = shared_sums(
        collective, jnp.sum(upstream, axis=1), jnp.sum(upstream * normed, axis=1), *extra
    )
    inner = upstream - shift_grad[:, None, :] / count - normed * (gain_grad / count)[:, None, :]
    return (inner * (gain * scale)[:, None, :], gain_grad, shift_grad, *extra)


PAD = 48
VMEM_BYTES = 60 * 1024 * 1024


def place():
    rows, cols = lax.axis_size("rows"), lax.axis_size("cols")
    row, col = lax.axis_index("rows"), lax.axis_index("cols")
    return rows, cols, row, col, row * cols + col


def greet_all():
    rows, cols, row, col, me = place()
    barrier = pltpu.get_barrier_semaphore()

    def greet(step, carry):
        other = lax.rem(me + step, rows * cols)
        pl.semaphore_signal(
            barrier, inc=1, device_id=(other // cols, lax.rem(other, cols)), device_id_type=MESH
        )
        return carry

    lax.fori_loop(1, rows * cols, greet, 0)


def await_all():
    rows, cols = lax.axis_size("rows"), lax.axis_size("cols")
    pl.semaphore_wait(pltpu.get_barrier_semaphore(), rows * cols - 1)


def share(slots, sems):
    rows, cols, row, col, me = place()

    def go(step, carry):
        other = lax.rem(me + step, rows * cols)
        pltpu.make_async_remote_copy(
            slots.at[me],
            slots.at[me],
            sems.at[0],
            sems.at[1],
            device_id=(other // cols, lax.rem(other, cols)),
            device_id_type=MESH,
        ).start()
        return carry

    lax.fori_loop(1, rows * cols, go, 0)


def shared(slots, sems):
    rows, cols, row, col, me = place()
    others = slots.at[pl.ds(0, rows * cols - 1)]
    pltpu.make_async_remote_copy(
        others,
        others,
        sems.at[0],
        sems.at[1],
        device_id=(row, lax.rem(col + 1, cols)),
        device_id_type=MESH,
    ).wait()


def put_row(slots, me, at, vector):
    for part in range(vector.shape[1] // LANES):
        slots[me, at + part : at + part + 1, :] = vector[:, part * LANES : (part + 1) * LANES]


def take_row(table, at, width):
    parts = [table[at + part : at + part + 1, :] for part in range(width // LANES)]
    return parts[0] if len(parts) == 1 else jnp.concatenate(parts, axis=1)


def merged(slots, half, share_size, count):
    center = jnp.mean(slots[:, :half, :], axis=0)
    apart = slots[:, :half, :] - center[None]
    spread = jnp.sum(slots[:, half : 2 * half, :], axis=0) + share_size * jnp.sum(apart * apart, axis=0)
    return center, lax.rsqrt(spread / count + EPS)


def sigmoid(value):
    return 1.0 / (1.0 + jnp.exp(-value))


def across(left, right):
    return lax.dot_general(left, right, (((1,), (1,)), ((), ())), preferred_element_type=jnp.float32)


def down(left, right):
    return lax.dot_general(left, right, (((0,), (0,)), ((), ())), preferred_element_type=jnp.float32)


def pyramid_kernel(
    height,
    trunk,
    depth,
    sep_point,
    aspp_point,
    crop_part,
    crop_count,
    members,
    proj_weight,
    gains,
    shifts,
    head_weight,
    head_bias,
    factors,
    info,
    crop_sums,
    branch_low,
    proj_part,
    head_part,
    crop_local,
    crop_pre,
    sums_five,
    sums_four,
    crop_table,
    field,
    send_main,
    recv_main,
    send_side,
    recv_side,
    pre,
    joined,
    crop_act,
    projected,
    united,
    head_low,
    upstream,
    proj_low,
    branch_up,
    crop_slots,
    four_slots,
    five_slots,
    back_five,
    back_four,
    crop_pieces,
    main_sems,
    side_sems,
    crop_sems,
    four_sems,
    five_sems,
    back_five_sems,
    back_four_sems,
    piece_sems,
    table_sems,
):
    rows, cols, row, col, me = place()
    low, wide = jnp.bfloat16, jnp.float32
    pixels = trunk.shape[0]
    width = pixels // height
    share_size = float(pixels)
    count = float(pixels * rows * cols)
    aspp = sep_point.shape[2]
    greet_all()

    def exists(target):
        return jnp.logical_and(target >= 0, target < rows)

    for index in range(3):
        step = BASE_RATE * (index + 1) // height
        for way in (0, 2):

            @pl.when(jnp.logical_not(exists(row - (1 - way) * step)))
            def _():
                recv_main[index, way] = jnp.zeros(recv_main.shape[2:], low)
                recv_side[index, way] = jnp.zeros(recv_side.shape[2:], low)

    half = crop_part.shape[0]
    crop_slots[me, :half, :] = crop_part[:, :LANES]
    crop_slots[me, half:, :] = crop_part[:, LANES:]
    pre[0] = jnp.dot(trunk[...], aspp_point[...], preferred_element_type=wide)
    await_all()
    share(crop_slots, crop_sems)
    crop_pieces[me] = crop_sums[me]

    def scatter(step, carry):
        other = lax.rem(me + step, rows * cols)
        pltpu.make_async_remote_copy(
            crop_sums.at[other],
            crop_pieces.at[me],
            piece_sems.at[0],
            piece_sems.at[1],
            device_id=(other // cols, lax.rem(other, cols)),
            device_id_type=MESH,
        ).start()
        return carry

    lax.fori_loop(1, rows * cols, scatter, 0)
    side_from = pl.multiple_of((1 - col) * (PAD + width), 16)
    side_to = pl.multiple_of((1 - col) * (width - PAD), 16)

    def main_copy(index, way, step):
        return pltpu.make_async_remote_copy(
            send_main.at[index, way],
            recv_main.at[index, way],
            main_sems.at[0, index, way],
            main_sems.at[1, index, way],
            device_id=(row + (1 - way) * step, col),
            device_id_type=MESH,
        )

    def side_copy(index, way, step):
        return pltpu.make_async_remote_copy(
            send_side.at[index, way],
            recv_side.at[index, way],
            side_sems.at[0, index, way],
            side_sems.at[1, index, way],
            device_id=(row + (1 - way) * step, 1 - col),
            device_id_type=MESH,
        )

    for index in (2, 1, 0):
        rate = BASE_RATE * (index + 1)
        step = rate // height

        def one_way(turn, carry):
            way = lax.rem(2 * turn, 3)
            for sign in (0, 1, -1):
                tap = depth[pl.ds(index * 9 + 3 * way + 1 - sign, 1), :].astype(low)
                made = jnp.dot(trunk[...] * tap, sep_point[index], preferred_element_type=wide)
                for line in range(height):
                    part = made[line * width : (line + 1) * width, :]
                    if sign == 0:
                        field[line, PAD : PAD + width, :] = part
                        field[line, :PAD, :] = jnp.zeros((PAD, aspp), wide)
                        field[line, PAD + width :, :] = jnp.zeros((PAD, aspp), wide)
                    else:
                        at = PAD + sign * rate
                        field[line, at : at + width, :] += part
            send_side[index, way] = field[:, pl.ds(side_from, PAD), :].astype(low)

            @pl.when(way == 1)
            def _():
                for line in range(height):
                    pre[index + 1, line * width : (line + 1) * width, :] = field[
                        line, PAD : PAD + width, :
                    ]

            @pl.when(way != 1)
            def _():
                send_main[index, way] = field[:, PAD : PAD + width, :].astype(low)

                @pl.when(exists(row + (1 - way) * step))
                def _():
                    main_copy(index, way, step).start()

            @pl.when(exists(row + (1 - way) * step))
            def _():
                side_copy(index, way, step).start()

            return carry

        lax.fori_loop(0, 3, one_way, 0)

    def lines(body, carry=0):
        def run(line, carry):
            return body(line, pl.ds(pl.multiple_of(line * width, width), width), carry)

        return lax.fori_loop(0, height, run, carry)

    zero_row = jnp.zeros((1, aspp), wide)

    def statistics(value_of, slots, at, half_rows):
        total = lines(
            lambda line, span, acc: acc + jnp.sum(value_of(span), axis=0, keepdims=True), zero_row
        )
        mean = total / share_size

        def squares(line, span, acc):
            apart = value_of(span) - mean
            return acc + jnp.sum(apart * apart, axis=0, keepdims=True)

        put_row(slots, me, at, mean)
        put_row(slots, me, half_rows + at, lines(squares, zero_row))

    per = aspp // LANES
    statistics(lambda span: pre[0, span, :], four_slots, 0, 4 * per)
    for index in (2, 1, 0):
        step = BASE_RATE * (index + 1) // height
        for way in (0, 2, 1):

            @pl.when(exists(row - (1 - way) * step))
            def _():
                if way != 1:
                    main_copy(index, way, step).wait_recv()
                side_copy(index, way, step).wait_recv()

        def assemble(line, span, carry):
            pre[index + 1, span, :] += recv_main[index, 0, line].astype(wide) + recv_main[
                index, 2, line
            ].astype(wide)
            edge = pl.ds(pl.multiple_of(line * width + side_to, 16), PAD)
            pre[index + 1, edge, :] += (
                recv_side[index, 0, line].astype(wide)
                + recv_side[index, 1, line].astype(wide)
                + recv_side[index, 2, line].astype(wide)
            )
            return carry

        lines(assemble)
        statistics(lambda span: pre[index + 1, span, :], four_slots, per * (index + 1), 4 * per)
    share(four_slots, four_sems)
    shared(crop_pieces, piece_sems)
    crop_table[me] = jnp.sum(crop_pieces[...], axis=0)
    share(crop_table, table_sems)
    shared(crop_slots, crop_sems)
    crop_total = jnp.sum(crop_slots[...], axis=0)
    crop_value = jnp.concatenate([crop_total[:half], crop_total[half:]], axis=1) / crop_count[...]
    crop_pre[...] = crop_value
    crop_act[...] = jnp.zeros(crop_act.shape, low)
    crop_act[:half, :] = (crop_value * sigmoid(crop_value)).astype(low)

    def spread(line, span, carry):
        joined[span, 4 * aspp :] = jnp.dot(
            members[span, :], crop_act[...], preferred_element_type=wide
        ).astype(low)
        return carry

    lines(spread)
    shared(four_slots, four_sems)
    center_four, scale_four = merged(four_slots, 4 * per, share_size, count)
    centers = [take_row(center_four, per * part, aspp) for part in range(4)]
    scales = [take_row(scale_four, per * part, aspp) for part in range(4)]

    def activate(line, span, carry):
        for part in range(4):
            normed = (pre[part, span, :] - centers[part]) * scales[part]
            gated = normed * gains[part : part + 1, :] + shifts[part : part + 1, :]
            joined[span, part * aspp : (part + 1) * aspp] = (gated * sigmoid(gated)).astype(low)
        return carry

    lines(activate)
    projected[...] = jnp.dot(joined[...], proj_weight[...], preferred_element_type=wide)
    five_slots[me] = jnp.zeros(five_slots.shape[1:], wide)
    statistics(lambda span: projected[span, :], five_slots, 0, per)
    share(five_slots, five_sems)
    shared(five_slots, five_sems)
    center_five, scale_five = merged(five_slots, per, share_size, count)
    center_five, scale_five = take_row(center_five, 0, aspp), take_row(scale_five, 0, aspp)
    gain_five, shift_five = gains[4:5, :], shifts[4:5, :]
    lane = lax.broadcasted_iota(jnp.int32, (width, LANES), 1)

    def heads_of(line, span, carry):
        losses, bias_sum, shift_sum, gain_sum = carry
        normed = (projected[span, :] - center_five) * scale_five
        gated = normed * gain_five + shift_five
        sigma = sigmoid(gated)
        act = (gated * sigma).astype(low)
        united[span, :] = act
        heads = jnp.dot(act, head_weight[...], preferred_element_type=wide) + head_bias[0:1, :]
        facts = info[span, :]
        label, keep, valid = facts[:, 0:1], facts[:, 1:2], facts[:, 2:3]
        is_class = lane < CLASSES
        hot = jnp.where(lane.astype(wide) == label, 1.0, 0.0)
        target = jnp.zeros((width, LANES), wide)
        for part in range(4):
            target = jnp.where(lane == CLASSES + part, facts[:, 3 + part : 4 + part], target)
        top = jnp.max(jnp.where(is_class, heads, -jnp.inf), axis=1, keepdims=True)
        exps = jnp.where(is_class, jnp.exp(heads - top), 0.0)
        totals = jnp.sum(exps, axis=1, keepdims=True)
        picked = jnp.sum(jnp.where(is_class, heads, 0.0) * hot, axis=1, keepdims=True)
        error = jnp.where(is_class, 0.0, heads - target)
        root = jnp.sqrt(error * error + 1.0)
        is_depth, is_normal = lane == CLASSES, jnp.logical_and(lane > CLASSES, lane < CLASSES + 4)
        semantic = keep * (top + jnp.log(totals) - picked)
        terms = jnp.where(lane == 0, semantic, 0.0)
        terms = jnp.where(is_depth, valid * (root - 1.0), terms)
        terms = jnp.where(is_normal, valid * error * error, terms)
        grad = jnp.where(is_class, keep * (exps / totals - hot), 0.0)
        grad = jnp.where(is_depth, valid * error / root, grad)
        grad = jnp.where(is_normal, valid * error, grad)
        grad = grad * factors[0:1, :]
        grad_low = grad.astype(low)
        head_low[span, :] = grad_low
        up = across(grad_low, head_weight[...]) * (sigma * (1.0 + gated * (1.0 - sigma)))
        upstream[span, :] = up
        return (
            losses + jnp.sum(terms, axis=0, keepdims=True),
            bias_sum + jnp.sum(grad, axis=0, keepdims=True),
            shift_sum + jnp.sum(up, axis=0, keepdims=True),
            gain_sum + jnp.sum(up * normed, axis=0, keepdims=True),
        )

    zero_lane = jnp.zeros((1, LANES), wide)
    losses, bias_sum, shift_sum, gain_sum = lines(
        heads_of, (zero_lane, zero_lane, zero_row, zero_row)
    )
    back_five[me] = jnp.zeros(back_five.shape[1:], wide)
    put_row(back_five, me, 0, shift_sum)
    put_row(back_five, me, per, gain_sum)
    put_row(back_five, me, 2 * per, losses)
    put_row(back_five, me, 2 * per + 1, bias_sum)
    share(back_five, back_five_sems)
    head_part[...] = down(united[...], head_low[...]).astype(low)
    shared(back_five, back_five_sems)
    total_five = jnp.sum(back_five[...], axis=0)
    sums_five[...] = total_five
    shift_mean = take_row(total_five, 0, aspp) / count
    gain_mean = take_row(total_five, per, aspp) / count

    def project_back(line, span, carry):
        normed = (projected[span, :] - center_five) * scale_five
        inner = upstream[span, :] - shift_mean - normed * gain_mean
        proj_low[span, :] = (inner * (gain_five * scale_five)).astype(low)
        return carry

    lines(project_back)
    for part in range(4):
        branch_up[part] = across(
            proj_low[...], proj_weight[part * aspp : (part + 1) * aspp, :]
        )
    crop_up = across(proj_low[...], proj_weight[4 * aspp :, :])
    crop_high = crop_up.astype(low)
    crop_rest = (crop_up - crop_high.astype(wide)).astype(low)
    crop_sum = down(members[...], crop_high) + down(members[...], crop_rest)
    crop_local[...] = crop_sum[:half, :]

    for part in range(4):

        def branch_sums(line, span, carry):
            shift_sum, gain_sum = carry
            normed = (pre[part, span, :] - centers[part]) * scales[part]
            gated = normed * gains[part : part + 1, :] + shifts[part : part + 1, :]
            sigma = sigmoid(gated)
            up = branch_up[part, span, :] * (sigma * (1.0 + gated * (1.0 - sigma)))
            branch_up[part, span, :] = up
            return (
                shift_sum + jnp.sum(up, axis=0, keepdims=True),
                gain_sum + jnp.sum(up * normed, axis=0, keepdims=True),
            )

        shift_sum, gain_sum = lines(branch_sums, (zero_row, zero_row))
        put_row(back_four, me, per * part, shift_sum)
        put_row(back_four, me, per * (4 + part), gain_sum)
    share(back_four, back_four_sems)
    proj_part[...] = down(joined[...], proj_low[...]).astype(low)
    shared(back_four, back_four_sems)
    total_four = jnp.sum(back_four[...], axis=0)
    sums_four[...] = total_four
    for part in range(4):
        shift_mean = take_row(total_four, per * part, aspp) / count
        gain_mean = take_row(total_four, per * (4 + part), aspp) / count
        factor = gains[part : part + 1, :] * scales[part]

        def branch_back(line, span, carry):
            normed = (pre[part, span, :] - centers[part]) * scales[part]
            inner = branch_up[part, span, :] - shift_mean - normed * gain_mean
            branch_low[part, span, :] = (inner * factor).astype(low)
            return carry

        lines(branch_back)
    shared(crop_table, table_sems)
    for index in range(3):
        step = BASE_RATE * (index + 1) // height
        for way in range(3):

            @pl.when(exists(row + (1 - way) * step))
            def _():
                if way != 1:
                    main_copy(index, way, step).wait_send()
                side_copy(index, way, step).wait_send()


def pyramid(height, trunk, depth, sep_point, aspp_point, crop_part, crop_count, members, proj_weight,
            gains, shifts, head_weight, head_bias, factors, info, crop_sums):
    devices = lax.axis_size("rows") * lax.axis_size("cols")
    pixels = trunk.shape[0]
    width = pixels // height
    aspp = sep_point.shape[2]
    crops = crop_part.shape[0]
    low, wide = jnp.bfloat16, jnp.float32
    shape = jax.ShapeDtypeStruct
    whole = pl.BlockSpec(memory_space=pltpu.VMEM)
    joined = proj_weight.shape[0]
    per = aspp // LANES
    outs = (
        shape((4, pixels, aspp), low),
        shape((joined, aspp), low),
        shape((aspp, LANES), low),
        shape((crops, aspp), wide),
        shape((crops, aspp), wide),
        shape((8, LANES), wide),
        shape((8 * per, LANES), wide),
        shape(crop_sums.shape, wide),
    )
    sems = pltpu.SemaphoreType.DMA
    return pl.pallas_call(
        functools.partial(pyramid_kernel, height),
        out_shape=outs,
        in_specs=[whole] * 15,
        out_specs=(whole,) * len(outs),
        scratch_shapes=[
            pltpu.VMEM((height, width + 2 * PAD, aspp), wide),
            pltpu.VMEM((3, 3, height, width, aspp), low),
            pltpu.VMEM((3, 3, height, width, aspp), low),
            pltpu.VMEM((3, 3, height, PAD, aspp), low),
            pltpu.VMEM((3, 3, height, PAD, aspp), low),
            pltpu.VMEM((4, pixels, aspp), wide),
            pltpu.VMEM((pixels, joined), low),
            pltpu.VMEM((LANES, aspp), low),
            pltpu.VMEM((pixels, aspp), wide),
            pltpu.VMEM((pixels, aspp), low),
            pltpu.VMEM((pixels, LANES), low),
            pltpu.VMEM((pixels, aspp), wide),
            pltpu.VMEM((pixels, aspp), low),
            pltpu.VMEM((4, pixels, aspp), wide),
            pltpu.VMEM((devices, 2 * crops, LANES), wide),
            pltpu.VMEM((devices, 8 * per, LANES), wide),
            pltpu.VMEM((devices, 8, LANES), wide),
            pltpu.VMEM((devices, 8, LANES), wide),
            pltpu.VMEM((devices, 8 * per, LANES), wide),
            pltpu.VMEM(crop_sums.shape, wide),
            sems((2, 3, 3)),
            sems((2, 3, 3)),
            sems((2,)),
            sems((2,)),
            sems((2,)),
            sems((2,)),
            sems((2,)),
            sems((2,)),
            sems((2,)),
        ],
        compiler_params=pltpu.CompilerParams(
            collective_id=10, has_side_effects=True, vmem_limit_bytes=VMEM_BYTES
        ),
        cost_estimate=pl.CostEstimate(
            flops=100 * pixels * trunk.shape[1] * aspp, bytes_accessed=64 * pixels * trunk.shape[1], transcendentals=0
        ),
        name="pyramid",
    )(trunk, depth, sep_point, aspp_point, crop_part, crop_count, members, proj_weight, gains, shifts,
      head_weight, head_bias, factors, info, crop_sums)


def pyramid_weights_kernel(
    branch_low,
    trunk,
    depth,
    sep_point,
    crop_local,
    proj_part,
    head_part,
    near,
    early,
    crop_total,
    depth_part,
    turned,
    shifted,
    moved,
    gathered,
    crop_slots,
    main_sems,
    edge_sems,
    crop_sems,
):
    rows, cols, row, col, me = place()
    low, wide = jnp.bfloat16, jnp.float32
    height, width, aspp = branch_low.shape[1:]
    pixels, channels = trunk.shape
    half = crop_local.shape[0]
    greet_all()

    def exists(target):
        return jnp.logical_and(target >= 0, target < rows)

    def step_of(index):
        return BASE_RATE * (index + 1) // height

    edge_from = pl.multiple_of((1 - col) * (width - PAD), 16)
    edge_to = pl.multiple_of(col * (width + PAD), 16)
    blank = pl.multiple_of(col * (width + PAD), 16)

    def main_copy(index, way):
        return pltpu.make_async_remote_copy(
            branch_low.at[index + 1],
            near.at[index, way, :, pl.ds(PAD, width), :],
            main_sems.at[0, index, way],
            main_sems.at[1, index, way],
            device_id=(row + (1 - way) * step_of(index), col),
            device_id_type=MESH,
        )

    def edge_copy(index, way):
        return pltpu.make_async_remote_copy(
            branch_low.at[index + 1, :, pl.ds(edge_from, PAD), :],
            near.at[index, way, :, pl.ds(edge_to, PAD), :],
            edge_sems.at[0, index, way],
            edge_sems.at[1, index, way],
            device_id=(row + (1 - way) * step_of(index), 1 - col),
            device_id_type=MESH,
        )

    for index in range(3):
        for way in range(3):
            near[index, way, :, pl.ds(blank, PAD), :] = jnp.zeros((height, PAD, aspp), low)
            if way == 1:
                near[index, way, :, PAD : PAD + width, :] = branch_low[index + 1]
            else:

                @pl.when(jnp.logical_not(exists(row - (1 - way) * step_of(index))))
                def _():
                    near[index, way] = jnp.zeros(near.shape[2:], low)

    crop_slots[me, :half, :] = crop_local[:, :LANES]
    crop_slots[me, half:, :] = crop_local[:, LANES:]
    await_all()
    for index in range(3):
        edge_copy(index, 1).start()
    for index in range(3):
        for way in (0, 2):

            @pl.when(exists(row + (1 - way) * step_of(index)))
            def _():
                main_copy(index, way).start()
                edge_copy(index, way).start()

    share(crop_slots, crop_sems)

    def turn(block, carry):
        span = pl.ds(pl.multiple_of(block * width, width), width)
        for line in range(height):
            turned[span, line * width : (line + 1) * width] = trunk[
                line * width : (line + 1) * width, span
            ].T
        return carry

    lax.fori_loop(0, channels // width, turn, 0)
    part_rows = channels // 2

    def point(part, carry):
        span = pl.ds(pl.multiple_of(part * part_rows, part_rows), part_rows)
        own = branch_low[0].reshape(pixels, aspp)
        early[pl.ds(pl.multiple_of(channels + part * part_rows, part_rows), part_rows), aspp:] = jnp.dot(
            turned[span, :], own, preferred_element_type=wide
        ).astype(low)
        return carry

    lax.fori_loop(0, 2, point, 0)
    lane = lax.broadcasted_iota(jnp.int32, (part_rows, LANES), 1)
    depth_part[...] = jnp.zeros(depth_part.shape, wide)
    gathered[...] = jnp.zeros(gathered.shape, wide)
    for index, way in ((0, 1), (1, 1), (2, 1), (0, 0), (0, 2), (1, 0), (1, 2), (2, 0), (2, 2)):
        rate = BASE_RATE * (index + 1)

        @pl.when(exists(row - (1 - way) * step_of(index)))
        def _():
            if way != 1:
                main_copy(index, way).wait_recv()
            edge_copy(index, way).wait_recv()

        shifted[...] = near[index, way].astype(wide)
        for side in range(3):
            tap = 3 * (2 - way) + side
            at = PAD - (side - 1) * rate
            for line in range(height):
                moved[line * width : (line + 1) * width, :] = shifted[line, at : at + width, :].astype(
                    low
                )
            order = 9 * index + tap

            def collect(part, carry):
                span = pl.ds(pl.multiple_of(part * part_rows, part_rows), part_rows)
                made = jnp.dot(turned[span, :], moved[...], preferred_element_type=wide)
                gathered[index, span, :] += made * depth[span, order : order + 1]
                total = jnp.sum(made * sep_point[index, span, :].astype(wide), axis=1, keepdims=True)
                depth_part[span, :] = jnp.where(lane == order, total, depth_part[span, :])
                return carry

            lax.fori_loop(0, 2, collect, 0)
    early[:channels, :aspp] = gathered[0].astype(low)
    early[:channels, aspp:] = gathered[1].astype(low)
    early[channels : 2 * channels, :aspp] = gathered[2].astype(low)
    at = 2 * channels
    for table in (proj_part, depth_part, head_part):
        extent = table.shape[1]
        blocks = 2 * aspp // extent
        size = table.shape[0] // blocks
        for block in range(blocks):
            early[at : at + size, block * extent : (block + 1) * extent] = table[
                block * size : (block + 1) * size, :
            ].astype(low)
        at += size
    if early.shape[0] > at:
        early[at:, :] = jnp.zeros((early.shape[0] - at, 2 * aspp), low)
    shared(crop_slots, crop_sems)
    total = jnp.sum(crop_slots[...], axis=0)
    crop_total[...] = jnp.concatenate([total[:half], total[half:]], axis=1)
    for index in range(3):
        for way in range(3):

            @pl.when(exists(row + (1 - way) * step_of(index)))
            def _():
                if way != 1:
                    main_copy(index, way).wait_send()
                edge_copy(index, way).wait_send()


def early_rows(channels, proj_part, head_part):
    rows = 2 * channels
    for size, extent in ((proj_part.shape[0], proj_part.shape[1]), (channels, LANES), head_part.shape):
        rows += size * extent // (2 * proj_part.shape[1])
    return rows


def pyramid_weights(branch_low, trunk, depth, sep_point, crop_local, proj_part, head_part):
    devices = lax.axis_size("rows") * lax.axis_size("cols")
    height, width, aspp = branch_low.shape[1:]
    pixels, channels = trunk.shape
    crops = crop_local.shape[0]
    low, wide = jnp.bfloat16, jnp.float32
    shape = jax.ShapeDtypeStruct
    whole = pl.BlockSpec(memory_space=pltpu.VMEM)
    sems = pltpu.SemaphoreType.DMA
    outs = (
        shape((3, 3, height, width + 2 * PAD, aspp), low),
        shape((sum_rows(early_rows(channels, proj_part, head_part)), 2 * aspp), low),
        shape((crops, aspp), wide),
    )
    return pl.pallas_call(
        pyramid_weights_kernel,
        out_shape=outs,
        in_specs=[whole] * 7,
        out_specs=(whole,) * len(outs),
        scratch_shapes=[
            pltpu.VMEM((channels, LANES), wide),
            pltpu.VMEM((channels, pixels), low),
            pltpu.VMEM((height, width + 2 * PAD, aspp), wide),
            pltpu.VMEM((pixels, aspp), low),
            pltpu.VMEM((3, channels, aspp), wide),
            pltpu.VMEM((devices, 2 * crops, LANES), wide),
            sems((2, 3, 3)),
            sems((2, 3, 3)),
            sems((2,)),
        ],
        compiler_params=pltpu.CompilerParams(
            collective_id=11, has_side_effects=True, vmem_limit_bytes=VMEM_BYTES
        ),
        cost_estimate=pl.CostEstimate(
            flops=100 * pixels * channels * aspp, bytes_accessed=64 * pixels * channels, transcendentals=0
        ),
        name="pyramid_weights",
    )(branch_low, trunk, depth, sep_point, crop_local, proj_part, head_part)


def share_rows(slots, at, size, sems):
    rows, cols, row, col, me = place()

    def go(step, carry):
        other = lax.rem(me + step, rows * cols)
        mine = slots.at[me, pl.ds(at, size), :]
        pltpu.make_async_remote_copy(
            mine,
            mine,
            sems.at[0],
            sems.at[1],
            device_id=(other // cols, lax.rem(other, cols)),
            device_id_type=MESH,
        ).start()
        return carry

    lax.fori_loop(1, rows * cols, go, 0)


def shared_rows(slots, at, size, sems):
    rows, cols, row, col, me = place()
    others = slots.at[pl.ds(0, rows * cols - 1), pl.ds(at, size), :]
    pltpu.make_async_remote_copy(
        others,
        others,
        sems.at[0],
        sems.at[1],
        device_id=(row, lax.rem(col + 1, cols)),
        device_id_type=MESH,
    ).wait()


def trunk_back_kernel(
    near,
    own_low,
    depth,
    sep_point,
    aspp_point,
    members,
    crop_high,
    crop_rest,
    expanded,
    features,
    three,
    dilated,
    two,
    second_act,
    expand_weight,
    early,
    pre_grad,
    expand_part,
    dilated_low,
    sums_three,
    sums_two,
    early_out,
    fetched,
    chunk_in,
    shifted,
    moved,
    maps,
    grown,
    expand_low,
    slots_three,
    slots_two,
    sems_three,
    sems_two,
    fetch_sems,
    chunk_sems,
    early_own,
    *early_refs,
):
    rows, cols, row, col, me = place()
    low, wide = jnp.bfloat16, jnp.float32
    height = near.shape[2]
    early_sum = Sum(early, early_own, early_out, *early_refs)
    aspp = sep_point.shape[2]
    pixels, channels = expanded.shape
    middle = dilated.shape[1]
    width = pixels // height
    count = float(pixels * rows * cols)
    per = aspp // LANES
    chunks = channels // aspp
    greet_all()

    def fetch(number):
        return pltpu.make_async_copy(
            near.at[number // 3, number % 3], fetched.at[number % 2], fetch_sems.at[number % 2]
        )

    fetch(0).start()
    own_half = pltpu.make_async_copy(
        early.at[early_sum.half_span(col)], early_own, early_refs[-1]
    )
    own_half.start()

    def chunk_of(block):
        return pl.ds(pl.multiple_of(block * aspp, aspp), aspp)

    def own(block, carry):
        span = chunk_of(block)
        grown[:, span] = (
            across(own_low[...], aspp_point[span, :])
            + jnp.dot(members[...], crop_high[:, span], preferred_element_type=wide)
            + jnp.dot(members[...], crop_rest[:, span], preferred_element_type=wide)
        )
        return carry

    lax.fori_loop(0, chunks, own, 0)
    await_all()
    own_half.wait()
    early_sum.start_halves()

    def fetch_chunk(block):
        slot = lax.rem(block, 2)
        return pltpu.make_async_copy(
            expanded.at[:, chunk_of(block)], chunk_in.at[slot], chunk_sems.at[slot]
        )

    def advance(block):
        @pl.when(block + 1 < chunks)
        def _():
            fetch_chunk(block + 1).start()

        fetch_chunk(block).wait()

    def back(block, line, span):
        rows_span = slice(line * width, (line + 1) * width)
        value = chunk_in[lax.rem(block, 2), rows_span, :]
        normed = (value - three[0:1, span]) * three[1:2, span]
        return rows_span, normed

    for index in range(3):
        rate = BASE_RATE * (index + 1)
        for way in range(3):
            number = 3 * index + way
            if number < 8:
                fetch(number + 1).start()
            fetch(number).wait()
            shifted[...] = fetched[number % 2].astype(wide)
            for side in range(3):
                tap = 3 * (2 - way) + side
                at = PAD - (side - 1) * rate
                for line in range(height):
                    moved[line * width : (line + 1) * width, tap * aspp : (tap + 1) * aspp] = shifted[
                        line, at : at + width, :
                    ].astype(low)

        def one_chunk(block, carry):
            span = chunk_of(block)
            rows_of = sep_point[index, span, :].astype(wide)
            for tap in range(9):
                order = 9 * index + tap
                maps[:, tap * aspp : (tap + 1) * aspp] = (
                    rows_of * depth[span, order : order + 1]
                ).astype(low)
            total = grown[:, span] + across(moved[...], maps[...])
            if index < 2:
                grown[:, span] = total
                return carry
            advance(block)
            shift_sum, gain_sum = jnp.zeros((1, aspp), wide), jnp.zeros((1, aspp), wide)
            for line in range(height):
                rows_span, normed = back(block, line, span)
                gated = (
                    normed * three[2:3, span]
                    + three[3:4, span]
                    + features[rows_span, span].astype(wide)
                )
                sigma = sigmoid(gated)
                up = total[rows_span, :] * (sigma * (1.0 + gated * (1.0 - sigma)))
                grown[rows_span, span] = up
                pre_grad[rows_span, span] = up.astype(low)
                shift_sum = shift_sum + jnp.sum(up, axis=0, keepdims=True)
                gain_sum = gain_sum + jnp.sum(up * normed, axis=0, keepdims=True)
            for part in range(per):
                lanes = slice(part * LANES, (part + 1) * LANES)
                slots_three[me, pl.ds(block * 2 * per + part, 1), :] = shift_sum[:, lanes]
                slots_three[me, pl.ds(block * 2 * per + per + part, 1), :] = gain_sum[:, lanes]
            pair = block // 2

            @pl.when(lax.rem(block, 2) == 1)
            def _():
                share_rows(slots_three, pl.multiple_of(pair * 4 * per, 8), 4 * per, sems_three.at[pair])

            return carry

        if index == 0:
            early_sum.start_quarters()
        if index == 2:
            fetch_chunk(0).start()
        lax.fori_loop(0, chunks, one_chunk, 0)
        if index == 1:
            early_sum.start_parts()

    def finish(block, carry):
        span = chunk_of(block)
        pair = block // 2
        at = pl.multiple_of(pair * 4 * per, 8)

        @pl.when(lax.rem(block, 2) == 0)
        def _():
            shared_rows(slots_three, at, 4 * per, sems_three.at[pair])
            sums_three[pl.ds(at, 4 * per), :] = jnp.sum(slots_three[:, pl.ds(at, 4 * per), :], axis=0)

        advance(block)

        def row_at(start):
            first = block * 2 * per + start
            return jnp.concatenate([sums_three[pl.ds(first + part, 1), :] for part in range(per)], axis=1)

        shift_mean = row_at(0) / count
        gain_mean = row_at(per) / count
        factor = three[2:3, span] * three[1:2, span]
        for line in range(height):
            rows_span, normed = back(block, line, span)
            inner = grown[rows_span, span] - shift_mean - normed * gain_mean
            expand_low[rows_span, span] = (inner * factor).astype(low)
        return carry

    early_sum.start_back_parts()
    fetch_chunk(0).start()
    lax.fori_loop(0, chunks, finish, 0)
    early_sum.start_back_quarters()
    grown_two = across(expand_low[...], expand_weight[...])
    shift_sum, gain_sum = jnp.zeros((1, middle), wide), jnp.zeros((1, middle), wide)
    for line in range(height):
        rows_span = slice(line * width, (line + 1) * width)
        normed = (dilated[rows_span, :] - two[0:1, :]) * two[1:2, :]
        gated = normed * two[2:3, :] + two[3:4, :]
        sigma = sigmoid(gated)
        up = grown_two[rows_span, :] * (sigma * (1.0 + gated * (1.0 - sigma)))
        grown[rows_span, :middle] = up
        shift_sum = shift_sum + jnp.sum(up, axis=0, keepdims=True)
        gain_sum = gain_sum + jnp.sum(up * normed, axis=0, keepdims=True)
    per_two = middle // LANES
    put_row(slots_two, me, 0, shift_sum)
    put_row(slots_two, me, per_two, gain_sum)
    share(slots_two, sems_two)
    for block in range(channels // middle):
        span = slice(block * middle, (block + 1) * middle)
        expand_part[block * middle : (block + 1) * middle, :] = down(
            second_act[...], expand_low[:, span]
        ).astype(low)
    shared(slots_two, sems_two)
    total = jnp.sum(slots_two[...], axis=0)
    sums_two[...] = total
    shift_mean = take_row(total, 0, middle) / count
    gain_mean = take_row(total, per_two, middle) / count
    factor = two[2:3, :] * two[1:2, :]
    for line in range(height):
        rows_span = slice(line * width, (line + 1) * width)
        normed = (dilated[rows_span, :] - two[0:1, :]) * two[1:2, :]
        inner = grown[rows_span, :middle] - shift_mean - normed * gain_mean
        dilated_low[rows_span, :] = (inner * factor).astype(low)
    early_sum.start_back_half()
    early_sum.finish()


def trunk_back(near, own_low, depth, sep_point, aspp_point, members, crop_high, crop_rest, expanded,
               features, three, dilated, two, second_act, expand_weight, early):
    devices = lax.axis_size("rows") * lax.axis_size("cols")
    height, extent, aspp = near.shape[2:]
    pixels, channels = expanded.shape
    middle = dilated.shape[1]
    chunks = channels // aspp
    low, wide = jnp.bfloat16, jnp.float32
    shape = jax.ShapeDtypeStruct
    whole = pl.BlockSpec(memory_space=pltpu.VMEM)
    away = pl.BlockSpec(memory_space=pl.ANY)
    sems = pltpu.SemaphoreType.DMA
    per_two = middle // LANES
    outs = (
        shape((pixels, channels), low),
        shape((channels, middle), low),
        shape((pixels, middle), low),
        shape((chunks * 2 * (aspp // LANES), LANES), wide),
        shape((2 * per_two, LANES), wide),
        shape(early.shape, low),
    )
    return pl.pallas_call(
        trunk_back_kernel,
        out_shape=outs,
        in_specs=[away] + [whole] * 7 + [away] + [whole] * 6 + [away],
        out_specs=(whole,) * 5 + (away,),
        scratch_shapes=[
            pltpu.VMEM((2, height, extent, aspp), low),
            pltpu.VMEM((2, pixels, aspp), wide),
            pltpu.VMEM((height, extent, aspp), wide),
            pltpu.VMEM((pixels, 9 * aspp), low),
            pltpu.VMEM((aspp, 9 * aspp), low),
            pltpu.VMEM((pixels, channels), wide),
            pltpu.VMEM((pixels, channels), low),
            pltpu.VMEM((devices, chunks * 2 * (aspp // LANES), LANES), wide),
            pltpu.VMEM((devices, 2 * per_two, LANES), wide),
            sems((chunks // 2, 2)),
            sems((2,)),
            sems((2,)),
            sems((2,)),
            pltpu.VMEM((early.shape[0] // 2, early.shape[1]), low),
            *sum_scratch(*early.shape),
        ],
        compiler_params=pltpu.CompilerParams(
            collective_id=12, has_side_effects=True, vmem_limit_bytes=VMEM_BYTES + (3 << 20)
        ),
        cost_estimate=pl.CostEstimate(
            flops=80 * pixels * channels * aspp, bytes_accessed=64 * pixels * channels, transcendentals=0
        ),
        name="trunk_back",
    )(near, own_low, depth, sep_point, aspp_point, members, crop_high, crop_rest, expanded, features,
      three, dilated, two, second_act, expand_weight, early)


EDGE = 16


class Halo:
    def __init__(self, near, direct, relay, edge):
        self.near, self.direct, self.relay, self.edge = near, direct, relay, edge
        self.rows, self.cols, self.row, self.col, _ = place()
        self.height, self.width = near.shape[1], near.shape[2] - 2 * EDGE
        self.odd = lax.rem(self.row, 2)
        self.pair = self.row + 1 - 2 * self.odd
        self.onward = self.row + 2 - 4 * self.odd
        self.far = self.row - 1 + 2 * self.odd
        self.pair_way = 2 - 2 * self.odd
        self.far_way = 2 * self.odd

    def exists(self, target):
        return jnp.logical_and(target >= 0, target < self.rows)

    def line_ref(self, way, line):
        return self.near.at[way, line, pl.ds(EDGE, self.width), :]

    def direct_copy(self, line):
        return pltpu.make_async_remote_copy(
            self.line_ref(1, line),
            self.line_ref(self.far_way, line),
            self.direct.at[0, line],
            self.direct.at[1, line],
            device_id=(self.pair, self.col),
            device_id_type=MESH,
        )

    def relay_copy(self, line):
        return pltpu.make_async_remote_copy(
            self.line_ref(self.pair_way, line),
            self.line_ref(self.far_way, line),
            self.relay.at[0, line],
            self.relay.at[1, line],
            device_id=(self.onward, self.col),
            device_id_type=MESH,
        )

    def edge_copy(self, way):
        start = pl.multiple_of(EDGE + (1 - self.col) * (self.width - EDGE), 16)
        end = pl.multiple_of(self.col * (self.width + EDGE), 16)
        return pltpu.make_async_remote_copy(
            self.near.at[1, :, pl.ds(start, EDGE), :],
            self.near.at[way, :, pl.ds(end, EDGE), :],
            self.edge.at[0, way],
            self.edge.at[1, way],
            device_id=(self.row + 1 - way, 1 - self.col),
            device_id_type=MESH,
        )

    def clear(self):
        near = self.near
        blank = pl.multiple_of(self.col * (self.width + EDGE), 16)
        for way in range(3):
            near[way, :, pl.ds(blank, EDGE), :] = jnp.zeros(
                (self.height, EDGE, near.shape[3]), near.dtype
            )

        @pl.when(jnp.logical_not(self.exists(self.far)))
        def _():
            near[self.far_way] = jnp.zeros(near.shape[1:], near.dtype)

    def start(self):
        self.edge_copy(1).start()
        for line in range(self.height):
            self.direct_copy(line).start()
        for way in (0, 2):

            @pl.when(self.exists(self.row + 1 - way))
            def _():
                self.edge_copy(way).start()

    def wait_own(self):
        self.edge_copy(1).wait_recv()

    def pass_on(self):
        for line in range(self.height):
            self.direct_copy(line).wait_recv()

            @pl.when(self.exists(self.onward))
            def _():
                self.relay_copy(line).start()

    def wait_rest(self):
        for way in (0, 2):

            @pl.when(self.exists(self.row - 1 + way))
            def _():
                self.edge_copy(way).wait_recv()

        @pl.when(self.exists(self.far))
        def _():
            for line in range(self.height):
                self.relay_copy(line).wait_recv()

    def drain(self):
        self.edge_copy(1).wait_send()
        for line in range(self.height):
            self.direct_copy(line).wait_send()
        for way in (0, 2):

            @pl.when(self.exists(self.row + 1 - way))
            def _():
                self.edge_copy(way).wait_send()

        @pl.when(self.exists(self.onward))
        def _():
            for line in range(self.height):
                self.relay_copy(line).wait_send()


PLANE = 4


class Sum:
    def __init__(self, full, own, out, half_in, quarter_in, part_in, half_sem, quarter_sem, part_sem, copy_sem):
        self.full, self.out = full, out
        self.half_in, self.quarter_in, self.part_in = half_in, quarter_in, part_in
        self.half_sem, self.quarter_sem, self.part_sem = half_sem, quarter_sem, part_sem
        self.copy_sem = copy_sem
        self.rows, self.cols, self.row, self.col, _ = place()
        self.parts = self.rows // PLANE
        self.quarter, self.part = lax.rem(self.row, PLANE), self.row // PLANE
        total = full.shape[0]
        self.half_rows, self.quarter_rows = total // 2, total // 8
        self.part_rows = self.quarter_rows // self.parts
        self.data = full.at[self.half_span(self.col)] if own is None else own

    def span(self, start, size):
        return pl.ds(pl.multiple_of(start, 16), size)

    def half_span(self, col):
        return self.span(col * self.half_rows, self.half_rows)

    def quarter_span(self, quarter):
        return self.span(quarter * self.quarter_rows, self.quarter_rows)

    def part_span(self, part):
        return self.span(
            self.quarter * self.quarter_rows + part * self.part_rows, self.part_rows
        )

    def out_at(self, span):
        return self.out.at[self.span(self.col * self.half_rows + span.start, span.size)]

    def plane_mate(self, step):
        mate = lax.rem(self.quarter + step, PLANE)
        return mate, (self.part * PLANE + mate, self.col)

    def part_mate(self, step):
        mate = lax.rem(self.part + step, self.parts)
        return mate, (mate * PLANE + self.quarter, self.col)

    def remote(self, src, dst, sems, out_at, in_at, target):
        return pltpu.make_async_remote_copy(
            src, dst, sems.at[0, out_at], sems.at[1, in_at], device_id=target, device_id_type=MESH
        )

    def half_copy(self):
        return self.remote(
            self.full.at[self.half_span(1 - self.col)],
            self.half_in,
            self.half_sem,
            0,
            0,
            (self.row, 1 - self.col),
        )

    def quarter_copy(self, step):
        mate, target = self.plane_mate(step)
        return self.remote(
            self.data.at[self.quarter_span(mate)],
            self.quarter_in.at[self.quarter],
            self.quarter_sem,
            mate,
            self.quarter,
            target,
        )

    def quarter_arrival(self, step):
        mate, target = self.plane_mate(step)
        return self.remote(
            self.quarter_in.at[mate], self.quarter_in.at[mate], self.quarter_sem, mate, mate, target
        )

    def part_copy(self, step):
        mate, target = self.part_mate(step)
        return self.remote(
            self.data.at[self.part_span(mate)],
            self.part_in.at[self.part],
            self.part_sem,
            mate,
            self.part,
            target,
        )

    def part_arrival(self, step):
        mate, target = self.part_mate(step)
        return self.remote(
            self.part_in.at[mate], self.part_in.at[mate], self.part_sem, mate, mate, target
        )

    def start_halves(self):
        self.half_copy().start()

    def add(self, span, sources):
        block = 64
        base = span.start

        def some(at, carry):
            rows = pl.ds(pl.multiple_of(base + at * block, 16), block)
            total = self.data[rows, :].astype(jnp.float32)
            for source in sources:
                total = total + source(pl.ds(pl.multiple_of(at * block, 16), block)).astype(jnp.float32)
            self.data[rows, :] = total.astype(self.data.dtype)
            return carry

        full = span.size // block
        lax.fori_loop(0, full, some, 0)
        rest = span.size - full * block
        if rest:
            rows = pl.ds(pl.multiple_of(base + full * block, 16), rest)
            total = self.data[rows, :].astype(jnp.float32)
            for source in sources:
                total = total + source(pl.ds(full * block, rest)).astype(jnp.float32)
            self.data[rows, :] = total.astype(self.data.dtype)

    def start_quarters(self):
        self.half_copy().wait()
        self.add(self.span(0, self.half_rows), [lambda rows: self.half_in[rows, :]])
        for step in range(1, PLANE):
            self.quarter_copy(step).start()

    def start_parts(self):
        for step in range(1, PLANE):
            self.quarter_copy(step).wait_send()
            self.quarter_arrival(step).wait_recv()
        mates = [self.plane_mate(step)[0] for step in range(1, PLANE)]
        self.add(
            self.quarter_span(self.quarter),
            [lambda rows, mate=mate: self.quarter_in[mate, rows, :] for mate in mates],
        )
        for step in range(1, self.parts):
            self.part_copy(step).start()

    def back_part(self, step):
        mate, target = self.part_mate(step)
        mine = self.out_at(self.part_span(self.part))
        apart = self.parts
        return self.remote(
            mine, mine, self.part_sem, apart + mate, apart + self.part, target
        )

    def back_part_arrival(self, step):
        mate, target = self.part_mate(step)
        theirs = self.out_at(self.part_span(mate))
        apart = self.parts
        return self.remote(theirs, theirs, self.part_sem, apart + mate, apart + mate, target)

    def back_quarter(self, step):
        mate, target = self.plane_mate(step)
        mine = self.out_at(self.quarter_span(self.quarter))
        return self.remote(
            mine, mine, self.quarter_sem, PLANE + mate, PLANE + self.quarter, target
        )

    def back_quarter_arrival(self, step):
        mate, target = self.plane_mate(step)
        theirs = self.out_at(self.quarter_span(mate))
        return self.remote(theirs, theirs, self.quarter_sem, PLANE + mate, PLANE + mate, target)

    def back_half(self):
        mine = self.out.at[self.half_span(self.col)]
        return self.remote(mine, mine, self.half_sem, 1, 1, (self.row, 1 - self.col))

    def back_half_arrival(self):
        theirs = self.out.at[self.half_span(1 - self.col)]
        return self.remote(theirs, theirs, self.half_sem, 1, 1, (self.row, 1 - self.col))

    def start_back_parts(self):
        for step in range(1, self.parts):
            self.part_copy(step).wait_send()
            self.part_arrival(step).wait_recv()
        mates = [self.part_mate(step)[0] for step in range(1, self.parts)]
        span = self.part_span(self.part)
        self.add(span, [lambda rows, mate=mate: self.part_in[mate, rows, :] for mate in mates])
        copy = pltpu.make_async_copy(self.data.at[span], self.out_at(span), self.copy_sem)
        copy.start()
        copy.wait()
        for step in range(1, self.parts):
            self.back_part(step).start()

    def start_back_quarters(self):
        for step in range(1, self.parts):
            self.back_part(step).wait_send()
            self.back_part_arrival(step).wait_recv()
        for step in range(1, PLANE):
            self.back_quarter(step).start()

    def start_back_half(self):
        for step in range(1, PLANE):
            self.back_quarter(step).wait_send()
            self.back_quarter_arrival(step).wait_recv()
        self.back_half().start()

    def finish(self):
        self.back_half().wait_send()
        self.back_half_arrival().wait_recv()


def sum_scratch(total, lanes):
    parts = lax.axis_size("rows") // PLANE
    low, sems = jnp.bfloat16, pltpu.SemaphoreType.DMA
    return [
        pltpu.VMEM((total // 2, lanes), low),
        pltpu.VMEM((PLANE, total // 8, lanes), low),
        pltpu.VMEM((parts, total // 8 // parts, lanes), low),
        sems((2, 2)),
        sems((2, 2 * PLANE)),
        sems((2, 2 * parts)),
        sems,
    ]


def sum_rows(rows):
    unit = 2 * lax.axis_size("rows") * 16
    return -(-rows // unit) * unit


def tail_kernel(
    dilated_low,
    first_act,
    dilated_weight,
    reduced,
    one,
    features,
    reduce_weight,
    pre_grad,
    expand_part,
    features_grad,
    expand_out,
    dilated_out,
    reduce_out,
    sums_one,
    near,
    shifted,
    moved,
    act_turned,
    features_turned,
    first_grad,
    reduced_low,
    expand_own,
    dilated_data,
    reduce_data,
    slots,
    direct,
    relay,
    edge,
    sems_one,
    *sum_refs,
):
    rows, cols, row, col, me = place()
    low, wide = jnp.bfloat16, jnp.float32
    height = near.shape[1]
    pixels, middle = dilated_low.shape
    channels = features.shape[1]
    width = pixels // height
    count = float(pixels * rows * cols)
    half = len(sum_refs) // 3
    sums = [
        Sum(full, own, out, *refs)
        for full, own, out, refs in (
            (expand_part, expand_own, expand_out, sum_refs[:half]),
            (dilated_data, None, dilated_out, sum_refs[half : 2 * half]),
            (reduce_data, None, reduce_out, sum_refs[2 * half :]),
        )
    ]
    expand_sum, dilated_sum, reduce_sum = sums
    halo = Halo(near, direct, relay, edge)
    greet_all()
    own_half = pltpu.make_async_copy(
        expand_part.at[expand_sum.half_span(col)], expand_own, sum_refs[half - 1]
    )
    own_half.start()
    halo.clear()
    for line in range(height):
        near[1, line, EDGE : EDGE + width, :] = dilated_low[line * width : (line + 1) * width, :]
    for data, used in ((dilated_data, 9 * middle), (reduce_data, channels)):
        if data.shape[0] > used:
            data[used:, :] = jnp.zeros((data.shape[0] - used, data.shape[1]), low)
    own_half.wait()
    await_all()
    halo.start()
    expand_sum.start_halves()

    def turn_features(block, carry):
        span = pl.ds(pl.multiple_of(block * width, width), width)
        for line in range(height):
            features_turned[span, line * width : (line + 1) * width] = features[
                line * width : (line + 1) * width, span
            ].T
        return carry

    def turn_act(block, carry):
        span = pl.ds(pl.multiple_of(block * width, width), width)
        for line in range(height):
            act_turned[span, line * width : (line + 1) * width] = first_act[
                line * width : (line + 1) * width, span
            ].T
        return carry

    lax.fori_loop(0, middle // width, turn_act, 0)

    def one_way(way):
        shifted[...] = near[way].astype(wide)
        for side in range(3):
            tap = 3 * (2 - way) + side
            at = EDGE - (side - 1) * MID_RATE
            for line in range(height):
                moved[line * width : (line + 1) * width, :] = shifted[line, at : at + width, :].astype(
                    low
                )
            made = across(moved[...], dilated_weight[tap])
            if way == 1 and side == 0:
                first_grad[...] = made
            else:
                first_grad[...] += made
            dilated_data[tap * middle : (tap + 1) * middle, :] = jnp.dot(
                act_turned[...], moved[...], preferred_element_type=wide
            ).astype(low)

    halo.wait_own()
    one_way(1)
    halo.pass_on()
    expand_sum.start_quarters()
    lax.fori_loop(0, channels // width, turn_features, 0)
    halo.wait_rest()
    one_way(0)
    one_way(2)
    dilated_sum.start_halves()
    expand_sum.start_parts()
    shift_sum, gain_sum = jnp.zeros((1, middle), wide), jnp.zeros((1, middle), wide)
    for line in range(height):
        span = slice(line * width, (line + 1) * width)
        normed = (reduced[span, :] - one[0:1, :]) * one[1:2, :]
        gated = normed * one[2:3, :] + one[3:4, :]
        sigma = sigmoid(gated)
        up = first_grad[span, :] * (sigma * (1.0 + gated * (1.0 - sigma)))
        first_grad[span, :] = up
        shift_sum = shift_sum + jnp.sum(up, axis=0, keepdims=True)
        gain_sum = gain_sum + jnp.sum(up * normed, axis=0, keepdims=True)
    per = middle // LANES
    put_row(slots, me, 0, shift_sum)
    put_row(slots, me, per, gain_sum)
    share(slots, sems_one)
    expand_sum.start_back_parts()
    dilated_sum.start_quarters()
    shared(slots, sems_one)
    total = jnp.sum(slots[...], axis=0)
    sums_one[...] = total
    shift_mean = take_row(total, 0, middle) / count
    gain_mean = take_row(total, per, middle) / count
    factor = one[2:3, :] * one[1:2, :]
    for line in range(height):
        span = slice(line * width, (line + 1) * width)
        normed = (reduced[span, :] - one[0:1, :]) * one[1:2, :]
        inner = first_grad[span, :] - shift_mean - normed * gain_mean
        reduced_low[span, :] = (inner * factor).astype(low)
    reduce_data[:channels, :] = jnp.dot(
        features_turned[...], reduced_low[...], preferred_element_type=wide
    ).astype(low)
    reduce_sum.start_halves()
    expand_sum.start_back_quarters()
    chunk = 2 * LANES

    def last(block, carry):
        span = pl.ds(pl.multiple_of(block * chunk, chunk), chunk)
        made = across(reduced_low[...], reduce_weight[span, :])
        features_grad[:, span] = (made + pre_grad[:, span].astype(wide)).astype(low)
        return carry

    lax.fori_loop(0, channels // chunk, last, 0)
    reduce_sum.start_quarters()
    dilated_sum.start_parts()
    expand_sum.start_back_half()
    reduce_sum.start_parts()
    dilated_sum.start_back_parts()
    reduce_sum.start_back_parts()
    dilated_sum.start_back_quarters()
    reduce_sum.start_back_quarters()
    dilated_sum.start_back_half()
    reduce_sum.start_back_half()
    for each in sums:
        each.finish()
    halo.drain()


def tail(height, dilated_low, first_act, dilated_weight, reduced, one, features, reduce_weight, pre_grad,
         expand_part):
    devices = lax.axis_size("rows") * lax.axis_size("cols")
    pixels, middle = dilated_low.shape
    channels = features.shape[1]
    width = pixels // height
    low, wide = jnp.bfloat16, jnp.float32
    shape = jax.ShapeDtypeStruct
    whole = pl.BlockSpec(memory_space=pltpu.VMEM)
    away = pl.BlockSpec(memory_space=pl.ANY)
    sems = pltpu.SemaphoreType.DMA
    per = middle // LANES
    expand_part = jnp.pad(
        expand_part, ((0, sum_rows(expand_part.shape[0]) - expand_part.shape[0]), (0, 0))
    )
    sizes = [sum_rows(expand_part.shape[0]), sum_rows(9 * middle), sum_rows(channels)]
    outs = (
        shape((pixels, channels), low),
        *[shape((size, middle), low) for size in sizes],
        shape((2 * per, LANES), wide),
    )
    scratch = [
        pltpu.VMEM((3, height, width + 2 * EDGE, middle), low),
        pltpu.VMEM((height, width + 2 * EDGE, middle), wide),
        pltpu.VMEM((pixels, middle), low),
        pltpu.VMEM((middle, pixels), low),
        pltpu.VMEM((channels, pixels), low),
        pltpu.VMEM((pixels, middle), wide),
        pltpu.VMEM((pixels, middle), low),
        pltpu.VMEM((sizes[0] // 2, middle), low),
        *[pltpu.VMEM((size, middle), low) for size in sizes[1:]],
        pltpu.VMEM((devices, 2 * per, LANES), wide),
        sems((2, height)),
        sems((2, height)),
        sems((2, 3)),
        sems((2,)),
    ]
    for size in sizes:
        scratch += sum_scratch(size, middle)
    return pl.pallas_call(
        functools.partial(tail_kernel),
        out_shape=outs,
        in_specs=[whole] * 8 + [away],
        out_specs=(whole, away, away, away, whole),
        scratch_shapes=scratch,
        compiler_params=pltpu.CompilerParams(
            collective_id=13, has_side_effects=True, vmem_limit_bytes=VMEM_BYTES + (3 << 20)
        ),
        cost_estimate=pl.CostEstimate(
            flops=400 * pixels * middle * middle, bytes_accessed=256 * pixels * channels, transcendentals=0
        ),
        name="tail",
    )(dilated_low, first_act, dilated_weight, reduced, one, features, reduce_weight, pre_grad, expand_part)


def on_device(
    features,
    reduce_weight,
    dilated_weight,
    expand_weight,
    mid_gain,
    mid_shift,
    out_gain,
    out_shift,
    aspp_point,
    sep_depth,
    sep_point,
    pool_weight,
    proj_weight,
    aspp_gain,
    aspp_shift,
    head_weight,
    head_bias,
    task_scales,
    crop_ids,
    labels,
    boundary_mask,
    valid_mask,
    geometry_target,
):
    height, width, channels = features.shape
    pixels = height * width
    share = float(pixels)
    count = float(pixels * lax.axis_size("rows") * lax.axis_size("cols"))
    highest = lax.Precision.HIGHEST
    low = jnp.bfloat16
    aspp_width = proj_weight.shape[1]
    crop_flat = crop_ids.reshape(pixels)
    members = (crop_flat[:, None] == jnp.arange(CROPS)[None, :]).astype(low)
    members_wide = members.astype(jnp.float32)
    keep = (1 - boundary_mask.reshape(pixels)).astype(jnp.float32)
    valid = valid_mask.reshape(pixels).astype(jnp.float32)
    flat = features.reshape(pixels, channels)
    reduced = matmul(flat, reduce_weight)[None]
    mean, square = local_stats(reduced)
    own_counts = (jnp.sum(members_wide, axis=0), jnp.sum(keep)[None], jnp.sum(valid)[None])
    gathered = gather_all(pack(mean, square, *own_counts), 0)
    means, squares, crop_counts, keeps, valids = unpack(
        gathered, mean.shape, square.shape, (CROPS,), (1,), (1,)
    )
    center_one, scale_one = merged_stats(means, squares, share, count)
    crop_count, keep_count, valid_count = (
        jnp.sum(crop_counts, axis=0), jnp.sum(keeps), jnp.sum(valids)
    )
    normed_one = normalize(reduced, center_one, scale_one)
    gated_one = normed_one[0] * mid_gain[0] + mid_shift[0]
    first_act = sigmoid_linear(gated_one).astype(low)
    first_field = first_act.reshape(height, width, -1)
    first_near = fetch(first_field, MID_RATE)
    dilated = jnp.zeros((pixels, dilated_weight.shape[2]), jnp.float32)
    for index in range(9):
        dilated = dilated + matmul(
            offset_piece(first_near, index, MID_RATE, width), dilated_weight[index]
        )
    dilated = dilated[None]
    mean, square = local_stats(dilated)
    means, squares = unpack(gather_all(pack(mean, square), 1), mean.shape, square.shape)
    center_two, scale_two = merged_stats(means, squares, share, count)
    normed_two = normalize(dilated, center_two, scale_two)
    gated_two = normed_two[0] * mid_gain[1] + mid_shift[1]
    second_act = sigmoid_linear(gated_two).astype(low)
    expanded = matmul(second_act, expand_weight)[None]
    mean, square = local_stats(expanded)
    means, squares = unpack(gather_all(pack(mean, square), 2), mean.shape, square.shape)
    center_three, scale_three = merged_stats(means, squares, share, count)
    normed_three = normalize(expanded, center_three, scale_three)
    pre_trunk = normed_three[0] * out_gain + out_shift + flat.astype(jnp.float32)
    trunk = sigmoid_linear(pre_trunk).astype(low)
    local_sums = jnp.einsum("pk,pc->kc", members, trunk, preferred_element_type=jnp.float32)
    crop_part = jnp.dot(local_sums, pool_weight.astype(jnp.float32), precision=highest)
    scale_exp = jnp.exp(task_scales)
    counts = jnp.stack([keep_count, valid_count, valid_count])
    factor = scale_exp / counts
    lane = jnp.arange(LANES)
    factors = jnp.where(
        lane < CLASSES, factor[0], jnp.where(lane == CLASSES, factor[1], 2.0 * factor[2])
    )
    outs = head_weight.shape[1]
    wide_row = ((0, 0), (0, LANES - outs))
    info = jnp.stack(
        [labels.reshape(pixels).astype(jnp.float32), keep, valid, *geometry_target.reshape(4, pixels)],
        axis=1,
    )
    devices = lax.axis_size("rows") * lax.axis_size("cols")
    crop_rows = CROPS * channels // LANES
    piece = -(-crop_rows // devices)
    crop_sums = jnp.pad(local_sums.reshape(crop_rows, LANES), ((0, piece * devices - crop_rows), (0, 0)))
    crop_sums = jnp.pad(
        crop_sums.reshape(devices, piece, LANES), ((0, 0), (0, -piece % 8), (0, 0))
    )
    branch_low, proj_part, head_part, crop_local, crop_pre, sums_five, sums_four, crop_table = pyramid(
        height,
        trunk,
        jnp.pad(sep_depth.reshape(27, channels).astype(jnp.float32), ((0, 5), (0, 0))),
        sep_point,
        aspp_point,
        crop_part,
        jnp.broadcast_to(crop_count[:, None], (CROPS, aspp_width)),
        jnp.pad(members, ((0, 0), (0, LANES - CROPS))),
        proj_weight,
        jnp.pad(aspp_gain, ((0, 3), (0, 0))),
        jnp.pad(aspp_shift, ((0, 3), (0, 0))),
        jnp.pad(head_weight, wide_row),
        jnp.pad(jnp.broadcast_to(head_bias, (8, outs)), wide_row),
        jnp.broadcast_to(factors, (8, LANES)),
        jnp.pad(info, ((0, 0), (0, 1))),
        crop_sums,
    )
    crop_table = crop_table[:, :piece].reshape(-1, LANES)[:crop_rows].reshape(CROPS, channels)
    per = aspp_width // LANES
    proj_shift_grad = sums_five[:per].reshape(1, aspp_width)
    proj_gain_grad = sums_five[per : 2 * per].reshape(1, aspp_width)
    loss_row = sums_five[2 * per]
    grad_head_bias = sums_five[2 * per + 1, :outs]
    branch_shift_grad = sums_four[: 4 * per].reshape(4, aspp_width)
    branch_gain_grad = sums_four[4 * per :].reshape(4, aspp_width)
    loss_sums = jnp.stack(
        [loss_row[0], loss_row[CLASSES], jnp.sum(loss_row[CLASSES + 1 : CLASSES + 4])]
    )
    losses = loss_sums / counts
    objective = jnp.sum(scale_exp * losses - task_scales)
    grad_scales = scale_exp * losses - 1.0
    near, early, crop_total = pyramid_weights(
        branch_low.reshape(4, height, width, aspp_width),
        trunk,
        jnp.pad(sep_depth.reshape(27, channels).astype(jnp.float32).T, ((0, 0), (0, LANES - 27))),
        sep_point,
        crop_local,
        proj_part,
        head_part,
    )
    crop_low = (crop_total * gate_slope(crop_pre)).astype(low)
    pooled = (crop_table / crop_count[:, None]).astype(low)
    grad_pool_weight = jnp.einsum("kc,kd->cd", pooled, crop_low, preferred_element_type=jnp.float32)
    pooled_grad = (
        jnp.einsum("kd,cd->kc", crop_low, pool_weight, preferred_element_type=jnp.float32)
        / crop_count[:, None]
    )
    pooled_grad = jnp.pad(pooled_grad, ((0, LANES - CROPS), (0, 0)))
    crop_high = pooled_grad.astype(low)
    crop_rest = (pooled_grad - crop_high.astype(jnp.float32)).astype(low)
    pre_low, expand_part, dilated_low, sums_three, sums_two, early_sum = trunk_back(
        near,
        branch_low[0],
        jnp.pad(sep_depth.reshape(27, channels).astype(jnp.float32).T, ((0, 0), (0, LANES - 27))),
        sep_point,
        aspp_point,
        jnp.pad(members, ((0, 0), (0, LANES - CROPS))),
        crop_high,
        crop_rest,
        expanded[0],
        flat,
        jnp.pad(
            jnp.concatenate([center_three, scale_three, out_gain[None], out_shift[None]]), ((0, 4), (0, 0))
        ),
        dilated[0],
        jnp.pad(
            jnp.concatenate([center_two, scale_two, mid_gain[1:2], mid_shift[1:2]]), ((0, 4), (0, 0))
        ),
        second_act,
        expand_weight,
        early,
    )
    folded = sums_three.reshape(-1, 2 * per, LANES)
    out_shift_grad = folded[:, :per].reshape(1, channels)
    out_gain_grad = folded[:, per:].reshape(1, channels)
    middle = dilated_low.shape[1]
    two_shift_grad, two_gain_grad = sums_two.reshape(2, 1, middle)
    grad_features, expand_sum, dilated_sum, reduce_sum, sums_one = tail(
        height,
        dilated_low,
        first_act,
        dilated_weight,
        reduced[0],
        jnp.pad(
            jnp.concatenate([center_one, scale_one, mid_gain[0:1], mid_shift[0:1]]), ((0, 4), (0, 0))
        ),
        flat,
        reduce_weight,
        pre_low,
        expand_part,
    )
    one_shift_grad, one_gain_grad = sums_one.reshape(2, 1, middle)
    grad_features = grad_features.reshape(height, width, channels)
    expand_sum = expand_sum[:channels].reshape(-1, middle, middle)
    grad_expand_weight = jnp.transpose(expand_sum, (1, 0, 2)).reshape(middle, channels)
    first, second = early_sum[:channels], early_sum[channels : 2 * channels]
    sep_sum = jnp.stack([first[:, :aspp_width], first[:, aspp_width:], second[:, :aspp_width]])
    at = 2 * channels
    tables = []
    for size, extent in ((proj_weight.shape[0], aspp_width), (channels, LANES), (aspp_width, LANES)):
        blocks = 2 * aspp_width // extent
        table = early_sum[at : at + size // blocks].reshape(size // blocks, blocks, extent)
        tables.append(jnp.transpose(table, (1, 0, 2)).reshape(size, extent))
        at += size // blocks
    summed = [
        value.astype(jnp.float32)
        for value in (
            reduce_sum[:channels],
            dilated_sum[: 9 * middle].reshape(9, middle, middle),
            grad_expand_weight,
            second[:, aspp_width:],
            tables[1][:, :27].T.reshape(3, 9, channels),
            sep_sum,
            tables[0],
            tables[2],
        )
    ]
    grad_mid_gain = jnp.concatenate([one_gain_grad, two_gain_grad], axis=0)
    grad_mid_shift = jnp.concatenate([one_shift_grad, two_shift_grad], axis=0)
    grad_aspp_gain = jnp.concatenate([branch_gain_grad, proj_gain_grad], axis=0)
    grad_aspp_shift = jnp.concatenate([branch_shift_grad, proj_shift_grad], axis=0)
    return (
        objective,
        grad_features,
        summed[0],
        summed[1],
        summed[2],
        grad_mid_gain,
        grad_mid_shift,
        out_gain_grad[0],
        out_shift_grad[0],
        summed[3],
        summed[4],
        summed[5],
        grad_pool_weight,
        summed[6],
        grad_aspp_gain,
        grad_aspp_shift,
        summed[7][:, : head_weight.shape[1]],
        grad_head_bias,
        grad_scales,
    )


def solution(mesh):
    in_specs = (
        P("rows", "cols", None),
        P(),
        P(),
        P(),
        P(),
        P(),
        P(),
        P(),
        P(),
        P(),
        P(),
        P(),
        P(),
        P(),
        P(),
        P(),
        P(),
        P(),
        P("rows", "cols"),
        P("rows", "cols"),
        P("rows", "cols"),
        P("rows", "cols"),
        P(None, "rows", "cols"),
    )
    out_specs = (
        P(),
        P("rows", "cols", None),
        P(),
        P(),
        P(),
        P(),
        P(),
        P(),
        P(),
        P(),
        P(),
        P(),
        P(),
        P(),
        P(),
        P(),
        P(),
        P(),
        P(),
    )
    return jax.shard_map(
        on_device, mesh=mesh, in_specs=in_specs, out_specs=out_specs, check_vma=False
    )
```

```python
import functools

import jax
import jax.numpy as jnp
from jax import lax
from jax.experimental import pallas as pl
from jax.experimental.pallas import tpu as pltpu
from jax.sharding import PartitionSpec as P

CLASSES = 13
CROPS = 16
MID_RATE = 4
BASE_RATE = 12
LANES = 128

EPS = 1e-05
MESH = pl.DeviceIdType.MESH


def gate_slope(value):
    sigma = jax.nn.sigmoid(value)
    return sigma * (1.0 + value * (1.0 - sigma))


PAD = 48
VMEM_BYTES = 60 * 1024 * 1024


def place():
    rows, cols = lax.axis_size("rows"), lax.axis_size("cols")
    row, col = lax.axis_index("rows"), lax.axis_index("cols")
    return rows, cols, row, col, row * cols + col


def greet_all():
    rows, cols, row, col, me = place()
    barrier = pltpu.get_barrier_semaphore()

    def greet(step, carry):
        other = lax.rem(me + step, rows * cols)
        pl.semaphore_signal(
            barrier, inc=1, device_id=(other // cols, lax.rem(other, cols)), device_id_type=MESH
        )
        return carry

    lax.fori_loop(1, rows * cols, greet, 0)


def await_all():
    rows, cols = lax.axis_size("rows"), lax.axis_size("cols")
    pl.semaphore_wait(pltpu.get_barrier_semaphore(), rows * cols - 1)


def share(slots, sems):
    rows, cols, row, col, me = place()

    def go(step, carry):
        other = lax.rem(me + step, rows * cols)
        pltpu.make_async_remote_copy(
            slots.at[me],
            slots.at[me],
            sems.at[0],
            sems.at[1],
            device_id=(other // cols, lax.rem(other, cols)),
            device_id_type=MESH,
        ).start()
        return carry

    lax.fori_loop(1, rows * cols, go, 0)


def shared(slots, sems):
    rows, cols, row, col, me = place()
    others = slots.at[pl.ds(0, rows * cols - 1)]
    pltpu.make_async_remote_copy(
        others,
        others,
        sems.at[0],
        sems.at[1],
        device_id=(row, lax.rem(col + 1, cols)),
        device_id_type=MESH,
    ).wait()


def share_column(slots, sems):
    rows, cols, row, col, me = place()

    def go(step, carry):
        other = lax.rem(row + step, rows)
        pltpu.make_async_remote_copy(
            slots.at[row],
            slots.at[row],
            sems.at[0],
            sems.at[1],
            device_id=(other, col),
            device_id_type=MESH,
        ).start()
        return carry

    lax.fori_loop(1, rows, go, 0)


def shared_column(slots, sems):
    rows, cols, row, col, me = place()
    others = slots.at[pl.ds(0, rows - 1)]
    pltpu.make_async_remote_copy(
        others,
        others,
        sems.at[0],
        sems.at[1],
        device_id=(lax.rem(row + 1, rows), col),
        device_id_type=MESH,
    ).wait()


class PairSum:
    def __init__(self, own, pair, slots, all_, sems):
        self.own, self.pair, self.slots, self.all_, self.sems = own, pair, slots, all_, sems
        self.rows, self.cols, self.row, self.col, _ = place()

    def to_pair(self, src, dst, at):
        return pltpu.make_async_remote_copy(
            src,
            dst,
            self.sems.at[at, 0],
            self.sems.at[at, 1],
            device_id=(self.row, 1 - self.col),
            device_id_type=MESH,
        )

    def out_copy(self):
        return self.to_pair(self.own.at[1 - self.col], self.pair, 0)

    def back_copy(self):
        return self.to_pair(self.all_.at[self.col], self.all_.at[self.col], 2)

    def put(self, value):
        self.own[0] = value[:, :LANES]
        self.own[1] = value[:, LANES:]

    def start(self):
        self.out_copy().start()

    def start_column(self):
        self.out_copy().wait()
        self.slots[self.row] = self.own[self.col] + self.pair[...]
        share_column(self.slots, self.sems.at[1])

    def start_back(self):
        shared_column(self.slots, self.sems.at[1])
        self.all_[self.col] = jnp.sum(self.slots[...], axis=0)
        self.back_copy().start()

    def finish(self):
        self.back_copy().wait()
        return jnp.concatenate([self.all_[0], self.all_[1]], axis=1)


def pair_sum_scratch(count):
    wide = jnp.float32
    return [
        pltpu.VMEM((2, count, LANES), wide),
        pltpu.VMEM((count, LANES), wide),
        pltpu.VMEM((lax.axis_size("rows"), count, LANES), wide),
        pltpu.VMEM((2, count, LANES), wide),
        pltpu.SemaphoreType.DMA((3, 2)),
    ]


def put_row(slots, me, at, vector):
    for part in range(vector.shape[1] // LANES):
        slots[me, at + part : at + part + 1, :] = vector[:, part * LANES : (part + 1) * LANES]


def take_row(table, at, width):
    parts = [table[at + part : at + part + 1, :] for part in range(width // LANES)]
    return parts[0] if len(parts) == 1 else jnp.concatenate(parts, axis=1)


def merged(slots, half, share_size, count):
    center = jnp.mean(slots[:, :half, :], axis=0)
    apart = slots[:, :half, :] - center[None]
    spread = jnp.sum(slots[:, half : 2 * half, :], axis=0) + share_size * jnp.sum(apart * apart, axis=0)
    return center, lax.rsqrt(spread / count + EPS)


def sigmoid(value):
    return 1.0 / (1.0 + jnp.exp(-value))


def across(left, right):
    return lax.dot_general(left, right, (((1,), (1,)), ((), ())), preferred_element_type=jnp.float32)


def down(left, right):
    return lax.dot_general(left, right, (((0,), (0,)), ((), ())), preferred_element_type=jnp.float32)


def pyramid_kernel(
    height,
    trunk,
    depth,
    sep_point,
    aspp_point,
    crop_part,
    crop_count,
    members,
    proj_weight,
    gains,
    shifts,
    head_weight,
    head_bias,
    factors,
    info,
    crop_sums,
    branch_low,
    proj_part,
    head_part,
    crop_local,
    crop_pre,
    sums_five,
    sums_four,
    crop_table,
    field,
    send_main,
    recv_main,
    send_side,
    recv_side,
    pre,
    joined,
    crop_act,
    projected,
    united,
    head_low,
    upstream,
    proj_low,
    branch_up,
    four_slots,
    five_slots,
    back_five,
    back_four,
    crop_pieces,
    main_sems,
    side_sems,
    four_sems,
    five_sems,
    back_five_sems,
    back_four_sems,
    piece_sems,
    table_sems,
    *crop_refs,
):
    rows, cols, row, col, me = place()
    low, wide = jnp.bfloat16, jnp.float32
    pixels = trunk.shape[0]
    width = pixels // height
    share_size = float(pixels)
    count = float(pixels * rows * cols)
    aspp = sep_point.shape[2]
    greet_all()

    def exists(target):
        return jnp.logical_and(target >= 0, target < rows)

    def step_of(index):
        return (BASE_RATE // height) * (index + 1)

    for index in range(3):
        step = BASE_RATE * (index + 1) // height
        for way in (0, 2):

            @pl.when(jnp.logical_not(exists(row - (1 - way) * step)))
            def _():
                recv_main[index, way] = jnp.zeros(recv_main.shape[2:], low)

    half = crop_part.shape[0]
    crop_total = PairSum(*crop_refs)
    crop_total.put(crop_part[...])
    pre[0] = jnp.dot(trunk[...], aspp_point[...], preferred_element_type=wide)
    await_all()
    crop_total.start()
    crop_pieces[me] = crop_sums[me]

    def scatter(step, carry):
        other = lax.rem(me + step, rows * cols)
        pltpu.make_async_remote_copy(
            crop_sums.at[other],
            crop_pieces.at[me],
            piece_sems.at[0],
            piece_sems.at[1],
            device_id=(other // cols, lax.rem(other, cols)),
            device_id_type=MESH,
        ).start()
        return carry

    lax.fori_loop(1, rows * cols, scatter, 0)
    side_from = pl.multiple_of((1 - col) * (PAD + width), 16)
    side_to = pl.multiple_of((1 - col) * (width - PAD), 16)

    def main_copy(index, way):
        return pltpu.make_async_remote_copy(
            send_main.at[index, way],
            recv_main.at[index, way],
            main_sems.at[0, index, way],
            main_sems.at[1, index, way],
            device_id=(row + (1 - way) * step_of(index), col),
            device_id_type=MESH,
        )

    def side_copy(index, way):
        return pltpu.make_async_remote_copy(
            send_side.at[index, way],
            recv_side.at[index, way],
            side_sems.at[0, index, way],
            side_sems.at[1, index, way],
            device_id=(row, 1 - col),
            device_id_type=MESH,
        )

    def flush(number):
        index, way = 2 - number // 3, lax.rem(2 * lax.rem(number, 3), 3)
        side_copy(index, way).wait_recv()

        @pl.when(way == 1)
        def _():
            for line in range(height):
                edge = pl.ds(pl.multiple_of(line * width + side_to, 16), PAD)
                pre[index + 1, edge, :] += recv_side[index, way, line].astype(wide)

        @pl.when(way != 1)
        def _():
            edge = pl.ds(side_to, PAD)
            send_main[index, way, :, edge, :] = (
                send_main[index, way, :, edge, :].astype(wide) + recv_side[index, way].astype(wide)
            ).astype(low)

            @pl.when(exists(row + (1 - way) * step_of(index)))
            def _():
                main_copy(index, way).start()

    for index in (2, 1, 0):
        rate = BASE_RATE * (index + 1)

        def one_way(turn, carry):
            way = lax.rem(2 * turn, 3)
            for sign in (0, 1, -1):
                tap = depth[pl.ds(index * 9 + 3 * way + 1 - sign, 1), :].astype(low)
                made = jnp.dot(trunk[...] * tap, sep_point[index], preferred_element_type=wide)
                for line in range(height):
                    part = made[line * width : (line + 1) * width, :]
                    if sign == 0:
                        field[line, PAD : PAD + width, :] = part
                        field[line, :PAD, :] = jnp.zeros((PAD, aspp), wide)
                        field[line, PAD + width :, :] = jnp.zeros((PAD, aspp), wide)
                    else:
                        at = PAD + sign * rate
                        field[line, at : at + width, :] += part
            send_side[index, way] = field[:, pl.ds(side_from, PAD), :].astype(low)

            @pl.when(way == 1)
            def _():
                for line in range(height):
                    pre[index + 1, line * width : (line + 1) * width, :] = field[
                        line, PAD : PAD + width, :
                    ]

            @pl.when(way != 1)
            def _():
                send_main[index, way] = field[:, PAD : PAD + width, :].astype(low)

            side_copy(index, way).start()
            number = 3 * (2 - index) + turn

            @pl.when(number > 0)
            def _():
                flush(number - 1)

            return carry

        lax.fori_loop(0, 3, one_way, 0)
    flush(8)
    crop_total.start_column()

    def lines(body, carry=0):
        def run(line, carry):
            return body(line, pl.ds(pl.multiple_of(line * width, width), width), carry)

        return lax.fori_loop(0, height, run, carry)

    zero_row = jnp.zeros((1, aspp), wide)

    def statistics(value_of, slots, at, half_rows):
        total = lines(
            lambda line, span, acc: acc + jnp.sum(value_of(span), axis=0, keepdims=True), zero_row
        )
        mean = total / share_size

        def squares(line, span, acc):
            apart = value_of(span) - mean
            return acc + jnp.sum(apart * apart, axis=0, keepdims=True)

        put_row(slots, me, at, mean)
        put_row(slots, me, half_rows + at, lines(squares, zero_row))

    per = aspp // LANES
    statistics(lambda span: pre[0, span, :], four_slots, 0, 4 * per)
    for index in (2, 1, 0):
        for way in (0, 2):

            @pl.when(exists(row - (1 - way) * step_of(index)))
            def _():
                main_copy(index, way).wait_recv()

        def assemble(line, span, carry):
            pre[index + 1, span, :] += recv_main[index, 0, line].astype(wide) + recv_main[
                index, 2, line
            ].astype(wide)
            return carry

        lines(assemble)
        statistics(lambda span: pre[index + 1, span, :], four_slots, per * (index + 1), 4 * per)
    share(four_slots, four_sems)
    crop_total.start_back()
    shared(crop_pieces, piece_sems)
    crop_table[me] = jnp.sum(crop_pieces[...], axis=0)
    share(crop_table, table_sems)
    crop_value = crop_total.finish() / crop_count[...]
    crop_pre[...] = crop_value
    crop_act[...] = jnp.zeros(crop_act.shape, low)
    crop_act[:half, :] = (crop_value * sigmoid(crop_value)).astype(low)

    def spread(line, span, carry):
        joined[span, 4 * aspp :] = jnp.dot(
            members[span, :], crop_act[...], preferred_element_type=wide
        ).astype(low)
        return carry

    lines(spread)
    shared(four_slots, four_sems)
    center_four, scale_four = merged(four_slots, 4 * per, share_size, count)
    centers = [take_row(center_four, per * part, aspp) for part in range(4)]
    scales = [take_row(scale_four, per * part, aspp) for part in range(4)]

    def activate(line, span, carry):
        for part in range(4):
            normed = (pre[part, span, :] - centers[part]) * scales[part]
            gated = normed * gains[part : part + 1, :] + shifts[part : part + 1, :]
            joined[span, part * aspp : (part + 1) * aspp] = (gated * sigmoid(gated)).astype(low)
        return carry

    lines(activate)
    projected[...] = jnp.dot(joined[...], proj_weight[...], preferred_element_type=wide)
    five_slots[me] = jnp.zeros(five_slots.shape[1:], wide)
    statistics(lambda span: projected[span, :], five_slots, 0, per)
    share(five_slots, five_sems)
    shared(five_slots, five_sems)
    center_five, scale_five = merged(five_slots, per, share_size, count)
    center_five, scale_five = take_row(center_five, 0, aspp), take_row(scale_five, 0, aspp)
    gain_five, shift_five = gains[4:5, :], shifts[4:5, :]
    lane = lax.broadcasted_iota(jnp.int32, (width, LANES), 1)

    def heads_of(line, span, carry):
        losses, bias_sum, shift_sum, gain_sum = carry
        normed = (projected[span, :] - center_five) * scale_five
        gated = normed * gain_five + shift_five
        sigma = sigmoid(gated)
        act = (gated * sigma).astype(low)
        united[span, :] = act
        heads = jnp.dot(act, head_weight[...], preferred_element_type=wide) + head_bias[0:1, :]
        facts = info[span, :]
        label, keep, valid = facts[:, 0:1], facts[:, 1:2], facts[:, 2:3]
        is_class = lane < CLASSES
        hot = jnp.where(lane.astype(wide) == label, 1.0, 0.0)
        target = jnp.zeros((width, LANES), wide)
        for part in range(4):
            target = jnp.where(lane == CLASSES + part, facts[:, 3 + part : 4 + part], target)
        top = jnp.max(jnp.where(is_class, heads, -jnp.inf), axis=1, keepdims=True)
        exps = jnp.where(is_class, jnp.exp(heads - top), 0.0)
        totals = jnp.sum(exps, axis=1, keepdims=True)
        picked = jnp.sum(jnp.where(is_class, heads, 0.0) * hot, axis=1, keepdims=True)
        error = jnp.where(is_class, 0.0, heads - target)
        root = jnp.sqrt(error * error + 1.0)
        is_depth, is_normal = lane == CLASSES, jnp.logical_and(lane > CLASSES, lane < CLASSES + 4)
        semantic = keep * (top + jnp.log(totals) - picked)
        terms = jnp.where(lane == 0, semantic, 0.0)
        terms = jnp.where(is_depth, valid * (root - 1.0), terms)
        terms = jnp.where(is_normal, valid * error * error, terms)
        grad = jnp.where(is_class, keep * (exps / totals - hot), 0.0)
        grad = jnp.where(is_depth, valid * error / root, grad)
        grad = jnp.where(is_normal, valid * error, grad)
        grad = grad * factors[0:1, :]
        grad_low = grad.astype(low)
        head_low[span, :] = grad_low
        up = across(grad_low, head_weight[...]) * (sigma * (1.0 + gated * (1.0 - sigma)))
        upstream[span, :] = up
        return (
            losses + jnp.sum(terms, axis=0, keepdims=True),
            bias_sum + jnp.sum(grad, axis=0, keepdims=True),
            shift_sum + jnp.sum(up, axis=0, keepdims=True),
            gain_sum + jnp.sum(up * normed, axis=0, keepdims=True),
        )

    zero_lane = jnp.zeros((1, LANES), wide)
    losses, bias_sum, shift_sum, gain_sum = lines(
        heads_of, (zero_lane, zero_lane, zero_row, zero_row)
    )
    back_five[me] = jnp.zeros(back_five.shape[1:], wide)
    put_row(back_five, me, 0, shift_sum)
    put_row(back_five, me, per, gain_sum)
    put_row(back_five, me, 2 * per, losses)
    put_row(back_five, me, 2 * per + 1, bias_sum)
    share(back_five, back_five_sems)
    head_part[...] = down(united[...], head_low[...]).astype(low)
    shared(back_five, back_five_sems)
    total_five = jnp.sum(back_five[...], axis=0)
    sums_five[...] = total_five
    shift_mean = take_row(total_five, 0, aspp) / count
    gain_mean = take_row(total_five, per, aspp) / count

    def project_back(line, span, carry):
        normed = (projected[span, :] - center_five) * scale_five
        inner = upstream[span, :] - shift_mean - normed * gain_mean
        proj_low[span, :] = (inner * (gain_five * scale_five)).astype(low)
        return carry

    lines(project_back)
    for part in range(4):
        branch_up[part] = across(
            proj_low[...], proj_weight[part * aspp : (part + 1) * aspp, :]
        )
    crop_up = across(proj_low[...], proj_weight[4 * aspp :, :])
    crop_high = crop_up.astype(low)
    crop_rest = (crop_up - crop_high.astype(wide)).astype(low)
    crop_sum = down(members[...], crop_high) + down(members[...], crop_rest)
    crop_local[...] = crop_sum[:half, :]

    for part in range(4):

        def branch_sums(line, span, carry):
            shift_sum, gain_sum = carry
            normed = (pre[part, span, :] - centers[part]) * scales[part]
            gated = normed * gains[part : part + 1, :] + shifts[part : part + 1, :]
            sigma = sigmoid(gated)
            up = branch_up[part, span, :] * (sigma * (1.0 + gated * (1.0 - sigma)))
            branch_up[part, span, :] = up
            return (
                shift_sum + jnp.sum(up, axis=0, keepdims=True),
                gain_sum + jnp.sum(up * normed, axis=0, keepdims=True),
            )

        shift_sum, gain_sum = lines(branch_sums, (zero_row, zero_row))
        put_row(back_four, me, per * part, shift_sum)
        put_row(back_four, me, per * (4 + part), gain_sum)
    share(back_four, back_four_sems)
    proj_part[...] = down(joined[...], proj_low[...]).astype(low)
    shared(back_four, back_four_sems)
    total_four = jnp.sum(back_four[...], axis=0)
    sums_four[...] = total_four
    for part in range(4):
        shift_mean = take_row(total_four, per * part, aspp) / count
        gain_mean = take_row(total_four, per * (4 + part), aspp) / count
        factor = gains[part : part + 1, :] * scales[part]

        def branch_back(line, span, carry):
            normed = (pre[part, span, :] - centers[part]) * scales[part]
            inner = branch_up[part, span, :] - shift_mean - normed * gain_mean
            branch_low[part, span, :] = (inner * factor).astype(low)
            return carry

        lines(branch_back)
    shared(crop_table, table_sems)
    for index in range(3):
        for way in range(3):
            side_copy(index, way).wait_send()
        for way in (0, 2):

            @pl.when(exists(row + (1 - way) * step_of(index)))
            def _():
                main_copy(index, way).wait_send()


def pyramid(height, trunk, depth, sep_point, aspp_point, crop_part, crop_count, members, proj_weight,
            gains, shifts, head_weight, head_bias, factors, info, crop_sums):
    devices = lax.axis_size("rows") * lax.axis_size("cols")
    pixels = trunk.shape[0]
    width = pixels // height
    aspp = sep_point.shape[2]
    crops = crop_part.shape[0]
    low, wide = jnp.bfloat16, jnp.float32
    shape = jax.ShapeDtypeStruct
    whole = pl.BlockSpec(memory_space=pltpu.VMEM)
    joined = proj_weight.shape[0]
    per = aspp // LANES
    outs = (
        shape((4, pixels, aspp), low),
        shape((joined, aspp), low),
        shape((aspp, LANES), low),
        shape((crops, aspp), wide),
        shape((crops, aspp), wide),
        shape((8, LANES), wide),
        shape((8 * per, LANES), wide),
        shape(crop_sums.shape, wide),
    )
    sems = pltpu.SemaphoreType.DMA
    return pl.pallas_call(
        functools.partial(pyramid_kernel, height),
        out_shape=outs,
        in_specs=[whole] * 15,
        out_specs=(whole,) * len(outs),
        scratch_shapes=[
            pltpu.VMEM((height, width + 2 * PAD, aspp), wide),
            pltpu.VMEM((3, 3, height, width, aspp), low),
            pltpu.VMEM((3, 3, height, width, aspp), low),
            pltpu.VMEM((3, 3, height, PAD, aspp), low),
            pltpu.VMEM((3, 3, height, PAD, aspp), low),
            pltpu.VMEM((4, pixels, aspp), wide),
            pltpu.VMEM((pixels, joined), low),
            pltpu.VMEM((LANES, aspp), low),
            pltpu.VMEM((pixels, aspp), wide),
            pltpu.VMEM((pixels, aspp), low),
            pltpu.VMEM((pixels, LANES), low),
            pltpu.VMEM((pixels, aspp), wide),
            pltpu.VMEM((pixels, aspp), low),
            pltpu.VMEM((4, pixels, aspp), wide),
            pltpu.VMEM((devices, 8 * per, LANES), wide),
            pltpu.VMEM((devices, 8, LANES), wide),
            pltpu.VMEM((devices, 8, LANES), wide),
            pltpu.VMEM((devices, 8 * per, LANES), wide),
            pltpu.VMEM(crop_sums.shape, wide),
            sems((2, 3, 3)),
            sems((2, 3, 3)),
            sems((2,)),
            sems((2,)),
            sems((2,)),
            sems((2,)),
            sems((2,)),
            sems((2,)),
            *pair_sum_scratch(crops),
        ],
        compiler_params=pltpu.CompilerParams(
            collective_id=10, has_side_effects=True, vmem_limit_bytes=VMEM_BYTES
        ),
        cost_estimate=pl.CostEstimate(
            flops=100 * pixels * trunk.shape[1] * aspp, bytes_accessed=64 * pixels * trunk.shape[1], transcendentals=0
        ),
        name="pyramid",
    )(trunk, depth, sep_point, aspp_point, crop_part, crop_count, members, proj_weight, gains, shifts,
      head_weight, head_bias, factors, info, crop_sums)


def pyramid_weights_kernel(
    branch_low,
    trunk,
    depth,
    sep_point,
    crop_local,
    proj_part,
    head_part,
    near,
    early,
    crop_total,
    depth_part,
    turned,
    shifted,
    moved,
    gathered,
    main_sems,
    edge_sems,
    *crop_refs,
):
    rows, cols, row, col, me = place()
    low, wide = jnp.bfloat16, jnp.float32
    height, width, aspp = branch_low.shape[1:]
    pixels, channels = trunk.shape
    crop_sum = PairSum(*crop_refs)
    crop_sum.put(crop_local[...])
    greet_all()

    def exists(target):
        return jnp.logical_and(target >= 0, target < rows)

    def step_of(index):
        return BASE_RATE * (index + 1) // height

    edge_from = pl.multiple_of(PAD + (1 - col) * (width - PAD), 16)
    edge_to = pl.multiple_of(col * (width + PAD), 16)
    blank = pl.multiple_of(col * (width + PAD), 16)

    def main_copy(index, way):
        return pltpu.make_async_remote_copy(
            branch_low.at[index + 1],
            near.at[index, way, :, pl.ds(PAD, width), :],
            main_sems.at[0, index, way],
            main_sems.at[1, index, way],
            device_id=(row + (1 - way) * step_of(index), col),
            device_id_type=MESH,
        )

    def edge_copy(index, way):
        return pltpu.make_async_remote_copy(
            near.at[index, way, :, pl.ds(edge_from, PAD), :],
            near.at[index, way, :, pl.ds(edge_to, PAD), :],
            edge_sems.at[0, index, way],
            edge_sems.at[1, index, way],
            device_id=(row, 1 - col),
            device_id_type=MESH,
        )

    for index in range(3):
        for way in range(3):
            near[index, way, :, pl.ds(blank, PAD), :] = jnp.zeros((height, PAD, aspp), low)
            if way == 1:
                near[index, way, :, PAD : PAD + width, :] = branch_low[index + 1]
            else:

                @pl.when(jnp.logical_not(exists(row - (1 - way) * step_of(index))))
                def _():
                    near[index, way] = jnp.zeros(near.shape[2:], low)

    await_all()
    for index in range(3):
        edge_copy(index, 1).start()

    def send(index):
        for way in (0, 2):

            @pl.when(exists(row + (1 - way) * step_of(index)))
            def _():
                main_copy(index, way).start()

    send(0)
    crop_sum.start()

    def turn(block, carry):
        span = pl.ds(pl.multiple_of(block * width, width), width)
        for line in range(height):
            turned[span, line * width : (line + 1) * width] = trunk[
                line * width : (line + 1) * width, span
            ].T
        return carry

    lax.fori_loop(0, channels // width, turn, 0)
    part_rows = channels // 2

    def point(part, carry):
        span = pl.ds(pl.multiple_of(part * part_rows, part_rows), part_rows)
        own = branch_low[0].reshape(pixels, aspp)
        early[pl.ds(pl.multiple_of(channels + part * part_rows, part_rows), part_rows), aspp:] = jnp.dot(
            turned[span, :], own, preferred_element_type=wide
        ).astype(low)
        return carry

    lax.fori_loop(0, 2, point, 0)
    lane = lax.broadcasted_iota(jnp.int32, (part_rows, LANES), 1)
    depth_part[...] = jnp.zeros(depth_part.shape, wide)
    gathered[...] = jnp.zeros(gathered.shape, wide)
    for index, way in ((0, 1), (1, 1), (2, 1), (0, 0), (0, 2), (1, 0), (1, 2), (2, 0), (2, 2)):
        rate = BASE_RATE * (index + 1)

        if way != 1:

            @pl.when(exists(row - (1 - way) * step_of(index)))
            def _():
                main_copy(index, way).wait_recv()
                edge_copy(index, way).start()

        for side in (1, 0, 2):
            if side == 0:

                @pl.when(exists(row - (1 - way) * step_of(index)))
                def _():
                    edge_copy(index, way).wait_recv()

                shifted[...] = near[index, way].astype(wide)
            tap = 3 * (2 - way) + side
            at = PAD - (side - 1) * rate
            for line in range(height):
                if side == 1:
                    piece = near[index, way, line, PAD : PAD + width, :]
                else:
                    piece = shifted[line, at : at + width, :].astype(low)
                moved[line * width : (line + 1) * width, :] = piece
            order = 9 * index + tap

            def collect(part, carry):
                span = pl.ds(pl.multiple_of(part * part_rows, part_rows), part_rows)
                made = jnp.dot(turned[span, :], moved[...], preferred_element_type=wide)
                gathered[index, span, :] += made * depth[span, order : order + 1]
                total = jnp.sum(made * sep_point[index, span, :].astype(wide), axis=1, keepdims=True)
                depth_part[span, :] = jnp.where(lane == order, total, depth_part[span, :])
                return carry

            lax.fori_loop(0, 2, collect, 0)
        if way == 1 and index > 0:
            send(index)
        if way == 1 and index == 0:
            crop_sum.start_column()
        if way == 0 and index == 0:
            crop_sum.start_back()
    early[:channels, :aspp] = gathered[0].astype(low)
    early[:channels, aspp:] = gathered[1].astype(low)
    early[channels : 2 * channels, :aspp] = gathered[2].astype(low)
    at = 2 * channels
    for table in (proj_part, depth_part, head_part):
        extent = table.shape[1]
        blocks = 2 * aspp // extent
        size = table.shape[0] // blocks
        for block in range(blocks):
            early[at : at + size, block * extent : (block + 1) * extent] = table[
                block * size : (block + 1) * size, :
            ].astype(low)
        at += size
    if early.shape[0] > at:
        early[at:, :] = jnp.zeros((early.shape[0] - at, 2 * aspp), low)
    crop_total[...] = crop_sum.finish()
    for index in range(3):
        for way in range(3):

            @pl.when(exists(row - (1 - way) * step_of(index)))
            def _():
                edge_copy(index, way).wait_send()

            if way != 1:

                @pl.when(exists(row + (1 - way) * step_of(index)))
                def _():
                    main_copy(index, way).wait_send()


def early_rows(channels, proj_part, head_part):
    rows = 2 * channels
    for size, extent in ((proj_part.shape[0], proj_part.shape[1]), (channels, LANES), head_part.shape):
        rows += size * extent // (2 * proj_part.shape[1])
    return rows


def pyramid_weights(branch_low, trunk, depth, sep_point, crop_local, proj_part, head_part):
    height, width, aspp = branch_low.shape[1:]
    pixels, channels = trunk.shape
    crops = crop_local.shape[0]
    low, wide = jnp.bfloat16, jnp.float32
    shape = jax.ShapeDtypeStruct
    whole = pl.BlockSpec(memory_space=pltpu.VMEM)
    sems = pltpu.SemaphoreType.DMA
    outs = (
        shape((3, 3, height, width + 2 * PAD, aspp), low),
        shape((sum_rows(early_rows(channels, proj_part, head_part)), 2 * aspp), low),
        shape((crops, aspp), wide),
    )
    return pl.pallas_call(
        pyramid_weights_kernel,
        out_shape=outs,
        in_specs=[whole] * 7,
        out_specs=(whole,) * len(outs),
        scratch_shapes=[
            pltpu.VMEM((channels, LANES), wide),
            pltpu.VMEM((channels, pixels), low),
            pltpu.VMEM((height, width + 2 * PAD, aspp), wide),
            pltpu.VMEM((pixels, aspp), low),
            pltpu.VMEM((3, channels, aspp), wide),
            sems((2, 3, 3)),
            sems((2, 3, 3)),
            *pair_sum_scratch(crops),
        ],
        compiler_params=pltpu.CompilerParams(
            collective_id=11, has_side_effects=True, vmem_limit_bytes=VMEM_BYTES
        ),
        cost_estimate=pl.CostEstimate(
            flops=100 * pixels * channels * aspp, bytes_accessed=64 * pixels * channels, transcendentals=0
        ),
        name="pyramid_weights",
    )(branch_low, trunk, depth, sep_point, crop_local, proj_part, head_part)


def share_rows(slots, at, size, sems):
    rows, cols, row, col, me = place()

    def go(step, carry):
        other = lax.rem(me + step, rows * cols)
        mine = slots.at[me, pl.ds(at, size), :]
        pltpu.make_async_remote_copy(
            mine,
            mine,
            sems.at[0],
            sems.at[1],
            device_id=(other // cols, lax.rem(other, cols)),
            device_id_type=MESH,
        ).start()
        return carry

    lax.fori_loop(1, rows * cols, go, 0)


def shared_rows(slots, at, size, sems):
    rows, cols, row, col, me = place()
    others = slots.at[pl.ds(0, rows * cols - 1), pl.ds(at, size), :]
    pltpu.make_async_remote_copy(
        others,
        others,
        sems.at[0],
        sems.at[1],
        device_id=(row, lax.rem(col + 1, cols)),
        device_id_type=MESH,
    ).wait()


def trunk_back_kernel(
    near,
    own_low,
    depth,
    sep_point,
    aspp_point,
    members,
    crop_high,
    crop_rest,
    expanded,
    features,
    three,
    dilated,
    two,
    second_act,
    expand_weight,
    early,
    pre_grad,
    expand_part,
    dilated_low,
    sums_three,
    sums_two,
    early_out,
    fetched,
    chunk_in,
    shifted,
    moved,
    maps,
    grown,
    expand_low,
    slots_three,
    slots_two,
    sems_three,
    sems_two,
    fetch_sems,
    chunk_sems,
    *early_refs,
):
    rows, cols, row, col, me = place()
    low, wide = jnp.bfloat16, jnp.float32
    height = near.shape[2]
    early_sum = Sums(early, True, early_out, early_refs)
    aspp = sep_point.shape[2]
    pixels, channels = expanded.shape
    middle = dilated.shape[1]
    width = pixels // height
    count = float(pixels * rows * cols)
    per = aspp // LANES
    chunks = channels // aspp
    greet_all()

    def fetch(number):
        return pltpu.make_async_copy(
            near.at[number // 3, number % 3], fetched.at[number % 2], fetch_sems.at[number % 2]
        )

    fetch(0).start()
    early_sum.fetch()

    def chunk_of(block):
        return pl.ds(pl.multiple_of(block * aspp, aspp), aspp)

    def own(block, carry):
        span = chunk_of(block)
        grown[:, span] = (
            across(own_low[...], aspp_point[span, :])
            + jnp.dot(members[...], crop_high[:, span], preferred_element_type=wide)
            + jnp.dot(members[...], crop_rest[:, span], preferred_element_type=wide)
        )
        return carry

    lax.fori_loop(0, chunks, own, 0)
    await_all()
    early_sum.fetched()
    early_sum.start_half()

    def fetch_chunk(block):
        slot = lax.rem(block, 2)
        return pltpu.make_async_copy(
            expanded.at[:, chunk_of(block)], chunk_in.at[slot], chunk_sems.at[slot]
        )

    def advance(block):
        @pl.when(block + 1 < chunks)
        def _():
            fetch_chunk(block + 1).start()

        fetch_chunk(block).wait()

    def back(block, line, span):
        rows_span = slice(line * width, (line + 1) * width)
        value = chunk_in[lax.rem(block, 2), rows_span, :]
        normed = (value - three[0:1, span]) * three[1:2, span]
        return rows_span, normed

    for index in range(3):
        rate = BASE_RATE * (index + 1)
        for way in range(3):
            number = 3 * index + way
            if number < 8:
                fetch(number + 1).start()
            fetch(number).wait()
            shifted[...] = fetched[number % 2].astype(wide)
            for side in range(3):
                tap = 3 * (2 - way) + side
                at = PAD - (side - 1) * rate
                for line in range(height):
                    moved[line * width : (line + 1) * width, tap * aspp : (tap + 1) * aspp] = shifted[
                        line, at : at + width, :
                    ].astype(low)

        def one_chunk(block, carry):
            span = chunk_of(block)
            rows_of = sep_point[index, span, :].astype(wide)
            for tap in range(9):
                order = 9 * index + tap
                maps[:, tap * aspp : (tap + 1) * aspp] = (
                    rows_of * depth[span, order : order + 1]
                ).astype(low)
            total = grown[:, span] + across(moved[...], maps[...])
            if index < 2:
                grown[:, span] = total
                return carry
            advance(block)
            shift_sum, gain_sum = jnp.zeros((1, aspp), wide), jnp.zeros((1, aspp), wide)
            for line in range(height):
                rows_span, normed = back(block, line, span)
                gated = (
                    normed * three[2:3, span]
                    + three[3:4, span]
                    + features[rows_span, span].astype(wide)
                )
                sigma = sigmoid(gated)
                up = total[rows_span, :] * (sigma * (1.0 + gated * (1.0 - sigma)))
                grown[rows_span, span] = up
                pre_grad[rows_span, span] = up.astype(low)
                shift_sum = shift_sum + jnp.sum(up, axis=0, keepdims=True)
                gain_sum = gain_sum + jnp.sum(up * normed, axis=0, keepdims=True)
            for part in range(per):
                lanes = slice(part * LANES, (part + 1) * LANES)
                slots_three[me, pl.ds(block * 2 * per + part, 1), :] = shift_sum[:, lanes]
                slots_three[me, pl.ds(block * 2 * per + per + part, 1), :] = gain_sum[:, lanes]
            pair = block // 2

            @pl.when(lax.rem(block, 2) == 1)
            def _():
                share_rows(slots_three, pl.multiple_of(pair * 4 * per, 8), 4 * per, sems_three.at[pair])

            return carry

        if index == 0:
            early_sum.start_level(0)
        if index == 2:
            fetch_chunk(0).start()
        lax.fori_loop(0, chunks, one_chunk, 0)
        if index == 1:
            early_sum.start_level(1)

    def finish(block, carry):
        span = chunk_of(block)
        pair = block // 2
        at = pl.multiple_of(pair * 4 * per, 8)

        @pl.when(lax.rem(block, 2) == 0)
        def _():
            shared_rows(slots_three, at, 4 * per, sems_three.at[pair])
            sums_three[pl.ds(at, 4 * per), :] = jnp.sum(slots_three[:, pl.ds(at, 4 * per), :], axis=0)

        advance(block)

        def row_at(start):
            first = block * 2 * per + start
            return jnp.concatenate([sums_three[pl.ds(first + part, 1), :] for part in range(per)], axis=1)

        shift_mean = row_at(0) / count
        gain_mean = row_at(per) / count
        factor = three[2:3, span] * three[1:2, span]
        for line in range(height):
            rows_span, normed = back(block, line, span)
            inner = grown[rows_span, span] - shift_mean - normed * gain_mean
            expand_low[rows_span, span] = (inner * factor).astype(low)
        return carry

    early_sum.start_back(1)
    fetch_chunk(0).start()
    lax.fori_loop(0, chunks, finish, 0)
    early_sum.start_back(0)
    grown_two = across(expand_low[...], expand_weight[...])
    shift_sum, gain_sum = jnp.zeros((1, middle), wide), jnp.zeros((1, middle), wide)
    for line in range(height):
        rows_span = slice(line * width, (line + 1) * width)
        normed = (dilated[rows_span, :] - two[0:1, :]) * two[1:2, :]
        gated = normed * two[2:3, :] + two[3:4, :]
        sigma = sigmoid(gated)
        up = grown_two[rows_span, :] * (sigma * (1.0 + gated * (1.0 - sigma)))
        grown[rows_span, :middle] = up
        shift_sum = shift_sum + jnp.sum(up, axis=0, keepdims=True)
        gain_sum = gain_sum + jnp.sum(up * normed, axis=0, keepdims=True)
    per_two = middle // LANES
    put_row(slots_two, me, 0, shift_sum)
    put_row(slots_two, me, per_two, gain_sum)
    share(slots_two, sems_two)
    for block in range(channels // middle):
        span = slice(block * middle, (block + 1) * middle)
        expand_part[block * middle : (block + 1) * middle, :] = down(
            second_act[...], expand_low[:, span]
        ).astype(low)
    shared(slots_two, sems_two)
    total = jnp.sum(slots_two[...], axis=0)
    sums_two[...] = total
    shift_mean = take_row(total, 0, middle) / count
    gain_mean = take_row(total, per_two, middle) / count
    factor = two[2:3, :] * two[1:2, :]
    for line in range(height):
        rows_span = slice(line * width, (line + 1) * width)
        normed = (dilated[rows_span, :] - two[0:1, :]) * two[1:2, :]
        inner = grown[rows_span, :middle] - shift_mean - normed * gain_mean
        dilated_low[rows_span, :] = (inner * factor).astype(low)
    early_sum.start_back_half()
    early_sum.finish()


def trunk_back(near, own_low, depth, sep_point, aspp_point, members, crop_high, crop_rest, expanded,
               features, three, dilated, two, second_act, expand_weight, early):
    devices = lax.axis_size("rows") * lax.axis_size("cols")
    height, extent, aspp = near.shape[2:]
    pixels, channels = expanded.shape
    middle = dilated.shape[1]
    chunks = channels // aspp
    low, wide = jnp.bfloat16, jnp.float32
    shape = jax.ShapeDtypeStruct
    whole = pl.BlockSpec(memory_space=pltpu.VMEM)
    away = pl.BlockSpec(memory_space=pl.ANY)
    sems = pltpu.SemaphoreType.DMA
    per_two = middle // LANES
    outs = (
        shape((pixels, channels), low),
        shape((channels, middle), low),
        shape((pixels, middle), low),
        shape((chunks * 2 * (aspp // LANES), LANES), wide),
        shape((2 * per_two, LANES), wide),
        shape(early.shape, low),
    )
    return pl.pallas_call(
        trunk_back_kernel,
        out_shape=outs,
        in_specs=[away] + [whole] * 7 + [away] + [whole] * 6 + [away],
        out_specs=(whole,) * 5 + (away,),
        scratch_shapes=[
            pltpu.VMEM((2, height, extent, aspp), low),
            pltpu.VMEM((2, pixels, aspp), wide),
            pltpu.VMEM((height, extent, aspp), wide),
            pltpu.VMEM((pixels, 9 * aspp), low),
            pltpu.VMEM((aspp, 9 * aspp), low),
            pltpu.VMEM((pixels, channels), wide),
            pltpu.VMEM((pixels, channels), low),
            pltpu.VMEM((devices, chunks * 2 * (aspp // LANES), LANES), wide),
            pltpu.VMEM((devices, 2 * per_two, LANES), wide),
            sems((chunks // 2, 2)),
            sems((2,)),
            sems((2,)),
            sems((2,)),
            *sums_scratch(*early.shape, True),
        ],
        compiler_params=pltpu.CompilerParams(
            collective_id=12, has_side_effects=True, vmem_limit_bytes=VMEM_BYTES + (3 << 20)
        ),
        cost_estimate=pl.CostEstimate(
            flops=80 * pixels * channels * aspp, bytes_accessed=64 * pixels * channels, transcendentals=0
        ),
        name="trunk_back",
    )(near, own_low, depth, sep_point, aspp_point, members, crop_high, crop_rest, expanded, features,
      three, dilated, two, second_act, expand_weight, early)


EDGE = 16


class Halo:
    def __init__(self, near, direct, relay, edge):
        self.near, self.direct, self.relay, self.edge = near, direct, relay, edge
        self.rows, self.cols, self.row, self.col, _ = place()
        self.height, self.width = near.shape[1], near.shape[2] - 2 * EDGE
        self.odd = lax.rem(self.row, 2)
        self.pair = self.row + 1 - 2 * self.odd
        self.onward = self.row + 2 - 4 * self.odd
        self.far = self.row - 1 + 2 * self.odd
        self.pair_way = 2 - 2 * self.odd
        self.far_way = 2 * self.odd

    def exists(self, target):
        return jnp.logical_and(target >= 0, target < self.rows)

    def line_ref(self, way, line):
        return self.near.at[way, line, pl.ds(EDGE, self.width), :]

    def direct_copy(self, line):
        return pltpu.make_async_remote_copy(
            self.line_ref(1, line),
            self.line_ref(self.far_way, line),
            self.direct.at[0, line],
            self.direct.at[1, line],
            device_id=(self.pair, self.col),
            device_id_type=MESH,
        )

    def relay_copy(self, line):
        return pltpu.make_async_remote_copy(
            self.line_ref(self.pair_way, line),
            self.line_ref(self.far_way, line),
            self.relay.at[0, line],
            self.relay.at[1, line],
            device_id=(self.onward, self.col),
            device_id_type=MESH,
        )

    def edge_copy(self, way):
        start = pl.multiple_of(EDGE + (1 - self.col) * (self.width - EDGE), 16)
        end = pl.multiple_of(self.col * (self.width + EDGE), 16)
        return pltpu.make_async_remote_copy(
            self.near.at[1, :, pl.ds(start, EDGE), :],
            self.near.at[way, :, pl.ds(end, EDGE), :],
            self.edge.at[0, way],
            self.edge.at[1, way],
            device_id=(self.row + 1 - way, 1 - self.col),
            device_id_type=MESH,
        )

    def clear(self):
        near = self.near
        blank = pl.multiple_of(self.col * (self.width + EDGE), 16)
        for way in range(3):
            near[way, :, pl.ds(blank, EDGE), :] = jnp.zeros(
                (self.height, EDGE, near.shape[3]), near.dtype
            )

        @pl.when(jnp.logical_not(self.exists(self.far)))
        def _():
            near[self.far_way] = jnp.zeros(near.shape[1:], near.dtype)

    def start(self):
        self.edge_copy(1).start()
        for line in range(self.height):
            self.direct_copy(line).start()
        for way in (0, 2):

            @pl.when(self.exists(self.row + 1 - way))
            def _():
                self.edge_copy(way).start()

    def wait_own(self):
        self.edge_copy(1).wait_recv()

    def pass_on(self):
        for line in range(self.height):
            self.direct_copy(line).wait_recv()

            @pl.when(self.exists(self.onward))
            def _():
                self.relay_copy(line).start()

    def wait_rest(self):
        self.wait_edges()
        self.wait_relay()

    def wait_edges(self):
        for way in (0, 2):

            @pl.when(self.exists(self.row - 1 + way))
            def _():
                self.edge_copy(way).wait_recv()

    def wait_relay(self):
        @pl.when(self.exists(self.far))
        def _():
            for line in range(self.height):
                self.relay_copy(line).wait_recv()

    def drain(self):
        self.edge_copy(1).wait_send()
        for line in range(self.height):
            self.direct_copy(line).wait_send()
        for way in (0, 2):

            @pl.when(self.exists(self.row + 1 - way))
            def _():
                self.edge_copy(way).wait_send()

        @pl.when(self.exists(self.onward))
        def _():
            for line in range(self.height):
                self.relay_copy(line).wait_send()


def front_kernel(
    features,
    reduce_weight,
    dilated_weight,
    expand_weight,
    pool_weight,
    one_in,
    two_in,
    three_in,
    counts,
    members,
    reduced,
    first_act,
    dilated,
    second_act,
    expanded,
    trunk,
    one,
    two,
    three,
    count_sums,
    crop_sums,
    crop_part,
    near,
    shifted,
    moved,
    one_slots,
    two_slots,
    three_own,
    three_pair,
    three_slots,
    three_all,
    direct,
    relay,
    edge,
    one_sems,
    two_sems,
    pair_sems,
    three_sems,
    all_sems,
):
    rows, cols, row, col, me = place()
    low, wide = jnp.bfloat16, jnp.float32
    height = near.shape[1]
    pixels, middle = reduced.shape
    channels = features.shape[1]
    width = pixels // height
    share_size = float(pixels)
    count = float(pixels * rows * cols)
    per = middle // LANES
    halo = Halo(near, direct, relay, edge)
    greet_all()
    halo.clear()
    reduced[...] = jnp.dot(features[...], reduce_weight[...], preferred_element_type=wide)

    def lines(body, carry=0):
        def run(line, carry):
            return body(line, pl.ds(pl.multiple_of(line * width, width), width), carry)

        return lax.fori_loop(0, height, run, carry)

    def keep_low(line, span, carry):
        near[1, line, EDGE : EDGE + width, :] = reduced[span, :].astype(low)
        return carry

    lines(keep_low)
    await_all()
    halo.start()

    def statistics(value_of, extent):
        zero = jnp.zeros((1, extent), wide)
        total = lines(lambda line, span, acc: acc + jnp.sum(value_of(span), axis=0, keepdims=True), zero)
        mean = total / share_size

        def squares(line, span, acc):
            apart = value_of(span) - mean
            return acc + jnp.sum(apart * apart, axis=0, keepdims=True)

        return mean, lines(squares, zero)

    def settle(table, given, center, scale):
        table[...] = jnp.zeros(table.shape, wide)
        table[0:1, :] = center
        table[1:2, :] = scale
        table[2:4, :] = given[0:2, :]

    def activated(value, table):
        gated = (value - table[0:1, :]) * table[1:2, :] * table[2:3, :] + table[3:4, :]
        return gated * sigmoid(gated)

    mean, square = statistics(lambda span: reduced[span, :], middle)
    one_slots[me] = jnp.zeros(one_slots.shape[1:], wide)
    put_row(one_slots, me, 0, mean)
    put_row(one_slots, me, per, square)
    put_row(one_slots, me, 2 * per, counts[0:1, :])
    share(one_slots, one_sems)
    shared(one_slots, one_sems)
    center, scale = merged(one_slots, per, share_size, count)
    settle(one, one_in, take_row(center, 0, middle), take_row(scale, 0, middle))
    count_sums[...] = jnp.sum(one_slots[:, 2 * per : 2 * per + 8, :], axis=0)

    def first(line, span, carry):
        first_act[span, :] = activated(reduced[span, :], one).astype(low)
        return carry

    lines(first)

    def one_way(way, own):
        alive = jnp.where(halo.exists(row - 1 + way), 1.0, 0.0)

        def open_line(line, span, carry):
            shifted[line] = activated(near[way, line].astype(wide), one) * alive
            if own:
                shifted[line, EDGE : EDGE + width, :] = first_act[span, :].astype(wide)
            blank = pl.multiple_of(col * (width + EDGE), 16)
            shifted[line, pl.ds(blank, EDGE), :] = jnp.zeros((EDGE, middle), wide)
            for side in range(3):
                at = EDGE + (side - 1) * MID_RATE
                moved[span, side * middle : (side + 1) * middle] = shifted[
                    line, at : at + width, :
                ].astype(low)
            return carry

        lines(open_line)
        made = jnp.dot(moved[...], dilated_weight[way], preferred_element_type=wide)
        if own:
            dilated[...] = made
        else:
            dilated[...] += made

    halo.wait_own()
    one_way(1, True)
    halo.pass_on()
    halo.wait_edges()
    one_way(halo.pair_way, False)
    halo.wait_relay()
    one_way(halo.far_way, False)
    mean, square = statistics(lambda span: dilated[span, :], middle)
    put_row(two_slots, me, 0, mean)
    put_row(two_slots, me, per, square)
    share(two_slots, two_sems)
    shared(two_slots, two_sems)
    center, scale = merged(two_slots, per, share_size, count)
    settle(two, two_in, take_row(center, 0, middle), take_row(scale, 0, middle))

    def second(line, span, carry):
        second_act[span, :] = activated(dilated[span, :], two).astype(low)
        return carry

    lines(second)
    chunk = 2 * LANES
    half_rows = channels // 2 // LANES
    half_chunks = channels // 2 // chunk

    def expand(block, carry):
        span = pl.ds(pl.multiple_of(block * chunk, chunk), chunk)
        expanded[:, span] = jnp.dot(second_act[...], expand_weight[:, span], preferred_element_type=wide)
        mean, square = statistics(lambda rows_span: expanded[rows_span, span], chunk)
        at = block // half_chunks * 2 * half_rows + lax.rem(block, half_chunks) * 2
        for part in range(2):
            lanes = slice(part * LANES, (part + 1) * LANES)
            three_own[pl.ds(at + part, 1), :] = mean[:, lanes]
            three_own[pl.ds(at + half_rows + part, 1), :] = square[:, lanes]
        return carry

    lax.fori_loop(0, channels // chunk, expand, 0)

    def to_pair(src, dst, sems):
        return pltpu.make_async_remote_copy(
            src, dst, sems.at[0], sems.at[1], device_id=(row, 1 - col), device_id_type=MESH
        )

    theirs = pl.ds(pl.multiple_of((1 - col) * 2 * half_rows, 8), 2 * half_rows)
    mine = pl.ds(pl.multiple_of(col * 2 * half_rows, 8), 2 * half_rows)
    copy = to_pair(three_own.at[theirs], three_pair, pair_sems)
    copy.start()
    copy.wait()
    own = three_own[mine, :]
    other = three_pair[...]
    apart = own[:half_rows] - other[:half_rows]
    three_slots[row, :half_rows, :] = 0.5 * (own[:half_rows] + other[:half_rows])
    three_slots[row, half_rows:, :] = (
        own[half_rows:] + other[half_rows:] + (0.5 * share_size) * (apart * apart)
    )
    share_column(three_slots, three_sems)
    shared_column(three_slots, three_sems)
    center, scale = merged(three_slots, half_rows, 2.0 * share_size, count)
    three_all[col, :half_rows, :] = center
    three_all[col, half_rows:, :] = scale
    copy = to_pair(three_all.at[col], three_all.at[col], all_sems)
    copy.start()
    copy.wait()
    for half in range(2):
        span = slice(half * channels // 2, (half + 1) * channels // 2)
        three[0:1, span] = take_row(three_all[half], 0, channels // 2)
        three[1:2, span] = take_row(three_all[half], half_rows, channels // 2)
    three[2:4, :] = three_in[0:2, :]
    three[4:8, :] = jnp.zeros((4, channels), wide)
    crops = crop_sums.shape[0]

    def last(block, carry):
        span = pl.ds(pl.multiple_of(block * chunk, chunk), chunk)

        def act_line(line, rows_span, carry):
            normed = (expanded[rows_span, span] - three[0:1, span]) * three[1:2, span]
            gated = (
                normed * three[2:3, span] + three[3:4, span] + features[rows_span, span].astype(wide)
            )
            trunk[rows_span, span] = (gated * sigmoid(gated)).astype(low)
            return carry

        lines(act_line)
        sums = jnp.dot(members[...], trunk[:, span], preferred_element_type=wide)[:crops, :]
        crop_sums[:, span] = sums
        high = sums.astype(low)
        rest = (sums - high.astype(wide)).astype(low)
        return (
            carry
            + jnp.dot(high, pool_weight[span, :], preferred_element_type=wide)
            + jnp.dot(rest, pool_weight[span, :], preferred_element_type=wide)
        )

    crop_part[...] = lax.fori_loop(
        0, channels // chunk, last, jnp.zeros((crops, pool_weight.shape[1]), wide)
    )
    halo.drain()


def front(height, features, reduce_weight, dilated_weight, expand_weight, pool_weight, one_in, two_in,
          three_in, counts, members):
    rows = lax.axis_size("rows")
    devices = rows * lax.axis_size("cols")
    pixels, channels = features.shape
    middle = reduce_weight.shape[1]
    width = pixels // height
    low, wide = jnp.bfloat16, jnp.float32
    shape = jax.ShapeDtypeStruct
    whole = pl.BlockSpec(memory_space=pltpu.VMEM)
    sems = pltpu.SemaphoreType.DMA
    per = middle // LANES
    half_rows = channels // 2 // LANES
    outs = (
        shape((pixels, middle), wide),
        shape((pixels, middle), low),
        shape((pixels, middle), wide),
        shape((pixels, middle), low),
        shape((pixels, channels), wide),
        shape((pixels, channels), low),
        shape((8, middle), wide),
        shape((8, middle), wide),
        shape((8, channels), wide),
        shape((8, LANES), wide),
        shape((CROPS, channels), wide),
        shape((CROPS, pool_weight.shape[1]), wide),
    )
    return pl.pallas_call(
        front_kernel,
        out_shape=outs,
        in_specs=[whole] * 10,
        out_specs=(whole,) * len(outs),
        scratch_shapes=[
            pltpu.VMEM((3, height, width + 2 * EDGE, middle), low),
            pltpu.VMEM((height, width + 2 * EDGE, middle), wide),
            pltpu.VMEM((pixels, 3 * middle), low),
            pltpu.VMEM((devices, 2 * per + 8, LANES), wide),
            pltpu.VMEM((devices, 2 * per, LANES), wide),
            pltpu.VMEM((4 * half_rows, LANES), wide),
            pltpu.VMEM((2 * half_rows, LANES), wide),
            pltpu.VMEM((rows, 2 * half_rows, LANES), wide),
            pltpu.VMEM((2, 2 * half_rows, LANES), wide),
            sems((2, height)),
            sems((2, height)),
            sems((2, 3)),
            sems((2,)),
            sems((2,)),
            sems((2,)),
            sems((2,)),
            sems((2,)),
        ],
        compiler_params=pltpu.CompilerParams(
            collective_id=14, has_side_effects=True, vmem_limit_bytes=VMEM_BYTES
        ),
        name="front",
    )(features, reduce_weight, dilated_weight, expand_weight, pool_weight, one_in, two_in, three_in,
      counts, members)


PLANE = 4


class Sum:
    def __init__(self, full, own, out, plane_first, half_in, near_in, far_in, half_sem, near_sem, far_sem, copy_sem):
        self.full, self.out, self.half_in = full, out, half_in
        self.half_sem, self.copy_sem = half_sem, copy_sem
        self.rows, self.cols, self.row, self.col, _ = place()
        parts = self.rows // PLANE
        quarter, part = lax.rem(self.row, PLANE), self.row // PLANE
        plane = (PLANE, quarter, lambda mate: part * PLANE + mate)
        rest = (parts, part, lambda mate: mate * PLANE + quarter)
        self.levels = (plane, rest) if plane_first else (rest, plane)
        self.arrivals, self.sems = (near_in, far_in), (near_sem, far_sem)
        self.half_rows = full.shape[0] // 2
        self.sizes = [self.half_rows // self.levels[0][0]]
        self.sizes.append(self.sizes[0] // self.levels[1][0])
        self.own = own
        self.data = full.at[self.half_span(self.col)] if own is None else own

    def span(self, start, size):
        return pl.ds(pl.multiple_of(start, 16), size)

    def half_span(self, col):
        return self.span(col * self.half_rows, self.half_rows)

    def level_span(self, level, at):
        base = 0 if level == 0 else self.levels[0][1] * self.sizes[0]
        return self.span(base + at * self.sizes[level], self.sizes[level])

    def out_at(self, span):
        return self.out.at[self.span(self.col * self.half_rows + span.start, span.size)]

    def mates(self, level):
        count, at, row_of = self.levels[level]
        for step in range(1, count):
            mate = lax.rem(at + step, count)
            yield mate, (row_of(mate), self.col)

    def remote(self, src, dst, sems, out_at, in_at, target):
        return pltpu.make_async_remote_copy(
            src, dst, sems.at[0, out_at], sems.at[1, in_at], device_id=target, device_id_type=MESH
        )

    def fetch(self):
        return pltpu.make_async_copy(self.full.at[self.half_span(self.col)], self.own, self.copy_sem)

    def half_copy(self):
        other = self.full.at[self.half_span(1 - self.col)]
        return self.remote(other, self.half_in, self.half_sem, 0, 0, (self.row, 1 - self.col))

    def level_copy(self, level, mate, target):
        at = self.levels[level][1]
        return self.remote(
            self.data.at[self.level_span(level, mate)],
            self.arrivals[level].at[at],
            self.sems[level],
            mate,
            at,
            target,
        )

    def level_arrival(self, level, mate, target):
        slot = self.arrivals[level].at[mate]
        return self.remote(slot, slot, self.sems[level], mate, mate, target)

    def back_copy(self, level, mate, target):
        count, at, _ = self.levels[level]
        mine = self.out_at(self.level_span(level, at))
        return self.remote(mine, mine, self.sems[level], count + mate, count + at, target)

    def back_arrival(self, level, mate, target):
        count = self.levels[level][0]
        theirs = self.out_at(self.level_span(level, mate))
        return self.remote(theirs, theirs, self.sems[level], count + mate, count + mate, target)

    def back_half(self, col):
        part = self.out.at[self.half_span(col)]
        return self.remote(part, part, self.half_sem, 1, 1, (self.row, 1 - self.col))

    def add(self, span, sources):
        block = 64
        base = span.start

        def some(at, carry):
            rows = pl.ds(pl.multiple_of(base + at * block, 16), block)
            total = self.data[rows, :].astype(jnp.float32)
            for source in sources:
                total = total + source(pl.ds(pl.multiple_of(at * block, 16), block)).astype(jnp.float32)
            self.data[rows, :] = total.astype(self.data.dtype)
            return carry

        full = span.size // block
        lax.fori_loop(0, full, some, 0)
        rest = span.size - full * block
        if rest:
            rows = pl.ds(pl.multiple_of(base + full * block, 16), rest)
            total = self.data[rows, :].astype(jnp.float32)
            for source in sources:
                total = total + source(pl.ds(full * block, rest)).astype(jnp.float32)
            self.data[rows, :] = total.astype(self.data.dtype)

    def start_half(self):
        self.half_copy().start()

    def start_level(self, level):
        if level == 0:
            self.half_copy().wait()
            self.add(self.span(0, self.half_rows), [lambda rows: self.half_in[rows, :]])
        else:
            self.gather(0)
        for mate, target in self.mates(level):
            self.level_copy(level, mate, target).start()

    def gather(self, level):
        for mate, target in self.mates(level):
            self.level_copy(level, mate, target).wait_send()
            self.level_arrival(level, mate, target).wait_recv()
        self.add(
            self.level_span(level, self.levels[level][1]),
            [lambda rows, mate=mate: self.arrivals[level][mate, rows, :] for mate, _ in self.mates(level)],
        )

    def start_back(self, level):
        if level == 1:
            self.gather(1)
            span = self.level_span(1, self.levels[1][1])
            copy = pltpu.make_async_copy(self.data.at[span], self.out_at(span), self.copy_sem)
            copy.start()
            copy.wait()
        else:
            for mate, target in self.mates(1):
                self.back_copy(1, mate, target).wait_send()
                self.back_arrival(1, mate, target).wait_recv()
        for mate, target in self.mates(level):
            self.back_copy(level, mate, target).start()

    def start_back_half(self):
        for mate, target in self.mates(0):
            self.back_copy(0, mate, target).wait_send()
            self.back_arrival(0, mate, target).wait_recv()
        self.back_half(self.col).start()

    def finish(self):
        self.back_half(self.col).wait_send()
        self.back_half(1 - self.col).wait_recv()


class Sums:
    def __init__(self, full, own, out, refs):
        self.each = []
        start = 0
        for size, plane_first in sum_pieces(full.shape[0]):
            span = pl.ds(start, size)
            count = 7 if own is None else 8
            mine, refs = list(refs[:count]), refs[count:]
            part = None if own is None else mine.pop(0)
            self.each.append(Sum(full.at[span], part, out.at[span], plane_first, *mine))
            start += size
        self.rest = refs

    def fetch(self):
        for each in self.each:
            each.fetch().start()

    def fetched(self):
        for each in self.each:
            each.fetch().wait()

    def start_half(self):
        for each in self.each:
            each.start_half()

    def start_level(self, level):
        for each in self.each:
            each.start_level(level)

    def start_back(self, level):
        for each in self.each:
            each.start_back(level)

    def start_back_half(self):
        for each in self.each:
            each.start_back_half()

    def finish(self):
        for each in self.each:
            each.finish()


def sum_unit():
    return 2 * lax.axis_size("rows") * 16


def sum_pieces(total):
    unit = sum_unit()
    units = total // unit
    second = units // 3
    pieces = [((units - second) * unit, True)]
    if second:
        pieces.append((second * unit, False))
    return pieces


def sums_scratch(total, lanes, away):
    parts = lax.axis_size("rows") // PLANE
    low, sems = jnp.bfloat16, pltpu.SemaphoreType.DMA
    scratch = []
    for size, plane_first in sum_pieces(total):
        counts = (PLANE, parts) if plane_first else (parts, PLANE)
        half = size // 2
        if away:
            scratch.append(pltpu.VMEM((half, lanes), low))
        scratch += [
            pltpu.VMEM((half, lanes), low),
            pltpu.VMEM((counts[0], half // counts[0], lanes), low),
            pltpu.VMEM((counts[1], half // counts[0] // counts[1], lanes), low),
            sems((2, 2)),
            sems((2, 2 * counts[0])),
            sems((2, 2 * counts[1])),
            sems,
        ]
    return scratch


def sum_rows(rows):
    unit = sum_unit()
    return -(-rows // unit) * unit


def tail_kernel(
    dilated_low,
    first_act,
    dilated_weight,
    reduced,
    one,
    features,
    reduce_weight,
    pre_grad,
    expand_part,
    features_grad,
    expand_out,
    dilated_out,
    reduce_out,
    sums_one,
    near,
    shifted,
    moved,
    act_turned,
    features_turned,
    first_grad,
    reduced_low,
    dilated_data,
    reduce_data,
    slots,
    direct,
    relay,
    edge,
    sems_one,
    *sum_refs,
):
    rows, cols, row, col, me = place()
    low, wide = jnp.bfloat16, jnp.float32
    height = near.shape[1]
    pixels, middle = dilated_low.shape
    channels = features.shape[1]
    width = pixels // height
    count = float(pixels * rows * cols)
    expand_sum = Sums(expand_part, True, expand_out, sum_refs)
    dilated_sum = Sums(dilated_data, None, dilated_out, expand_sum.rest)
    reduce_sum = Sums(reduce_data, None, reduce_out, dilated_sum.rest)
    sums = (expand_sum, dilated_sum, reduce_sum)
    halo = Halo(near, direct, relay, edge)
    greet_all()
    expand_sum.fetch()
    halo.clear()
    for line in range(height):
        near[1, line, EDGE : EDGE + width, :] = dilated_low[line * width : (line + 1) * width, :]
    for data, used in ((dilated_data, 9 * middle), (reduce_data, channels)):
        if data.shape[0] > used:
            data[used:, :] = jnp.zeros((data.shape[0] - used, data.shape[1]), low)
    expand_sum.fetched()
    await_all()
    halo.start()
    expand_sum.start_half()

    def turn_features(block, carry):
        span = pl.ds(pl.multiple_of(block * width, width), width)
        for line in range(height):
            features_turned[span, line * width : (line + 1) * width] = features[
                line * width : (line + 1) * width, span
            ].T
        return carry

    def turn_act(block, carry):
        span = pl.ds(pl.multiple_of(block * width, width), width)
        for line in range(height):
            act_turned[span, line * width : (line + 1) * width] = first_act[
                line * width : (line + 1) * width, span
            ].T
        return carry

    lax.fori_loop(0, middle // width, turn_act, 0)

    def one_way(way):
        shifted[...] = near[way].astype(wide)
        for side in range(3):
            tap = 3 * (2 - way) + side
            at = EDGE - (side - 1) * MID_RATE
            for line in range(height):
                moved[line * width : (line + 1) * width, :] = shifted[line, at : at + width, :].astype(
                    low
                )
            made = across(moved[...], dilated_weight[tap])
            if way == 1 and side == 0:
                first_grad[...] = made
            else:
                first_grad[...] += made
            dilated_data[tap * middle : (tap + 1) * middle, :] = jnp.dot(
                act_turned[...], moved[...], preferred_element_type=wide
            ).astype(low)

    halo.wait_own()
    one_way(1)
    halo.pass_on()
    expand_sum.start_level(0)
    lax.fori_loop(0, channels // width, turn_features, 0)
    halo.wait_rest()
    one_way(0)
    one_way(2)
    dilated_sum.start_half()
    expand_sum.start_level(1)
    shift_sum, gain_sum = jnp.zeros((1, middle), wide), jnp.zeros((1, middle), wide)
    for line in range(height):
        span = slice(line * width, (line + 1) * width)
        normed = (reduced[span, :] - one[0:1, :]) * one[1:2, :]
        gated = normed * one[2:3, :] + one[3:4, :]
        sigma = sigmoid(gated)
        up = first_grad[span, :] * (sigma * (1.0 + gated * (1.0 - sigma)))
        first_grad[span, :] = up
        shift_sum = shift_sum + jnp.sum(up, axis=0, keepdims=True)
        gain_sum = gain_sum + jnp.sum(up * normed, axis=0, keepdims=True)
    per = middle // LANES
    put_row(slots, me, 0, shift_sum)
    put_row(slots, me, per, gain_sum)
    share(slots, sems_one)
    dilated_sum.start_level(0)
    shared(slots, sems_one)
    total = jnp.sum(slots[...], axis=0)
    sums_one[...] = total
    shift_mean = take_row(total, 0, middle) / count
    gain_mean = take_row(total, per, middle) / count
    factor = one[2:3, :] * one[1:2, :]
    for line in range(height):
        span = slice(line * width, (line + 1) * width)
        normed = (reduced[span, :] - one[0:1, :]) * one[1:2, :]
        inner = first_grad[span, :] - shift_mean - normed * gain_mean
        reduced_low[span, :] = (inner * factor).astype(low)
    reduce_data[:channels, :] = jnp.dot(
        features_turned[...], reduced_low[...], preferred_element_type=wide
    ).astype(low)
    reduce_sum.start_half()
    expand_sum.start_back(1)
    chunk = 2 * LANES

    def last(block, carry):
        span = pl.ds(pl.multiple_of(block * chunk, chunk), chunk)
        made = across(reduced_low[...], reduce_weight[span, :])
        features_grad[:, span] = (made + pre_grad[:, span].astype(wide)).astype(low)
        return carry

    lax.fori_loop(0, channels // chunk, last, 0)
    reduce_sum.start_level(0)
    expand_sum.start_back(0)
    dilated_sum.start_level(1)
    reduce_sum.start_level(1)
    expand_sum.start_back_half()
    dilated_sum.start_back(1)
    reduce_sum.start_back(1)
    dilated_sum.start_back(0)
    reduce_sum.start_back(0)
    dilated_sum.start_back_half()
    reduce_sum.start_back_half()
    for each in sums:
        each.finish()
    halo.drain()


def tail(height, dilated_low, first_act, dilated_weight, reduced, one, features, reduce_weight, pre_grad,
         expand_part):
    devices = lax.axis_size("rows") * lax.axis_size("cols")
    pixels, middle = dilated_low.shape
    channels = features.shape[1]
    width = pixels // height
    low, wide = jnp.bfloat16, jnp.float32
    shape = jax.ShapeDtypeStruct
    whole = pl.BlockSpec(memory_space=pltpu.VMEM)
    away = pl.BlockSpec(memory_space=pl.ANY)
    sems = pltpu.SemaphoreType.DMA
    per = middle // LANES
    expand_part = jnp.pad(
        expand_part, ((0, sum_rows(expand_part.shape[0]) - expand_part.shape[0]), (0, 0))
    )
    sizes = [sum_rows(expand_part.shape[0]), sum_rows(9 * middle), sum_rows(channels)]
    outs = (
        shape((pixels, channels), low),
        *[shape((size, middle), low) for size in sizes],
        shape((2 * per, LANES), wide),
    )
    scratch = [
        pltpu.VMEM((3, height, width + 2 * EDGE, middle), low),
        pltpu.VMEM((height, width + 2 * EDGE, middle), wide),
        pltpu.VMEM((pixels, middle), low),
        pltpu.VMEM((middle, pixels), low),
        pltpu.VMEM((channels, pixels), low),
        pltpu.VMEM((pixels, middle), wide),
        pltpu.VMEM((pixels, middle), low),
        *[pltpu.VMEM((size, middle), low) for size in sizes[1:]],
        pltpu.VMEM((devices, 2 * per, LANES), wide),
        sems((2, height)),
        sems((2, height)),
        sems((2, 3)),
        sems((2,)),
    ]
    for size, apart in zip(sizes, (True, False, False)):
        scratch += sums_scratch(size, middle, apart)
    return pl.pallas_call(
        functools.partial(tail_kernel),
        out_shape=outs,
        in_specs=[whole] * 8 + [away],
        out_specs=(whole, away, away, away, whole),
        scratch_shapes=scratch,
        compiler_params=pltpu.CompilerParams(
            collective_id=13, has_side_effects=True, vmem_limit_bytes=VMEM_BYTES + (3 << 20)
        ),
        cost_estimate=pl.CostEstimate(
            flops=400 * pixels * middle * middle, bytes_accessed=256 * pixels * channels, transcendentals=0
        ),
        name="tail",
    )(dilated_low, first_act, dilated_weight, reduced, one, features, reduce_weight, pre_grad, expand_part)


def on_device(
    features,
    reduce_weight,
    dilated_weight,
    expand_weight,
    mid_gain,
    mid_shift,
    out_gain,
    out_shift,
    aspp_point,
    sep_depth,
    sep_point,
    pool_weight,
    proj_weight,
    aspp_gain,
    aspp_shift,
    head_weight,
    head_bias,
    task_scales,
    crop_ids,
    labels,
    boundary_mask,
    valid_mask,
    geometry_target,
):
    height, width, channels = features.shape
    pixels = height * width
    low = jnp.bfloat16
    aspp_width = proj_weight.shape[1]
    crop_flat = crop_ids.reshape(pixels)
    members = (crop_flat[:, None] == jnp.arange(LANES)[None, :]).astype(low)
    members_wide = members[:, :CROPS].astype(jnp.float32)
    keep = (1 - boundary_mask.reshape(pixels)).astype(jnp.float32)
    valid = valid_mask.reshape(pixels).astype(jnp.float32)
    flat = features.reshape(pixels, channels)
    middle = reduce_weight.shape[1]

    def pair_of(gain, shift):
        return jnp.pad(jnp.stack([gain, shift]), ((0, 6), (0, 0)))

    lanes = jnp.arange(LANES)
    count_row = jnp.zeros((LANES,), jnp.float32)
    count_row = count_row.at[:CROPS].set(jnp.sum(members_wide, axis=0))
    count_row = count_row.at[CROPS].set(jnp.sum(keep)).at[CROPS + 1].set(jnp.sum(valid))
    (
        reduced, first_act, dilated, second_act, expanded, trunk, one, two, three, count_sums,
        local_sums, crop_part,
    ) = front(
        height,
        flat,
        reduce_weight,
        dilated_weight.reshape(3, 3 * middle, middle),
        expand_weight,
        pool_weight,
        pair_of(mid_gain[0], mid_shift[0]),
        pair_of(mid_gain[1], mid_shift[1]),
        pair_of(out_gain, out_shift),
        jnp.broadcast_to(count_row, (8, LANES)),
        (lanes[:, None] == crop_flat[None, :]).astype(low),
    )
    crop_count = count_sums[0, :CROPS]
    keep_count, valid_count = count_sums[0, CROPS], count_sums[0, CROPS + 1]
    scale_exp = jnp.exp(task_scales)
    counts = jnp.stack([keep_count, valid_count, valid_count])
    factor = scale_exp / counts
    lane = jnp.arange(LANES)
    factors = jnp.where(
        lane < CLASSES, factor[0], jnp.where(lane == CLASSES, factor[1], 2.0 * factor[2])
    )
    outs = head_weight.shape[1]
    wide_row = ((0, 0), (0, LANES - outs))
    info = jnp.stack(
        [labels.reshape(pixels).astype(jnp.float32), keep, valid, *geometry_target.reshape(4, pixels)],
        axis=1,
    )
    devices = lax.axis_size("rows") * lax.axis_size("cols")
    crop_rows = CROPS * channels // LANES
    piece = -(-crop_rows // devices)
    crop_sums = jnp.pad(local_sums.reshape(crop_rows, LANES), ((0, piece * devices - crop_rows), (0, 0)))
    crop_sums = jnp.pad(
        crop_sums.reshape(devices, piece, LANES), ((0, 0), (0, -piece % 8), (0, 0))
    )
    branch_low, proj_part, head_part, crop_local, crop_pre, sums_five, sums_four, crop_table = pyramid(
        height,
        trunk,
        jnp.pad(sep_depth.reshape(27, channels).astype(jnp.float32), ((0, 5), (0, 0))),
        sep_point,
        aspp_point,
        crop_part,
        jnp.broadcast_to(crop_count[:, None], (CROPS, aspp_width)),
        members,
        proj_weight,
        jnp.pad(aspp_gain, ((0, 3), (0, 0))),
        jnp.pad(aspp_shift, ((0, 3), (0, 0))),
        jnp.pad(head_weight, wide_row),
        jnp.pad(jnp.broadcast_to(head_bias, (8, outs)), wide_row),
        jnp.broadcast_to(factors, (8, LANES)),
        jnp.pad(info, ((0, 0), (0, 1))),
        crop_sums,
    )
    crop_table = crop_table[:, :piece].reshape(-1, LANES)[:crop_rows].reshape(CROPS, channels)
    per = aspp_width // LANES
    proj_shift_grad = sums_five[:per].reshape(1, aspp_width)
    proj_gain_grad = sums_five[per : 2 * per].reshape(1, aspp_width)
    loss_row = sums_five[2 * per]
    grad_head_bias = sums_five[2 * per + 1, :outs]
    branch_shift_grad = sums_four[: 4 * per].reshape(4, aspp_width)
    branch_gain_grad = sums_four[4 * per :].reshape(4, aspp_width)
    loss_sums = jnp.stack(
        [loss_row[0], loss_row[CLASSES], jnp.sum(loss_row[CLASSES + 1 : CLASSES + 4])]
    )
    losses = loss_sums / counts
    objective = jnp.sum(scale_exp * losses - task_scales)
    grad_scales = scale_exp * losses - 1.0
    near, early, crop_total = pyramid_weights(
        branch_low.reshape(4, height, width, aspp_width),
        trunk,
        jnp.pad(sep_depth.reshape(27, channels).astype(jnp.float32).T, ((0, 0), (0, LANES - 27))),
        sep_point,
        crop_local,
        proj_part,
        head_part,
    )
    crop_low = (crop_total * gate_slope(crop_pre)).astype(low)
    pooled = (crop_table / crop_count[:, None]).astype(low)
    grad_pool_weight = jnp.einsum("kc,kd->cd", pooled, crop_low, preferred_element_type=jnp.float32)
    pooled_grad = (
        jnp.einsum("kd,cd->kc", crop_low, pool_weight, preferred_element_type=jnp.float32)
        / crop_count[:, None]
    )
    pooled_grad = jnp.pad(pooled_grad, ((0, LANES - CROPS), (0, 0)))
    crop_high = pooled_grad.astype(low)
    crop_rest = (pooled_grad - crop_high.astype(jnp.float32)).astype(low)
    pre_low, expand_part, dilated_low, sums_three, sums_two, early_sum = trunk_back(
        near,
        branch_low[0],
        jnp.pad(sep_depth.reshape(27, channels).astype(jnp.float32).T, ((0, 0), (0, LANES - 27))),
        sep_point,
        aspp_point,
        members,
        crop_high,
        crop_rest,
        expanded,
        flat,
        three,
        dilated,
        two,
        second_act,
        expand_weight,
        early,
    )
    folded = sums_three.reshape(-1, 2 * per, LANES)
    out_shift_grad = folded[:, :per].reshape(1, channels)
    out_gain_grad = folded[:, per:].reshape(1, channels)
    two_shift_grad, two_gain_grad = sums_two.reshape(2, 1, middle)
    grad_features, expand_sum, dilated_sum, reduce_sum, sums_one = tail(
        height,
        dilated_low,
        first_act,
        dilated_weight,
        reduced,
        one,
        flat,
        reduce_weight,
        pre_low,
        expand_part,
    )
    one_shift_grad, one_gain_grad = sums_one.reshape(2, 1, middle)
    grad_features = grad_features.reshape(height, width, channels)
    expand_sum = expand_sum[:channels].reshape(-1, middle, middle)
    grad_expand_weight = jnp.transpose(expand_sum, (1, 0, 2)).reshape(middle, channels)
    first, second = early_sum[:channels], early_sum[channels : 2 * channels]
    sep_sum = jnp.stack([first[:, :aspp_width], first[:, aspp_width:], second[:, :aspp_width]])
    at = 2 * channels
    tables = []
    for size, extent in ((proj_weight.shape[0], aspp_width), (channels, LANES), (aspp_width, LANES)):
        blocks = 2 * aspp_width // extent
        table = early_sum[at : at + size // blocks].reshape(size // blocks, blocks, extent)
        tables.append(jnp.transpose(table, (1, 0, 2)).reshape(size, extent))
        at += size // blocks
    summed = [
        value.astype(jnp.float32)
        for value in (
            reduce_sum[:channels],
            dilated_sum[: 9 * middle].reshape(9, middle, middle),
            grad_expand_weight,
            second[:, aspp_width:],
            tables[1][:, :27].T.reshape(3, 9, channels),
            sep_sum,
            tables[0],
            tables[2],
        )
    ]
    grad_mid_gain = jnp.concatenate([one_gain_grad, two_gain_grad], axis=0)
    grad_mid_shift = jnp.concatenate([one_shift_grad, two_shift_grad], axis=0)
    grad_aspp_gain = jnp.concatenate([branch_gain_grad, proj_gain_grad], axis=0)
    grad_aspp_shift = jnp.concatenate([branch_shift_grad, proj_shift_grad], axis=0)
    return (
        objective,
        grad_features,
        summed[0],
        summed[1],
        summed[2],
        grad_mid_gain,
        grad_mid_shift,
        out_gain_grad[0],
        out_shift_grad[0],
        summed[3],
        summed[4],
        summed[5],
        grad_pool_weight,
        summed[6],
        grad_aspp_gain,
        grad_aspp_shift,
        summed[7][:, : head_weight.shape[1]],
        grad_head_bias,
        grad_scales,
    )


def solution(mesh):
    in_specs = (
        P("rows", "cols", None),
        P(),
        P(),
        P(),
        P(),
        P(),
        P(),
        P(),
        P(),
        P(),
        P(),
        P(),
        P(),
        P(),
        P(),
        P(),
        P(),
        P(),
        P("rows", "cols"),
        P("rows", "cols"),
        P("rows", "cols"),
        P("rows", "cols"),
        P(None, "rows", "cols"),
    )
    out_specs = (
        P(),
        P("rows", "cols", None),
        P(),
        P(),
        P(),
        P(),
        P(),
        P(),
        P(),
        P(),
        P(),
        P(),
        P(),
        P(),
        P(),
        P(),
        P(),
        P(),
        P(),
    )
    return jax.shard_map(
        on_device, mesh=mesh, in_specs=in_specs, out_specs=out_specs, check_vma=False
    )
```

```python
import functools

import jax
import jax.numpy as jnp
from jax import lax
from jax.experimental import pallas as pl
from jax.experimental.pallas import tpu as pltpu
from jax.sharding import PartitionSpec as P

CLASSES = 13
CROPS = 16
MID_RATE = 4
BASE_RATE = 12
LANES = 128

EPS = 1e-05
MESH = pl.DeviceIdType.MESH


def gate_slope(value):
    sigma = jax.nn.sigmoid(value)
    return sigma * (1.0 + value * (1.0 - sigma))


PAD = 48
VMEM_BYTES = 60 * 1024 * 1024


def place():
    rows, cols = lax.axis_size("rows"), lax.axis_size("cols")
    row, col = lax.axis_index("rows"), lax.axis_index("cols")
    return rows, cols, row, col, row * cols + col


def greet_all():
    rows, cols, row, col, me = place()
    barrier = pltpu.get_barrier_semaphore()

    def greet(step, carry):
        other = lax.rem(me + step, rows * cols)
        pl.semaphore_signal(
            barrier, inc=1, device_id=(other // cols, lax.rem(other, cols)), device_id_type=MESH
        )
        return carry

    lax.fori_loop(1, rows * cols, greet, 0)


def await_all():
    rows, cols = lax.axis_size("rows"), lax.axis_size("cols")
    pl.semaphore_wait(pltpu.get_barrier_semaphore(), rows * cols - 1)


def share(slots, sems):
    rows, cols, row, col, me = place()

    def go(step, carry):
        other = lax.rem(me + step, rows * cols)
        pltpu.make_async_remote_copy(
            slots.at[me],
            slots.at[me],
            sems.at[0],
            sems.at[1],
            device_id=(other // cols, lax.rem(other, cols)),
            device_id_type=MESH,
        ).start()
        return carry

    lax.fori_loop(1, rows * cols, go, 0)


def shared(slots, sems):
    rows, cols, row, col, me = place()
    others = slots.at[pl.ds(0, rows * cols - 1)]
    pltpu.make_async_remote_copy(
        others,
        others,
        sems.at[0],
        sems.at[1],
        device_id=(row, lax.rem(col + 1, cols)),
        device_id_type=MESH,
    ).wait()


def share_column(slots, sems):
    rows, cols, row, col, me = place()

    def go(step, carry):
        other = lax.rem(row + step, rows)
        pltpu.make_async_remote_copy(
            slots.at[row],
            slots.at[row],
            sems.at[0],
            sems.at[1],
            device_id=(other, col),
            device_id_type=MESH,
        ).start()
        return carry

    lax.fori_loop(1, rows, go, 0)


def shared_column(slots, sems):
    rows, cols, row, col, me = place()
    others = slots.at[pl.ds(0, rows - 1)]
    pltpu.make_async_remote_copy(
        others,
        others,
        sems.at[0],
        sems.at[1],
        device_id=(lax.rem(row + 1, rows), col),
        device_id_type=MESH,
    ).wait()


class PairSum:
    def __init__(self, own, pair, slots, all_, sems):
        self.own, self.pair, self.slots, self.all_, self.sems = own, pair, slots, all_, sems
        self.rows, self.cols, self.row, self.col, _ = place()

    def to_pair(self, src, dst, at):
        return pltpu.make_async_remote_copy(
            src,
            dst,
            self.sems.at[at, 0],
            self.sems.at[at, 1],
            device_id=(self.row, 1 - self.col),
            device_id_type=MESH,
        )

    def out_copy(self):
        return self.to_pair(self.own.at[1 - self.col], self.pair, 0)

    def back_copy(self):
        return self.to_pair(self.all_.at[self.col], self.all_.at[self.col], 2)

    def put(self, value):
        self.own[0] = value[:, :LANES]
        self.own[1] = value[:, LANES:]

    def start(self):
        self.out_copy().start()

    def start_column(self):
        self.out_copy().wait()
        self.slots[self.row] = self.own[self.col] + self.pair[...]
        share_column(self.slots, self.sems.at[1])

    def start_back(self):
        shared_column(self.slots, self.sems.at[1])
        self.all_[self.col] = jnp.sum(self.slots[...], axis=0)
        self.back_copy().start()

    def finish(self):
        self.back_copy().wait()
        return jnp.concatenate([self.all_[0], self.all_[1]], axis=1)


def pair_sum_scratch(count):
    wide = jnp.float32
    return [
        pltpu.VMEM((2, count, LANES), wide),
        pltpu.VMEM((count, LANES), wide),
        pltpu.VMEM((lax.axis_size("rows"), count, LANES), wide),
        pltpu.VMEM((2, count, LANES), wide),
        pltpu.SemaphoreType.DMA((3, 2)),
    ]


def put_row(slots, me, at, vector):
    for part in range(vector.shape[1] // LANES):
        slots[me, at + part : at + part + 1, :] = vector[:, part * LANES : (part + 1) * LANES]


def take_row(table, at, width):
    parts = [table[at + part : at + part + 1, :] for part in range(width // LANES)]
    return parts[0] if len(parts) == 1 else jnp.concatenate(parts, axis=1)


def merged(slots, half, share_size, count):
    center = jnp.mean(slots[:, :half, :], axis=0)
    apart = slots[:, :half, :] - center[None]
    spread = jnp.sum(slots[:, half : 2 * half, :], axis=0) + share_size * jnp.sum(apart * apart, axis=0)
    return center, lax.rsqrt(spread / count + EPS)


def sigmoid(value):
    return 1.0 / (1.0 + jnp.exp(-value))


def across(left, right):
    return lax.dot_general(left, right, (((1,), (1,)), ((), ())), preferred_element_type=jnp.float32)


def down(left, right):
    return lax.dot_general(left, right, (((0,), (0,)), ((), ())), preferred_element_type=jnp.float32)


def pyramid_kernel(
    height,
    trunk,
    depth,
    sep_point,
    aspp_point,
    crop_part,
    count_sums,
    members,
    proj_weight,
    gains,
    shifts,
    head_raw,
    bias_raw,
    weights,
    labels,
    boundary,
    valid_mask,
    geometry,
    crop_sums,
    branch_low,
    proj_part,
    head_part,
    crop_local,
    crop_pre,
    sums_five,
    sums_four,
    crop_table,
    own_low,
    closing,
    head_weight,
    head_bias,
    field,
    send_main,
    recv_main,
    send_side,
    recv_side,
    pre,
    joined,
    crop_act,
    projected,
    united,
    head_low,
    upstream,
    proj_low,
    branch_up,
    four_slots,
    five_slots,
    back_five,
    back_four,
    crop_pieces,
    main_sems,
    side_sems,
    four_sems,
    five_sems,
    back_five_sems,
    back_four_sems,
    piece_sems,
    table_sems,
    *crop_refs,
):
    rows, cols, row, col, me = place()
    low, wide = jnp.bfloat16, jnp.float32
    pixels = trunk.shape[0]
    width = pixels // height
    share_size = float(pixels)
    count = float(pixels * rows * cols)
    aspp = sep_point.shape[2]
    greet_all()

    def exists(target):
        return jnp.logical_and(target >= 0, target < rows)

    def step_of(index):
        return (BASE_RATE // height) * (index + 1)

    for index in range(3):
        step = BASE_RATE * (index + 1) // height
        for way in (0, 2):

            @pl.when(jnp.logical_not(exists(row - (1 - way) * step)))
            def _():
                recv_main[index, way] = jnp.zeros(recv_main.shape[2:], low)

    half = crop_part.shape[0]
    crop_total = PairSum(*crop_refs)
    crop_total.put(crop_part[...])
    pre[0] = jnp.dot(trunk[...], aspp_point[...], preferred_element_type=wide)
    await_all()
    crop_total.start()
    crop_pieces[me] = crop_sums[me]

    def scatter(step, carry):
        other = lax.rem(me + step, rows * cols)
        pltpu.make_async_remote_copy(
            crop_sums.at[other],
            crop_pieces.at[me],
            piece_sems.at[0],
            piece_sems.at[1],
            device_id=(other // cols, lax.rem(other, cols)),
            device_id_type=MESH,
        ).start()
        return carry

    lax.fori_loop(1, rows * cols, scatter, 0)
    side_from = pl.multiple_of((1 - col) * (PAD + width), 16)
    side_to = pl.multiple_of((1 - col) * (width - PAD), 16)

    def main_copy(index, way):
        return pltpu.make_async_remote_copy(
            send_main.at[index, way],
            recv_main.at[index, way],
            main_sems.at[0, index, way],
            main_sems.at[1, index, way],
            device_id=(row + (1 - way) * step_of(index), col),
            device_id_type=MESH,
        )

    def side_copy(index, way):
        return pltpu.make_async_remote_copy(
            send_side.at[index, way],
            recv_side.at[index, way],
            side_sems.at[0, index, way],
            side_sems.at[1, index, way],
            device_id=(row, 1 - col),
            device_id_type=MESH,
        )

    def flush(number):
        index, way = 2 - number // 3, lax.rem(2 * lax.rem(number, 3), 3)
        side_copy(index, way).wait_recv()

        @pl.when(way == 1)
        def _():
            for line in range(height):
                edge = pl.ds(pl.multiple_of(line * width + side_to, 16), PAD)
                pre[index + 1, edge, :] += recv_side[index, way, line].astype(wide)

        @pl.when(way != 1)
        def _():
            edge = pl.ds(side_to, PAD)
            send_main[index, way, :, edge, :] = (
                send_main[index, way, :, edge, :].astype(wide) + recv_side[index, way].astype(wide)
            ).astype(low)

            @pl.when(exists(row + (1 - way) * step_of(index)))
            def _():
                main_copy(index, way).start()

    for index in (2, 1, 0):
        rate = BASE_RATE * (index + 1)

        def one_way(turn, carry):
            way = lax.rem(2 * turn, 3)
            for sign in (0, 1, -1):
                tap = depth[pl.ds(index * 9 + 3 * way + 1 - sign, 1), :].astype(low)
                made = jnp.dot(trunk[...] * tap, sep_point[index], preferred_element_type=wide)
                for line in range(height):
                    part = made[line * width : (line + 1) * width, :]
                    if sign == 0:
                        field[line, PAD : PAD + width, :] = part
                        field[line, :PAD, :] = jnp.zeros((PAD, aspp), wide)
                        field[line, PAD + width :, :] = jnp.zeros((PAD, aspp), wide)
                    else:
                        at = PAD + sign * rate
                        field[line, at : at + width, :] += part
            send_side[index, way] = field[:, pl.ds(side_from, PAD), :].astype(low)

            @pl.when(way == 1)
            def _():
                for line in range(height):
                    pre[index + 1, line * width : (line + 1) * width, :] = field[
                        line, PAD : PAD + width, :
                    ]

            @pl.when(way != 1)
            def _():
                send_main[index, way] = field[:, PAD : PAD + width, :].astype(low)

            side_copy(index, way).start()
            number = 3 * (2 - index) + turn

            @pl.when(number > 0)
            def _():
                flush(number - 1)

            return carry

        lax.fori_loop(0, 3, one_way, 0)
    flush(8)
    crop_total.start_column()

    def lines(body, carry=0):
        def run(line, carry):
            return body(line, pl.ds(pl.multiple_of(line * width, width), width), carry)

        return lax.fori_loop(0, height, run, carry)

    zero_row = jnp.zeros((1, aspp), wide)

    def statistics(value_of, slots, at, half_rows):
        total = lines(
            lambda line, span, acc: acc + jnp.sum(value_of(span), axis=0, keepdims=True), zero_row
        )
        mean = total / share_size

        def squares(line, span, acc):
            apart = value_of(span) - mean
            return acc + jnp.sum(apart * apart, axis=0, keepdims=True)

        put_row(slots, me, at, mean)
        put_row(slots, me, half_rows + at, lines(squares, zero_row))

    per = aspp // LANES
    statistics(lambda span: pre[0, span, :], four_slots, 0, 4 * per)
    for index in (2, 1, 0):
        for way in (0, 2):

            @pl.when(exists(row - (1 - way) * step_of(index)))
            def _():
                main_copy(index, way).wait_recv()

        def assemble(line, span, carry):
            pre[index + 1, span, :] += recv_main[index, 0, line].astype(wide) + recv_main[
                index, 2, line
            ].astype(wide)
            return carry

        lines(assemble)
        statistics(lambda span: pre[index + 1, span, :], four_slots, per * (index + 1), 4 * per)
    share(four_slots, four_sems)
    crop_total.start_back()
    shared(crop_pieces, piece_sems)
    crop_table[me] = jnp.sum(crop_pieces[...], axis=0)
    share(crop_table, table_sems)
    crop_row = lax.broadcasted_iota(jnp.int32, (half, LANES), 0)
    crop_lane = lax.broadcasted_iota(jnp.int32, (half, LANES), 1)
    crop_count = jnp.sum(
        jnp.where(crop_row == crop_lane, count_sums[0:1, :], 0.0), axis=1, keepdims=True
    )
    crop_value = crop_total.finish() / crop_count
    crop_pre[...] = crop_value
    crop_act[...] = jnp.zeros(crop_act.shape, low)
    crop_act[:half, :] = (crop_value * sigmoid(crop_value)).astype(low)

    def spread(line, span, carry):
        joined[span, 4 * aspp :] = jnp.dot(
            members[span, :], crop_act[...], preferred_element_type=wide
        ).astype(low)
        return carry

    lines(spread)
    shared(four_slots, four_sems)
    center_four, scale_four = merged(four_slots, 4 * per, share_size, count)
    centers = [take_row(center_four, per * part, aspp) for part in range(4)]
    scales = [take_row(scale_four, per * part, aspp) for part in range(4)]

    def activate(line, span, carry):
        for part in range(4):
            normed = (pre[part, span, :] - centers[part]) * scales[part]
            gated = normed * gains[part : part + 1, :] + shifts[part : part + 1, :]
            joined[span, part * aspp : (part + 1) * aspp] = (gated * sigmoid(gated)).astype(low)
        return carry

    lines(activate)
    projected[...] = jnp.dot(joined[...], proj_weight[...], preferred_element_type=wide)
    five_slots[me] = jnp.zeros(five_slots.shape[1:], wide)
    statistics(lambda span: projected[span, :], five_slots, 0, per)
    share(five_slots, five_sems)
    shared(five_slots, five_sems)
    center_five, scale_five = merged(five_slots, per, share_size, count)
    center_five, scale_five = take_row(center_five, 0, aspp), take_row(scale_five, 0, aspp)
    gain_five, shift_five = gains[4:5, :], shifts[4:5, :]
    lane = lax.broadcasted_iota(jnp.int32, (width, LANES), 1)
    outs = head_raw.shape[1]
    head_weight[...] = jnp.zeros(head_weight.shape, low)
    head_weight[:, :outs] = head_raw[...]
    head_bias[...] = jnp.zeros(head_bias.shape, wide)
    head_bias[0:1, :outs] = bias_raw[...]
    one_lane = lax.broadcasted_iota(jnp.int32, (1, LANES), 1)
    pixel_count = jnp.where(
        one_lane < CLASSES, count_sums[0:1, CROPS : CROPS + 1], count_sums[0:1, CROPS + 1 : CROPS + 2]
    )
    factors = weights[0:1, :] / pixel_count

    def heads_of(line, span, carry):
        losses, bias_sum, shift_sum, gain_sum = carry
        normed = (projected[span, :] - center_five) * scale_five
        gated = normed * gain_five + shift_five
        sigma = sigmoid(gated)
        act = (gated * sigma).astype(low)
        united[span, :] = act
        heads = jnp.dot(act, head_weight[...], preferred_element_type=wide) + head_bias[0:1, :]
        row_of = pl.ds(line, 1)
        facts = jnp.concatenate(
            [
                labels[row_of, :].astype(wide),
                1.0 - boundary[row_of, :].astype(wide),
                valid_mask[row_of, :].astype(wide),
                *[geometry[part, row_of, :] for part in range(4)],
                jnp.zeros((1, width), wide),
            ],
            axis=0,
        ).T
        label, keep, valid = facts[:, 0:1], facts[:, 1:2], facts[:, 2:3]
        is_class = lane < CLASSES
        hot = jnp.where(lane.astype(wide) == label, 1.0, 0.0)
        target = jnp.zeros((width, LANES), wide)
        for part in range(4):
            target = jnp.where(lane == CLASSES + part, facts[:, 3 + part : 4 + part], target)
        top = jnp.max(jnp.where(is_class, heads, -jnp.inf), axis=1, keepdims=True)
        exps = jnp.where(is_class, jnp.exp(heads - top), 0.0)
        totals = jnp.sum(exps, axis=1, keepdims=True)
        picked = jnp.sum(jnp.where(is_class, heads, 0.0) * hot, axis=1, keepdims=True)
        error = jnp.where(is_class, 0.0, heads - target)
        root = jnp.sqrt(error * error + 1.0)
        is_depth, is_normal = lane == CLASSES, jnp.logical_and(lane > CLASSES, lane < CLASSES + 4)
        semantic = keep * (top + jnp.log(totals) - picked)
        terms = jnp.where(lane == 0, semantic, 0.0)
        terms = jnp.where(is_depth, valid * (root - 1.0), terms)
        terms = jnp.where(is_normal, valid * error * error, terms)
        grad = jnp.where(is_class, keep * (exps / totals - hot), 0.0)
        grad = jnp.where(is_depth, valid * error / root, grad)
        grad = jnp.where(is_normal, valid * error, grad)
        grad = grad * factors
        grad_low = grad.astype(low)
        head_low[span, :] = grad_low
        up = across(grad_low, head_weight[...]) * (sigma * (1.0 + gated * (1.0 - sigma)))
        upstream[span, :] = up
        return (
            losses + jnp.sum(terms, axis=0, keepdims=True),
            bias_sum + jnp.sum(grad, axis=0, keepdims=True),
            shift_sum + jnp.sum(up, axis=0, keepdims=True),
            gain_sum + jnp.sum(up * normed, axis=0, keepdims=True),
        )

    zero_lane = jnp.zeros((1, LANES), wide)
    losses, bias_sum, shift_sum, gain_sum = lines(
        heads_of, (zero_lane, zero_lane, zero_row, zero_row)
    )
    back_five[me] = jnp.zeros(back_five.shape[1:], wide)
    put_row(back_five, me, 0, shift_sum)
    put_row(back_five, me, per, gain_sum)
    put_row(back_five, me, 2 * per, losses)
    put_row(back_five, me, 2 * per + 1, bias_sum)
    share(back_five, back_five_sems)
    head_part[...] = down(united[...], head_low[...]).astype(low)
    shared(back_five, back_five_sems)
    total_five = jnp.sum(back_five[...], axis=0)
    sums_five[...] = total_five
    weighted = weights[1:2, :] * total_five[2 * per : 2 * per + 1, :] / pixel_count

    def lanes_sum(row_value, first, last):
        picked = jnp.where(jnp.logical_and(one_lane >= first, one_lane < last), row_value, 0.0)
        return jnp.sum(picked, axis=1, keepdims=True)

    tasks = (
        lanes_sum(weighted, 0, 1),
        lanes_sum(weighted, CLASSES, CLASSES + 1),
        lanes_sum(weighted, CLASSES + 1, CLASSES + 4),
    )
    closing[...] = jnp.zeros(closing.shape, wide)
    for part in range(3):
        closing[0:1, part : part + 1] = tasks[part] - 1.0
    closing[1:2, 0:1] = tasks[0] + tasks[1] + tasks[2] - lanes_sum(weights[2:3, :], 0, 3)
    shift_mean = take_row(total_five, 0, aspp) / count
    gain_mean = take_row(total_five, per, aspp) / count

    def project_back(line, span, carry):
        normed = (projected[span, :] - center_five) * scale_five
        inner = upstream[span, :] - shift_mean - normed * gain_mean
        proj_low[span, :] = (inner * (gain_five * scale_five)).astype(low)
        return carry

    lines(project_back)
    for part in range(4):
        branch_up[part] = across(
            proj_low[...], proj_weight[part * aspp : (part + 1) * aspp, :]
        )
    crop_up = across(proj_low[...], proj_weight[4 * aspp :, :])
    crop_high = crop_up.astype(low)
    crop_rest = (crop_up - crop_high.astype(wide)).astype(low)
    crop_sum = down(members[...], crop_high) + down(members[...], crop_rest)
    crop_local[...] = crop_sum[:half, :]

    for part in range(4):

        def branch_sums(line, span, carry):
            shift_sum, gain_sum = carry
            normed = (pre[part, span, :] - centers[part]) * scales[part]
            gated = normed * gains[part : part + 1, :] + shifts[part : part + 1, :]
            sigma = sigmoid(gated)
            up = branch_up[part, span, :] * (sigma * (1.0 + gated * (1.0 - sigma)))
            branch_up[part, span, :] = up
            return (
                shift_sum + jnp.sum(up, axis=0, keepdims=True),
                gain_sum + jnp.sum(up * normed, axis=0, keepdims=True),
            )

        shift_sum, gain_sum = lines(branch_sums, (zero_row, zero_row))
        put_row(back_four, me, per * part, shift_sum)
        put_row(back_four, me, per * (4 + part), gain_sum)
    share(back_four, back_four_sems)
    proj_part[...] = down(joined[...], proj_low[...]).astype(low)
    shared(back_four, back_four_sems)
    total_four = jnp.sum(back_four[...], axis=0)
    sums_four[...] = total_four
    for part in range(4):
        shift_mean = take_row(total_four, per * part, aspp) / count
        gain_mean = take_row(total_four, per * (4 + part), aspp) / count
        factor = gains[part : part + 1, :] * scales[part]

        def branch_back(line, span, carry):
            normed = (pre[part, span, :] - centers[part]) * scales[part]
            inner = branch_up[part, span, :] - shift_mean - normed * gain_mean
            value = (inner * factor).astype(low)
            branch_low[part, span, :] = value
            if part == 0:
                own_low[span, :] = value
            return carry

        lines(branch_back)
    shared(crop_table, table_sems)
    for index in range(3):
        for way in range(3):
            side_copy(index, way).wait_send()
        for way in (0, 2):

            @pl.when(exists(row + (1 - way) * step_of(index)))
            def _():
                main_copy(index, way).wait_send()


def pyramid(height, trunk, depth, sep_point, aspp_point, crop_part, count_sums, members, proj_weight,
            gains, shifts, head_weight, head_bias, weights, labels, boundary, valid, geometry, crop_sums):
    devices = lax.axis_size("rows") * lax.axis_size("cols")
    pixels = trunk.shape[0]
    width = pixels // height
    aspp = sep_point.shape[2]
    crops = crop_part.shape[0]
    low, wide = jnp.bfloat16, jnp.float32
    shape = jax.ShapeDtypeStruct
    whole = pl.BlockSpec(memory_space=pltpu.VMEM)
    joined = proj_weight.shape[0]
    per = aspp // LANES
    outs = (
        shape((4, pixels, aspp), low),
        shape((joined, aspp), low),
        shape((aspp, LANES), low),
        shape((crops, aspp), wide),
        shape((crops, aspp), wide),
        shape((8, LANES), wide),
        shape((8 * per, LANES), wide),
        shape(crop_sums.shape, wide),
        shape((pixels, aspp), low),
        shape((8, LANES), wide),
    )
    sems = pltpu.SemaphoreType.DMA
    return pl.pallas_call(
        functools.partial(pyramid_kernel, height),
        out_shape=outs,
        in_specs=[whole] * 18,
        out_specs=(whole,) * len(outs),
        scratch_shapes=[
            pltpu.VMEM((aspp, LANES), low),
            pltpu.VMEM((8, LANES), wide),
            pltpu.VMEM((height, width + 2 * PAD, aspp), wide),
            pltpu.VMEM((3, 3, height, width, aspp), low),
            pltpu.VMEM((3, 3, height, width, aspp), low),
            pltpu.VMEM((3, 3, height, PAD, aspp), low),
            pltpu.VMEM((3, 3, height, PAD, aspp), low),
            pltpu.VMEM((4, pixels, aspp), wide),
            pltpu.VMEM((pixels, joined), low),
            pltpu.VMEM((LANES, aspp), low),
            pltpu.VMEM((pixels, aspp), wide),
            pltpu.VMEM((pixels, aspp), low),
            pltpu.VMEM((pixels, LANES), low),
            pltpu.VMEM((pixels, aspp), wide),
            pltpu.VMEM((pixels, aspp), low),
            pltpu.VMEM((4, pixels, aspp), wide),
            pltpu.VMEM((devices, 8 * per, LANES), wide),
            pltpu.VMEM((devices, 8, LANES), wide),
            pltpu.VMEM((devices, 8, LANES), wide),
            pltpu.VMEM((devices, 8 * per, LANES), wide),
            pltpu.VMEM(crop_sums.shape, wide),
            sems((2, 3, 3)),
            sems((2, 3, 3)),
            sems((2,)),
            sems((2,)),
            sems((2,)),
            sems((2,)),
            sems((2,)),
            sems((2,)),
            *pair_sum_scratch(crops),
        ],
        compiler_params=pltpu.CompilerParams(
            collective_id=10, has_side_effects=True, vmem_limit_bytes=VMEM_BYTES
        ),
        cost_estimate=pl.CostEstimate(
            flops=100 * pixels * trunk.shape[1] * aspp, bytes_accessed=64 * pixels * trunk.shape[1], transcendentals=0
        ),
        name="pyramid",
    )(trunk, depth, sep_point, aspp_point, crop_part, count_sums, members, proj_weight, gains, shifts,
      head_weight, head_bias, weights, labels, boundary, valid, geometry, crop_sums)


def pyramid_weights_kernel(
    branch_low,
    trunk,
    depth,
    sep_point,
    crop_local,
    proj_part,
    head_part,
    near,
    early,
    crop_total,
    depth_part,
    turned,
    shifted,
    moved,
    gathered,
    main_sems,
    edge_sems,
    *crop_refs,
):
    rows, cols, row, col, me = place()
    low, wide = jnp.bfloat16, jnp.float32
    height, width, aspp = branch_low.shape[1:]
    pixels, channels = trunk.shape
    crop_sum = PairSum(*crop_refs)
    crop_sum.put(crop_local[...])
    greet_all()

    def exists(target):
        return jnp.logical_and(target >= 0, target < rows)

    def step_of(index):
        return BASE_RATE * (index + 1) // height

    edge_from = pl.multiple_of(PAD + (1 - col) * (width - PAD), 16)
    edge_to = pl.multiple_of(col * (width + PAD), 16)
    blank = pl.multiple_of(col * (width + PAD), 16)

    def main_copy(index, way):
        return pltpu.make_async_remote_copy(
            branch_low.at[index + 1],
            near.at[index, way, :, pl.ds(PAD, width), :],
            main_sems.at[0, index, way],
            main_sems.at[1, index, way],
            device_id=(row + (1 - way) * step_of(index), col),
            device_id_type=MESH,
        )

    def edge_copy(index, way):
        return pltpu.make_async_remote_copy(
            near.at[index, way, :, pl.ds(edge_from, PAD), :],
            near.at[index, way, :, pl.ds(edge_to, PAD), :],
            edge_sems.at[0, index, way],
            edge_sems.at[1, index, way],
            device_id=(row, 1 - col),
            device_id_type=MESH,
        )

    for index in range(3):
        for way in range(3):
            near[index, way, :, pl.ds(blank, PAD), :] = jnp.zeros((height, PAD, aspp), low)
            if way == 1:
                near[index, way, :, PAD : PAD + width, :] = branch_low[index + 1]
            else:

                @pl.when(jnp.logical_not(exists(row - (1 - way) * step_of(index))))
                def _():
                    near[index, way] = jnp.zeros(near.shape[2:], low)

    await_all()
    for index in range(3):
        edge_copy(index, 1).start()

    def send(index):
        for way in (0, 2):

            @pl.when(exists(row + (1 - way) * step_of(index)))
            def _():
                main_copy(index, way).start()

    send(0)
    crop_sum.start()

    def turn(block, carry):
        span = pl.ds(pl.multiple_of(block * width, width), width)
        for line in range(height):
            turned[span, line * width : (line + 1) * width] = trunk[
                line * width : (line + 1) * width, span
            ].T
        return carry

    lax.fori_loop(0, channels // width, turn, 0)
    part_rows = channels // 2

    def point(part, carry):
        span = pl.ds(pl.multiple_of(part * part_rows, part_rows), part_rows)
        own = branch_low[0].reshape(pixels, aspp)
        early[pl.ds(pl.multiple_of(channels + part * part_rows, part_rows), part_rows), aspp:] = jnp.dot(
            turned[span, :], own, preferred_element_type=wide
        ).astype(low)
        return carry

    lax.fori_loop(0, 2, point, 0)
    lane = lax.broadcasted_iota(jnp.int32, (part_rows, LANES), 1)
    depth_part[...] = jnp.zeros(depth_part.shape, wide)
    gathered[...] = jnp.zeros(gathered.shape, wide)
    for index, way in ((0, 1), (1, 1), (2, 1), (0, 0), (0, 2), (1, 0), (1, 2), (2, 0), (2, 2)):
        rate = BASE_RATE * (index + 1)

        if way != 1:

            @pl.when(exists(row - (1 - way) * step_of(index)))
            def _():
                main_copy(index, way).wait_recv()
                edge_copy(index, way).start()

        for side in (1, 0, 2):
            if side == 0:

                @pl.when(exists(row - (1 - way) * step_of(index)))
                def _():
                    edge_copy(index, way).wait_recv()

                shifted[...] = near[index, way].astype(wide)
            tap = 3 * (2 - way) + side
            at = PAD - (side - 1) * rate
            for line in range(height):
                if side == 1:
                    piece = near[index, way, line, PAD : PAD + width, :]
                else:
                    piece = shifted[line, at : at + width, :].astype(low)
                moved[line * width : (line + 1) * width, :] = piece
            order = 9 * index + tap

            def collect(part, carry):
                span = pl.ds(pl.multiple_of(part * part_rows, part_rows), part_rows)
                made = jnp.dot(turned[span, :], moved[...], preferred_element_type=wide)
                gathered[index, span, :] += made * depth[span, order : order + 1]
                total = jnp.sum(made * sep_point[index, span, :].astype(wide), axis=1, keepdims=True)
                depth_part[span, :] = jnp.where(lane == order, total, depth_part[span, :])
                return carry

            lax.fori_loop(0, 2, collect, 0)
        if way == 1 and index > 0:
            send(index)
        if way == 1 and index == 0:
            crop_sum.start_column()
        if way == 0 and index == 0:
            crop_sum.start_back()
    early[:channels, :aspp] = gathered[0].astype(low)
    early[:channels, aspp:] = gathered[1].astype(low)
    early[channels : 2 * channels, :aspp] = gathered[2].astype(low)
    at = 2 * channels
    for table in (proj_part, depth_part, head_part):
        extent = table.shape[1]
        blocks = 2 * aspp // extent
        size = table.shape[0] // blocks
        for block in range(blocks):
            early[at : at + size, block * extent : (block + 1) * extent] = table[
                block * size : (block + 1) * size, :
            ].astype(low)
        at += size
    if early.shape[0] > at:
        early[at:, :] = jnp.zeros((early.shape[0] - at, 2 * aspp), low)
    crop_total[...] = crop_sum.finish()
    for index in range(3):
        for way in range(3):

            @pl.when(exists(row - (1 - way) * step_of(index)))
            def _():
                edge_copy(index, way).wait_send()

            if way != 1:

                @pl.when(exists(row + (1 - way) * step_of(index)))
                def _():
                    main_copy(index, way).wait_send()


def early_rows(channels, proj_part, head_part):
    rows = 2 * channels
    for size, extent in ((proj_part.shape[0], proj_part.shape[1]), (channels, LANES), head_part.shape):
        rows += size * extent // (2 * proj_part.shape[1])
    return rows


def pyramid_weights(branch_low, trunk, depth, sep_point, crop_local, proj_part, head_part):
    height, width, aspp = branch_low.shape[1:]
    pixels, channels = trunk.shape
    crops = crop_local.shape[0]
    low, wide = jnp.bfloat16, jnp.float32
    shape = jax.ShapeDtypeStruct
    whole = pl.BlockSpec(memory_space=pltpu.VMEM)
    sems = pltpu.SemaphoreType.DMA
    outs = (
        shape((3, 3, height, width + 2 * PAD, aspp), low),
        shape((sum_rows(early_rows(channels, proj_part, head_part)), 2 * aspp), low),
        shape((crops, aspp), wide),
    )
    return pl.pallas_call(
        pyramid_weights_kernel,
        out_shape=outs,
        in_specs=[whole] * 7,
        out_specs=(whole,) * len(outs),
        scratch_shapes=[
            pltpu.VMEM((channels, LANES), wide),
            pltpu.VMEM((channels, pixels), low),
            pltpu.VMEM((height, width + 2 * PAD, aspp), wide),
            pltpu.VMEM((pixels, aspp), low),
            pltpu.VMEM((3, channels, aspp), wide),
            sems((2, 3, 3)),
            sems((2, 3, 3)),
            *pair_sum_scratch(crops),
        ],
        compiler_params=pltpu.CompilerParams(
            collective_id=11, has_side_effects=True, vmem_limit_bytes=VMEM_BYTES
        ),
        cost_estimate=pl.CostEstimate(
            flops=100 * pixels * channels * aspp, bytes_accessed=64 * pixels * channels, transcendentals=0
        ),
        name="pyramid_weights",
    )(branch_low, trunk, depth, sep_point, crop_local, proj_part, head_part)


def share_rows(slots, at, size, sems):
    rows, cols, row, col, me = place()

    def go(step, carry):
        other = lax.rem(me + step, rows * cols)
        mine = slots.at[me, pl.ds(at, size), :]
        pltpu.make_async_remote_copy(
            mine,
            mine,
            sems.at[0],
            sems.at[1],
            device_id=(other // cols, lax.rem(other, cols)),
            device_id_type=MESH,
        ).start()
        return carry

    lax.fori_loop(1, rows * cols, go, 0)


def shared_rows(slots, at, size, sems):
    rows, cols, row, col, me = place()
    others = slots.at[pl.ds(0, rows * cols - 1), pl.ds(at, size), :]
    pltpu.make_async_remote_copy(
        others,
        others,
        sems.at[0],
        sems.at[1],
        device_id=(row, lax.rem(col + 1, cols)),
        device_id_type=MESH,
    ).wait()


def trunk_back_kernel(
    near,
    own_low,
    depth,
    sep_point,
    aspp_point,
    members,
    crop_high,
    crop_rest,
    expanded,
    features,
    three,
    dilated,
    two,
    second_act,
    expand_weight,
    early,
    pre_grad,
    expand_part,
    dilated_low,
    sums_three,
    sums_two,
    early_out,
    fetched,
    chunk_in,
    shifted,
    moved,
    maps,
    grown,
    expand_low,
    slots_three,
    slots_two,
    sems_three,
    sems_two,
    fetch_sems,
    chunk_sems,
    *early_refs,
):
    rows, cols, row, col, me = place()
    low, wide = jnp.bfloat16, jnp.float32
    height = near.shape[2]
    early_sum = Sums(early, True, early_out, early_refs)
    aspp = sep_point.shape[2]
    pixels, channels = expanded.shape
    middle = dilated.shape[1]
    width = pixels // height
    count = float(pixels * rows * cols)
    per = aspp // LANES
    chunks = channels // aspp
    greet_all()

    def fetch(number):
        return pltpu.make_async_copy(
            near.at[number // 3, number % 3], fetched.at[number % 2], fetch_sems.at[number % 2]
        )

    fetch(0).start()
    early_sum.fetch()

    def chunk_of(block):
        return pl.ds(pl.multiple_of(block * aspp, aspp), aspp)

    def own(block, carry):
        span = chunk_of(block)
        grown[:, span] = (
            across(own_low[...], aspp_point[span, :])
            + jnp.dot(members[...], crop_high[:, span], preferred_element_type=wide)
            + jnp.dot(members[...], crop_rest[:, span], preferred_element_type=wide)
        )
        return carry

    lax.fori_loop(0, chunks, own, 0)
    await_all()
    early_sum.fetched()
    early_sum.start_half()

    def fetch_chunk(block):
        slot = lax.rem(block, 2)
        return pltpu.make_async_copy(
            expanded.at[:, chunk_of(block)], chunk_in.at[slot], chunk_sems.at[slot]
        )

    def advance(block):
        @pl.when(block + 1 < chunks)
        def _():
            fetch_chunk(block + 1).start()

        fetch_chunk(block).wait()

    def back(block, line, span):
        rows_span = slice(line * width, (line + 1) * width)
        value = chunk_in[lax.rem(block, 2), rows_span, :]
        normed = (value - three[0:1, span]) * three[1:2, span]
        return rows_span, normed

    for index in range(3):
        rate = BASE_RATE * (index + 1)
        for way in range(3):
            number = 3 * index + way
            if number < 8:
                fetch(number + 1).start()
            fetch(number).wait()
            shifted[...] = fetched[number % 2].astype(wide)
            for side in range(3):
                tap = 3 * (2 - way) + side
                at = PAD - (side - 1) * rate
                for line in range(height):
                    moved[line * width : (line + 1) * width, tap * aspp : (tap + 1) * aspp] = shifted[
                        line, at : at + width, :
                    ].astype(low)

        def one_chunk(block, carry):
            span = chunk_of(block)
            rows_of = sep_point[index, span, :].astype(wide)
            for tap in range(9):
                order = 9 * index + tap
                maps[:, tap * aspp : (tap + 1) * aspp] = (
                    rows_of * depth[span, order : order + 1]
                ).astype(low)
            total = grown[:, span] + across(moved[...], maps[...])
            if index < 2:
                grown[:, span] = total
                return carry
            advance(block)
            shift_sum, gain_sum = jnp.zeros((1, aspp), wide), jnp.zeros((1, aspp), wide)
            for line in range(height):
                rows_span, normed = back(block, line, span)
                gated = (
                    normed * three[2:3, span]
                    + three[3:4, span]
                    + features[rows_span, span].astype(wide)
                )
                sigma = sigmoid(gated)
                up = total[rows_span, :] * (sigma * (1.0 + gated * (1.0 - sigma)))
                grown[rows_span, span] = up
                pre_grad[rows_span, span] = up.astype(low)
                shift_sum = shift_sum + jnp.sum(up, axis=0, keepdims=True)
                gain_sum = gain_sum + jnp.sum(up * normed, axis=0, keepdims=True)
            for part in range(per):
                lanes = slice(part * LANES, (part + 1) * LANES)
                slots_three[me, pl.ds(block * 2 * per + part, 1), :] = shift_sum[:, lanes]
                slots_three[me, pl.ds(block * 2 * per + per + part, 1), :] = gain_sum[:, lanes]
            pair = block // 2

            @pl.when(lax.rem(block, 2) == 1)
            def _():
                share_rows(slots_three, pl.multiple_of(pair * 4 * per, 8), 4 * per, sems_three.at[pair])

            return carry

        if index == 0:
            early_sum.start_level(0)
        if index == 2:
            fetch_chunk(0).start()
        lax.fori_loop(0, chunks, one_chunk, 0)
        if index == 0:
            early_sum.start_level(1)
        if index == 1:
            early_sum.start_back(1)

    def finish(block, carry):
        span = chunk_of(block)
        pair = block // 2
        at = pl.multiple_of(pair * 4 * per, 8)

        @pl.when(lax.rem(block, 2) == 0)
        def _():
            shared_rows(slots_three, at, 4 * per, sems_three.at[pair])
            sums_three[pl.ds(at, 4 * per), :] = jnp.sum(slots_three[:, pl.ds(at, 4 * per), :], axis=0)

        advance(block)

        def row_at(start):
            first = block * 2 * per + start
            return jnp.concatenate([sums_three[pl.ds(first + part, 1), :] for part in range(per)], axis=1)

        shift_mean = row_at(0) / count
        gain_mean = row_at(per) / count
        factor = three[2:3, span] * three[1:2, span]
        for line in range(height):
            rows_span, normed = back(block, line, span)
            inner = grown[rows_span, span] - shift_mean - normed * gain_mean
            expand_low[rows_span, span] = (inner * factor).astype(low)
        return carry

    early_sum.start_back(0)
    fetch_chunk(0).start()
    lax.fori_loop(0, chunks, finish, 0)
    grown_two = across(expand_low[...], expand_weight[...])
    shift_sum, gain_sum = jnp.zeros((1, middle), wide), jnp.zeros((1, middle), wide)
    for line in range(height):
        rows_span = slice(line * width, (line + 1) * width)
        normed = (dilated[rows_span, :] - two[0:1, :]) * two[1:2, :]
        gated = normed * two[2:3, :] + two[3:4, :]
        sigma = sigmoid(gated)
        up = grown_two[rows_span, :] * (sigma * (1.0 + gated * (1.0 - sigma)))
        grown[rows_span, :middle] = up
        shift_sum = shift_sum + jnp.sum(up, axis=0, keepdims=True)
        gain_sum = gain_sum + jnp.sum(up * normed, axis=0, keepdims=True)
    per_two = middle // LANES
    put_row(slots_two, me, 0, shift_sum)
    put_row(slots_two, me, per_two, gain_sum)
    share(slots_two, sems_two)
    for block in range(channels // middle):
        span = slice(block * middle, (block + 1) * middle)
        expand_part[block * middle : (block + 1) * middle, :] = down(
            second_act[...], expand_low[:, span]
        ).astype(low)
    shared(slots_two, sems_two)
    total = jnp.sum(slots_two[...], axis=0)
    sums_two[...] = total
    shift_mean = take_row(total, 0, middle) / count
    gain_mean = take_row(total, per_two, middle) / count
    factor = two[2:3, :] * two[1:2, :]
    for line in range(height):
        rows_span = slice(line * width, (line + 1) * width)
        normed = (dilated[rows_span, :] - two[0:1, :]) * two[1:2, :]
        inner = grown[rows_span, :middle] - shift_mean - normed * gain_mean
        dilated_low[rows_span, :] = (inner * factor).astype(low)
    early_sum.start_back_half()
    early_sum.finish()


def trunk_back(near, own_low, depth, sep_point, aspp_point, members, crop_high, crop_rest, expanded,
               features, three, dilated, two, second_act, expand_weight, early):
    devices = lax.axis_size("rows") * lax.axis_size("cols")
    height, extent, aspp = near.shape[2:]
    pixels, channels = expanded.shape
    middle = dilated.shape[1]
    chunks = channels // aspp
    low, wide = jnp.bfloat16, jnp.float32
    shape = jax.ShapeDtypeStruct
    whole = pl.BlockSpec(memory_space=pltpu.VMEM)
    away = pl.BlockSpec(memory_space=pl.ANY)
    sems = pltpu.SemaphoreType.DMA
    per_two = middle // LANES
    outs = (
        shape((pixels, channels), low),
        shape((channels, middle), low),
        shape((pixels, middle), low),
        shape((chunks * 2 * (aspp // LANES), LANES), wide),
        shape((2 * per_two, LANES), wide),
        shape(early.shape, low),
    )
    return pl.pallas_call(
        trunk_back_kernel,
        out_shape=outs,
        in_specs=[away] + [whole] * 7 + [away] + [whole] * 6 + [away],
        out_specs=(whole,) * 5 + (away,),
        scratch_shapes=[
            pltpu.VMEM((2, height, extent, aspp), low),
            pltpu.VMEM((2, pixels, aspp), wide),
            pltpu.VMEM((height, extent, aspp), wide),
            pltpu.VMEM((pixels, 9 * aspp), low),
            pltpu.VMEM((aspp, 9 * aspp), low),
            pltpu.VMEM((pixels, channels), wide),
            pltpu.VMEM((pixels, channels), low),
            pltpu.VMEM((devices, chunks * 2 * (aspp // LANES), LANES), wide),
            pltpu.VMEM((devices, 2 * per_two, LANES), wide),
            sems((chunks // 2, 2)),
            sems((2,)),
            sems((2,)),
            sems((2,)),
            *sums_scratch(*early.shape, True),
        ],
        compiler_params=pltpu.CompilerParams(
            collective_id=12, has_side_effects=True, vmem_limit_bytes=VMEM_BYTES + (3 << 20)
        ),
        cost_estimate=pl.CostEstimate(
            flops=80 * pixels * channels * aspp, bytes_accessed=64 * pixels * channels, transcendentals=0
        ),
        name="trunk_back",
    )(near, own_low, depth, sep_point, aspp_point, members, crop_high, crop_rest, expanded, features,
      three, dilated, two, second_act, expand_weight, early)


EDGE = 16


class Halo:
    def __init__(self, near, direct, relay, edge):
        self.near, self.direct, self.relay, self.edge = near, direct, relay, edge
        self.rows, self.cols, self.row, self.col, _ = place()
        self.height, self.width = near.shape[1], near.shape[2] - 2 * EDGE
        self.odd = lax.rem(self.row, 2)
        self.pair = self.row + 1 - 2 * self.odd
        self.onward = self.row + 2 - 4 * self.odd
        self.far = self.row - 1 + 2 * self.odd
        self.pair_way = 2 - 2 * self.odd
        self.far_way = 2 * self.odd

    def exists(self, target):
        return jnp.logical_and(target >= 0, target < self.rows)

    def line_ref(self, way, line):
        return self.near.at[way, line, pl.ds(EDGE, self.width), :]

    def direct_copy(self, line):
        return pltpu.make_async_remote_copy(
            self.line_ref(1, line),
            self.line_ref(self.far_way, line),
            self.direct.at[0, line],
            self.direct.at[1, line],
            device_id=(self.pair, self.col),
            device_id_type=MESH,
        )

    def relay_copy(self, line):
        return pltpu.make_async_remote_copy(
            self.line_ref(self.pair_way, line),
            self.line_ref(self.far_way, line),
            self.relay.at[0, line],
            self.relay.at[1, line],
            device_id=(self.onward, self.col),
            device_id_type=MESH,
        )

    def edge_copy(self, way):
        start = pl.multiple_of(EDGE + (1 - self.col) * (self.width - EDGE), 16)
        end = pl.multiple_of(self.col * (self.width + EDGE), 16)
        return pltpu.make_async_remote_copy(
            self.near.at[1, :, pl.ds(start, EDGE), :],
            self.near.at[way, :, pl.ds(end, EDGE), :],
            self.edge.at[0, way],
            self.edge.at[1, way],
            device_id=(self.row + 1 - way, 1 - self.col),
            device_id_type=MESH,
        )

    def clear(self):
        near = self.near
        blank = pl.multiple_of(self.col * (self.width + EDGE), 16)
        for way in range(3):
            near[way, :, pl.ds(blank, EDGE), :] = jnp.zeros(
                (self.height, EDGE, near.shape[3]), near.dtype
            )

        @pl.when(jnp.logical_not(self.exists(self.far)))
        def _():
            near[self.far_way] = jnp.zeros(near.shape[1:], near.dtype)

    def start(self):
        self.edge_copy(1).start()
        for line in range(self.height // 2):
            self.direct_copy(line).start()
        for way in (0, 2):

            @pl.when(self.exists(self.row + 1 - way))
            def _():
                self.edge_copy(way).start()

    def wait_own(self):
        self.edge_copy(1).wait_recv()

    def pass_line(self, line):
        self.direct_copy(line).wait_recv()

        @pl.when(self.exists(self.onward))
        def _():
            self.relay_copy(line).start()

    def pass_first(self):
        for line in range(self.height // 2):
            self.pass_line(line)
        for line in range(self.height // 2, self.height):
            self.direct_copy(line).start()

    def pass_rest(self):
        for line in range(self.height // 2, self.height):
            self.pass_line(line)

    def wait_rest(self):
        self.wait_edges()
        self.wait_relay()

    def wait_edges(self):
        for way in (0, 2):

            @pl.when(self.exists(self.row - 1 + way))
            def _():
                self.edge_copy(way).wait_recv()

    def wait_relay(self):
        @pl.when(self.exists(self.far))
        def _():
            for line in range(self.height):
                self.relay_copy(line).wait_recv()

    def drain(self):
        self.edge_copy(1).wait_send()
        for line in range(self.height):
            self.direct_copy(line).wait_send()
        for way in (0, 2):

            @pl.when(self.exists(self.row + 1 - way))
            def _():
                self.edge_copy(way).wait_send()

        @pl.when(self.exists(self.onward))
        def _():
            for line in range(self.height):
                self.relay_copy(line).wait_send()


def front_kernel(
    features,
    reduce_weight,
    dilated_weight,
    expand_weight,
    pool_weight,
    mid_gain,
    mid_shift,
    out_gain,
    out_shift,
    crop_ids,
    boundary,
    valid,
    reduced,
    first_act,
    dilated,
    second_act,
    expanded,
    trunk,
    one,
    two,
    three,
    count_sums,
    crop_sums,
    crop_part,
    pixel_crops,
    near,
    shifted,
    moved,
    members,
    one_slots,
    two_slots,
    three_own,
    three_pair,
    three_slots,
    three_all,
    direct,
    relay,
    edge,
    one_sems,
    two_sems,
    pair_sems,
    three_sems,
    all_sems,
):
    rows, cols, row, col, me = place()
    low, wide = jnp.bfloat16, jnp.float32
    height = near.shape[1]
    pixels, middle = reduced.shape
    channels = features.shape[1]
    width = pixels // height
    share_size = float(pixels)
    count = float(pixels * rows * cols)
    per = middle // LANES
    halo = Halo(near, direct, relay, edge)
    greet_all()
    halo.clear()
    reduced[...] = jnp.dot(features[...], reduce_weight[...], preferred_element_type=wide)

    def lines(body, carry=0):
        def run(line, carry):
            return body(line, pl.ds(pl.multiple_of(line * width, width), width), carry)

        return lax.fori_loop(0, height, run, carry)

    def keep_low(line, span, carry):
        near[1, line, EDGE : EDGE + width, :] = reduced[span, :].astype(low)
        return carry

    lines(keep_low)
    await_all()
    halo.start()

    def statistics(value_of, extent):
        zero = jnp.zeros((1, extent), wide)
        total = lines(lambda line, span, acc: acc + jnp.sum(value_of(span), axis=0, keepdims=True), zero)
        mean = total / share_size

        def squares(line, span, acc):
            apart = value_of(span) - mean
            return acc + jnp.sum(apart * apart, axis=0, keepdims=True)

        return mean, lines(squares, zero)

    def settle(table, at, center, scale):
        table[...] = jnp.zeros(table.shape, wide)
        table[0:1, :] = center
        table[1:2, :] = scale
        table[2:3, :] = mid_gain[at : at + 1, :]
        table[3:4, :] = mid_shift[at : at + 1, :]

    def activated(value, table):
        gated = (value - table[0:1, :]) * table[1:2, :] * table[2:3, :] + table[3:4, :]
        return gated * sigmoid(gated)

    mean, square = statistics(lambda span: reduced[span, :], middle)
    one_slots[me] = jnp.zeros(one_slots.shape[1:], wide)
    put_row(one_slots, me, 0, mean)
    put_row(one_slots, me, per, square)
    crop_of = lax.broadcasted_iota(jnp.int32, (LANES, width), 0)
    for line in range(height):
        hot = jnp.where(crop_of == crop_ids[line : line + 1, :], 1.0, 0.0)
        members[:, line * width : (line + 1) * width] = hot.astype(low)
        pixel_crops[line * width : (line + 1) * width, :] = hot.T.astype(low)
    lane = lax.broadcasted_iota(jnp.int32, (8, LANES), 1)

    def whole_sum(table):
        part = jnp.sum(table[...].astype(wide), axis=0, keepdims=True)
        return jnp.sum(part, axis=1, keepdims=True)

    counts = across(jnp.ones((8, pixels), low), members[...])
    counts = jnp.where(lane == CROPS, share_size - whole_sum(boundary), counts)
    counts = jnp.where(lane == CROPS + 1, whole_sum(valid), counts)
    put_row(one_slots, me, 2 * per, counts[0:1, :])
    share(one_slots, one_sems)
    shared(one_slots, one_sems)
    center, scale = merged(one_slots, per, share_size, count)
    settle(one, 0, take_row(center, 0, middle), take_row(scale, 0, middle))
    count_sums[...] = jnp.sum(one_slots[:, 2 * per : 2 * per + 8, :], axis=0)

    def first(line, span, carry):
        first_act[span, :] = activated(reduced[span, :], one).astype(low)
        return carry

    lines(first)

    def one_way(way, own):
        alive = jnp.where(halo.exists(row - 1 + way), 1.0, 0.0)

        def open_line(line, span, carry):
            shifted[line] = activated(near[way, line].astype(wide), one) * alive
            if own:
                shifted[line, EDGE : EDGE + width, :] = first_act[span, :].astype(wide)
            blank = pl.multiple_of(col * (width + EDGE), 16)
            shifted[line, pl.ds(blank, EDGE), :] = jnp.zeros((EDGE, middle), wide)
            for side in range(3):
                at = EDGE + (side - 1) * MID_RATE
                moved[span, side * middle : (side + 1) * middle] = shifted[
                    line, at : at + width, :
                ].astype(low)
            return carry

        lines(open_line)
        made = jnp.dot(moved[...], dilated_weight[way], preferred_element_type=wide)
        if own:
            dilated[...] = made
        else:
            dilated[...] += made

    halo.pass_first()
    halo.wait_own()
    one_way(1, True)
    halo.pass_rest()
    halo.wait_edges()
    one_way(halo.pair_way, False)
    halo.wait_relay()
    one_way(halo.far_way, False)
    mean, square = statistics(lambda span: dilated[span, :], middle)
    put_row(two_slots, me, 0, mean)
    put_row(two_slots, me, per, square)
    share(two_slots, two_sems)
    shared(two_slots, two_sems)
    center, scale = merged(two_slots, per, share_size, count)
    settle(two, 1, take_row(center, 0, middle), take_row(scale, 0, middle))

    def second(line, span, carry):
        second_act[span, :] = activated(dilated[span, :], two).astype(low)
        return carry

    lines(second)
    chunk = 2 * LANES
    half_rows = channels // 2 // LANES
    half_chunks = channels // 2 // chunk

    def expand(block, carry):
        span = pl.ds(pl.multiple_of(block * chunk, chunk), chunk)
        expanded[:, span] = jnp.dot(second_act[...], expand_weight[:, span], preferred_element_type=wide)
        mean, square = statistics(lambda rows_span: expanded[rows_span, span], chunk)
        at = block // half_chunks * 2 * half_rows + lax.rem(block, half_chunks) * 2
        for part in range(2):
            lanes = slice(part * LANES, (part + 1) * LANES)
            three_own[pl.ds(at + part, 1), :] = mean[:, lanes]
            three_own[pl.ds(at + half_rows + part, 1), :] = square[:, lanes]
        return carry

    lax.fori_loop(0, channels // chunk, expand, 0)

    def to_pair(src, dst, sems):
        return pltpu.make_async_remote_copy(
            src, dst, sems.at[0], sems.at[1], device_id=(row, 1 - col), device_id_type=MESH
        )

    theirs = pl.ds(pl.multiple_of((1 - col) * 2 * half_rows, 8), 2 * half_rows)
    mine = pl.ds(pl.multiple_of(col * 2 * half_rows, 8), 2 * half_rows)
    copy = to_pair(three_own.at[theirs], three_pair, pair_sems)
    copy.start()
    copy.wait()
    own = three_own[mine, :]
    other = three_pair[...]
    apart = own[:half_rows] - other[:half_rows]
    three_slots[row, :half_rows, :] = 0.5 * (own[:half_rows] + other[:half_rows])
    three_slots[row, half_rows:, :] = (
        own[half_rows:] + other[half_rows:] + (0.5 * share_size) * (apart * apart)
    )
    share_column(three_slots, three_sems)
    shared_column(three_slots, three_sems)
    center, scale = merged(three_slots, half_rows, 2.0 * share_size, count)
    three_all[col, :half_rows, :] = center
    three_all[col, half_rows:, :] = scale
    copy = to_pair(three_all.at[col], three_all.at[col], all_sems)
    copy.start()
    copy.wait()
    for half in range(2):
        span = slice(half * channels // 2, (half + 1) * channels // 2)
        three[0:1, span] = take_row(three_all[half], 0, channels // 2)
        three[1:2, span] = take_row(three_all[half], half_rows, channels // 2)
    three[2:3, :] = out_gain[...]
    three[3:4, :] = out_shift[...]
    three[4:8, :] = jnp.zeros((4, channels), wide)
    crops = CROPS

    def last(block, carry):
        span = pl.ds(pl.multiple_of(block * chunk, chunk), chunk)

        def act_line(line, rows_span, carry):
            normed = (expanded[rows_span, span] - three[0:1, span]) * three[1:2, span]
            gated = (
                normed * three[2:3, span] + three[3:4, span] + features[rows_span, span].astype(wide)
            )
            trunk[rows_span, span] = (gated * sigmoid(gated)).astype(low)
            return carry

        lines(act_line)
        sums = jnp.dot(members[...], trunk[:, span], preferred_element_type=wide)[:crops, :]
        for part in range(2):
            at = pl.multiple_of((2 * block + part) * crops, 8)
            crop_sums[pl.ds(at, crops), :] = sums[:, part * LANES : (part + 1) * LANES]
        high = sums.astype(low)
        rest = (sums - high.astype(wide)).astype(low)
        return (
            carry
            + jnp.dot(high, pool_weight[span, :], preferred_element_type=wide)
            + jnp.dot(rest, pool_weight[span, :], preferred_element_type=wide)
        )

    crop_part[...] = lax.fori_loop(
        0, channels // chunk, last, jnp.zeros((crops, pool_weight.shape[1]), wide)
    )
    halo.drain()


def front(height, features, reduce_weight, dilated_weight, expand_weight, pool_weight, mid_gain,
          mid_shift, out_gain, out_shift, crop_ids, boundary, valid):
    rows = lax.axis_size("rows")
    devices = rows * lax.axis_size("cols")
    pixels, channels = features.shape
    middle = reduce_weight.shape[1]
    width = pixels // height
    low, wide = jnp.bfloat16, jnp.float32
    shape = jax.ShapeDtypeStruct
    whole = pl.BlockSpec(memory_space=pltpu.VMEM)
    sems = pltpu.SemaphoreType.DMA
    per = middle // LANES
    half_rows = channels // 2 // LANES
    outs = (
        shape((pixels, middle), wide),
        shape((pixels, middle), low),
        shape((pixels, middle), wide),
        shape((pixels, middle), low),
        shape((pixels, channels), wide),
        shape((pixels, channels), low),
        shape((8, middle), wide),
        shape((8, middle), wide),
        shape((8, channels), wide),
        shape((8, LANES), wide),
        shape((CROPS * channels // LANES, LANES), wide),
        shape((CROPS, pool_weight.shape[1]), wide),
        shape((pixels, LANES), low),
    )
    return pl.pallas_call(
        front_kernel,
        out_shape=outs,
        in_specs=[whole] * 12,
        out_specs=(whole,) * len(outs),
        scratch_shapes=[
            pltpu.VMEM((3, height, width + 2 * EDGE, middle), low),
            pltpu.VMEM((height, width + 2 * EDGE, middle), wide),
            pltpu.VMEM((pixels, 3 * middle), low),
            pltpu.VMEM((LANES, pixels), low),
            pltpu.VMEM((devices, 2 * per + 8, LANES), wide),
            pltpu.VMEM((devices, 2 * per, LANES), wide),
            pltpu.VMEM((4 * half_rows, LANES), wide),
            pltpu.VMEM((2 * half_rows, LANES), wide),
            pltpu.VMEM((rows, 2 * half_rows, LANES), wide),
            pltpu.VMEM((2, 2 * half_rows, LANES), wide),
            sems((2, height)),
            sems((2, height)),
            sems((2, 3)),
            sems((2,)),
            sems((2,)),
            sems((2,)),
            sems((2,)),
            sems((2,)),
        ],
        compiler_params=pltpu.CompilerParams(
            collective_id=14, has_side_effects=True, vmem_limit_bytes=VMEM_BYTES
        ),
        name="front",
    )(features, reduce_weight, dilated_weight, expand_weight, pool_weight, mid_gain, mid_shift,
      out_gain, out_shift, crop_ids, boundary, valid)


PLANE = 4


class Sum:
    def __init__(self, full, own, out, plane_first, half_in, near_in, far_in, half_sem, near_sem, far_sem, copy_sem):
        self.full, self.out, self.half_in = full, out, half_in
        self.half_sem, self.copy_sem = half_sem, copy_sem
        self.rows, self.cols, self.row, self.col, _ = place()
        parts = self.rows // PLANE
        quarter, part = lax.rem(self.row, PLANE), self.row // PLANE
        plane = (PLANE, quarter, lambda mate: part * PLANE + mate)
        rest = (parts, part, lambda mate: mate * PLANE + quarter)
        self.levels = (plane, rest) if plane_first else (rest, plane)
        self.arrivals, self.sems = (near_in, far_in), (near_sem, far_sem)
        self.half_rows = full.shape[0] // 2
        self.sizes = [self.half_rows // self.levels[0][0]]
        self.sizes.append(self.sizes[0] // self.levels[1][0])
        self.own = own
        self.data = full.at[self.half_span(self.col)] if own is None else own

    def span(self, start, size):
        return pl.ds(pl.multiple_of(start, 16), size)

    def half_span(self, col):
        return self.span(col * self.half_rows, self.half_rows)

    def level_span(self, level, at):
        base = 0 if level == 0 else self.levels[0][1] * self.sizes[0]
        return self.span(base + at * self.sizes[level], self.sizes[level])

    def out_at(self, span):
        return self.out.at[self.span(self.col * self.half_rows + span.start, span.size)]

    def mates(self, level):
        count, at, row_of = self.levels[level]
        for step in range(1, count):
            mate = lax.rem(at + step, count)
            yield mate, (row_of(mate), self.col)

    def remote(self, src, dst, sems, out_at, in_at, target):
        return pltpu.make_async_remote_copy(
            src, dst, sems.at[0, out_at], sems.at[1, in_at], device_id=target, device_id_type=MESH
        )

    def fetch(self):
        return pltpu.make_async_copy(self.full.at[self.half_span(self.col)], self.own, self.copy_sem)

    def half_copy(self):
        other = self.full.at[self.half_span(1 - self.col)]
        return self.remote(other, self.half_in, self.half_sem, 0, 0, (self.row, 1 - self.col))

    def level_copy(self, level, mate, target):
        at = self.levels[level][1]
        return self.remote(
            self.data.at[self.level_span(level, mate)],
            self.arrivals[level].at[at],
            self.sems[level],
            mate,
            at,
            target,
        )

    def level_arrival(self, level, mate, target):
        slot = self.arrivals[level].at[mate]
        return self.remote(slot, slot, self.sems[level], mate, mate, target)

    def back_copy(self, level, mate, target):
        count, at, _ = self.levels[level]
        mine = self.out_at(self.level_span(level, at))
        return self.remote(mine, mine, self.sems[level], count + mate, count + at, target)

    def back_arrival(self, level, mate, target):
        count = self.levels[level][0]
        theirs = self.out_at(self.level_span(level, mate))
        return self.remote(theirs, theirs, self.sems[level], count + mate, count + mate, target)

    def back_half(self, col):
        part = self.out.at[self.half_span(col)]
        return self.remote(part, part, self.half_sem, 1, 1, (self.row, 1 - self.col))

    def add(self, span, sources):
        block = 64
        base = span.start

        def some(at, carry):
            rows = pl.ds(pl.multiple_of(base + at * block, 16), block)
            total = self.data[rows, :].astype(jnp.float32)
            for source in sources:
                total = total + source(pl.ds(pl.multiple_of(at * block, 16), block)).astype(jnp.float32)
            self.data[rows, :] = total.astype(self.data.dtype)
            return carry

        full = span.size // block
        lax.fori_loop(0, full, some, 0)
        rest = span.size - full * block
        if rest:
            rows = pl.ds(pl.multiple_of(base + full * block, 16), rest)
            total = self.data[rows, :].astype(jnp.float32)
            for source in sources:
                total = total + source(pl.ds(full * block, rest)).astype(jnp.float32)
            self.data[rows, :] = total.astype(self.data.dtype)

    def start_half(self):
        self.half_copy().start()

    def start_level(self, level):
        if level == 0:
            self.half_copy().wait()
            self.add(self.span(0, self.half_rows), [lambda rows: self.half_in[rows, :]])
        else:
            self.gather(0)
        for mate, target in self.mates(level):
            self.level_copy(level, mate, target).start()

    def gather(self, level):
        for mate, target in self.mates(level):
            self.level_copy(level, mate, target).wait_send()
            self.level_arrival(level, mate, target).wait_recv()
        self.add(
            self.level_span(level, self.levels[level][1]),
            [lambda rows, mate=mate: self.arrivals[level][mate, rows, :] for mate, _ in self.mates(level)],
        )

    def start_back(self, level):
        if level == 1:
            self.gather(1)
            span = self.level_span(1, self.levels[1][1])
            copy = pltpu.make_async_copy(self.data.at[span], self.out_at(span), self.copy_sem)
            copy.start()
            copy.wait()
        else:
            for mate, target in self.mates(1):
                self.back_copy(1, mate, target).wait_send()
                self.back_arrival(1, mate, target).wait_recv()
        for mate, target in self.mates(level):
            self.back_copy(level, mate, target).start()

    def start_back_half(self):
        for mate, target in self.mates(0):
            self.back_copy(0, mate, target).wait_send()
            self.back_arrival(0, mate, target).wait_recv()
        self.back_half(self.col).start()

    def finish(self):
        self.back_half(self.col).wait_send()
        self.back_half(1 - self.col).wait_recv()


class Sums:
    def __init__(self, full, own, out, refs):
        self.each = []
        start = 0
        for size, plane_first in sum_pieces(full.shape[0]):
            span = pl.ds(start, size)
            count = 7 if own is None else 8
            mine, refs = list(refs[:count]), refs[count:]
            part = None if own is None else mine.pop(0)
            self.each.append(Sum(full.at[span], part, out.at[span], plane_first, *mine))
            start += size
        self.rest = refs

    def fetch(self):
        for each in self.each:
            each.fetch().start()

    def fetched(self):
        for each in self.each:
            each.fetch().wait()

    def start_half(self):
        for each in self.each:
            each.start_half()

    def start_level(self, level):
        for each in self.each:
            each.start_level(level)

    def start_back(self, level):
        for each in self.each:
            each.start_back(level)

    def start_back_half(self):
        for each in self.each:
            each.start_back_half()

    def finish(self):
        for each in self.each:
            each.finish()


def sum_unit():
    return 2 * lax.axis_size("rows") * 16


def sum_pieces(total):
    unit = sum_unit()
    units = total // unit
    second = units // 3
    pieces = [((units - second) * unit, True)]
    if second:
        pieces.append((second * unit, False))
    return pieces


def sums_scratch(total, lanes, away):
    parts = lax.axis_size("rows") // PLANE
    low, sems = jnp.bfloat16, pltpu.SemaphoreType.DMA
    scratch = []
    for size, plane_first in sum_pieces(total):
        counts = (PLANE, parts) if plane_first else (parts, PLANE)
        half = size // 2
        if away:
            scratch.append(pltpu.VMEM((half, lanes), low))
        scratch += [
            pltpu.VMEM((half, lanes), low),
            pltpu.VMEM((counts[0], half // counts[0], lanes), low),
            pltpu.VMEM((counts[1], half // counts[0] // counts[1], lanes), low),
            sems((2, 2)),
            sems((2, 2 * counts[0])),
            sems((2, 2 * counts[1])),
            sems,
        ]
    return scratch


def sum_rows(rows):
    unit = sum_unit()
    return -(-rows // unit) * unit


def tail_kernel(
    dilated_low,
    first_act,
    dilated_weight,
    reduced,
    one,
    features,
    reduce_weight,
    pre_grad,
    expand_part,
    features_grad,
    expand_out,
    dilated_out,
    reduce_out,
    sums_one,
    near,
    shifted,
    moved,
    act_turned,
    features_turned,
    first_grad,
    reduced_low,
    dilated_data,
    reduce_data,
    slots,
    direct,
    relay,
    edge,
    sems_one,
    *sum_refs,
):
    rows, cols, row, col, me = place()
    low, wide = jnp.bfloat16, jnp.float32
    height = near.shape[1]
    pixels, middle = dilated_low.shape
    channels = features.shape[1]
    width = pixels // height
    count = float(pixels * rows * cols)
    expand_sum = Sums(expand_part, True, expand_out, sum_refs)
    dilated_sum = Sums(dilated_data, None, dilated_out, expand_sum.rest)
    reduce_sum = Sums(reduce_data, None, reduce_out, dilated_sum.rest)
    sums = (expand_sum, dilated_sum, reduce_sum)
    halo = Halo(near, direct, relay, edge)
    greet_all()
    expand_sum.fetch()
    halo.clear()
    for line in range(height):
        near[1, line, EDGE : EDGE + width, :] = dilated_low[line * width : (line + 1) * width, :]
    for data, used in ((dilated_data, 9 * middle), (reduce_data, channels)):
        if data.shape[0] > used:
            data[used:, :] = jnp.zeros((data.shape[0] - used, data.shape[1]), low)
    expand_sum.fetched()
    await_all()
    halo.start()
    expand_sum.start_half()

    def turn_features(block, carry):
        span = pl.ds(pl.multiple_of(block * width, width), width)
        for line in range(height):
            features_turned[span, line * width : (line + 1) * width] = features[
                line * width : (line + 1) * width, span
            ].T
        return carry

    def turn_act(block, carry):
        span = pl.ds(pl.multiple_of(block * width, width), width)
        for line in range(height):
            act_turned[span, line * width : (line + 1) * width] = first_act[
                line * width : (line + 1) * width, span
            ].T
        return carry

    lax.fori_loop(0, middle // width, turn_act, 0)

    def one_way(way):
        shifted[...] = near[way].astype(wide)
        for side in range(3):
            tap = 3 * (2 - way) + side
            rows_of = pl.ds(pl.multiple_of(tap * middle, middle), middle)
            at = EDGE - (side - 1) * MID_RATE
            for line in range(height):
                moved[line * width : (line + 1) * width, :] = shifted[line, at : at + width, :].astype(
                    low
                )
            made = across(moved[...], dilated_weight[tap])
            if isinstance(way, int) and side == 0:
                first_grad[...] = made
            else:
                first_grad[...] += made
            dilated_data[rows_of, :] = jnp.dot(
                act_turned[...], moved[...], preferred_element_type=wide
            ).astype(low)

    expand_sum.start_level(0)
    halo.wait_own()
    one_way(1)
    halo.pass_first()
    expand_sum.start_level(1)
    lax.fori_loop(0, channels // width, turn_features, 0)
    halo.pass_rest()
    expand_sum.start_back(1)
    halo.wait_edges()
    one_way(halo.pair_way)
    expand_sum.start_back(0)
    halo.wait_relay()
    one_way(halo.far_way)
    dilated_sum.start_half()
    expand_sum.start_back_half()
    shift_sum, gain_sum = jnp.zeros((1, middle), wide), jnp.zeros((1, middle), wide)
    for line in range(height):
        span = slice(line * width, (line + 1) * width)
        normed = (reduced[span, :] - one[0:1, :]) * one[1:2, :]
        gated = normed * one[2:3, :] + one[3:4, :]
        sigma = sigmoid(gated)
        up = first_grad[span, :] * (sigma * (1.0 + gated * (1.0 - sigma)))
        first_grad[span, :] = up
        shift_sum = shift_sum + jnp.sum(up, axis=0, keepdims=True)
        gain_sum = gain_sum + jnp.sum(up * normed, axis=0, keepdims=True)
    per = middle // LANES
    put_row(slots, me, 0, shift_sum)
    put_row(slots, me, per, gain_sum)
    share(slots, sems_one)
    dilated_sum.start_level(0)
    shared(slots, sems_one)
    total = jnp.sum(slots[...], axis=0)
    sums_one[...] = total
    shift_mean = take_row(total, 0, middle) / count
    gain_mean = take_row(total, per, middle) / count
    factor = one[2:3, :] * one[1:2, :]
    for line in range(height):
        span = slice(line * width, (line + 1) * width)
        normed = (reduced[span, :] - one[0:1, :]) * one[1:2, :]
        inner = first_grad[span, :] - shift_mean - normed * gain_mean
        reduced_low[span, :] = (inner * factor).astype(low)
    reduce_data[:channels, :] = jnp.dot(
        features_turned[...], reduced_low[...], preferred_element_type=wide
    ).astype(low)
    reduce_sum.start_half()
    chunk = 2 * LANES

    def last(block, carry):
        span = pl.ds(pl.multiple_of(block * chunk, chunk), chunk)
        made = across(reduced_low[...], reduce_weight[span, :])
        features_grad[:, span] = (made + pre_grad[:, span].astype(wide)).astype(low)
        return carry

    lax.fori_loop(0, channels // chunk, last, 0)
    reduce_sum.start_level(0)
    dilated_sum.start_level(1)
    reduce_sum.start_level(1)
    dilated_sum.start_back(1)
    reduce_sum.start_back(1)
    dilated_sum.start_back(0)
    reduce_sum.start_back(0)
    dilated_sum.start_back_half()
    reduce_sum.start_back_half()
    for each in sums:
        each.finish()
    halo.drain()


def tail(height, dilated_low, first_act, dilated_weight, reduced, one, features, reduce_weight, pre_grad,
         expand_part):
    devices = lax.axis_size("rows") * lax.axis_size("cols")
    pixels, middle = dilated_low.shape
    channels = features.shape[1]
    width = pixels // height
    low, wide = jnp.bfloat16, jnp.float32
    shape = jax.ShapeDtypeStruct
    whole = pl.BlockSpec(memory_space=pltpu.VMEM)
    away = pl.BlockSpec(memory_space=pl.ANY)
    sems = pltpu.SemaphoreType.DMA
    per = middle // LANES
    expand_part = jnp.pad(
        expand_part, ((0, sum_rows(expand_part.shape[0]) - expand_part.shape[0]), (0, 0))
    )
    sizes = [sum_rows(expand_part.shape[0]), sum_rows(9 * middle), sum_rows(channels)]
    outs = (
        shape((pixels, channels), low),
        *[shape((size, middle), low) for size in sizes],
        shape((2 * per, LANES), wide),
    )
    scratch = [
        pltpu.VMEM((3, height, width + 2 * EDGE, middle), low),
        pltpu.VMEM((height, width + 2 * EDGE, middle), wide),
        pltpu.VMEM((pixels, middle), low),
        pltpu.VMEM((middle, pixels), low),
        pltpu.VMEM((channels, pixels), low),
        pltpu.VMEM((pixels, middle), wide),
        pltpu.VMEM((pixels, middle), low),
        *[pltpu.VMEM((size, middle), low) for size in sizes[1:]],
        pltpu.VMEM((devices, 2 * per, LANES), wide),
        sems((2, height)),
        sems((2, height)),
        sems((2, 3)),
        sems((2,)),
    ]
    for size, apart in zip(sizes, (True, False, False)):
        scratch += sums_scratch(size, middle, apart)
    return pl.pallas_call(
        functools.partial(tail_kernel),
        out_shape=outs,
        in_specs=[whole] * 8 + [away],
        out_specs=(whole, away, away, away, whole),
        scratch_shapes=scratch,
        compiler_params=pltpu.CompilerParams(
            collective_id=13, has_side_effects=True, vmem_limit_bytes=VMEM_BYTES + (3 << 20)
        ),
        cost_estimate=pl.CostEstimate(
            flops=400 * pixels * middle * middle, bytes_accessed=256 * pixels * channels, transcendentals=0
        ),
        name="tail",
    )(dilated_low, first_act, dilated_weight, reduced, one, features, reduce_weight, pre_grad, expand_part)


def widen_kernel(first, second, expand, dilated, reduce, sep_out, point_out, expand_out, dilated_out, reduce_out):
    wide = jnp.float32
    aspp, middle = point_out.shape[1], expand.shape[2]
    sep_out[0] = first[:, :aspp].astype(wide)
    sep_out[1] = first[:, aspp:].astype(wide)
    sep_out[2] = second[:, :aspp].astype(wide)
    point_out[...] = second[:, aspp:].astype(wide)
    for block in range(expand.shape[0]):
        expand_out[:, block * middle : (block + 1) * middle] = expand[block].astype(wide)
    dilated_out[...] = dilated[...].astype(wide)
    reduce_out[...] = reduce[...].astype(wide)


def widen(early, expand, dilated, reduce, channels, aspp):
    middle = reduce.shape[1]
    wide = jnp.float32
    steps = 8
    rows = channels // steps
    taps = 9 * middle // steps
    lines = middle // steps
    blocks = channels // middle
    shape = jax.ShapeDtypeStruct
    return pl.pallas_call(
        widen_kernel,
        grid=(steps,),
        out_shape=(
            shape((3, channels, aspp), wide),
            shape((channels, aspp), wide),
            shape((middle, channels), wide),
            shape((9 * middle, middle), wide),
            shape((channels, middle), wide),
        ),
        in_specs=[
            pl.BlockSpec((rows, 2 * aspp), lambda step: (step, 0)),
            pl.BlockSpec((rows, 2 * aspp), lambda step: (steps + step, 0)),
            pl.BlockSpec((blocks, lines, middle), lambda step: (0, step, 0)),
            pl.BlockSpec((taps, middle), lambda step: (step, 0)),
            pl.BlockSpec((rows, middle), lambda step: (step, 0)),
        ],
        out_specs=(
            pl.BlockSpec((3, rows, aspp), lambda step: (0, step, 0)),
            pl.BlockSpec((rows, aspp), lambda step: (step, 0)),
            pl.BlockSpec((lines, channels), lambda step: (step, 0)),
            pl.BlockSpec((taps, middle), lambda step: (step, 0)),
            pl.BlockSpec((rows, middle), lambda step: (step, 0)),
        ),
        compiler_params=pltpu.CompilerParams(vmem_limit_bytes=VMEM_BYTES),
        name="widen",
    )(early, early, expand[:channels].reshape(blocks, middle, middle), dilated, reduce)


def on_device(
    features,
    reduce_weight,
    dilated_weight,
    expand_weight,
    mid_gain,
    mid_shift,
    out_gain,
    out_shift,
    aspp_point,
    sep_depth,
    sep_point,
    pool_weight,
    proj_weight,
    aspp_gain,
    aspp_shift,
    head_weight,
    head_bias,
    task_scales,
    crop_ids,
    labels,
    boundary_mask,
    valid_mask,
    geometry_target,
):
    height, width, channels = features.shape
    pixels = height * width
    low = jnp.bfloat16
    aspp_width = proj_weight.shape[1]
    flat = features.reshape(pixels, channels)
    middle = reduce_weight.shape[1]

    (
        reduced, first_act, dilated, second_act, expanded, trunk, one, two, three, count_sums,
        local_sums, crop_part, members,
    ) = front(
        height,
        flat,
        reduce_weight,
        dilated_weight.reshape(3, 3 * middle, middle),
        expand_weight,
        pool_weight,
        mid_gain,
        mid_shift,
        out_gain.reshape(1, channels),
        out_shift.reshape(1, channels),
        crop_ids,
        boundary_mask,
        valid_mask,
    )
    crop_count = count_sums[0, :CROPS]
    lane = jnp.arange(LANES)
    scale_exp = jnp.exp(task_scales)
    task_of = jnp.where(lane < CLASSES, scale_exp[0], jnp.where(lane == CLASSES, scale_exp[1], scale_exp[2]))
    weights = jnp.stack(
        [jnp.where(lane > CLASSES, 2.0, 1.0) * task_of, task_of, jnp.pad(task_scales, (0, LANES - 3))]
    )
    outs = head_weight.shape[1]
    devices = lax.axis_size("rows") * lax.axis_size("cols")
    crop_rows = CROPS * channels // LANES
    piece = -(-crop_rows // devices)
    crop_sums = jnp.pad(local_sums, ((0, piece * devices - crop_rows), (0, 0)))
    crop_sums = jnp.pad(
        crop_sums.reshape(devices, piece, LANES), ((0, 0), (0, -piece % 8), (0, 0))
    )
    branch_low, proj_part, head_part, crop_local, crop_pre, sums_five, sums_four, crop_table, own_low, closing = pyramid(
        height,
        trunk,
        jnp.pad(sep_depth.reshape(27, channels).astype(jnp.float32), ((0, 5), (0, 0))),
        sep_point,
        aspp_point,
        crop_part,
        count_sums,
        members,
        proj_weight,
        aspp_gain,
        aspp_shift,
        head_weight,
        head_bias.reshape(1, outs),
        jnp.pad(weights, ((0, 5), (0, 0))),
        labels,
        boundary_mask,
        valid_mask,
        geometry_target,
        crop_sums,
    )
    crop_table = crop_table[:, :piece].reshape(-1, LANES)[:crop_rows].reshape(-1, CROPS, LANES)
    crop_table = jnp.transpose(crop_table, (1, 0, 2)).reshape(CROPS, channels)
    per = aspp_width // LANES
    proj_shift_grad = sums_five[:per].reshape(1, aspp_width)
    proj_gain_grad = sums_five[per : 2 * per].reshape(1, aspp_width)
    grad_head_bias = sums_five[2 * per + 1, :outs]
    branch_shift_grad = sums_four[: 4 * per].reshape(4, aspp_width)
    branch_gain_grad = sums_four[4 * per :].reshape(4, aspp_width)
    objective, grad_scales = closing[1, 0], closing[0, :3]
    near, early, crop_total = pyramid_weights(
        branch_low.reshape(4, height, width, aspp_width),
        trunk,
        jnp.pad(sep_depth.reshape(27, channels).astype(jnp.float32).T, ((0, 0), (0, LANES - 27))),
        sep_point,
        crop_local,
        proj_part,
        head_part,
    )
    crop_low = (crop_total * gate_slope(crop_pre)).astype(low)
    pooled = (crop_table / crop_count[:, None]).astype(low)
    grad_pool_weight = jnp.einsum("kc,kd->cd", pooled, crop_low, preferred_element_type=jnp.float32)
    pooled_grad = (
        jnp.einsum("kd,cd->kc", crop_low, pool_weight, preferred_element_type=jnp.float32)
        / crop_count[:, None]
    )
    pooled_grad = jnp.pad(pooled_grad, ((0, LANES - CROPS), (0, 0)))
    crop_high = pooled_grad.astype(low)
    crop_rest = (pooled_grad - crop_high.astype(jnp.float32)).astype(low)
    pre_low, expand_part, dilated_low, sums_three, sums_two, early_sum = trunk_back(
        near,
        own_low,
        jnp.pad(sep_depth.reshape(27, channels).astype(jnp.float32).T, ((0, 0), (0, LANES - 27))),
        sep_point,
        aspp_point,
        members,
        crop_high,
        crop_rest,
        expanded,
        flat,
        three,
        dilated,
        two,
        second_act,
        expand_weight,
        early,
    )
    folded = sums_three.reshape(-1, 2 * per, LANES)
    out_shift_grad = folded[:, :per].reshape(1, channels)
    out_gain_grad = folded[:, per:].reshape(1, channels)
    two_shift_grad, two_gain_grad = sums_two.reshape(2, 1, middle)
    grad_features, expand_sum, dilated_sum, reduce_sum, sums_one = tail(
        height,
        dilated_low,
        first_act,
        dilated_weight,
        reduced,
        one,
        flat,
        reduce_weight,
        pre_low,
        expand_part,
    )
    one_shift_grad, one_gain_grad = sums_one.reshape(2, 1, middle)
    grad_features = grad_features.reshape(height, width, channels)
    sep_sum, point_sum, grad_expand_weight, dilated_wide, reduce_wide = widen(
        early_sum, expand_sum, dilated_sum, reduce_sum, channels, aspp_width
    )
    at = 2 * channels
    tables = []
    for size, extent in ((proj_weight.shape[0], aspp_width), (channels, LANES), (aspp_width, LANES)):
        blocks = 2 * aspp_width // extent
        table = early_sum[at : at + size // blocks].reshape(size // blocks, blocks, extent)
        table = table.astype(jnp.float32)
        tables.append(jnp.transpose(table, (1, 0, 2)).reshape(size, extent))
        at += size // blocks
    summed = [
        reduce_wide,
        dilated_wide.reshape(9, middle, middle),
        grad_expand_weight,
        point_sum,
        tables[1][:, :27].T.reshape(3, 9, channels),
        sep_sum,
        tables[0],
        tables[2],
    ]
    grad_mid_gain = jnp.concatenate([one_gain_grad, two_gain_grad], axis=0)
    grad_mid_shift = jnp.concatenate([one_shift_grad, two_shift_grad], axis=0)
    grad_aspp_gain = jnp.concatenate([branch_gain_grad, proj_gain_grad], axis=0)
    grad_aspp_shift = jnp.concatenate([branch_shift_grad, proj_shift_grad], axis=0)
    return (
        objective,
        grad_features,
        summed[0],
        summed[1],
        summed[2],
        grad_mid_gain,
        grad_mid_shift,
        out_gain_grad[0],
        out_shift_grad[0],
        summed[3],
        summed[4],
        summed[5],
        grad_pool_weight,
        summed[6],
        grad_aspp_gain,
        grad_aspp_shift,
        summed[7][:, : head_weight.shape[1]],
        grad_head_bias,
        grad_scales,
    )


def solution(mesh):
    in_specs = (
        P("rows", "cols", None),
        P(),
        P(),
        P(),
        P(),
        P(),
        P(),
        P(),
        P(),
        P(),
        P(),
        P(),
        P(),
        P(),
        P(),
        P(),
        P(),
        P(),
        P("rows", "cols"),
        P("rows", "cols"),
        P("rows", "cols"),
        P("rows", "cols"),
        P(None, "rows", "cols"),
    )
    out_specs = (
        P(),
        P("rows", "cols", None),
        P(),
        P(),
        P(),
        P(),
        P(),
        P(),
        P(),
        P(),
        P(),
        P(),
        P(),
        P(),
        P(),
        P(),
        P(),
        P(),
        P(),
    )
    return jax.shard_map(
        on_device, mesh=mesh, in_specs=in_specs, out_specs=out_specs, check_vma=False
    )
```

```python
import functools

import jax
import jax.numpy as jnp
from jax import lax
from jax.experimental import pallas as pl
from jax.experimental.pallas import tpu as pltpu
from jax.sharding import PartitionSpec as P

CLASSES = 13
CROPS = 16
MID_RATE = 4
BASE_RATE = 12
LANES = 128

EPS = 1e-05
MESH = pl.DeviceIdType.MESH


def gate_slope(value):
    sigma = jax.nn.sigmoid(value)
    return sigma * (1.0 + value * (1.0 - sigma))


PAD = 48
VMEM_BYTES = 60 * 1024 * 1024


def place():
    rows, cols = lax.axis_size("rows"), lax.axis_size("cols")
    row, col = lax.axis_index("rows"), lax.axis_index("cols")
    return rows, cols, row, col, row * cols + col


def greet_all():
    rows, cols, row, col, me = place()
    barrier = pltpu.get_barrier_semaphore()

    def greet(step, carry):
        other = lax.rem(me + step, rows * cols)
        pl.semaphore_signal(
            barrier, inc=1, device_id=(other // cols, lax.rem(other, cols)), device_id_type=MESH
        )
        return carry

    lax.fori_loop(1, rows * cols, greet, 0)


def await_all():
    rows, cols = lax.axis_size("rows"), lax.axis_size("cols")
    pl.semaphore_wait(pltpu.get_barrier_semaphore(), rows * cols - 1)


def share(slots, sems):
    rows, cols, row, col, me = place()

    def go(step, carry):
        other = lax.rem(me + step, rows * cols)
        pltpu.make_async_remote_copy(
            slots.at[me],
            slots.at[me],
            sems.at[0],
            sems.at[1],
            device_id=(other // cols, lax.rem(other, cols)),
            device_id_type=MESH,
        ).start()
        return carry

    lax.fori_loop(1, rows * cols, go, 0)


def shared(slots, sems):
    rows, cols, row, col, me = place()
    others = slots.at[pl.ds(0, rows * cols - 1)]
    pltpu.make_async_remote_copy(
        others,
        others,
        sems.at[0],
        sems.at[1],
        device_id=(row, lax.rem(col + 1, cols)),
        device_id_type=MESH,
    ).wait()


def share_column(slots, sems):
    rows, cols, row, col, me = place()

    def go(step, carry):
        other = lax.rem(row + step, rows)
        pltpu.make_async_remote_copy(
            slots.at[row],
            slots.at[row],
            sems.at[0],
            sems.at[1],
            device_id=(other, col),
            device_id_type=MESH,
        ).start()
        return carry

    lax.fori_loop(1, rows, go, 0)


def shared_column(slots, sems):
    rows, cols, row, col, me = place()
    others = slots.at[pl.ds(0, rows - 1)]
    pltpu.make_async_remote_copy(
        others,
        others,
        sems.at[0],
        sems.at[1],
        device_id=(lax.rem(row + 1, rows), col),
        device_id_type=MESH,
    ).wait()


class PairSum:
    def __init__(self, own, pair, slots, all_, sems):
        self.own, self.pair, self.slots, self.all_, self.sems = own, pair, slots, all_, sems
        self.rows, self.cols, self.row, self.col, _ = place()

    def to_pair(self, src, dst, at):
        return pltpu.make_async_remote_copy(
            src,
            dst,
            self.sems.at[at, 0],
            self.sems.at[at, 1],
            device_id=(self.row, 1 - self.col),
            device_id_type=MESH,
        )

    def out_copy(self):
        return self.to_pair(self.own.at[1 - self.col], self.pair, 0)

    def back_copy(self):
        return self.to_pair(self.all_.at[self.col], self.all_.at[self.col], 2)

    def put(self, value):
        self.own[0] = value[:, :LANES]
        self.own[1] = value[:, LANES:]

    def start(self):
        self.out_copy().start()

    def start_column(self):
        self.out_copy().wait()
        self.slots[self.row] = self.own[self.col] + self.pair[...]
        share_column(self.slots, self.sems.at[1])

    def start_back(self):
        shared_column(self.slots, self.sems.at[1])
        self.all_[self.col] = jnp.sum(self.slots[...], axis=0)
        self.back_copy().start()

    def finish(self):
        self.back_copy().wait()
        return jnp.concatenate([self.all_[0], self.all_[1]], axis=1)


def pair_sum_scratch(count):
    wide = jnp.float32
    return [
        pltpu.VMEM((2, count, LANES), wide),
        pltpu.VMEM((count, LANES), wide),
        pltpu.VMEM((lax.axis_size("rows"), count, LANES), wide),
        pltpu.VMEM((2, count, LANES), wide),
        pltpu.SemaphoreType.DMA((3, 2)),
    ]


def put_row(slots, me, at, vector):
    for part in range(vector.shape[1] // LANES):
        slots[me, at + part : at + part + 1, :] = vector[:, part * LANES : (part + 1) * LANES]


def take_row(table, at, width):
    parts = [table[at + part : at + part + 1, :] for part in range(width // LANES)]
    return parts[0] if len(parts) == 1 else jnp.concatenate(parts, axis=1)


def merged(slots, half, share_size, count):
    center = jnp.mean(slots[:, :half, :], axis=0)
    apart = slots[:, :half, :] - center[None]
    spread = jnp.sum(slots[:, half : 2 * half, :], axis=0) + share_size * jnp.sum(apart * apart, axis=0)
    return center, lax.rsqrt(spread / count + EPS)


def sigmoid(value):
    return 1.0 / (1.0 + jnp.exp(-value))


def across(left, right):
    return lax.dot_general(left, right, (((1,), (1,)), ((), ())), preferred_element_type=jnp.float32)


def down(left, right):
    return lax.dot_general(left, right, (((0,), (0,)), ((), ())), preferred_element_type=jnp.float32)


def pyramid_kernel(
    height,
    trunk,
    depth,
    sep_point,
    aspp_point,
    crop_part,
    count_sums,
    members,
    proj_weight,
    gains,
    shifts,
    head_raw,
    bias_raw,
    weights,
    labels,
    boundary,
    valid_mask,
    geometry,
    crop_sums,
    branch_low,
    proj_part,
    head_part,
    crop_local,
    crop_pre,
    sums_five,
    sums_four,
    crop_table,
    own_low,
    closing,
    head_weight,
    head_bias,
    field,
    send_main,
    recv_main,
    send_side,
    recv_side,
    pre,
    joined,
    crop_act,
    projected,
    united,
    head_low,
    upstream,
    proj_low,
    branch_up,
    four_slots,
    five_slots,
    back_five,
    back_four,
    crop_pieces,
    main_sems,
    side_sems,
    four_sems,
    five_sems,
    back_five_sems,
    back_four_sems,
    piece_sems,
    table_sems,
    *crop_refs,
):
    rows, cols, row, col, me = place()
    low, wide = jnp.bfloat16, jnp.float32
    pixels = trunk.shape[0]
    width = pixels // height
    share_size = float(pixels)
    count = float(pixels * rows * cols)
    aspp = sep_point.shape[2]
    greet_all()

    def exists(target):
        return jnp.logical_and(target >= 0, target < rows)

    def step_of(index):
        return (BASE_RATE // height) * (index + 1)

    for index in range(3):
        step = BASE_RATE * (index + 1) // height
        for way in (0, 2):

            @pl.when(jnp.logical_not(exists(row - (1 - way) * step)))
            def _():
                recv_main[index, way] = jnp.zeros(recv_main.shape[2:], low)

    half = crop_part.shape[0]
    crop_total = PairSum(*crop_refs)
    crop_total.put(crop_part[...])
    pre[0] = jnp.dot(trunk[...], aspp_point[...], preferred_element_type=wide)
    await_all()
    crop_total.start()
    crop_pieces[me] = crop_sums[me]

    def scatter(step, carry):
        other = lax.rem(me + step, rows * cols)
        pltpu.make_async_remote_copy(
            crop_sums.at[other],
            crop_pieces.at[me],
            piece_sems.at[0],
            piece_sems.at[1],
            device_id=(other // cols, lax.rem(other, cols)),
            device_id_type=MESH,
        ).start()
        return carry

    lax.fori_loop(1, rows * cols, scatter, 0)
    side_from = pl.multiple_of((1 - col) * (PAD + width), 16)
    side_to = pl.multiple_of((1 - col) * (width - PAD), 16)

    def main_copy(index, way):
        return pltpu.make_async_remote_copy(
            send_main.at[index, way],
            recv_main.at[index, way],
            main_sems.at[0, index, way],
            main_sems.at[1, index, way],
            device_id=(row + (1 - way) * step_of(index), col),
            device_id_type=MESH,
        )

    def side_copy(index, way):
        return pltpu.make_async_remote_copy(
            send_side.at[index, way],
            recv_side.at[index, way],
            side_sems.at[0, index, way],
            side_sems.at[1, index, way],
            device_id=(row, 1 - col),
            device_id_type=MESH,
        )

    def flush(number):
        own = number // 6
        index = (1 - own) * (2 - number // 2) + own * (8 - number)
        way = (1 - own) * 2 * lax.rem(number, 2) + own
        side_copy(index, way).wait_recv()

        @pl.when(way == 1)
        def _():
            for line in range(height):
                edge = pl.ds(pl.multiple_of(line * width + side_to, 16), PAD)
                pre[index + 1, edge, :] += recv_side[index, way, line].astype(wide)

        @pl.when(way != 1)
        def _():
            edge = pl.ds(side_to, PAD)
            send_main[index, way, :, edge, :] = (
                send_main[index, way, :, edge, :].astype(wide) + recv_side[index, way].astype(wide)
            ).astype(low)

            @pl.when(exists(row + (1 - way) * step_of(index)))
            def _():
                main_copy(index, way).start()

    for index, own in ((2, 0), (1, 0), (0, 0), (2, 1), (1, 1), (0, 1)):
        rate = BASE_RATE * (index + 1)

        def one_way(turn, carry):
            way = 1 if own else 2 * turn
            for sign in (0, 1, -1):
                tap = depth[pl.ds(index * 9 + 3 * way + 1 - sign, 1), :].astype(low)
                made = jnp.dot(trunk[...] * tap, sep_point[index], preferred_element_type=wide)
                for line in range(height):
                    part = made[line * width : (line + 1) * width, :]
                    if sign == 0:
                        field[line, PAD : PAD + width, :] = part
                        field[line, :PAD, :] = jnp.zeros((PAD, aspp), wide)
                        field[line, PAD + width :, :] = jnp.zeros((PAD, aspp), wide)
                    else:
                        at = PAD + sign * rate
                        field[line, at : at + width, :] += part
            send_side[index, way] = field[:, pl.ds(side_from, PAD), :].astype(low)

            if own:
                for line in range(height):
                    pre[index + 1, line * width : (line + 1) * width, :] = field[
                        line, PAD : PAD + width, :
                    ]
            else:
                send_main[index, way] = field[:, PAD : PAD + width, :].astype(low)
            side_copy(index, way).start()
            number = turn + (8 - index if own else 2 * (2 - index))

            @pl.when(number > 0)
            def _():
                flush(number - 1)

            return carry

        lax.fori_loop(0, 1 if own else 2, one_way, 0)
    flush(jnp.int32(8))
    crop_total.start_column()

    def lines(body, carry=0):
        def run(line, carry):
            return body(line, pl.ds(pl.multiple_of(line * width, width), width), carry)

        return lax.fori_loop(0, height, run, carry)

    zero_row = jnp.zeros((1, aspp), wide)

    def statistics(value_of, slots, at, half_rows):
        total = lines(
            lambda line, span, acc: acc + jnp.sum(value_of(span), axis=0, keepdims=True), zero_row
        )
        mean = total / share_size

        def squares(line, span, acc):
            apart = value_of(span) - mean
            return acc + jnp.sum(apart * apart, axis=0, keepdims=True)

        put_row(slots, me, at, mean)
        put_row(slots, me, half_rows + at, lines(squares, zero_row))

    per = aspp // LANES
    statistics(lambda span: pre[0, span, :], four_slots, 0, 4 * per)
    for index in (2, 1, 0):
        for way in (0, 2):

            @pl.when(exists(row - (1 - way) * step_of(index)))
            def _():
                main_copy(index, way).wait_recv()

        def assemble(line, span, carry):
            pre[index + 1, span, :] += recv_main[index, 0, line].astype(wide) + recv_main[
                index, 2, line
            ].astype(wide)
            return carry

        lines(assemble)
        statistics(lambda span: pre[index + 1, span, :], four_slots, per * (index + 1), 4 * per)
    share(four_slots, four_sems)
    crop_total.start_back()
    shared(crop_pieces, piece_sems)
    crop_table[me] = jnp.sum(crop_pieces[...], axis=0)
    share(crop_table, table_sems)
    crop_row = lax.broadcasted_iota(jnp.int32, (half, LANES), 0)
    crop_lane = lax.broadcasted_iota(jnp.int32, (half, LANES), 1)
    crop_count = jnp.sum(
        jnp.where(crop_row == crop_lane, count_sums[0:1, :], 0.0), axis=1, keepdims=True
    )
    crop_value = crop_total.finish() / crop_count
    crop_pre[...] = crop_value
    crop_act[...] = jnp.zeros(crop_act.shape, low)
    crop_act[:half, :] = (crop_value * sigmoid(crop_value)).astype(low)

    def spread(line, span, carry):
        joined[span, 4 * aspp :] = jnp.dot(
            members[span, :], crop_act[...], preferred_element_type=wide
        ).astype(low)
        return carry

    lines(spread)
    shared(four_slots, four_sems)
    center_four, scale_four = merged(four_slots, 4 * per, share_size, count)
    centers = [take_row(center_four, per * part, aspp) for part in range(4)]
    scales = [take_row(scale_four, per * part, aspp) for part in range(4)]

    def activate(line, span, carry):
        for part in range(4):
            normed = (pre[part, span, :] - centers[part]) * scales[part]
            gated = normed * gains[part : part + 1, :] + shifts[part : part + 1, :]
            joined[span, part * aspp : (part + 1) * aspp] = (gated * sigmoid(gated)).astype(low)
        return carry

    lines(activate)
    projected[...] = jnp.dot(joined[...], proj_weight[...], preferred_element_type=wide)
    five_slots[me] = jnp.zeros(five_slots.shape[1:], wide)
    statistics(lambda span: projected[span, :], five_slots, 0, per)
    share(five_slots, five_sems)
    shared(five_slots, five_sems)
    center_five, scale_five = merged(five_slots, per, share_size, count)
    center_five, scale_five = take_row(center_five, 0, aspp), take_row(scale_five, 0, aspp)
    gain_five, shift_five = gains[4:5, :], shifts[4:5, :]
    lane = lax.broadcasted_iota(jnp.int32, (width, LANES), 1)
    outs = head_raw.shape[1]
    head_weight[...] = jnp.zeros(head_weight.shape, low)
    head_weight[:, :outs] = head_raw[...]
    head_bias[...] = jnp.zeros(head_bias.shape, wide)
    head_bias[0:1, :outs] = bias_raw[...]
    one_lane = lax.broadcasted_iota(jnp.int32, (1, LANES), 1)
    pixel_count = jnp.where(
        one_lane < CLASSES, count_sums[0:1, CROPS : CROPS + 1], count_sums[0:1, CROPS + 1 : CROPS + 2]
    )
    factors = weights[0:1, :] / pixel_count

    def heads_of(line, span, carry):
        losses, bias_sum, shift_sum, gain_sum = carry
        normed = (projected[span, :] - center_five) * scale_five
        gated = normed * gain_five + shift_five
        sigma = sigmoid(gated)
        act = (gated * sigma).astype(low)
        united[span, :] = act
        heads = jnp.dot(act, head_weight[...], preferred_element_type=wide) + head_bias[0:1, :]
        row_of = pl.ds(line, 1)
        facts = jnp.concatenate(
            [
                labels[row_of, :].astype(wide),
                1.0 - boundary[row_of, :].astype(wide),
                valid_mask[row_of, :].astype(wide),
                *[geometry[part, row_of, :] for part in range(4)],
                jnp.zeros((1, width), wide),
            ],
            axis=0,
        ).T
        label, keep, valid = facts[:, 0:1], facts[:, 1:2], facts[:, 2:3]
        is_class = lane < CLASSES
        hot = jnp.where(lane.astype(wide) == label, 1.0, 0.0)
        target = jnp.zeros((width, LANES), wide)
        for part in range(4):
            target = jnp.where(lane == CLASSES + part, facts[:, 3 + part : 4 + part], target)
        top = jnp.max(jnp.where(is_class, heads, -jnp.inf), axis=1, keepdims=True)
        exps = jnp.where(is_class, jnp.exp(heads - top), 0.0)
        totals = jnp.sum(exps, axis=1, keepdims=True)
        picked = jnp.sum(jnp.where(is_class, heads, 0.0) * hot, axis=1, keepdims=True)
        error = jnp.where(is_class, 0.0, heads - target)
        root = jnp.sqrt(error * error + 1.0)
        is_depth, is_normal = lane == CLASSES, jnp.logical_and(lane > CLASSES, lane < CLASSES + 4)
        semantic = keep * (top + jnp.log(totals) - picked)
        terms = jnp.where(lane == 0, semantic, 0.0)
        terms = jnp.where(is_depth, valid * (root - 1.0), terms)
        terms = jnp.where(is_normal, valid * error * error, terms)
        grad = jnp.where(is_class, keep * (exps / totals - hot), 0.0)
        grad = jnp.where(is_depth, valid * error / root, grad)
        grad = jnp.where(is_normal, valid * error, grad)
        grad = grad * factors
        grad_low = grad.astype(low)
        head_low[span, :] = grad_low
        up = across(grad_low, head_weight[...]) * (sigma * (1.0 + gated * (1.0 - sigma)))
        upstream[span, :] = up
        return (
            losses + jnp.sum(terms, axis=0, keepdims=True),
            bias_sum + jnp.sum(grad, axis=0, keepdims=True),
            shift_sum + jnp.sum(up, axis=0, keepdims=True),
            gain_sum + jnp.sum(up * normed, axis=0, keepdims=True),
        )

    zero_lane = jnp.zeros((1, LANES), wide)
    losses, bias_sum, shift_sum, gain_sum = lines(
        heads_of, (zero_lane, zero_lane, zero_row, zero_row)
    )
    back_five[me] = jnp.zeros(back_five.shape[1:], wide)
    put_row(back_five, me, 0, shift_sum)
    put_row(back_five, me, per, gain_sum)
    put_row(back_five, me, 2 * per, losses)
    put_row(back_five, me, 2 * per + 1, bias_sum)
    share(back_five, back_five_sems)
    head_part[...] = down(united[...], head_low[...]).astype(low)
    shared(back_five, back_five_sems)
    total_five = jnp.sum(back_five[...], axis=0)
    sums_five[...] = total_five
    weighted = weights[1:2, :] * total_five[2 * per : 2 * per + 1, :] / pixel_count

    def lanes_sum(row_value, first, last):
        picked = jnp.where(jnp.logical_and(one_lane >= first, one_lane < last), row_value, 0.0)
        return jnp.sum(picked, axis=1, keepdims=True)

    tasks = (
        lanes_sum(weighted, 0, 1),
        lanes_sum(weighted, CLASSES, CLASSES + 1),
        lanes_sum(weighted, CLASSES + 1, CLASSES + 4),
    )
    closing[...] = jnp.zeros(closing.shape, wide)
    for part in range(3):
        closing[0:1, part : part + 1] = tasks[part] - 1.0
    closing[1:2, 0:1] = tasks[0] + tasks[1] + tasks[2] - lanes_sum(weights[2:3, :], 0, 3)
    shift_mean = take_row(total_five, 0, aspp) / count
    gain_mean = take_row(total_five, per, aspp) / count

    def project_back(line, span, carry):
        normed = (projected[span, :] - center_five) * scale_five
        inner = upstream[span, :] - shift_mean - normed * gain_mean
        proj_low[span, :] = (inner * (gain_five * scale_five)).astype(low)
        return carry

    lines(project_back)
    for part in range(4):
        branch_up[part] = across(
            proj_low[...], proj_weight[part * aspp : (part + 1) * aspp, :]
        )
    crop_up = across(proj_low[...], proj_weight[4 * aspp :, :])
    crop_high = crop_up.astype(low)
    crop_rest = (crop_up - crop_high.astype(wide)).astype(low)
    crop_sum = down(members[...], crop_high) + down(members[...], crop_rest)
    crop_local[...] = crop_sum[:half, :]

    for part in range(4):

        def branch_sums(line, span, carry):
            shift_sum, gain_sum = carry
            normed = (pre[part, span, :] - centers[part]) * scales[part]
            gated = normed * gains[part : part + 1, :] + shifts[part : part + 1, :]
            sigma = sigmoid(gated)
            up = branch_up[part, span, :] * (sigma * (1.0 + gated * (1.0 - sigma)))
            branch_up[part, span, :] = up
            return (
                shift_sum + jnp.sum(up, axis=0, keepdims=True),
                gain_sum + jnp.sum(up * normed, axis=0, keepdims=True),
            )

        shift_sum, gain_sum = lines(branch_sums, (zero_row, zero_row))
        put_row(back_four, me, per * part, shift_sum)
        put_row(back_four, me, per * (4 + part), gain_sum)
    share(back_four, back_four_sems)
    proj_part[...] = down(joined[...], proj_low[...]).astype(low)
    shared(back_four, back_four_sems)
    total_four = jnp.sum(back_four[...], axis=0)
    sums_four[...] = total_four
    for part in range(4):
        shift_mean = take_row(total_four, per * part, aspp) / count
        gain_mean = take_row(total_four, per * (4 + part), aspp) / count
        factor = gains[part : part + 1, :] * scales[part]

        def branch_back(line, span, carry):
            normed = (pre[part, span, :] - centers[part]) * scales[part]
            inner = branch_up[part, span, :] - shift_mean - normed * gain_mean
            value = (inner * factor).astype(low)
            branch_low[part, span, :] = value
            if part == 0:
                own_low[span, :] = value
            return carry

        lines(branch_back)
    shared(crop_table, table_sems)
    for index in range(3):
        for way in range(3):
            side_copy(index, way).wait_send()
        for way in (0, 2):

            @pl.when(exists(row + (1 - way) * step_of(index)))
            def _():
                main_copy(index, way).wait_send()


def pyramid(height, trunk, depth, sep_point, aspp_point, crop_part, count_sums, members, proj_weight,
            gains, shifts, head_weight, head_bias, weights, labels, boundary, valid, geometry, crop_sums):
    devices = lax.axis_size("rows") * lax.axis_size("cols")
    pixels = trunk.shape[0]
    width = pixels // height
    aspp = sep_point.shape[2]
    crops = crop_part.shape[0]
    low, wide = jnp.bfloat16, jnp.float32
    shape = jax.ShapeDtypeStruct
    whole = pl.BlockSpec(memory_space=pltpu.VMEM)
    joined = proj_weight.shape[0]
    per = aspp // LANES
    outs = (
        shape((4, pixels, aspp), low),
        shape((joined, aspp), low),
        shape((aspp, LANES), low),
        shape((crops, aspp), wide),
        shape((crops, aspp), wide),
        shape((8, LANES), wide),
        shape((8 * per, LANES), wide),
        shape(crop_sums.shape, wide),
        shape((pixels, aspp), low),
        shape((8, LANES), wide),
    )
    sems = pltpu.SemaphoreType.DMA
    return pl.pallas_call(
        functools.partial(pyramid_kernel, height),
        out_shape=outs,
        in_specs=[whole] * 18,
        out_specs=(whole,) * len(outs),
        scratch_shapes=[
            pltpu.VMEM((aspp, LANES), low),
            pltpu.VMEM((8, LANES), wide),
            pltpu.VMEM((height, width + 2 * PAD, aspp), wide),
            pltpu.VMEM((3, 3, height, width, aspp), low),
            pltpu.VMEM((3, 3, height, width, aspp), low),
            pltpu.VMEM((3, 3, height, PAD, aspp), low),
            pltpu.VMEM((3, 3, height, PAD, aspp), low),
            pltpu.VMEM((4, pixels, aspp), wide),
            pltpu.VMEM((pixels, joined), low),
            pltpu.VMEM((LANES, aspp), low),
            pltpu.VMEM((pixels, aspp), wide),
            pltpu.VMEM((pixels, aspp), low),
            pltpu.VMEM((pixels, LANES), low),
            pltpu.VMEM((pixels, aspp), wide),
            pltpu.VMEM((pixels, aspp), low),
            pltpu.VMEM((4, pixels, aspp), wide),
            pltpu.VMEM((devices, 8 * per, LANES), wide),
            pltpu.VMEM((devices, 8, LANES), wide),
            pltpu.VMEM((devices, 8, LANES), wide),
            pltpu.VMEM((devices, 8 * per, LANES), wide),
            pltpu.VMEM(crop_sums.shape, wide),
            sems((2, 3, 3)),
            sems((2, 3, 3)),
            sems((2,)),
            sems((2,)),
            sems((2,)),
            sems((2,)),
            sems((2,)),
            sems((2,)),
            *pair_sum_scratch(crops),
        ],
        compiler_params=pltpu.CompilerParams(
            collective_id=10, has_side_effects=True, vmem_limit_bytes=VMEM_BYTES
        ),
        cost_estimate=pl.CostEstimate(
            flops=100 * pixels * trunk.shape[1] * aspp, bytes_accessed=64 * pixels * trunk.shape[1], transcendentals=0
        ),
        name="pyramid",
    )(trunk, depth, sep_point, aspp_point, crop_part, count_sums, members, proj_weight, gains, shifts,
      head_weight, head_bias, weights, labels, boundary, valid, geometry, crop_sums)


def pyramid_weights_kernel(
    branch_low,
    trunk,
    depth,
    sep_point,
    crop_local,
    proj_part,
    head_part,
    near,
    early,
    crop_total,
    depth_part,
    turned,
    shifted,
    moved,
    gathered,
    main_sems,
    edge_sems,
    *crop_refs,
):
    rows, cols, row, col, me = place()
    low, wide = jnp.bfloat16, jnp.float32
    height, width, aspp = branch_low.shape[1:]
    pixels, channels = trunk.shape
    crop_sum = PairSum(*crop_refs)
    crop_sum.put(crop_local[...])
    greet_all()

    def exists(target):
        return jnp.logical_and(target >= 0, target < rows)

    def step_of(index):
        return BASE_RATE * (index + 1) // height

    edge_from = pl.multiple_of(PAD + (1 - col) * (width - PAD), 16)
    edge_to = pl.multiple_of(col * (width + PAD), 16)
    blank = pl.multiple_of(col * (width + PAD), 16)

    def main_copy(index, way):
        return pltpu.make_async_remote_copy(
            branch_low.at[index + 1],
            near.at[index, way, :, pl.ds(PAD, width), :],
            main_sems.at[0, index, way],
            main_sems.at[1, index, way],
            device_id=(row + (1 - way) * step_of(index), col),
            device_id_type=MESH,
        )

    def edge_copy(index, way):
        return pltpu.make_async_remote_copy(
            near.at[index, way, :, pl.ds(edge_from, PAD), :],
            near.at[index, way, :, pl.ds(edge_to, PAD), :],
            edge_sems.at[0, index, way],
            edge_sems.at[1, index, way],
            device_id=(row, 1 - col),
            device_id_type=MESH,
        )

    for index in range(3):
        for way in range(3):
            near[index, way, :, pl.ds(blank, PAD), :] = jnp.zeros((height, PAD, aspp), low)
            if way == 1:
                near[index, way, :, PAD : PAD + width, :] = branch_low[index + 1]
            else:

                @pl.when(jnp.logical_not(exists(row - (1 - way) * step_of(index))))
                def _():
                    near[index, way] = jnp.zeros(near.shape[2:], low)

    await_all()
    for index in range(3):
        edge_copy(index, 1).start()

    def send(index):
        for way in (0, 2):

            @pl.when(exists(row + (1 - way) * step_of(index)))
            def _():
                main_copy(index, way).start()

    send(0)
    crop_sum.start()

    def turn(block, carry):
        span = pl.ds(pl.multiple_of(block * width, width), width)
        for line in range(height):
            turned[span, line * width : (line + 1) * width] = trunk[
                line * width : (line + 1) * width, span
            ].T
        return carry

    lax.fori_loop(0, channels // width, turn, 0)
    part_rows = channels // 2

    def point(part, carry):
        span = pl.ds(pl.multiple_of(part * part_rows, part_rows), part_rows)
        own = branch_low[0].reshape(pixels, aspp)
        early[pl.ds(pl.multiple_of(channels + part * part_rows, part_rows), part_rows), aspp:] = jnp.dot(
            turned[span, :], own, preferred_element_type=wide
        ).astype(low)
        return carry

    lax.fori_loop(0, 2, point, 0)
    lane = lax.broadcasted_iota(jnp.int32, (part_rows, LANES), 1)
    depth_part[...] = jnp.zeros(depth_part.shape, wide)
    gathered[...] = jnp.zeros(gathered.shape, wide)
    for index, way in ((0, 1), (1, 1), (2, 1), (0, 0), (0, 2), (1, 0), (1, 2), (2, 0), (2, 2)):
        rate = BASE_RATE * (index + 1)

        if way != 1:

            @pl.when(exists(row - (1 - way) * step_of(index)))
            def _():
                main_copy(index, way).wait_recv()
                edge_copy(index, way).start()

        for side in (1, 0, 2):
            if side == 0:

                @pl.when(exists(row - (1 - way) * step_of(index)))
                def _():
                    edge_copy(index, way).wait_recv()

                shifted[...] = near[index, way].astype(wide)
            tap = 3 * (2 - way) + side
            at = PAD - (side - 1) * rate
            for line in range(height):
                if side == 1:
                    piece = near[index, way, line, PAD : PAD + width, :]
                else:
                    piece = shifted[line, at : at + width, :].astype(low)
                moved[line * width : (line + 1) * width, :] = piece
            order = 9 * index + tap

            def collect(part, carry):
                span = pl.ds(pl.multiple_of(part * part_rows, part_rows), part_rows)
                made = jnp.dot(turned[span, :], moved[...], preferred_element_type=wide)
                gathered[index, span, :] += made * depth[span, order : order + 1]
                total = jnp.sum(made * sep_point[index, span, :].astype(wide), axis=1, keepdims=True)
                depth_part[span, :] = jnp.where(lane == order, total, depth_part[span, :])
                return carry

            lax.fori_loop(0, 2, collect, 0)
        if way == 1 and index == 2:
            send(1)
        if way == 2 and index == 0:
            send(2)
        if way == 1 and index == 0:
            crop_sum.start_column()
        if way == 0 and index == 0:
            crop_sum.start_back()
    early[:channels, :aspp] = gathered[0].astype(low)
    early[:channels, aspp:] = gathered[1].astype(low)
    early[channels : 2 * channels, :aspp] = gathered[2].astype(low)
    at = 2 * channels
    for table in (proj_part, depth_part, head_part):
        extent = table.shape[1]
        blocks = 2 * aspp // extent
        size = table.shape[0] // blocks
        for block in range(blocks):
            early[at : at + size, block * extent : (block + 1) * extent] = table[
                block * size : (block + 1) * size, :
            ].astype(low)
        at += size
    if early.shape[0] > at:
        early[at:, :] = jnp.zeros((early.shape[0] - at, 2 * aspp), low)
    crop_total[...] = crop_sum.finish()
    for index in range(3):
        for way in range(3):

            @pl.when(exists(row - (1 - way) * step_of(index)))
            def _():
                edge_copy(index, way).wait_send()

            if way != 1:

                @pl.when(exists(row + (1 - way) * step_of(index)))
                def _():
                    main_copy(index, way).wait_send()


def early_rows(channels, proj_part, head_part):
    rows = 2 * channels
    for size, extent in ((proj_part.shape[0], proj_part.shape[1]), (channels, LANES), head_part.shape):
        rows += size * extent // (2 * proj_part.shape[1])
    return rows


def pyramid_weights(branch_low, trunk, depth, sep_point, crop_local, proj_part, head_part):
    height, width, aspp = branch_low.shape[1:]
    pixels, channels = trunk.shape
    crops = crop_local.shape[0]
    low, wide = jnp.bfloat16, jnp.float32
    shape = jax.ShapeDtypeStruct
    whole = pl.BlockSpec(memory_space=pltpu.VMEM)
    sems = pltpu.SemaphoreType.DMA
    outs = (
        shape((3, 3, height, width + 2 * PAD, aspp), low),
        shape((sum_rows(early_rows(channels, proj_part, head_part)), 2 * aspp), low),
        shape((crops, aspp), wide),
    )
    return pl.pallas_call(
        pyramid_weights_kernel,
        out_shape=outs,
        in_specs=[whole] * 7,
        out_specs=(whole,) * len(outs),
        scratch_shapes=[
            pltpu.VMEM((channels, LANES), wide),
            pltpu.VMEM((channels, pixels), low),
            pltpu.VMEM((height, width + 2 * PAD, aspp), wide),
            pltpu.VMEM((pixels, aspp), low),
            pltpu.VMEM((3, channels, aspp), wide),
            sems((2, 3, 3)),
            sems((2, 3, 3)),
            *pair_sum_scratch(crops),
        ],
        compiler_params=pltpu.CompilerParams(
            collective_id=11, has_side_effects=True, vmem_limit_bytes=VMEM_BYTES
        ),
        cost_estimate=pl.CostEstimate(
            flops=100 * pixels * channels * aspp, bytes_accessed=64 * pixels * channels, transcendentals=0
        ),
        name="pyramid_weights",
    )(branch_low, trunk, depth, sep_point, crop_local, proj_part, head_part)


def share_rows(slots, at, size, sems):
    rows, cols, row, col, me = place()

    def go(step, carry):
        other = lax.rem(me + step, rows * cols)
        mine = slots.at[me, pl.ds(at, size), :]
        pltpu.make_async_remote_copy(
            mine,
            mine,
            sems.at[0],
            sems.at[1],
            device_id=(other // cols, lax.rem(other, cols)),
            device_id_type=MESH,
        ).start()
        return carry

    lax.fori_loop(1, rows * cols, go, 0)


def shared_rows(slots, at, size, sems):
    rows, cols, row, col, me = place()
    others = slots.at[pl.ds(0, rows * cols - 1), pl.ds(at, size), :]
    pltpu.make_async_remote_copy(
        others,
        others,
        sems.at[0],
        sems.at[1],
        device_id=(row, lax.rem(col + 1, cols)),
        device_id_type=MESH,
    ).wait()


def trunk_back_kernel(
    near,
    own_low,
    depth,
    sep_point,
    aspp_point,
    members,
    crop_high,
    crop_rest,
    expanded,
    features,
    three,
    dilated,
    two,
    second_act,
    expand_weight,
    early,
    pre_grad,
    expand_part,
    dilated_low,
    sums_three,
    sums_two,
    early_out,
    fetched,
    chunk_in,
    shifted,
    moved,
    maps,
    grown,
    expand_low,
    slots_three,
    slots_two,
    sems_three,
    sems_two,
    fetch_sems,
    chunk_sems,
    *early_refs,
):
    rows, cols, row, col, me = place()
    low, wide = jnp.bfloat16, jnp.float32
    height = near.shape[2]
    early_sum = Sums(early, True, early_out, early_refs)
    aspp = sep_point.shape[2]
    pixels, channels = expanded.shape
    middle = dilated.shape[1]
    width = pixels // height
    count = float(pixels * rows * cols)
    per = aspp // LANES
    chunks = channels // aspp
    greet_all()

    def fetch(number):
        return pltpu.make_async_copy(
            near.at[number // 3, number % 3], fetched.at[number % 2], fetch_sems.at[number % 2]
        )

    fetch(0).start()
    early_sum.fetch()

    def chunk_of(block):
        return pl.ds(pl.multiple_of(block * aspp, aspp), aspp)

    def own(block, carry):
        span = chunk_of(block)
        grown[:, span] = (
            across(own_low[...], aspp_point[span, :])
            + jnp.dot(members[...], crop_high[:, span], preferred_element_type=wide)
            + jnp.dot(members[...], crop_rest[:, span], preferred_element_type=wide)
        )
        return carry

    lax.fori_loop(0, chunks, own, 0)
    await_all()
    early_sum.fetched()
    early_sum.start_half()

    def fetch_chunk(block):
        slot = lax.rem(block, 2)
        return pltpu.make_async_copy(
            expanded.at[:, chunk_of(block)], chunk_in.at[slot], chunk_sems.at[slot]
        )

    def advance(block):
        @pl.when(block + 1 < chunks)
        def _():
            fetch_chunk(block + 1).start()

        fetch_chunk(block).wait()

    def back(block, line, span):
        rows_span = slice(line * width, (line + 1) * width)
        value = chunk_in[lax.rem(block, 2), rows_span, :]
        normed = (value - three[0:1, span]) * three[1:2, span]
        return rows_span, normed

    for index in range(3):
        rate = BASE_RATE * (index + 1)
        for way in range(3):
            number = 3 * index + way
            if number < 8:
                fetch(number + 1).start()
            fetch(number).wait()
            shifted[...] = fetched[number % 2].astype(wide)
            for side in range(3):
                tap = 3 * (2 - way) + side
                at = PAD - (side - 1) * rate
                for line in range(height):
                    moved[line * width : (line + 1) * width, tap * aspp : (tap + 1) * aspp] = shifted[
                        line, at : at + width, :
                    ].astype(low)

        def one_chunk(block, carry):
            span = chunk_of(block)
            rows_of = sep_point[index, span, :].astype(wide)
            for tap in range(9):
                order = 9 * index + tap
                maps[:, tap * aspp : (tap + 1) * aspp] = (
                    rows_of * depth[span, order : order + 1]
                ).astype(low)
            total = grown[:, span] + across(moved[...], maps[...])
            if index < 2:
                grown[:, span] = total
                return carry
            advance(block)
            shift_sum, gain_sum = jnp.zeros((1, aspp), wide), jnp.zeros((1, aspp), wide)
            for line in range(height):
                rows_span, normed = back(block, line, span)
                gated = (
                    normed * three[2:3, span]
                    + three[3:4, span]
                    + features[rows_span, span].astype(wide)
                )
                sigma = sigmoid(gated)
                up = total[rows_span, :] * (sigma * (1.0 + gated * (1.0 - sigma)))
                grown[rows_span, span] = up
                pre_grad[rows_span, span] = up.astype(low)
                shift_sum = shift_sum + jnp.sum(up, axis=0, keepdims=True)
                gain_sum = gain_sum + jnp.sum(up * normed, axis=0, keepdims=True)
            for part in range(per):
                lanes = slice(part * LANES, (part + 1) * LANES)
                slots_three[me, pl.ds(block * 2 * per + part, 1), :] = shift_sum[:, lanes]
                slots_three[me, pl.ds(block * 2 * per + per + part, 1), :] = gain_sum[:, lanes]
            pair = block // 2

            @pl.when(lax.rem(block, 2) == 1)
            def _():
                share_rows(slots_three, pl.multiple_of(pair * 4 * per, 8), 4 * per, sems_three.at[pair])

            return carry

        if index == 0:
            early_sum.start_level(0)
        if index == 2:
            fetch_chunk(0).start()
        lax.fori_loop(0, chunks, one_chunk, 0)
        if index == 0:
            early_sum.start_level(1)
        if index == 1:
            early_sum.start_back(1)

    def finish(block, carry):
        span = chunk_of(block)
        pair = block // 2
        at = pl.multiple_of(pair * 4 * per, 8)

        @pl.when(lax.rem(block, 2) == 0)
        def _():
            shared_rows(slots_three, at, 4 * per, sems_three.at[pair])
            sums_three[pl.ds(at, 4 * per), :] = jnp.sum(slots_three[:, pl.ds(at, 4 * per), :], axis=0)

        advance(block)

        def row_at(start):
            first = block * 2 * per + start
            return jnp.concatenate([sums_three[pl.ds(first + part, 1), :] for part in range(per)], axis=1)

        shift_mean = row_at(0) / count
        gain_mean = row_at(per) / count
        factor = three[2:3, span] * three[1:2, span]
        for line in range(height):
            rows_span, normed = back(block, line, span)
            inner = grown[rows_span, span] - shift_mean - normed * gain_mean
            expand_low[rows_span, span] = (inner * factor).astype(low)
        return carry

    early_sum.start_back(0)
    fetch_chunk(0).start()
    lax.fori_loop(0, chunks, finish, 0)
    grown_two = across(expand_low[...], expand_weight[...])
    shift_sum, gain_sum = jnp.zeros((1, middle), wide), jnp.zeros((1, middle), wide)
    for line in range(height):
        rows_span = slice(line * width, (line + 1) * width)
        normed = (dilated[rows_span, :] - two[0:1, :]) * two[1:2, :]
        gated = normed * two[2:3, :] + two[3:4, :]
        sigma = sigmoid(gated)
        up = grown_two[rows_span, :] * (sigma * (1.0 + gated * (1.0 - sigma)))
        grown[rows_span, :middle] = up
        shift_sum = shift_sum + jnp.sum(up, axis=0, keepdims=True)
        gain_sum = gain_sum + jnp.sum(up * normed, axis=0, keepdims=True)
    per_two = middle // LANES
    put_row(slots_two, me, 0, shift_sum)
    put_row(slots_two, me, per_two, gain_sum)
    share(slots_two, sems_two)
    for block in range(channels // middle):
        span = slice(block * middle, (block + 1) * middle)
        expand_part[block * middle : (block + 1) * middle, :] = down(
            second_act[...], expand_low[:, span]
        ).astype(low)
    shared(slots_two, sems_two)
    total = jnp.sum(slots_two[...], axis=0)
    sums_two[...] = total
    shift_mean = take_row(total, 0, middle) / count
    gain_mean = take_row(total, per_two, middle) / count
    factor = two[2:3, :] * two[1:2, :]
    for line in range(height):
        rows_span = slice(line * width, (line + 1) * width)
        normed = (dilated[rows_span, :] - two[0:1, :]) * two[1:2, :]
        inner = grown[rows_span, :middle] - shift_mean - normed * gain_mean
        dilated_low[rows_span, :] = (inner * factor).astype(low)
    early_sum.start_back_half()
    early_sum.finish()


def trunk_back(near, own_low, depth, sep_point, aspp_point, members, crop_high, crop_rest, expanded,
               features, three, dilated, two, second_act, expand_weight, early):
    devices = lax.axis_size("rows") * lax.axis_size("cols")
    height, extent, aspp = near.shape[2:]
    pixels, channels = expanded.shape
    middle = dilated.shape[1]
    chunks = channels // aspp
    low, wide = jnp.bfloat16, jnp.float32
    shape = jax.ShapeDtypeStruct
    whole = pl.BlockSpec(memory_space=pltpu.VMEM)
    away = pl.BlockSpec(memory_space=pl.ANY)
    sems = pltpu.SemaphoreType.DMA
    per_two = middle // LANES
    outs = (
        shape((pixels, channels), low),
        shape((channels, middle), low),
        shape((pixels, middle), low),
        shape((chunks * 2 * (aspp // LANES), LANES), wide),
        shape((2 * per_two, LANES), wide),
        shape(early.shape, low),
    )
    return pl.pallas_call(
        trunk_back_kernel,
        out_shape=outs,
        in_specs=[away] + [whole] * 7 + [away] + [whole] * 6 + [away],
        out_specs=(whole,) * 5 + (away,),
        scratch_shapes=[
            pltpu.VMEM((2, height, extent, aspp), low),
            pltpu.VMEM((2, pixels, aspp), wide),
            pltpu.VMEM((height, extent, aspp), wide),
            pltpu.VMEM((pixels, 9 * aspp), low),
            pltpu.VMEM((aspp, 9 * aspp), low),
            pltpu.VMEM((pixels, channels), wide),
            pltpu.VMEM((pixels, channels), low),
            pltpu.VMEM((devices, chunks * 2 * (aspp // LANES), LANES), wide),
            pltpu.VMEM((devices, 2 * per_two, LANES), wide),
            sems((chunks // 2, 2)),
            sems((2,)),
            sems((2,)),
            sems((2,)),
            *sums_scratch(*early.shape, True),
        ],
        compiler_params=pltpu.CompilerParams(
            collective_id=12, has_side_effects=True, vmem_limit_bytes=VMEM_BYTES + (3 << 20)
        ),
        cost_estimate=pl.CostEstimate(
            flops=80 * pixels * channels * aspp, bytes_accessed=64 * pixels * channels, transcendentals=0
        ),
        name="trunk_back",
    )(near, own_low, depth, sep_point, aspp_point, members, crop_high, crop_rest, expanded, features,
      three, dilated, two, second_act, expand_weight, early)


EDGE = 16


class Halo:
    def __init__(self, near, direct, relay, edge):
        self.near, self.direct, self.relay, self.edge = near, direct, relay, edge
        self.rows, self.cols, self.row, self.col, _ = place()
        self.height, self.width = near.shape[1], near.shape[2] - 2 * EDGE
        self.odd = lax.rem(self.row, 2)
        self.pair = self.row + 1 - 2 * self.odd
        self.onward = self.row + 2 - 4 * self.odd
        self.far = self.row - 1 + 2 * self.odd
        self.pair_way = 2 - 2 * self.odd
        self.far_way = 2 * self.odd

    def exists(self, target):
        return jnp.logical_and(target >= 0, target < self.rows)

    def line_ref(self, way, line):
        return self.near.at[way, line, pl.ds(EDGE, self.width), :]

    def direct_copy(self, line):
        return pltpu.make_async_remote_copy(
            self.line_ref(1, line),
            self.line_ref(self.far_way, line),
            self.direct.at[0, line],
            self.direct.at[1, line],
            device_id=(self.pair, self.col),
            device_id_type=MESH,
        )

    def relay_copy(self, line):
        return pltpu.make_async_remote_copy(
            self.line_ref(self.pair_way, line),
            self.line_ref(self.far_way, line),
            self.relay.at[0, line],
            self.relay.at[1, line],
            device_id=(self.onward, self.col),
            device_id_type=MESH,
        )

    def edge_copy(self, way):
        start = pl.multiple_of(EDGE + (1 - self.col) * (self.width - EDGE), 16)
        end = pl.multiple_of(self.col * (self.width + EDGE), 16)
        return pltpu.make_async_remote_copy(
            self.near.at[1, :, pl.ds(start, EDGE), :],
            self.near.at[way, :, pl.ds(end, EDGE), :],
            self.edge.at[0, way],
            self.edge.at[1, way],
            device_id=(self.row + 1 - way, 1 - self.col),
            device_id_type=MESH,
        )

    def clear(self):
        near = self.near
        blank = pl.multiple_of(self.col * (self.width + EDGE), 16)
        for way in range(3):
            near[way, :, pl.ds(blank, EDGE), :] = jnp.zeros(
                (self.height, EDGE, near.shape[3]), near.dtype
            )

        @pl.when(jnp.logical_not(self.exists(self.far)))
        def _():
            near[self.far_way] = jnp.zeros(near.shape[1:], near.dtype)

    def start(self):
        self.edge_copy(1).start()
        for line in range(self.height // 2):
            self.direct_copy(line).start()
        for way in (0, 2):

            @pl.when(self.exists(self.row + 1 - way))
            def _():
                self.edge_copy(way).start()

    def wait_own(self):
        self.edge_copy(1).wait_recv()

    def pass_line(self, line):
        self.direct_copy(line).wait_recv()

        @pl.when(self.exists(self.onward))
        def _():
            self.relay_copy(line).start()

    def pass_first(self):
        for line in range(self.height // 2):
            self.pass_line(line)
        for line in range(self.height // 2, self.height):
            self.direct_copy(line).start()

    def pass_rest(self):
        for line in range(self.height // 2, self.height):
            self.pass_line(line)

    def wait_rest(self):
        self.wait_edges()
        self.wait_relay()

    def wait_edges(self):
        for way in (0, 2):

            @pl.when(self.exists(self.row - 1 + way))
            def _():
                self.edge_copy(way).wait_recv()

    def wait_relay(self):
        @pl.when(self.exists(self.far))
        def _():
            for line in range(self.height):
                self.relay_copy(line).wait_recv()

    def drain(self):
        self.edge_copy(1).wait_send()
        for line in range(self.height):
            self.direct_copy(line).wait_send()
        for way in (0, 2):

            @pl.when(self.exists(self.row + 1 - way))
            def _():
                self.edge_copy(way).wait_send()

        @pl.when(self.exists(self.onward))
        def _():
            for line in range(self.height):
                self.relay_copy(line).wait_send()


def front_kernel(
    features,
    reduce_weight,
    dilated_weight,
    expand_weight,
    pool_weight,
    mid_gain,
    mid_shift,
    out_gain,
    out_shift,
    crop_ids,
    boundary,
    valid,
    reduced,
    first_act,
    dilated,
    second_act,
    expanded,
    trunk,
    one,
    two,
    three,
    count_sums,
    crop_sums,
    crop_part,
    pixel_crops,
    near,
    shifted,
    moved,
    members,
    one_slots,
    two_slots,
    three_own,
    three_pair,
    three_slots,
    three_all,
    direct,
    relay,
    edge,
    one_sems,
    two_sems,
    pair_sems,
    three_sems,
    all_sems,
):
    rows, cols, row, col, me = place()
    low, wide = jnp.bfloat16, jnp.float32
    height = near.shape[1]
    pixels, middle = reduced.shape
    channels = features.shape[1]
    width = pixels // height
    share_size = float(pixels)
    count = float(pixels * rows * cols)
    per = middle // LANES
    halo = Halo(near, direct, relay, edge)
    greet_all()
    halo.clear()
    reduced[...] = jnp.dot(features[...], reduce_weight[...], preferred_element_type=wide)

    def lines(body, carry=0):
        def run(line, carry):
            return body(line, pl.ds(pl.multiple_of(line * width, width), width), carry)

        return lax.fori_loop(0, height, run, carry)

    def keep_low(line, span, carry):
        near[1, line, EDGE : EDGE + width, :] = reduced[span, :].astype(low)
        return carry

    lines(keep_low)
    await_all()
    halo.start()

    def statistics(value_of, extent):
        zero = jnp.zeros((1, extent), wide)
        total = lines(lambda line, span, acc: acc + jnp.sum(value_of(span), axis=0, keepdims=True), zero)
        mean = total / share_size

        def squares(line, span, acc):
            apart = value_of(span) - mean
            return acc + jnp.sum(apart * apart, axis=0, keepdims=True)

        return mean, lines(squares, zero)

    def settle(table, at, center, scale):
        table[...] = jnp.zeros(table.shape, wide)
        table[0:1, :] = center
        table[1:2, :] = scale
        table[2:3, :] = mid_gain[at : at + 1, :]
        table[3:4, :] = mid_shift[at : at + 1, :]

    def activated(value, table):
        gated = (value - table[0:1, :]) * table[1:2, :] * table[2:3, :] + table[3:4, :]
        return gated * sigmoid(gated)

    mean, square = statistics(lambda span: reduced[span, :], middle)
    one_slots[me] = jnp.zeros(one_slots.shape[1:], wide)
    put_row(one_slots, me, 0, mean)
    put_row(one_slots, me, per, square)
    crop_of = lax.broadcasted_iota(jnp.int32, (LANES, width), 0)
    for line in range(height):
        hot = jnp.where(crop_of == crop_ids[line : line + 1, :], 1.0, 0.0)
        members[:, line * width : (line + 1) * width] = hot.astype(low)
        pixel_crops[line * width : (line + 1) * width, :] = hot.T.astype(low)
    lane = lax.broadcasted_iota(jnp.int32, (8, LANES), 1)

    def whole_sum(table):
        part = jnp.sum(table[...].astype(wide), axis=0, keepdims=True)
        return jnp.sum(part, axis=1, keepdims=True)

    counts = across(jnp.ones((8, pixels), low), members[...])
    counts = jnp.where(lane == CROPS, share_size - whole_sum(boundary), counts)
    counts = jnp.where(lane == CROPS + 1, whole_sum(valid), counts)
    put_row(one_slots, me, 2 * per, counts[0:1, :])
    share(one_slots, one_sems)
    shared(one_slots, one_sems)
    center, scale = merged(one_slots, per, share_size, count)
    settle(one, 0, take_row(center, 0, middle), take_row(scale, 0, middle))
    count_sums[...] = jnp.sum(one_slots[:, 2 * per : 2 * per + 8, :], axis=0)

    def first(line, span, carry):
        first_act[span, :] = activated(reduced[span, :], one).astype(low)
        return carry

    lines(first)

    def one_way(way, own):
        alive = jnp.where(halo.exists(row - 1 + way), 1.0, 0.0)

        def open_line(line, span, carry):
            shifted[line] = activated(near[way, line].astype(wide), one) * alive
            if own:
                shifted[line, EDGE : EDGE + width, :] = first_act[span, :].astype(wide)
            blank = pl.multiple_of(col * (width + EDGE), 16)
            shifted[line, pl.ds(blank, EDGE), :] = jnp.zeros((EDGE, middle), wide)
            for side in range(3):
                at = EDGE + (side - 1) * MID_RATE
                moved[span, side * middle : (side + 1) * middle] = shifted[
                    line, at : at + width, :
                ].astype(low)
            return carry

        lines(open_line)
        made = jnp.dot(moved[...], dilated_weight[way], preferred_element_type=wide)
        if own:
            dilated[...] = made
        else:
            dilated[...] += made

    halo.pass_first()
    halo.wait_own()
    one_way(1, True)
    halo.pass_rest()
    halo.wait_edges()
    one_way(halo.pair_way, False)
    halo.wait_relay()
    one_way(halo.far_way, False)
    mean, square = statistics(lambda span: dilated[span, :], middle)
    put_row(two_slots, me, 0, mean)
    put_row(two_slots, me, per, square)
    share(two_slots, two_sems)
    shared(two_slots, two_sems)
    center, scale = merged(two_slots, per, share_size, count)
    settle(two, 1, take_row(center, 0, middle), take_row(scale, 0, middle))

    def second(line, span, carry):
        second_act[span, :] = activated(dilated[span, :], two).astype(low)
        return carry

    lines(second)
    chunk = 2 * LANES
    half_rows = channels // 2 // LANES
    half_chunks = channels // 2 // chunk

    def expand(block, carry):
        span = pl.ds(pl.multiple_of(block * chunk, chunk), chunk)
        expanded[:, span] = jnp.dot(second_act[...], expand_weight[:, span], preferred_element_type=wide)
        mean, square = statistics(lambda rows_span: expanded[rows_span, span], chunk)
        at = block // half_chunks * 2 * half_rows + lax.rem(block, half_chunks) * 2
        for part in range(2):
            lanes = slice(part * LANES, (part + 1) * LANES)
            three_own[pl.ds(at + part, 1), :] = mean[:, lanes]
            three_own[pl.ds(at + half_rows + part, 1), :] = square[:, lanes]
        return carry

    lax.fori_loop(0, channels // chunk, expand, 0)

    def to_pair(src, dst, sems):
        return pltpu.make_async_remote_copy(
            src, dst, sems.at[0], sems.at[1], device_id=(row, 1 - col), device_id_type=MESH
        )

    theirs = pl.ds(pl.multiple_of((1 - col) * 2 * half_rows, 8), 2 * half_rows)
    mine = pl.ds(pl.multiple_of(col * 2 * half_rows, 8), 2 * half_rows)
    copy = to_pair(three_own.at[theirs], three_pair, pair_sems)
    copy.start()
    copy.wait()
    own = three_own[mine, :]
    other = three_pair[...]
    apart = own[:half_rows] - other[:half_rows]
    three_slots[row, :half_rows, :] = 0.5 * (own[:half_rows] + other[:half_rows])
    three_slots[row, half_rows:, :] = (
        own[half_rows:] + other[half_rows:] + (0.5 * share_size) * (apart * apart)
    )
    share_column(three_slots, three_sems)
    shared_column(three_slots, three_sems)
    center, scale = merged(three_slots, half_rows, 2.0 * share_size, count)
    three_all[col, :half_rows, :] = center
    three_all[col, half_rows:, :] = scale
    copy = to_pair(three_all.at[col], three_all.at[col], all_sems)
    copy.start()
    copy.wait()
    for half in range(2):
        span = slice(half * channels // 2, (half + 1) * channels // 2)
        three[0:1, span] = take_row(three_all[half], 0, channels // 2)
        three[1:2, span] = take_row(three_all[half], half_rows, channels // 2)
    three[2:3, :] = out_gain[...]
    three[3:4, :] = out_shift[...]
    three[4:8, :] = jnp.zeros((4, channels), wide)
    crops = CROPS

    def last(block, carry):
        span = pl.ds(pl.multiple_of(block * chunk, chunk), chunk)

        def act_line(line, rows_span, carry):
            normed = (expanded[rows_span, span] - three[0:1, span]) * three[1:2, span]
            gated = (
                normed * three[2:3, span] + three[3:4, span] + features[rows_span, span].astype(wide)
            )
            trunk[rows_span, span] = (gated * sigmoid(gated)).astype(low)
            return carry

        lines(act_line)
        sums = jnp.dot(members[...], trunk[:, span], preferred_element_type=wide)[:crops, :]
        for part in range(2):
            at = pl.multiple_of((2 * block + part) * crops, 8)
            crop_sums[pl.ds(at, crops), :] = sums[:, part * LANES : (part + 1) * LANES]
        high = sums.astype(low)
        rest = (sums - high.astype(wide)).astype(low)
        return (
            carry
            + jnp.dot(high, pool_weight[span, :], preferred_element_type=wide)
            + jnp.dot(rest, pool_weight[span, :], preferred_element_type=wide)
        )

    crop_part[...] = lax.fori_loop(
        0, channels // chunk, last, jnp.zeros((crops, pool_weight.shape[1]), wide)
    )
    halo.drain()


def front(height, features, reduce_weight, dilated_weight, expand_weight, pool_weight, mid_gain,
          mid_shift, out_gain, out_shift, crop_ids, boundary, valid):
    rows = lax.axis_size("rows")
    devices = rows * lax.axis_size("cols")
    pixels, channels = features.shape
    middle = reduce_weight.shape[1]
    width = pixels // height
    low, wide = jnp.bfloat16, jnp.float32
    shape = jax.ShapeDtypeStruct
    whole = pl.BlockSpec(memory_space=pltpu.VMEM)
    sems = pltpu.SemaphoreType.DMA
    per = middle // LANES
    half_rows = channels // 2 // LANES
    outs = (
        shape((pixels, middle), wide),
        shape((pixels, middle), low),
        shape((pixels, middle), wide),
        shape((pixels, middle), low),
        shape((pixels, channels), wide),
        shape((pixels, channels), low),
        shape((8, middle), wide),
        shape((8, middle), wide),
        shape((8, channels), wide),
        shape((8, LANES), wide),
        shape((CROPS * channels // LANES, LANES), wide),
        shape((CROPS, pool_weight.shape[1]), wide),
        shape((pixels, LANES), low),
    )
    return pl.pallas_call(
        front_kernel,
        out_shape=outs,
        in_specs=[whole] * 12,
        out_specs=(whole,) * len(outs),
        scratch_shapes=[
            pltpu.VMEM((3, height, width + 2 * EDGE, middle), low),
            pltpu.VMEM((height, width + 2 * EDGE, middle), wide),
            pltpu.VMEM((pixels, 3 * middle), low),
            pltpu.VMEM((LANES, pixels), low),
            pltpu.VMEM((devices, 2 * per + 8, LANES), wide),
            pltpu.VMEM((devices, 2 * per, LANES), wide),
            pltpu.VMEM((4 * half_rows, LANES), wide),
            pltpu.VMEM((2 * half_rows, LANES), wide),
            pltpu.VMEM((rows, 2 * half_rows, LANES), wide),
            pltpu.VMEM((2, 2 * half_rows, LANES), wide),
            sems((2, height)),
            sems((2, height)),
            sems((2, 3)),
            sems((2,)),
            sems((2,)),
            sems((2,)),
            sems((2,)),
            sems((2,)),
        ],
        compiler_params=pltpu.CompilerParams(
            collective_id=14, has_side_effects=True, vmem_limit_bytes=VMEM_BYTES
        ),
        name="front",
    )(features, reduce_weight, dilated_weight, expand_weight, pool_weight, mid_gain, mid_shift,
      out_gain, out_shift, crop_ids, boundary, valid)


PLANE = 4


class Sum:
    def __init__(self, full, own, out, plane_first, half_in, near_in, far_in, half_sem, near_sem, far_sem, copy_sem):
        self.full, self.out, self.half_in = full, out, half_in
        self.half_sem, self.copy_sem = half_sem, copy_sem
        self.rows, self.cols, self.row, self.col, _ = place()
        parts = self.rows // PLANE
        quarter, part = lax.rem(self.row, PLANE), self.row // PLANE
        plane = (PLANE, quarter, lambda mate: part * PLANE + mate)
        rest = (parts, part, lambda mate: mate * PLANE + quarter)
        self.levels = (plane, rest) if plane_first else (rest, plane)
        self.arrivals, self.sems = (near_in, far_in), (near_sem, far_sem)
        self.half_rows = full.shape[0] // 2
        self.sizes = [self.half_rows // self.levels[0][0]]
        self.sizes.append(self.sizes[0] // self.levels[1][0])
        self.own = own
        self.data = full.at[self.half_span(self.col)] if own is None else own

    def span(self, start, size):
        return pl.ds(pl.multiple_of(start, 16), size)

    def half_span(self, col):
        return self.span(col * self.half_rows, self.half_rows)

    def level_span(self, level, at):
        base = 0 if level == 0 else self.levels[0][1] * self.sizes[0]
        return self.span(base + at * self.sizes[level], self.sizes[level])

    def out_at(self, span):
        return self.out.at[self.span(self.col * self.half_rows + span.start, span.size)]

    def mates(self, level):
        count, at, row_of = self.levels[level]
        for step in range(1, count):
            mate = lax.rem(at + step, count)
            yield mate, (row_of(mate), self.col)

    def remote(self, src, dst, sems, out_at, in_at, target):
        return pltpu.make_async_remote_copy(
            src, dst, sems.at[0, out_at], sems.at[1, in_at], device_id=target, device_id_type=MESH
        )

    def fetch(self):
        return pltpu.make_async_copy(self.full.at[self.half_span(self.col)], self.own, self.copy_sem)

    def half_copy(self):
        other = self.full.at[self.half_span(1 - self.col)]
        return self.remote(other, self.half_in, self.half_sem, 0, 0, (self.row, 1 - self.col))

    def level_copy(self, level, mate, target):
        at = self.levels[level][1]
        return self.remote(
            self.data.at[self.level_span(level, mate)],
            self.arrivals[level].at[at],
            self.sems[level],
            mate,
            at,
            target,
        )

    def level_arrival(self, level, mate, target):
        slot = self.arrivals[level].at[mate]
        return self.remote(slot, slot, self.sems[level], mate, mate, target)

    def back_copy(self, level, mate, target):
        count, at, _ = self.levels[level]
        mine = self.out_at(self.level_span(level, at))
        return self.remote(mine, mine, self.sems[level], count + mate, count + at, target)

    def back_arrival(self, level, mate, target):
        count = self.levels[level][0]
        theirs = self.out_at(self.level_span(level, mate))
        return self.remote(theirs, theirs, self.sems[level], count + mate, count + mate, target)

    def back_half(self, col):
        part = self.out.at[self.half_span(col)]
        return self.remote(part, part, self.half_sem, 1, 1, (self.row, 1 - self.col))

    def add(self, span, sources):
        block = 64
        base = span.start

        def some(at, carry):
            rows = pl.ds(pl.multiple_of(base + at * block, 16), block)
            total = self.data[rows, :].astype(jnp.float32)
            for source in sources:
                total = total + source(pl.ds(pl.multiple_of(at * block, 16), block)).astype(jnp.float32)
            self.data[rows, :] = total.astype(self.data.dtype)
            return carry

        full = span.size // block
        lax.fori_loop(0, full, some, 0)
        rest = span.size - full * block
        if rest:
            rows = pl.ds(pl.multiple_of(base + full * block, 16), rest)
            total = self.data[rows, :].astype(jnp.float32)
            for source in sources:
                total = total + source(pl.ds(full * block, rest)).astype(jnp.float32)
            self.data[rows, :] = total.astype(self.data.dtype)

    def start_half(self):
        self.half_copy().start()

    def start_level(self, level):
        if level == 0:
            self.half_copy().wait()
            self.add(self.span(0, self.half_rows), [lambda rows: self.half_in[rows, :]])
        else:
            self.gather(0)
        for mate, target in self.mates(level):
            self.level_copy(level, mate, target).start()

    def gather(self, level):
        for mate, target in self.mates(level):
            self.level_copy(level, mate, target).wait_send()
            self.level_arrival(level, mate, target).wait_recv()
        self.add(
            self.level_span(level, self.levels[level][1]),
            [lambda rows, mate=mate: self.arrivals[level][mate, rows, :] for mate, _ in self.mates(level)],
        )

    def start_back(self, level):
        if level == 1:
            self.gather(1)
            span = self.level_span(1, self.levels[1][1])
            copy = pltpu.make_async_copy(self.data.at[span], self.out_at(span), self.copy_sem)
            copy.start()
            copy.wait()
        else:
            for mate, target in self.mates(1):
                self.back_copy(1, mate, target).wait_send()
                self.back_arrival(1, mate, target).wait_recv()
        for mate, target in self.mates(level):
            self.back_copy(level, mate, target).start()

    def start_back_half(self):
        for mate, target in self.mates(0):
            self.back_copy(0, mate, target).wait_send()
            self.back_arrival(0, mate, target).wait_recv()
        self.back_half(self.col).start()

    def finish(self):
        self.back_half(self.col).wait_send()
        self.back_half(1 - self.col).wait_recv()


class Sums:
    def __init__(self, full, own, out, refs):
        self.each = []
        start = 0
        for size, plane_first in sum_pieces(full.shape[0]):
            span = pl.ds(start, size)
            count = 7 if own is None else 8
            mine, refs = list(refs[:count]), refs[count:]
            part = None if own is None else mine.pop(0)
            self.each.append(Sum(full.at[span], part, out.at[span], plane_first, *mine))
            start += size
        self.rest = refs

    def fetch(self):
        for each in self.each:
            each.fetch().start()

    def fetched(self):
        for each in self.each:
            each.fetch().wait()

    def start_half(self):
        for each in self.each:
            each.start_half()

    def start_level(self, level):
        for each in self.each:
            each.start_level(level)

    def start_back(self, level):
        for each in self.each:
            each.start_back(level)

    def start_back_half(self):
        for each in self.each:
            each.start_back_half()

    def finish(self):
        for each in self.each:
            each.finish()


def sum_unit():
    return 2 * lax.axis_size("rows") * 16


def sum_pieces(total):
    unit = sum_unit()
    units = total // unit
    second = units // 3
    pieces = [((units - second) * unit, True)]
    if second:
        pieces.append((second * unit, False))
    return pieces


def sums_scratch(total, lanes, away):
    parts = lax.axis_size("rows") // PLANE
    low, sems = jnp.bfloat16, pltpu.SemaphoreType.DMA
    scratch = []
    for size, plane_first in sum_pieces(total):
        counts = (PLANE, parts) if plane_first else (parts, PLANE)
        half = size // 2
        if away:
            scratch.append(pltpu.VMEM((half, lanes), low))
        scratch += [
            pltpu.VMEM((half, lanes), low),
            pltpu.VMEM((counts[0], half // counts[0], lanes), low),
            pltpu.VMEM((counts[1], half // counts[0] // counts[1], lanes), low),
            sems((2, 2)),
            sems((2, 2 * counts[0])),
            sems((2, 2 * counts[1])),
            sems,
        ]
    return scratch


def sum_rows(rows):
    unit = sum_unit()
    return -(-rows // unit) * unit


def tail_kernel(
    dilated_low,
    first_act,
    dilated_weight,
    reduced,
    one,
    features,
    reduce_weight,
    pre_grad,
    expand_part,
    features_grad,
    expand_out,
    dilated_out,
    reduce_out,
    sums_one,
    near,
    shifted,
    moved,
    act_turned,
    features_turned,
    first_grad,
    reduced_low,
    dilated_data,
    reduce_data,
    slots,
    direct,
    relay,
    edge,
    sems_one,
    *sum_refs,
):
    rows, cols, row, col, me = place()
    low, wide = jnp.bfloat16, jnp.float32
    height = near.shape[1]
    pixels, middle = dilated_low.shape
    channels = features.shape[1]
    width = pixels // height
    count = float(pixels * rows * cols)
    expand_sum = Sums(expand_part, True, expand_out, sum_refs)
    dilated_sum = Sums(dilated_data, None, dilated_out, expand_sum.rest)
    reduce_sum = Sums(reduce_data, None, reduce_out, dilated_sum.rest)
    sums = (expand_sum, dilated_sum, reduce_sum)
    halo = Halo(near, direct, relay, edge)
    greet_all()
    expand_sum.fetch()
    halo.clear()
    for line in range(height):
        near[1, line, EDGE : EDGE + width, :] = dilated_low[line * width : (line + 1) * width, :]
    for data, used in ((dilated_data, 9 * middle), (reduce_data, channels)):
        if data.shape[0] > used:
            data[used:, :] = jnp.zeros((data.shape[0] - used, data.shape[1]), low)
    expand_sum.fetched()
    await_all()
    halo.start()
    expand_sum.start_half()

    def turn_features(block, carry):
        span = pl.ds(pl.multiple_of(block * width, width), width)
        for line in range(height):
            features_turned[span, line * width : (line + 1) * width] = features[
                line * width : (line + 1) * width, span
            ].T
        return carry

    def turn_act(block, carry):
        span = pl.ds(pl.multiple_of(block * width, width), width)
        for line in range(height):
            act_turned[span, line * width : (line + 1) * width] = first_act[
                line * width : (line + 1) * width, span
            ].T
        return carry

    lax.fori_loop(0, middle // width, turn_act, 0)

    def one_way(way):
        shifted[...] = near[way].astype(wide)
        for side in range(3):
            tap = 3 * (2 - way) + side
            rows_of = pl.ds(pl.multiple_of(tap * middle, middle), middle)
            at = EDGE - (side - 1) * MID_RATE
            for line in range(height):
                moved[line * width : (line + 1) * width, :] = shifted[line, at : at + width, :].astype(
                    low
                )
            made = across(moved[...], dilated_weight[tap])
            if isinstance(way, int) and side == 0:
                first_grad[...] = made
            else:
                first_grad[...] += made
            dilated_data[rows_of, :] = jnp.dot(
                act_turned[...], moved[...], preferred_element_type=wide
            ).astype(low)

    halo.wait_own()
    one_way(1)
    halo.pass_first()
    lax.fori_loop(0, channels // width, turn_features, 0)
    halo.pass_rest()
    halo.wait_edges()
    one_way(halo.pair_way)
    halo.wait_relay()
    expand_sum.start_level(0)
    one_way(halo.far_way)
    dilated_sum.start_half()
    expand_sum.start_level(1)
    shift_sum, gain_sum = jnp.zeros((1, middle), wide), jnp.zeros((1, middle), wide)
    for line in range(height):
        span = slice(line * width, (line + 1) * width)
        normed = (reduced[span, :] - one[0:1, :]) * one[1:2, :]
        gated = normed * one[2:3, :] + one[3:4, :]
        sigma = sigmoid(gated)
        up = first_grad[span, :] * (sigma * (1.0 + gated * (1.0 - sigma)))
        first_grad[span, :] = up
        shift_sum = shift_sum + jnp.sum(up, axis=0, keepdims=True)
        gain_sum = gain_sum + jnp.sum(up * normed, axis=0, keepdims=True)
    per = middle // LANES
    put_row(slots, me, 0, shift_sum)
    put_row(slots, me, per, gain_sum)
    share(slots, sems_one)
    dilated_sum.start_level(0)
    shared(slots, sems_one)
    total = jnp.sum(slots[...], axis=0)
    sums_one[...] = total
    shift_mean = take_row(total, 0, middle) / count
    gain_mean = take_row(total, per, middle) / count
    factor = one[2:3, :] * one[1:2, :]
    for line in range(height):
        span = slice(line * width, (line + 1) * width)
        normed = (reduced[span, :] - one[0:1, :]) * one[1:2, :]
        inner = first_grad[span, :] - shift_mean - normed * gain_mean
        reduced_low[span, :] = (inner * factor).astype(low)
    reduce_data[:channels, :] = jnp.dot(
        features_turned[...], reduced_low[...], preferred_element_type=wide
    ).astype(low)
    reduce_sum.start_half()
    expand_sum.start_back(1)
    chunk = 2 * LANES

    def last(block, carry):
        span = pl.ds(pl.multiple_of(block * chunk, chunk), chunk)
        made = across(reduced_low[...], reduce_weight[span, :])
        features_grad[:, span] = (made + pre_grad[:, span].astype(wide)).astype(low)
        return carry

    lax.fori_loop(0, channels // chunk, last, 0)
    reduce_sum.start_level(0)
    expand_sum.start_back(0)
    dilated_sum.start_level(1)
    reduce_sum.start_level(1)
    expand_sum.start_back_half()
    dilated_sum.start_back(1)
    reduce_sum.start_back(1)
    dilated_sum.start_back(0)
    reduce_sum.start_back(0)
    dilated_sum.start_back_half()
    reduce_sum.start_back_half()
    for each in sums:
        each.finish()
    halo.drain()


def tail(height, dilated_low, first_act, dilated_weight, reduced, one, features, reduce_weight, pre_grad,
         expand_part):
    devices = lax.axis_size("rows") * lax.axis_size("cols")
    pixels, middle = dilated_low.shape
    channels = features.shape[1]
    width = pixels // height
    low, wide = jnp.bfloat16, jnp.float32
    shape = jax.ShapeDtypeStruct
    whole = pl.BlockSpec(memory_space=pltpu.VMEM)
    away = pl.BlockSpec(memory_space=pl.ANY)
    sems = pltpu.SemaphoreType.DMA
    per = middle // LANES
    expand_part = jnp.pad(
        expand_part, ((0, sum_rows(expand_part.shape[0]) - expand_part.shape[0]), (0, 0))
    )
    sizes = [sum_rows(expand_part.shape[0]), sum_rows(9 * middle), sum_rows(channels)]
    outs = (
        shape((pixels, channels), low),
        *[shape((size, middle), low) for size in sizes],
        shape((2 * per, LANES), wide),
    )
    scratch = [
        pltpu.VMEM((3, height, width + 2 * EDGE, middle), low),
        pltpu.VMEM((height, width + 2 * EDGE, middle), wide),
        pltpu.VMEM((pixels, middle), low),
        pltpu.VMEM((middle, pixels), low),
        pltpu.VMEM((channels, pixels), low),
        pltpu.VMEM((pixels, middle), wide),
        pltpu.VMEM((pixels, middle), low),
        *[pltpu.VMEM((size, middle), low) for size in sizes[1:]],
        pltpu.VMEM((devices, 2 * per, LANES), wide),
        sems((2, height)),
        sems((2, height)),
        sems((2, 3)),
        sems((2,)),
    ]
    for size, apart in zip(sizes, (True, False, False)):
        scratch += sums_scratch(size, middle, apart)
    return pl.pallas_call(
        functools.partial(tail_kernel),
        out_shape=outs,
        in_specs=[whole] * 8 + [away],
        out_specs=(whole, away, away, away, whole),
        scratch_shapes=scratch,
        compiler_params=pltpu.CompilerParams(
            collective_id=13, has_side_effects=True, vmem_limit_bytes=VMEM_BYTES + (3 << 20)
        ),
        cost_estimate=pl.CostEstimate(
            flops=400 * pixels * middle * middle, bytes_accessed=256 * pixels * channels, transcendentals=0
        ),
        name="tail",
    )(dilated_low, first_act, dilated_weight, reduced, one, features, reduce_weight, pre_grad, expand_part)


def widen_kernel(first, second, expand, dilated, reduce, sep_out, point_out, expand_out, dilated_out, reduce_out):
    wide = jnp.float32
    aspp, middle = point_out.shape[1], expand.shape[2]
    sep_out[0] = first[:, :aspp].astype(wide)
    sep_out[1] = first[:, aspp:].astype(wide)
    sep_out[2] = second[:, :aspp].astype(wide)
    point_out[...] = second[:, aspp:].astype(wide)
    for block in range(expand.shape[0]):
        expand_out[:, block * middle : (block + 1) * middle] = expand[block].astype(wide)
    dilated_out[...] = dilated[...].astype(wide)
    reduce_out[...] = reduce[...].astype(wide)


def widen(early, expand, dilated, reduce, channels, aspp):
    middle = reduce.shape[1]
    wide = jnp.float32
    steps = 8
    rows = channels // steps
    taps = 9 * middle // steps
    lines = middle // steps
    blocks = channels // middle
    shape = jax.ShapeDtypeStruct
    return pl.pallas_call(
        widen_kernel,
        grid=(steps,),
        out_shape=(
            shape((3, channels, aspp), wide),
            shape((channels, aspp), wide),
            shape((middle, channels), wide),
            shape((9 * middle, middle), wide),
            shape((channels, middle), wide),
        ),
        in_specs=[
            pl.BlockSpec((rows, 2 * aspp), lambda step: (step, 0)),
            pl.BlockSpec((rows, 2 * aspp), lambda step: (steps + step, 0)),
            pl.BlockSpec((blocks, lines, middle), lambda step: (0, step, 0)),
            pl.BlockSpec((taps, middle), lambda step: (step, 0)),
            pl.BlockSpec((rows, middle), lambda step: (step, 0)),
        ],
        out_specs=(
            pl.BlockSpec((3, rows, aspp), lambda step: (0, step, 0)),
            pl.BlockSpec((rows, aspp), lambda step: (step, 0)),
            pl.BlockSpec((lines, channels), lambda step: (step, 0)),
            pl.BlockSpec((taps, middle), lambda step: (step, 0)),
            pl.BlockSpec((rows, middle), lambda step: (step, 0)),
        ),
        compiler_params=pltpu.CompilerParams(vmem_limit_bytes=VMEM_BYTES),
        name="widen",
    )(early, early, expand[:channels].reshape(blocks, middle, middle), dilated, reduce)


def on_device(
    features,
    reduce_weight,
    dilated_weight,
    expand_weight,
    mid_gain,
    mid_shift,
    out_gain,
    out_shift,
    aspp_point,
    sep_depth,
    sep_point,
    pool_weight,
    proj_weight,
    aspp_gain,
    aspp_shift,
    head_weight,
    head_bias,
    task_scales,
    crop_ids,
    labels,
    boundary_mask,
    valid_mask,
    geometry_target,
):
    height, width, channels = features.shape
    pixels = height * width
    low = jnp.bfloat16
    aspp_width = proj_weight.shape[1]
    flat = features.reshape(pixels, channels)
    middle = reduce_weight.shape[1]

    (
        reduced, first_act, dilated, second_act, expanded, trunk, one, two, three, count_sums,
        local_sums, crop_part, members,
    ) = front(
        height,
        flat,
        reduce_weight,
        dilated_weight.reshape(3, 3 * middle, middle),
        expand_weight,
        pool_weight,
        mid_gain,
        mid_shift,
        out_gain.reshape(1, channels),
        out_shift.reshape(1, channels),
        crop_ids,
        boundary_mask,
        valid_mask,
    )
    crop_count = count_sums[0, :CROPS]
    lane = jnp.arange(LANES)
    scale_exp = jnp.exp(task_scales)
    task_of = jnp.where(lane < CLASSES, scale_exp[0], jnp.where(lane == CLASSES, scale_exp[1], scale_exp[2]))
    weights = jnp.stack(
        [jnp.where(lane > CLASSES, 2.0, 1.0) * task_of, task_of, jnp.pad(task_scales, (0, LANES - 3))]
    )
    outs = head_weight.shape[1]
    devices = lax.axis_size("rows") * lax.axis_size("cols")
    crop_rows = CROPS * channels // LANES
    piece = -(-crop_rows // devices)
    crop_sums = jnp.pad(local_sums, ((0, piece * devices - crop_rows), (0, 0)))
    crop_sums = jnp.pad(
        crop_sums.reshape(devices, piece, LANES), ((0, 0), (0, -piece % 8), (0, 0))
    )
    branch_low, proj_part, head_part, crop_local, crop_pre, sums_five, sums_four, crop_table, own_low, closing = pyramid(
        height,
        trunk,
        jnp.pad(sep_depth.reshape(27, channels).astype(jnp.float32), ((0, 5), (0, 0))),
        sep_point,
        aspp_point,
        crop_part,
        count_sums,
        members,
        proj_weight,
        aspp_gain,
        aspp_shift,
        head_weight,
        head_bias.reshape(1, outs),
        jnp.pad(weights, ((0, 5), (0, 0))),
        labels,
        boundary_mask,
        valid_mask,
        geometry_target,
        crop_sums,
    )
    crop_table = crop_table[:, :piece].reshape(-1, LANES)[:crop_rows].reshape(-1, CROPS, LANES)
    crop_table = jnp.transpose(crop_table, (1, 0, 2)).reshape(CROPS, channels)
    per = aspp_width // LANES
    proj_shift_grad = sums_five[:per].reshape(1, aspp_width)
    proj_gain_grad = sums_five[per : 2 * per].reshape(1, aspp_width)
    grad_head_bias = sums_five[2 * per + 1, :outs]
    branch_shift_grad = sums_four[: 4 * per].reshape(4, aspp_width)
    branch_gain_grad = sums_four[4 * per :].reshape(4, aspp_width)
    objective, grad_scales = closing[1, 0], closing[0, :3]
    near, early, crop_total = pyramid_weights(
        branch_low.reshape(4, height, width, aspp_width),
        trunk,
        jnp.pad(sep_depth.reshape(27, channels).astype(jnp.float32).T, ((0, 0), (0, LANES - 27))),
        sep_point,
        crop_local,
        proj_part,
        head_part,
    )
    crop_low = (crop_total * gate_slope(crop_pre)).astype(low)
    pooled = (crop_table / crop_count[:, None]).astype(low)
    grad_pool_weight = jnp.einsum("kc,kd->cd", pooled, crop_low, preferred_element_type=jnp.float32)
    pooled_grad = (
        jnp.einsum("kd,cd->kc", crop_low, pool_weight, preferred_element_type=jnp.float32)
        / crop_count[:, None]
    )
    pooled_grad = jnp.pad(pooled_grad, ((0, LANES - CROPS), (0, 0)))
    crop_high = pooled_grad.astype(low)
    crop_rest = (pooled_grad - crop_high.astype(jnp.float32)).astype(low)
    pre_low, expand_part, dilated_low, sums_three, sums_two, early_sum = trunk_back(
        near,
        own_low,
        jnp.pad(sep_depth.reshape(27, channels).astype(jnp.float32).T, ((0, 0), (0, LANES - 27))),
        sep_point,
        aspp_point,
        members,
        crop_high,
        crop_rest,
        expanded,
        flat,
        three,
        dilated,
        two,
        second_act,
        expand_weight,
        early,
    )
    folded = sums_three.reshape(-1, 2 * per, LANES)
    out_shift_grad = folded[:, :per].reshape(1, channels)
    out_gain_grad = folded[:, per:].reshape(1, channels)
    two_shift_grad, two_gain_grad = sums_two.reshape(2, 1, middle)
    grad_features, expand_sum, dilated_sum, reduce_sum, sums_one = tail(
        height,
        dilated_low,
        first_act,
        dilated_weight,
        reduced,
        one,
        flat,
        reduce_weight,
        pre_low,
        expand_part,
    )
    one_shift_grad, one_gain_grad = sums_one.reshape(2, 1, middle)
    grad_features = grad_features.reshape(height, width, channels)
    sep_sum, point_sum, grad_expand_weight, dilated_wide, reduce_wide = widen(
        early_sum, expand_sum, dilated_sum, reduce_sum, channels, aspp_width
    )
    at = 2 * channels
    tables = []
    for size, extent in ((proj_weight.shape[0], aspp_width), (channels, LANES), (aspp_width, LANES)):
        blocks = 2 * aspp_width // extent
        table = early_sum[at : at + size // blocks].reshape(size // blocks, blocks, extent)
        table = table.astype(jnp.float32)
        tables.append(jnp.transpose(table, (1, 0, 2)).reshape(size, extent))
        at += size // blocks
    summed = [
        reduce_wide,
        dilated_wide.reshape(9, middle, middle),
        grad_expand_weight,
        point_sum,
        tables[1][:, :27].T.reshape(3, 9, channels),
        sep_sum,
        tables[0],
        tables[2],
    ]
    grad_mid_gain = jnp.concatenate([one_gain_grad, two_gain_grad], axis=0)
    grad_mid_shift = jnp.concatenate([one_shift_grad, two_shift_grad], axis=0)
    grad_aspp_gain = jnp.concatenate([branch_gain_grad, proj_gain_grad], axis=0)
    grad_aspp_shift = jnp.concatenate([branch_shift_grad, proj_shift_grad], axis=0)
    return (
        objective,
        grad_features,
        summed[0],
        summed[1],
        summed[2],
        grad_mid_gain,
        grad_mid_shift,
        out_gain_grad[0],
        out_shift_grad[0],
        summed[3],
        summed[4],
        summed[5],
        grad_pool_weight,
        summed[6],
        grad_aspp_gain,
        grad_aspp_shift,
        summed[7][:, : head_weight.shape[1]],
        grad_head_bias,
        grad_scales,
    )


def solution(mesh):
    in_specs = (
        P("rows", "cols", None),
        P(),
        P(),
        P(),
        P(),
        P(),
        P(),
        P(),
        P(),
        P(),
        P(),
        P(),
        P(),
        P(),
        P(),
        P(),
        P(),
        P(),
        P("rows", "cols"),
        P("rows", "cols"),
        P("rows", "cols"),
        P("rows", "cols"),
        P(None, "rows", "cols"),
    )
    out_specs = (
        P(),
        P("rows", "cols", None),
        P(),
        P(),
        P(),
        P(),
        P(),
        P(),
        P(),
        P(),
        P(),
        P(),
        P(),
        P(),
        P(),
        P(),
        P(),
        P(),
        P(),
    )
    return jax.shard_map(
        on_device, mesh=mesh, in_specs=in_specs, out_specs=out_specs, check_vma=False
    )
```

```python
import functools

import jax
import jax.numpy as jnp
from jax import lax
from jax.experimental import pallas as pl
from jax.experimental.pallas import tpu as pltpu
from jax.sharding import PartitionSpec as P

CLASSES = 13
CROPS = 16
MID_RATE = 4
BASE_RATE = 12
LANES = 128

EPS = 1e-05
MESH = pl.DeviceIdType.MESH


def gate_slope(value):
    sigma = jax.nn.sigmoid(value)
    return sigma * (1.0 + value * (1.0 - sigma))


PAD = 48
VMEM_BYTES = 60 * 1024 * 1024


def place():
    rows, cols = lax.axis_size("rows"), lax.axis_size("cols")
    row, col = lax.axis_index("rows"), lax.axis_index("cols")
    return rows, cols, row, col, row * cols + col


def greet_all():
    rows, cols, row, col, me = place()
    barrier = pltpu.get_barrier_semaphore()

    def greet(step, carry):
        other = lax.rem(me + step, rows * cols)
        pl.semaphore_signal(
            barrier, inc=1, device_id=(other // cols, lax.rem(other, cols)), device_id_type=MESH
        )
        return carry

    lax.fori_loop(1, rows * cols, greet, 0)


def await_all():
    rows, cols = lax.axis_size("rows"), lax.axis_size("cols")
    pl.semaphore_wait(pltpu.get_barrier_semaphore(), rows * cols - 1)


def share(slots, sems):
    rows, cols, row, col, me = place()

    def go(step, carry):
        other = lax.rem(me + step, rows * cols)
        pltpu.make_async_remote_copy(
            slots.at[me],
            slots.at[me],
            sems.at[0],
            sems.at[1],
            device_id=(other // cols, lax.rem(other, cols)),
            device_id_type=MESH,
        ).start()
        return carry

    lax.fori_loop(1, rows * cols, go, 0)


def shared(slots, sems):
    rows, cols, row, col, me = place()
    others = slots.at[pl.ds(0, rows * cols - 1)]
    pltpu.make_async_remote_copy(
        others,
        others,
        sems.at[0],
        sems.at[1],
        device_id=(row, lax.rem(col + 1, cols)),
        device_id_type=MESH,
    ).wait()


def share_column(slots, sems):
    rows, cols, row, col, me = place()

    def go(step, carry):
        other = lax.rem(row + step, rows)
        pltpu.make_async_remote_copy(
            slots.at[row],
            slots.at[row],
            sems.at[0],
            sems.at[1],
            device_id=(other, col),
            device_id_type=MESH,
        ).start()
        return carry

    lax.fori_loop(1, rows, go, 0)


def shared_column(slots, sems):
    rows, cols, row, col, me = place()
    others = slots.at[pl.ds(0, rows - 1)]
    pltpu.make_async_remote_copy(
        others,
        others,
        sems.at[0],
        sems.at[1],
        device_id=(lax.rem(row + 1, rows), col),
        device_id_type=MESH,
    ).wait()


class PairSum:
    def __init__(self, own, pair, slots, all_, sems):
        self.own, self.pair, self.slots, self.all_, self.sems = own, pair, slots, all_, sems
        self.rows, self.cols, self.row, self.col, _ = place()

    def to_pair(self, src, dst, at):
        return pltpu.make_async_remote_copy(
            src,
            dst,
            self.sems.at[at, 0],
            self.sems.at[at, 1],
            device_id=(self.row, 1 - self.col),
            device_id_type=MESH,
        )

    def out_copy(self):
        return self.to_pair(self.own.at[1 - self.col], self.pair, 0)

    def back_copy(self):
        return self.to_pair(self.all_.at[self.col], self.all_.at[self.col], 2)

    def put(self, value):
        self.own[0] = value[:, :LANES]
        self.own[1] = value[:, LANES:]

    def start(self):
        self.out_copy().start()

    def start_column(self):
        self.out_copy().wait()
        self.slots[self.row] = self.own[self.col] + self.pair[...]
        share_column(self.slots, self.sems.at[1])

    def start_back(self):
        shared_column(self.slots, self.sems.at[1])
        self.all_[self.col] = jnp.sum(self.slots[...], axis=0)
        self.back_copy().start()

    def finish(self):
        self.back_copy().wait()
        return jnp.concatenate([self.all_[0], self.all_[1]], axis=1)


def pair_sum_scratch(count):
    wide = jnp.float32
    return [
        pltpu.VMEM((2, count, LANES), wide),
        pltpu.VMEM((count, LANES), wide),
        pltpu.VMEM((lax.axis_size("rows"), count, LANES), wide),
        pltpu.VMEM((2, count, LANES), wide),
        pltpu.SemaphoreType.DMA((3, 2)),
    ]


def put_row(slots, me, at, vector):
    for part in range(vector.shape[1] // LANES):
        slots[me, at + part : at + part + 1, :] = vector[:, part * LANES : (part + 1) * LANES]


def take_row(table, at, width):
    parts = [table[at + part : at + part + 1, :] for part in range(width // LANES)]
    return parts[0] if len(parts) == 1 else jnp.concatenate(parts, axis=1)


def merged(slots, half, share_size, count):
    center = jnp.mean(slots[:, :half, :], axis=0)
    apart = slots[:, :half, :] - center[None]
    spread = jnp.sum(slots[:, half : 2 * half, :], axis=0) + share_size * jnp.sum(apart * apart, axis=0)
    return center, lax.rsqrt(spread / count + EPS)


def sigmoid(value):
    return 1.0 / (1.0 + jnp.exp(-value))


def across(left, right):
    return lax.dot_general(left, right, (((1,), (1,)), ((), ())), preferred_element_type=jnp.float32)


def down(left, right):
    return lax.dot_general(left, right, (((0,), (0,)), ((), ())), preferred_element_type=jnp.float32)


def pyramid_kernel(
    height,
    trunk,
    depth,
    sep_point,
    aspp_point,
    crop_part,
    count_sums,
    members,
    proj_weight,
    gains,
    shifts,
    head_raw,
    bias_raw,
    weights,
    labels,
    boundary,
    valid_mask,
    geometry,
    crop_sums,
    branch_low,
    proj_part,
    head_part,
    crop_local,
    crop_pre,
    sums_five,
    sums_four,
    crop_table,
    own_low,
    closing,
    head_weight,
    head_bias,
    field,
    send_main,
    recv_main,
    send_side,
    recv_side,
    pre,
    joined,
    crop_act,
    projected,
    united,
    head_low,
    upstream,
    proj_low,
    branch_up,
    four_slots,
    five_slots,
    back_five,
    back_four,
    crop_pieces,
    main_sems,
    side_sems,
    four_sems,
    five_sems,
    back_five_sems,
    back_four_sems,
    piece_sems,
    table_sems,
    *crop_refs,
):
    rows, cols, row, col, me = place()
    low, wide = jnp.bfloat16, jnp.float32
    pixels = trunk.shape[0]
    width = pixels // height
    share_size = float(pixels)
    count = float(pixels * rows * cols)
    aspp = sep_point.shape[2]
    greet_all()

    def exists(target):
        return jnp.logical_and(target >= 0, target < rows)

    def step_of(index):
        return (BASE_RATE // height) * (index + 1)

    for index in range(3):
        step = BASE_RATE * (index + 1) // height
        for way in (0, 2):

            @pl.when(jnp.logical_not(exists(row - (1 - way) * step)))
            def _():
                recv_main[index, way] = jnp.zeros(recv_main.shape[2:], low)

    half = crop_part.shape[0]
    crop_total = PairSum(*crop_refs)
    crop_total.put(crop_part[...])
    pre[0] = jnp.dot(trunk[...], aspp_point[...], preferred_element_type=wide)
    await_all()
    crop_total.start()
    crop_pieces[me] = crop_sums[me]

    def scatter(step, carry):
        other = lax.rem(me + step, rows * cols)
        pltpu.make_async_remote_copy(
            crop_sums.at[other],
            crop_pieces.at[me],
            piece_sems.at[0],
            piece_sems.at[1],
            device_id=(other // cols, lax.rem(other, cols)),
            device_id_type=MESH,
        ).start()
        return carry

    lax.fori_loop(1, rows * cols, scatter, 0)
    side_from = pl.multiple_of((1 - col) * (PAD + width), 16)
    side_to = pl.multiple_of((1 - col) * (width - PAD), 16)

    def main_copy(index, way):
        return pltpu.make_async_remote_copy(
            send_main.at[index, way],
            recv_main.at[index, way],
            main_sems.at[0, index, way],
            main_sems.at[1, index, way],
            device_id=(row + (1 - way) * step_of(index), col),
            device_id_type=MESH,
        )

    def side_copy(index, way):
        return pltpu.make_async_remote_copy(
            send_side.at[index, way],
            recv_side.at[index, way],
            side_sems.at[0, index, way],
            side_sems.at[1, index, way],
            device_id=(row, 1 - col),
            device_id_type=MESH,
        )

    def flush(number):
        own = number // 6
        index = (1 - own) * (2 - number // 2) + own * (8 - number)
        way = (1 - own) * 2 * lax.rem(number, 2) + own
        side_copy(index, way).wait_recv()

        @pl.when(way == 1)
        def _():
            for line in range(height):
                edge = pl.ds(pl.multiple_of(line * width + side_to, 16), PAD)
                pre[index + 1, edge, :] += recv_side[index, way, line].astype(wide)

        @pl.when(way != 1)
        def _():
            edge = pl.ds(side_to, PAD)
            send_main[index, way, :, edge, :] = (
                send_main[index, way, :, edge, :].astype(wide) + recv_side[index, way].astype(wide)
            ).astype(low)

            @pl.when(exists(row + (1 - way) * step_of(index)))
            def _():
                main_copy(index, way).start()

    for index, own in ((2, 0), (1, 0), (0, 0), (2, 1), (1, 1), (0, 1)):
        rate = BASE_RATE * (index + 1)

        def one_way(turn, carry):
            way = 1 if own else 2 * turn
            for sign in (0, 1, -1):
                tap = depth[pl.ds(index * 9 + 3 * way + 1 - sign, 1), :].astype(low)
                made = jnp.dot(trunk[...] * tap, sep_point[index], preferred_element_type=wide)
                for line in range(height):
                    part = made[line * width : (line + 1) * width, :]
                    if sign == 0:
                        field[line, PAD : PAD + width, :] = part
                        field[line, :PAD, :] = jnp.zeros((PAD, aspp), wide)
                        field[line, PAD + width :, :] = jnp.zeros((PAD, aspp), wide)
                    else:
                        at = PAD + sign * rate
                        field[line, at : at + width, :] += part
            send_side[index, way] = field[:, pl.ds(side_from, PAD), :].astype(low)

            if own:
                for line in range(height):
                    pre[index + 1, line * width : (line + 1) * width, :] = field[
                        line, PAD : PAD + width, :
                    ]
            else:
                send_main[index, way] = field[:, PAD : PAD + width, :].astype(low)
            side_copy(index, way).start()
            number = turn + (8 - index if own else 2 * (2 - index))

            @pl.when(number > 0)
            def _():
                flush(number - 1)

            return carry

        lax.fori_loop(0, 1 if own else 2, one_way, 0)
    flush(jnp.int32(8))
    crop_total.start_column()

    def lines(body, carry=0):
        def run(line, carry):
            return body(line, pl.ds(pl.multiple_of(line * width, width), width), carry)

        return lax.fori_loop(0, height, run, carry)

    zero_row = jnp.zeros((1, aspp), wide)

    def statistics(value_of, slots, at, half_rows):
        total = lines(
            lambda line, span, acc: acc + jnp.sum(value_of(span), axis=0, keepdims=True), zero_row
        )
        mean = total / share_size

        def squares(line, span, acc):
            apart = value_of(span) - mean
            return acc + jnp.sum(apart * apart, axis=0, keepdims=True)

        put_row(slots, me, at, mean)
        put_row(slots, me, half_rows + at, lines(squares, zero_row))

    per = aspp // LANES
    statistics(lambda span: pre[0, span, :], four_slots, 0, 4 * per)
    for index in (2, 1, 0):
        for way in (0, 2):

            @pl.when(exists(row - (1 - way) * step_of(index)))
            def _():
                main_copy(index, way).wait_recv()

        def assemble(line, span, carry):
            pre[index + 1, span, :] += recv_main[index, 0, line].astype(wide) + recv_main[
                index, 2, line
            ].astype(wide)
            return carry

        lines(assemble)
        statistics(lambda span: pre[index + 1, span, :], four_slots, per * (index + 1), 4 * per)
    share(four_slots, four_sems)
    crop_total.start_back()
    shared(crop_pieces, piece_sems)
    crop_table[me] = jnp.sum(crop_pieces[...], axis=0)
    share(crop_table, table_sems)
    crop_row = lax.broadcasted_iota(jnp.int32, (half, LANES), 0)
    crop_lane = lax.broadcasted_iota(jnp.int32, (half, LANES), 1)
    crop_count = jnp.sum(
        jnp.where(crop_row == crop_lane, count_sums[0:1, :], 0.0), axis=1, keepdims=True
    )
    crop_value = crop_total.finish() / crop_count
    crop_pre[...] = crop_value
    crop_act[...] = jnp.zeros(crop_act.shape, low)
    crop_act[:half, :] = (crop_value * sigmoid(crop_value)).astype(low)

    def spread(line, span, carry):
        joined[span, 4 * aspp :] = jnp.dot(
            members[span, :], crop_act[...], preferred_element_type=wide
        ).astype(low)
        return carry

    lines(spread)
    shared(four_slots, four_sems)
    center_four, scale_four = merged(four_slots, 4 * per, share_size, count)
    centers = [take_row(center_four, per * part, aspp) for part in range(4)]
    scales = [take_row(scale_four, per * part, aspp) for part in range(4)]

    def activate(line, span, carry):
        for part in range(4):
            normed = (pre[part, span, :] - centers[part]) * scales[part]
            gated = normed * gains[part : part + 1, :] + shifts[part : part + 1, :]
            joined[span, part * aspp : (part + 1) * aspp] = (gated * sigmoid(gated)).astype(low)
        return carry

    lines(activate)
    projected[...] = jnp.dot(joined[...], proj_weight[...], preferred_element_type=wide)
    five_slots[me] = jnp.zeros(five_slots.shape[1:], wide)
    statistics(lambda span: projected[span, :], five_slots, 0, per)
    share(five_slots, five_sems)
    shared(five_slots, five_sems)
    center_five, scale_five = merged(five_slots, per, share_size, count)
    center_five, scale_five = take_row(center_five, 0, aspp), take_row(scale_five, 0, aspp)
    gain_five, shift_five = gains[4:5, :], shifts[4:5, :]
    lane = lax.broadcasted_iota(jnp.int32, (width, LANES), 1)
    outs = head_raw.shape[1]
    head_weight[...] = jnp.zeros(head_weight.shape, low)
    head_weight[:, :outs] = head_raw[...]
    head_bias[...] = jnp.zeros(head_bias.shape, wide)
    head_bias[0:1, :outs] = bias_raw[...]
    one_lane = lax.broadcasted_iota(jnp.int32, (1, LANES), 1)
    pixel_count = jnp.where(
        one_lane < CLASSES, count_sums[0:1, CROPS : CROPS + 1], count_sums[0:1, CROPS + 1 : CROPS + 2]
    )
    factors = weights[0:1, :] / pixel_count

    def heads_of(line, span, carry):
        losses, bias_sum, shift_sum, gain_sum = carry
        normed = (projected[span, :] - center_five) * scale_five
        gated = normed * gain_five + shift_five
        sigma = sigmoid(gated)
        act = (gated * sigma).astype(low)
        united[span, :] = act
        heads = jnp.dot(act, head_weight[...], preferred_element_type=wide) + head_bias[0:1, :]
        row_of = pl.ds(line, 1)
        facts = jnp.concatenate(
            [
                labels[row_of, :].astype(wide),
                1.0 - boundary[row_of, :].astype(wide),
                valid_mask[row_of, :].astype(wide),
                *[geometry[part, row_of, :] for part in range(4)],
                jnp.zeros((1, width), wide),
            ],
            axis=0,
        ).T
        label, keep, valid = facts[:, 0:1], facts[:, 1:2], facts[:, 2:3]
        is_class = lane < CLASSES
        hot = jnp.where(lane.astype(wide) == label, 1.0, 0.0)
        target = jnp.zeros((width, LANES), wide)
        for part in range(4):
            target = jnp.where(lane == CLASSES + part, facts[:, 3 + part : 4 + part], target)
        top = jnp.max(jnp.where(is_class, heads, -jnp.inf), axis=1, keepdims=True)
        exps = jnp.where(is_class, jnp.exp(heads - top), 0.0)
        totals = jnp.sum(exps, axis=1, keepdims=True)
        picked = jnp.sum(jnp.where(is_class, heads, 0.0) * hot, axis=1, keepdims=True)
        error = jnp.where(is_class, 0.0, heads - target)
        root = jnp.sqrt(error * error + 1.0)
        is_depth, is_normal = lane == CLASSES, jnp.logical_and(lane > CLASSES, lane < CLASSES + 4)
        semantic = keep * (top + jnp.log(totals) - picked)
        terms = jnp.where(lane == 0, semantic, 0.0)
        terms = jnp.where(is_depth, valid * (root - 1.0), terms)
        terms = jnp.where(is_normal, valid * error * error, terms)
        grad = jnp.where(is_class, keep * (exps / totals - hot), 0.0)
        grad = jnp.where(is_depth, valid * error / root, grad)
        grad = jnp.where(is_normal, valid * error, grad)
        grad = grad * factors
        grad_low = grad.astype(low)
        head_low[span, :] = grad_low
        up = across(grad_low, head_weight[...]) * (sigma * (1.0 + gated * (1.0 - sigma)))
        upstream[span, :] = up
        return (
            losses + jnp.sum(terms, axis=0, keepdims=True),
            bias_sum + jnp.sum(grad, axis=0, keepdims=True),
            shift_sum + jnp.sum(up, axis=0, keepdims=True),
            gain_sum + jnp.sum(up * normed, axis=0, keepdims=True),
        )

    zero_lane = jnp.zeros((1, LANES), wide)
    losses, bias_sum, shift_sum, gain_sum = lines(
        heads_of, (zero_lane, zero_lane, zero_row, zero_row)
    )
    back_five[me] = jnp.zeros(back_five.shape[1:], wide)
    put_row(back_five, me, 0, shift_sum)
    put_row(back_five, me, per, gain_sum)
    put_row(back_five, me, 2 * per, losses)
    put_row(back_five, me, 2 * per + 1, bias_sum)
    share(back_five, back_five_sems)
    head_part[...] = down(united[...], head_low[...]).astype(low)
    shared(back_five, back_five_sems)
    total_five = jnp.sum(back_five[...], axis=0)
    sums_five[...] = total_five
    weighted = weights[1:2, :] * total_five[2 * per : 2 * per + 1, :] / pixel_count

    def lanes_sum(row_value, first, last):
        picked = jnp.where(jnp.logical_and(one_lane >= first, one_lane < last), row_value, 0.0)
        return jnp.sum(picked, axis=1, keepdims=True)

    tasks = (
        lanes_sum(weighted, 0, 1),
        lanes_sum(weighted, CLASSES, CLASSES + 1),
        lanes_sum(weighted, CLASSES + 1, CLASSES + 4),
    )
    closing[...] = jnp.zeros(closing.shape, wide)
    for part in range(3):
        closing[0:1, part : part + 1] = tasks[part] - 1.0
    closing[1:2, 0:1] = tasks[0] + tasks[1] + tasks[2] - lanes_sum(weights[2:3, :], 0, 3)
    shift_mean = take_row(total_five, 0, aspp) / count
    gain_mean = take_row(total_five, per, aspp) / count

    def project_back(line, span, carry):
        normed = (projected[span, :] - center_five) * scale_five
        inner = upstream[span, :] - shift_mean - normed * gain_mean
        proj_low[span, :] = (inner * (gain_five * scale_five)).astype(low)
        return carry

    lines(project_back)
    for part in range(4):
        branch_up[part] = across(
            proj_low[...], proj_weight[part * aspp : (part + 1) * aspp, :]
        )
    crop_up = across(proj_low[...], proj_weight[4 * aspp :, :])
    crop_high = crop_up.astype(low)
    crop_rest = (crop_up - crop_high.astype(wide)).astype(low)
    crop_sum = down(members[...], crop_high) + down(members[...], crop_rest)
    crop_local[...] = crop_sum[:half, :]

    for part in range(4):

        def branch_sums(line, span, carry):
            shift_sum, gain_sum = carry
            normed = (pre[part, span, :] - centers[part]) * scales[part]
            gated = normed * gains[part : part + 1, :] + shifts[part : part + 1, :]
            sigma = sigmoid(gated)
            up = branch_up[part, span, :] * (sigma * (1.0 + gated * (1.0 - sigma)))
            branch_up[part, span, :] = up
            return (
                shift_sum + jnp.sum(up, axis=0, keepdims=True),
                gain_sum + jnp.sum(up * normed, axis=0, keepdims=True),
            )

        shift_sum, gain_sum = lines(branch_sums, (zero_row, zero_row))
        put_row(back_four, me, per * part, shift_sum)
        put_row(back_four, me, per * (4 + part), gain_sum)
    share(back_four, back_four_sems)
    proj_part[...] = down(joined[...], proj_low[...]).astype(low)
    shared(back_four, back_four_sems)
    total_four = jnp.sum(back_four[...], axis=0)
    sums_four[...] = total_four
    for part in range(4):
        shift_mean = take_row(total_four, per * part, aspp) / count
        gain_mean = take_row(total_four, per * (4 + part), aspp) / count
        factor = gains[part : part + 1, :] * scales[part]

        def branch_back(line, span, carry):
            normed = (pre[part, span, :] - centers[part]) * scales[part]
            inner = branch_up[part, span, :] - shift_mean - normed * gain_mean
            value = (inner * factor).astype(low)
            branch_low[part, span, :] = value
            if part == 0:
                own_low[span, :] = value
            return carry

        lines(branch_back)
    shared(crop_table, table_sems)
    for index in range(3):
        for way in range(3):
            side_copy(index, way).wait_send()
        for way in (0, 2):

            @pl.when(exists(row + (1 - way) * step_of(index)))
            def _():
                main_copy(index, way).wait_send()


def pyramid(height, trunk, depth, sep_point, aspp_point, crop_part, count_sums, members, proj_weight,
            gains, shifts, head_weight, head_bias, weights, labels, boundary, valid, geometry, crop_sums):
    devices = lax.axis_size("rows") * lax.axis_size("cols")
    pixels = trunk.shape[0]
    width = pixels // height
    aspp = sep_point.shape[2]
    crops = crop_part.shape[0]
    low, wide = jnp.bfloat16, jnp.float32
    shape = jax.ShapeDtypeStruct
    whole = pl.BlockSpec(memory_space=pltpu.VMEM)
    joined = proj_weight.shape[0]
    per = aspp // LANES
    outs = (
        shape((4, pixels, aspp), low),
        shape((joined, aspp), low),
        shape((aspp, LANES), low),
        shape((crops, aspp), wide),
        shape((crops, aspp), wide),
        shape((8, LANES), wide),
        shape((8 * per, LANES), wide),
        shape(crop_sums.shape, wide),
        shape((pixels, aspp), low),
        shape((8, LANES), wide),
    )
    sems = pltpu.SemaphoreType.DMA
    return pl.pallas_call(
        functools.partial(pyramid_kernel, height),
        out_shape=outs,
        in_specs=[whole] * 18,
        out_specs=(whole,) * len(outs),
        scratch_shapes=[
            pltpu.VMEM((aspp, LANES), low),
            pltpu.VMEM((8, LANES), wide),
            pltpu.VMEM((height, width + 2 * PAD, aspp), wide),
            pltpu.VMEM((3, 3, height, width, aspp), low),
            pltpu.VMEM((3, 3, height, width, aspp), low),
            pltpu.VMEM((3, 3, height, PAD, aspp), low),
            pltpu.VMEM((3, 3, height, PAD, aspp), low),
            pltpu.VMEM((4, pixels, aspp), wide),
            pltpu.VMEM((pixels, joined), low),
            pltpu.VMEM((LANES, aspp), low),
            pltpu.VMEM((pixels, aspp), wide),
            pltpu.VMEM((pixels, aspp), low),
            pltpu.VMEM((pixels, LANES), low),
            pltpu.VMEM((pixels, aspp), wide),
            pltpu.VMEM((pixels, aspp), low),
            pltpu.VMEM((4, pixels, aspp), wide),
            pltpu.VMEM((devices, 8 * per, LANES), wide),
            pltpu.VMEM((devices, 8, LANES), wide),
            pltpu.VMEM((devices, 8, LANES), wide),
            pltpu.VMEM((devices, 8 * per, LANES), wide),
            pltpu.VMEM(crop_sums.shape, wide),
            sems((2, 3, 3)),
            sems((2, 3, 3)),
            sems((2,)),
            sems((2,)),
            sems((2,)),
            sems((2,)),
            sems((2,)),
            sems((2,)),
            *pair_sum_scratch(crops),
        ],
        compiler_params=pltpu.CompilerParams(
            collective_id=10, has_side_effects=True, vmem_limit_bytes=VMEM_BYTES
        ),
        cost_estimate=pl.CostEstimate(
            flops=100 * pixels * trunk.shape[1] * aspp, bytes_accessed=64 * pixels * trunk.shape[1], transcendentals=0
        ),
        name="pyramid",
    )(trunk, depth, sep_point, aspp_point, crop_part, count_sums, members, proj_weight, gains, shifts,
      head_weight, head_bias, weights, labels, boundary, valid, geometry, crop_sums)


def pyramid_weights_kernel(
    branch_low,
    trunk,
    depth,
    sep_point,
    crop_local,
    proj_part,
    head_part,
    near,
    early,
    crop_total,
    depth_part,
    turned,
    shifted,
    moved,
    gathered,
    main_sems,
    edge_sems,
    *crop_refs,
):
    rows, cols, row, col, me = place()
    low, wide = jnp.bfloat16, jnp.float32
    height, width, aspp = branch_low.shape[1:]
    pixels, channels = trunk.shape
    crop_sum = PairSum(*crop_refs)
    crop_sum.put(crop_local[...])
    greet_all()

    def exists(target):
        return jnp.logical_and(target >= 0, target < rows)

    def step_of(index):
        return BASE_RATE * (index + 1) // height

    edge_from = pl.multiple_of(PAD + (1 - col) * (width - PAD), 16)
    edge_to = pl.multiple_of(col * (width + PAD), 16)
    blank = pl.multiple_of(col * (width + PAD), 16)

    def main_copy(index, way):
        return pltpu.make_async_remote_copy(
            branch_low.at[index + 1],
            near.at[index, way, :, pl.ds(PAD, width), :],
            main_sems.at[0, index, way],
            main_sems.at[1, index, way],
            device_id=(row + (1 - way) * step_of(index), col),
            device_id_type=MESH,
        )

    def edge_copy(index, way):
        return pltpu.make_async_remote_copy(
            near.at[index, way, :, pl.ds(edge_from, PAD), :],
            near.at[index, way, :, pl.ds(edge_to, PAD), :],
            edge_sems.at[0, index, way],
            edge_sems.at[1, index, way],
            device_id=(row, 1 - col),
            device_id_type=MESH,
        )

    for index in range(3):
        for way in range(3):
            near[index, way, :, pl.ds(blank, PAD), :] = jnp.zeros((height, PAD, aspp), low)
            if way == 1:
                near[index, way, :, PAD : PAD + width, :] = branch_low[index + 1]
            else:

                @pl.when(jnp.logical_not(exists(row - (1 - way) * step_of(index))))
                def _():
                    near[index, way] = jnp.zeros(near.shape[2:], low)

    await_all()
    for index in range(3):
        edge_copy(index, 1).start()

    def send(index):
        for way in (0, 2):

            @pl.when(exists(row + (1 - way) * step_of(index)))
            def _():
                main_copy(index, way).start()

    send(0)
    crop_sum.start()

    def turn(block, carry):
        span = pl.ds(pl.multiple_of(block * width, width), width)
        for line in range(height):
            turned[span, line * width : (line + 1) * width] = trunk[
                line * width : (line + 1) * width, span
            ].T
        return carry

    lax.fori_loop(0, channels // width, turn, 0)
    part_rows = channels // 2

    def point(part, carry):
        span = pl.ds(pl.multiple_of(part * part_rows, part_rows), part_rows)
        own = branch_low[0].reshape(pixels, aspp)
        early[pl.ds(pl.multiple_of(channels + part * part_rows, part_rows), part_rows), aspp:] = jnp.dot(
            turned[span, :], own, preferred_element_type=wide
        ).astype(low)
        return carry

    lax.fori_loop(0, 2, point, 0)
    lane = lax.broadcasted_iota(jnp.int32, (part_rows, LANES), 1)
    depth_part[...] = jnp.zeros(depth_part.shape, wide)
    gathered[...] = jnp.zeros(gathered.shape, wide)
    for index, way in ((0, 1), (1, 1), (2, 1), (0, 0), (0, 2), (1, 0), (1, 2), (2, 0), (2, 2)):
        rate = BASE_RATE * (index + 1)

        if way != 1:

            @pl.when(exists(row - (1 - way) * step_of(index)))
            def _():
                main_copy(index, way).wait_recv()
                edge_copy(index, way).start()

        for side in (1, 0, 2):
            if side == 0:

                @pl.when(exists(row - (1 - way) * step_of(index)))
                def _():
                    edge_copy(index, way).wait_recv()

                shifted[...] = near[index, way].astype(wide)
            tap = 3 * (2 - way) + side
            at = PAD - (side - 1) * rate
            for line in range(height):
                if side == 1:
                    piece = near[index, way, line, PAD : PAD + width, :]
                else:
                    piece = shifted[line, at : at + width, :].astype(low)
                moved[line * width : (line + 1) * width, :] = piece
            order = 9 * index + tap

            def collect(part, carry):
                span = pl.ds(pl.multiple_of(part * part_rows, part_rows), part_rows)
                made = jnp.dot(turned[span, :], moved[...], preferred_element_type=wide)
                gathered[index, span, :] += made * depth[span, order : order + 1]
                total = jnp.sum(made * sep_point[index, span, :].astype(wide), axis=1, keepdims=True)
                depth_part[span, :] = jnp.where(lane == order, total, depth_part[span, :])
                return carry

            lax.fori_loop(0, 2, collect, 0)
        if way == 1 and index == 1:
            send(1)
        if way == 2 and index == 0:
            send(2)
        if way == 1 and index == 0:
            crop_sum.start_column()
        if way == 0 and index == 0:
            crop_sum.start_back()
    early[:channels, :aspp] = gathered[0].astype(low)
    early[:channels, aspp:] = gathered[1].astype(low)
    early[channels : 2 * channels, :aspp] = gathered[2].astype(low)
    at = 2 * channels
    for table in (proj_part, depth_part, head_part):
        extent = table.shape[1]
        blocks = 2 * aspp // extent
        size = table.shape[0] // blocks
        for block in range(blocks):
            early[at : at + size, block * extent : (block + 1) * extent] = table[
                block * size : (block + 1) * size, :
            ].astype(low)
        at += size
    if early.shape[0] > at:
        early[at:, :] = jnp.zeros((early.shape[0] - at, 2 * aspp), low)
    crop_total[...] = crop_sum.finish()
    for index in range(3):
        for way in range(3):

            @pl.when(exists(row - (1 - way) * step_of(index)))
            def _():
                edge_copy(index, way).wait_send()

            if way != 1:

                @pl.when(exists(row + (1 - way) * step_of(index)))
                def _():
                    main_copy(index, way).wait_send()


def early_rows(channels, proj_part, head_part):
    rows = 2 * channels
    for size, extent in ((proj_part.shape[0], proj_part.shape[1]), (channels, LANES), head_part.shape):
        rows += size * extent // (2 * proj_part.shape[1])
    return rows


def pyramid_weights(branch_low, trunk, depth, sep_point, crop_local, proj_part, head_part):
    height, width, aspp = branch_low.shape[1:]
    pixels, channels = trunk.shape
    crops = crop_local.shape[0]
    low, wide = jnp.bfloat16, jnp.float32
    shape = jax.ShapeDtypeStruct
    whole = pl.BlockSpec(memory_space=pltpu.VMEM)
    sems = pltpu.SemaphoreType.DMA
    outs = (
        shape((3, 3, height, width + 2 * PAD, aspp), low),
        shape((sum_rows(early_rows(channels, proj_part, head_part)), 2 * aspp), low),
        shape((crops, aspp), wide),
    )
    return pl.pallas_call(
        pyramid_weights_kernel,
        out_shape=outs,
        in_specs=[whole] * 7,
        out_specs=(whole,) * len(outs),
        scratch_shapes=[
            pltpu.VMEM((channels, LANES), wide),
            pltpu.VMEM((channels, pixels), low),
            pltpu.VMEM((height, width + 2 * PAD, aspp), wide),
            pltpu.VMEM((pixels, aspp), low),
            pltpu.VMEM((3, channels, aspp), wide),
            sems((2, 3, 3)),
            sems((2, 3, 3)),
            *pair_sum_scratch(crops),
        ],
        compiler_params=pltpu.CompilerParams(
            collective_id=11, has_side_effects=True, vmem_limit_bytes=VMEM_BYTES
        ),
        cost_estimate=pl.CostEstimate(
            flops=100 * pixels * channels * aspp, bytes_accessed=64 * pixels * channels, transcendentals=0
        ),
        name="pyramid_weights",
    )(branch_low, trunk, depth, sep_point, crop_local, proj_part, head_part)


def share_rows(slots, at, size, sems):
    rows, cols, row, col, me = place()

    def go(step, carry):
        other = lax.rem(me + step, rows * cols)
        mine = slots.at[me, pl.ds(at, size), :]
        pltpu.make_async_remote_copy(
            mine,
            mine,
            sems.at[0],
            sems.at[1],
            device_id=(other // cols, lax.rem(other, cols)),
            device_id_type=MESH,
        ).start()
        return carry

    lax.fori_loop(1, rows * cols, go, 0)


def shared_rows(slots, at, size, sems):
    rows, cols, row, col, me = place()
    others = slots.at[pl.ds(0, rows * cols - 1), pl.ds(at, size), :]
    pltpu.make_async_remote_copy(
        others,
        others,
        sems.at[0],
        sems.at[1],
        device_id=(row, lax.rem(col + 1, cols)),
        device_id_type=MESH,
    ).wait()


def trunk_back_kernel(
    near,
    own_low,
    depth,
    sep_point,
    aspp_point,
    members,
    crop_high,
    crop_rest,
    expanded,
    features,
    three,
    dilated,
    two,
    second_act,
    expand_weight,
    early,
    pre_grad,
    expand_part,
    dilated_low,
    sums_three,
    sums_two,
    early_out,
    fetched,
    chunk_in,
    shifted,
    moved,
    maps,
    grown,
    expand_low,
    slots_three,
    slots_two,
    sems_three,
    sems_two,
    fetch_sems,
    chunk_sems,
    *early_refs,
):
    rows, cols, row, col, me = place()
    low, wide = jnp.bfloat16, jnp.float32
    height = near.shape[2]
    early_sum = Sums(early, True, early_out, early_refs)
    aspp = sep_point.shape[2]
    pixels, channels = expanded.shape
    middle = dilated.shape[1]
    width = pixels // height
    count = float(pixels * rows * cols)
    per = aspp // LANES
    chunks = channels // aspp
    greet_all()

    def fetch(number):
        return pltpu.make_async_copy(
            near.at[number // 3, number % 3], fetched.at[number % 2], fetch_sems.at[number % 2]
        )

    fetch(0).start()
    early_sum.fetch()

    def chunk_of(block):
        return pl.ds(pl.multiple_of(block * aspp, aspp), aspp)

    def own(block, carry):
        span = chunk_of(block)
        grown[:, span] = (
            across(own_low[...], aspp_point[span, :])
            + jnp.dot(members[...], crop_high[:, span], preferred_element_type=wide)
            + jnp.dot(members[...], crop_rest[:, span], preferred_element_type=wide)
        )
        return carry

    lax.fori_loop(0, chunks, own, 0)
    await_all()
    early_sum.fetched()
    early_sum.start_half()

    def fetch_chunk(block):
        slot = lax.rem(block, 2)
        return pltpu.make_async_copy(
            expanded.at[:, chunk_of(block)], chunk_in.at[slot], chunk_sems.at[slot]
        )

    def advance(block):
        @pl.when(block + 1 < chunks)
        def _():
            fetch_chunk(block + 1).start()

        fetch_chunk(block).wait()

    def back(block, line, span):
        rows_span = slice(line * width, (line + 1) * width)
        value = chunk_in[lax.rem(block, 2), rows_span, :]
        normed = (value - three[0:1, span]) * three[1:2, span]
        return rows_span, normed

    for index in range(3):
        rate = BASE_RATE * (index + 1)
        for way in range(3):
            number = 3 * index + way
            if number < 8:
                fetch(number + 1).start()
            fetch(number).wait()
            shifted[...] = fetched[number % 2].astype(wide)
            for side in range(3):
                tap = 3 * (2 - way) + side
                at = PAD - (side - 1) * rate
                for line in range(height):
                    moved[line * width : (line + 1) * width, tap * aspp : (tap + 1) * aspp] = shifted[
                        line, at : at + width, :
                    ].astype(low)

        def one_chunk(block, carry):
            span = chunk_of(block)
            rows_of = sep_point[index, span, :].astype(wide)
            for tap in range(9):
                order = 9 * index + tap
                maps[:, tap * aspp : (tap + 1) * aspp] = (
                    rows_of * depth[span, order : order + 1]
                ).astype(low)
            total = grown[:, span] + across(moved[...], maps[...])
            if index < 2:
                grown[:, span] = total
                return carry
            advance(block)
            shift_sum, gain_sum = jnp.zeros((1, aspp), wide), jnp.zeros((1, aspp), wide)
            for line in range(height):
                rows_span, normed = back(block, line, span)
                gated = (
                    normed * three[2:3, span]
                    + three[3:4, span]
                    + features[rows_span, span].astype(wide)
                )
                sigma = sigmoid(gated)
                up = total[rows_span, :] * (sigma * (1.0 + gated * (1.0 - sigma)))
                grown[rows_span, span] = up
                pre_grad[rows_span, span] = up.astype(low)
                shift_sum = shift_sum + jnp.sum(up, axis=0, keepdims=True)
                gain_sum = gain_sum + jnp.sum(up * normed, axis=0, keepdims=True)
            for part in range(per):
                lanes = slice(part * LANES, (part + 1) * LANES)
                slots_three[me, pl.ds(block * 2 * per + part, 1), :] = shift_sum[:, lanes]
                slots_three[me, pl.ds(block * 2 * per + per + part, 1), :] = gain_sum[:, lanes]
            pair = block // 2

            @pl.when(lax.rem(block, 2) == 1)
            def _():
                share_rows(slots_three, pl.multiple_of(pair * 4 * per, 8), 4 * per, sems_three.at[pair])

            return carry

        if index == 0:
            early_sum.start_level(0)
        if index == 2:
            fetch_chunk(0).start()
        lax.fori_loop(0, chunks, one_chunk, 0)
        if index == 0:
            early_sum.start_level(1)
        if index == 1:
            early_sum.start_back(1)

    def finish(block, carry):
        span = chunk_of(block)
        pair = block // 2
        at = pl.multiple_of(pair * 4 * per, 8)

        @pl.when(lax.rem(block, 2) == 0)
        def _():
            shared_rows(slots_three, at, 4 * per, sems_three.at[pair])
            sums_three[pl.ds(at, 4 * per), :] = jnp.sum(slots_three[:, pl.ds(at, 4 * per), :], axis=0)

        advance(block)

        def row_at(start):
            first = block * 2 * per + start
            return jnp.concatenate([sums_three[pl.ds(first + part, 1), :] for part in range(per)], axis=1)

        shift_mean = row_at(0) / count
        gain_mean = row_at(per) / count
        factor = three[2:3, span] * three[1:2, span]
        for line in range(height):
            rows_span, normed = back(block, line, span)
            inner = grown[rows_span, span] - shift_mean - normed * gain_mean
            expand_low[rows_span, span] = (inner * factor).astype(low)
        return carry

    early_sum.start_back(0)
    fetch_chunk(0).start()
    lax.fori_loop(0, chunks, finish, 0)
    grown_two = across(expand_low[...], expand_weight[...])
    shift_sum, gain_sum = jnp.zeros((1, middle), wide), jnp.zeros((1, middle), wide)
    for line in range(height):
        rows_span = slice(line * width, (line + 1) * width)
        normed = (dilated[rows_span, :] - two[0:1, :]) * two[1:2, :]
        gated = normed * two[2:3, :] + two[3:4, :]
        sigma = sigmoid(gated)
        up = grown_two[rows_span, :] * (sigma * (1.0 + gated * (1.0 - sigma)))
        grown[rows_span, :middle] = up
        shift_sum = shift_sum + jnp.sum(up, axis=0, keepdims=True)
        gain_sum = gain_sum + jnp.sum(up * normed, axis=0, keepdims=True)
    per_two = middle // LANES
    put_row(slots_two, me, 0, shift_sum)
    put_row(slots_two, me, per_two, gain_sum)
    share(slots_two, sems_two)
    for block in range(channels // middle):
        span = slice(block * middle, (block + 1) * middle)
        expand_part[block * middle : (block + 1) * middle, :] = down(
            second_act[...], expand_low[:, span]
        ).astype(low)
    shared(slots_two, sems_two)
    total = jnp.sum(slots_two[...], axis=0)
    sums_two[...] = total
    shift_mean = take_row(total, 0, middle) / count
    gain_mean = take_row(total, per_two, middle) / count
    factor = two[2:3, :] * two[1:2, :]
    for line in range(height):
        rows_span = slice(line * width, (line + 1) * width)
        normed = (dilated[rows_span, :] - two[0:1, :]) * two[1:2, :]
        inner = grown[rows_span, :middle] - shift_mean - normed * gain_mean
        dilated_low[rows_span, :] = (inner * factor).astype(low)
    early_sum.start_back_half()
    early_sum.finish()


def trunk_back(near, own_low, depth, sep_point, aspp_point, members, crop_high, crop_rest, expanded,
               features, three, dilated, two, second_act, expand_weight, early):
    devices = lax.axis_size("rows") * lax.axis_size("cols")
    height, extent, aspp = near.shape[2:]
    pixels, channels = expanded.shape
    middle = dilated.shape[1]
    chunks = channels // aspp
    low, wide = jnp.bfloat16, jnp.float32
    shape = jax.ShapeDtypeStruct
    whole = pl.BlockSpec(memory_space=pltpu.VMEM)
    away = pl.BlockSpec(memory_space=pl.ANY)
    sems = pltpu.SemaphoreType.DMA
    per_two = middle // LANES
    outs = (
        shape((pixels, channels), low),
        shape((channels, middle), low),
        shape((pixels, middle), low),
        shape((chunks * 2 * (aspp // LANES), LANES), wide),
        shape((2 * per_two, LANES), wide),
        shape(early.shape, low),
    )
    return pl.pallas_call(
        trunk_back_kernel,
        out_shape=outs,
        in_specs=[away] + [whole] * 7 + [away] + [whole] * 6 + [away],
        out_specs=(whole,) * 5 + (away,),
        scratch_shapes=[
            pltpu.VMEM((2, height, extent, aspp), low),
            pltpu.VMEM((2, pixels, aspp), wide),
            pltpu.VMEM((height, extent, aspp), wide),
            pltpu.VMEM((pixels, 9 * aspp), low),
            pltpu.VMEM((aspp, 9 * aspp), low),
            pltpu.VMEM((pixels, channels), wide),
            pltpu.VMEM((pixels, channels), low),
            pltpu.VMEM((devices, chunks * 2 * (aspp // LANES), LANES), wide),
            pltpu.VMEM((devices, 2 * per_two, LANES), wide),
            sems((chunks // 2, 2)),
            sems((2,)),
            sems((2,)),
            sems((2,)),
            *sums_scratch(*early.shape, True),
        ],
        compiler_params=pltpu.CompilerParams(
            collective_id=12, has_side_effects=True, vmem_limit_bytes=VMEM_BYTES + (3 << 20)
        ),
        cost_estimate=pl.CostEstimate(
            flops=80 * pixels * channels * aspp, bytes_accessed=64 * pixels * channels, transcendentals=0
        ),
        name="trunk_back",
    )(near, own_low, depth, sep_point, aspp_point, members, crop_high, crop_rest, expanded, features,
      three, dilated, two, second_act, expand_weight, early)


EDGE = 16


class Halo:
    def __init__(self, near, direct, relay, edge):
        self.near, self.direct, self.relay, self.edge = near, direct, relay, edge
        self.rows, self.cols, self.row, self.col, _ = place()
        self.height, self.width = near.shape[1], near.shape[2] - 2 * EDGE
        self.odd = lax.rem(self.row, 2)
        self.pair = self.row + 1 - 2 * self.odd
        self.onward = self.row + 2 - 4 * self.odd
        self.far = self.row - 1 + 2 * self.odd
        self.pair_way = 2 - 2 * self.odd
        self.far_way = 2 * self.odd

    def exists(self, target):
        return jnp.logical_and(target >= 0, target < self.rows)

    def line_ref(self, way, line):
        return self.near.at[way, line, pl.ds(EDGE, self.width), :]

    def direct_copy(self, line):
        return pltpu.make_async_remote_copy(
            self.line_ref(1, line),
            self.line_ref(self.far_way, line),
            self.direct.at[0, line],
            self.direct.at[1, line],
            device_id=(self.pair, self.col),
            device_id_type=MESH,
        )

    def relay_copy(self, line):
        return pltpu.make_async_remote_copy(
            self.line_ref(self.pair_way, line),
            self.line_ref(self.far_way, line),
            self.relay.at[0, line],
            self.relay.at[1, line],
            device_id=(self.onward, self.col),
            device_id_type=MESH,
        )

    def edge_copy(self, way):
        start = pl.multiple_of(EDGE + (1 - self.col) * (self.width - EDGE), 16)
        end = pl.multiple_of(self.col * (self.width + EDGE), 16)
        return pltpu.make_async_remote_copy(
            self.near.at[1, :, pl.ds(start, EDGE), :],
            self.near.at[way, :, pl.ds(end, EDGE), :],
            self.edge.at[0, way],
            self.edge.at[1, way],
            device_id=(self.row + 1 - way, 1 - self.col),
            device_id_type=MESH,
        )

    def clear(self):
        near = self.near
        blank = pl.multiple_of(self.col * (self.width + EDGE), 16)
        for way in range(3):
            near[way, :, pl.ds(blank, EDGE), :] = jnp.zeros(
                (self.height, EDGE, near.shape[3]), near.dtype
            )

        @pl.when(jnp.logical_not(self.exists(self.far)))
        def _():
            near[self.far_way] = jnp.zeros(near.shape[1:], near.dtype)

    def start(self):
        self.edge_copy(1).start()
        for line in range(self.height // 2):
            self.direct_copy(line).start()
        for way in (0, 2):

            @pl.when(self.exists(self.row + 1 - way))
            def _():
                self.edge_copy(way).start()

    def wait_own(self):
        self.edge_copy(1).wait_recv()

    def pass_line(self, line):
        self.direct_copy(line).wait_recv()

        @pl.when(self.exists(self.onward))
        def _():
            self.relay_copy(line).start()

    def pass_first(self):
        for line in range(self.height // 2):
            self.pass_line(line)
        for line in range(self.height // 2, self.height):
            self.direct_copy(line).start()

    def pass_rest(self):
        for line in range(self.height // 2, self.height):
            self.pass_line(line)

    def wait_rest(self):
        self.wait_edges()
        self.wait_relay()

    def wait_edges(self):
        for way in (0, 2):

            @pl.when(self.exists(self.row - 1 + way))
            def _():
                self.edge_copy(way).wait_recv()

    def wait_relay(self):
        @pl.when(self.exists(self.far))
        def _():
            for line in range(self.height):
                self.relay_copy(line).wait_recv()

    def drain(self):
        self.edge_copy(1).wait_send()
        for line in range(self.height):
            self.direct_copy(line).wait_send()
        for way in (0, 2):

            @pl.when(self.exists(self.row + 1 - way))
            def _():
                self.edge_copy(way).wait_send()

        @pl.when(self.exists(self.onward))
        def _():
            for line in range(self.height):
                self.relay_copy(line).wait_send()


def front_kernel(
    features,
    reduce_weight,
    dilated_weight,
    expand_weight,
    pool_weight,
    mid_gain,
    mid_shift,
    out_gain,
    out_shift,
    crop_ids,
    boundary,
    valid,
    reduced,
    first_act,
    dilated,
    second_act,
    expanded,
    trunk,
    one,
    two,
    three,
    count_sums,
    crop_sums,
    crop_part,
    pixel_crops,
    near,
    shifted,
    moved,
    members,
    one_slots,
    two_slots,
    three_own,
    three_pair,
    three_slots,
    three_all,
    direct,
    relay,
    edge,
    one_sems,
    two_sems,
    pair_sems,
    three_sems,
    all_sems,
):
    rows, cols, row, col, me = place()
    low, wide = jnp.bfloat16, jnp.float32
    height = near.shape[1]
    pixels, middle = reduced.shape
    channels = features.shape[1]
    width = pixels // height
    share_size = float(pixels)
    count = float(pixels * rows * cols)
    per = middle // LANES
    halo = Halo(near, direct, relay, edge)
    greet_all()
    halo.clear()
    reduced[...] = jnp.dot(features[...], reduce_weight[...], preferred_element_type=wide)

    def lines(body, carry=0):
        def run(line, carry):
            return body(line, pl.ds(pl.multiple_of(line * width, width), width), carry)

        return lax.fori_loop(0, height, run, carry)

    def keep_low(line, span, carry):
        near[1, line, EDGE : EDGE + width, :] = reduced[span, :].astype(low)
        return carry

    lines(keep_low)
    await_all()
    halo.start()

    def statistics(value_of, extent):
        zero = jnp.zeros((1, extent), wide)
        total = lines(lambda line, span, acc: acc + jnp.sum(value_of(span), axis=0, keepdims=True), zero)
        mean = total / share_size

        def squares(line, span, acc):
            apart = value_of(span) - mean
            return acc + jnp.sum(apart * apart, axis=0, keepdims=True)

        return mean, lines(squares, zero)

    def settle(table, at, center, scale):
        table[...] = jnp.zeros(table.shape, wide)
        table[0:1, :] = center
        table[1:2, :] = scale
        table[2:3, :] = mid_gain[at : at + 1, :]
        table[3:4, :] = mid_shift[at : at + 1, :]

    def activated(value, table):
        gated = (value - table[0:1, :]) * table[1:2, :] * table[2:3, :] + table[3:4, :]
        return gated * sigmoid(gated)

    mean, square = statistics(lambda span: reduced[span, :], middle)
    one_slots[me] = jnp.zeros(one_slots.shape[1:], wide)
    put_row(one_slots, me, 0, mean)
    put_row(one_slots, me, per, square)
    crop_of = lax.broadcasted_iota(jnp.int32, (LANES, width), 0)
    for line in range(height):
        hot = jnp.where(crop_of == crop_ids[line : line + 1, :], 1.0, 0.0)
        members[:, line * width : (line + 1) * width] = hot.astype(low)
        pixel_crops[line * width : (line + 1) * width, :] = hot.T.astype(low)
    lane = lax.broadcasted_iota(jnp.int32, (8, LANES), 1)

    def whole_sum(table):
        part = jnp.sum(table[...].astype(wide), axis=0, keepdims=True)
        return jnp.sum(part, axis=1, keepdims=True)

    counts = across(jnp.ones((8, pixels), low), members[...])
    counts = jnp.where(lane == CROPS, share_size - whole_sum(boundary), counts)
    counts = jnp.where(lane == CROPS + 1, whole_sum(valid), counts)
    put_row(one_slots, me, 2 * per, counts[0:1, :])
    share(one_slots, one_sems)
    shared(one_slots, one_sems)
    center, scale = merged(one_slots, per, share_size, count)
    settle(one, 0, take_row(center, 0, middle), take_row(scale, 0, middle))
    count_sums[...] = jnp.sum(one_slots[:, 2 * per : 2 * per + 8, :], axis=0)

    def first(line, span, carry):
        first_act[span, :] = activated(reduced[span, :], one).astype(low)
        return carry

    lines(first)

    def one_way(way, own):
        alive = jnp.where(halo.exists(row - 1 + way), 1.0, 0.0)

        def open_line(line, span, carry):
            shifted[line] = activated(near[way, line].astype(wide), one) * alive
            if own:
                shifted[line, EDGE : EDGE + width, :] = first_act[span, :].astype(wide)
            blank = pl.multiple_of(col * (width + EDGE), 16)
            shifted[line, pl.ds(blank, EDGE), :] = jnp.zeros((EDGE, middle), wide)
            for side in range(3):
                at = EDGE + (side - 1) * MID_RATE
                moved[span, side * middle : (side + 1) * middle] = shifted[
                    line, at : at + width, :
                ].astype(low)
            return carry

        lines(open_line)
        made = jnp.dot(moved[...], dilated_weight[way], preferred_element_type=wide)
        if own:
            dilated[...] = made
        else:
            dilated[...] += made

    halo.pass_first()
    halo.wait_own()
    one_way(1, True)
    halo.pass_rest()
    halo.wait_edges()
    one_way(halo.pair_way, False)
    halo.wait_relay()
    one_way(halo.far_way, False)
    mean, square = statistics(lambda span: dilated[span, :], middle)
    put_row(two_slots, me, 0, mean)
    put_row(two_slots, me, per, square)
    share(two_slots, two_sems)
    shared(two_slots, two_sems)
    center, scale = merged(two_slots, per, share_size, count)
    settle(two, 1, take_row(center, 0, middle), take_row(scale, 0, middle))

    def second(line, span, carry):
        second_act[span, :] = activated(dilated[span, :], two).astype(low)
        return carry

    lines(second)
    chunk = 2 * LANES
    half_rows = channels // 2 // LANES
    half_chunks = channels // 2 // chunk

    def expand(block, carry):
        span = pl.ds(pl.multiple_of(block * chunk, chunk), chunk)
        expanded[:, span] = jnp.dot(second_act[...], expand_weight[:, span], preferred_element_type=wide)
        mean, square = statistics(lambda rows_span: expanded[rows_span, span], chunk)
        at = block // half_chunks * 2 * half_rows + lax.rem(block, half_chunks) * 2
        for part in range(2):
            lanes = slice(part * LANES, (part + 1) * LANES)
            three_own[pl.ds(at + part, 1), :] = mean[:, lanes]
            three_own[pl.ds(at + half_rows + part, 1), :] = square[:, lanes]
        return carry

    lax.fori_loop(0, channels // chunk, expand, 0)

    def to_pair(src, dst, sems):
        return pltpu.make_async_remote_copy(
            src, dst, sems.at[0], sems.at[1], device_id=(row, 1 - col), device_id_type=MESH
        )

    theirs = pl.ds(pl.multiple_of((1 - col) * 2 * half_rows, 8), 2 * half_rows)
    mine = pl.ds(pl.multiple_of(col * 2 * half_rows, 8), 2 * half_rows)
    copy = to_pair(three_own.at[theirs], three_pair, pair_sems)
    copy.start()
    copy.wait()
    own = three_own[mine, :]
    other = three_pair[...]
    apart = own[:half_rows] - other[:half_rows]
    three_slots[row, :half_rows, :] = 0.5 * (own[:half_rows] + other[:half_rows])
    three_slots[row, half_rows:, :] = (
        own[half_rows:] + other[half_rows:] + (0.5 * share_size) * (apart * apart)
    )
    share_column(three_slots, three_sems)
    shared_column(three_slots, three_sems)
    center, scale = merged(three_slots, half_rows, 2.0 * share_size, count)
    three_all[col, :half_rows, :] = center
    three_all[col, half_rows:, :] = scale
    copy = to_pair(three_all.at[col], three_all.at[col], all_sems)
    copy.start()
    copy.wait()
    for half in range(2):
        span = slice(half * channels // 2, (half + 1) * channels // 2)
        three[0:1, span] = take_row(three_all[half], 0, channels // 2)
        three[1:2, span] = take_row(three_all[half], half_rows, channels // 2)
    three[2:3, :] = out_gain[...]
    three[3:4, :] = out_shift[...]
    three[4:8, :] = jnp.zeros((4, channels), wide)
    crops = CROPS

    def last(block, carry):
        span = pl.ds(pl.multiple_of(block * chunk, chunk), chunk)

        def act_line(line, rows_span, carry):
            normed = (expanded[rows_span, span] - three[0:1, span]) * three[1:2, span]
            gated = (
                normed * three[2:3, span] + three[3:4, span] + features[rows_span, span].astype(wide)
            )
            trunk[rows_span, span] = (gated * sigmoid(gated)).astype(low)
            return carry

        lines(act_line)
        sums = jnp.dot(members[...], trunk[:, span], preferred_element_type=wide)[:crops, :]
        for part in range(2):
            at = pl.multiple_of((2 * block + part) * crops, 8)
            crop_sums[pl.ds(at, crops), :] = sums[:, part * LANES : (part + 1) * LANES]
        high = sums.astype(low)
        rest = (sums - high.astype(wide)).astype(low)
        return (
            carry
            + jnp.dot(high, pool_weight[span, :], preferred_element_type=wide)
            + jnp.dot(rest, pool_weight[span, :], preferred_element_type=wide)
        )

    crop_part[...] = lax.fori_loop(
        0, channels // chunk, last, jnp.zeros((crops, pool_weight.shape[1]), wide)
    )
    halo.drain()


def front(height, features, reduce_weight, dilated_weight, expand_weight, pool_weight, mid_gain,
          mid_shift, out_gain, out_shift, crop_ids, boundary, valid):
    rows = lax.axis_size("rows")
    devices = rows * lax.axis_size("cols")
    pixels, channels = features.shape
    middle = reduce_weight.shape[1]
    width = pixels // height
    low, wide = jnp.bfloat16, jnp.float32
    shape = jax.ShapeDtypeStruct
    whole = pl.BlockSpec(memory_space=pltpu.VMEM)
    sems = pltpu.SemaphoreType.DMA
    per = middle // LANES
    half_rows = channels // 2 // LANES
    outs = (
        shape((pixels, middle), wide),
        shape((pixels, middle), low),
        shape((pixels, middle), wide),
        shape((pixels, middle), low),
        shape((pixels, channels), wide),
        shape((pixels, channels), low),
        shape((8, middle), wide),
        shape((8, middle), wide),
        shape((8, channels), wide),
        shape((8, LANES), wide),
        shape((CROPS * channels // LANES, LANES), wide),
        shape((CROPS, pool_weight.shape[1]), wide),
        shape((pixels, LANES), low),
    )
    return pl.pallas_call(
        front_kernel,
        out_shape=outs,
        in_specs=[whole] * 12,
        out_specs=(whole,) * len(outs),
        scratch_shapes=[
            pltpu.VMEM((3, height, width + 2 * EDGE, middle), low),
            pltpu.VMEM((height, width + 2 * EDGE, middle), wide),
            pltpu.VMEM((pixels, 3 * middle), low),
            pltpu.VMEM((LANES, pixels), low),
            pltpu.VMEM((devices, 2 * per + 8, LANES), wide),
            pltpu.VMEM((devices, 2 * per, LANES), wide),
            pltpu.VMEM((4 * half_rows, LANES), wide),
            pltpu.VMEM((2 * half_rows, LANES), wide),
            pltpu.VMEM((rows, 2 * half_rows, LANES), wide),
            pltpu.VMEM((2, 2 * half_rows, LANES), wide),
            sems((2, height)),
            sems((2, height)),
            sems((2, 3)),
            sems((2,)),
            sems((2,)),
            sems((2,)),
            sems((2,)),
            sems((2,)),
        ],
        compiler_params=pltpu.CompilerParams(
            collective_id=14, has_side_effects=True, vmem_limit_bytes=VMEM_BYTES
        ),
        name="front",
    )(features, reduce_weight, dilated_weight, expand_weight, pool_weight, mid_gain, mid_shift,
      out_gain, out_shift, crop_ids, boundary, valid)


PLANE = 4


class Sum:
    def __init__(self, full, own, out, plane_first, half_in, near_in, far_in, half_sem, near_sem, far_sem, copy_sem):
        self.full, self.out, self.half_in = full, out, half_in
        self.half_sem, self.copy_sem = half_sem, copy_sem
        self.rows, self.cols, self.row, self.col, _ = place()
        parts = self.rows // PLANE
        quarter, part = lax.rem(self.row, PLANE), self.row // PLANE
        plane = (PLANE, quarter, lambda mate: part * PLANE + mate)
        rest = (parts, part, lambda mate: mate * PLANE + quarter)
        self.levels = (plane, rest) if plane_first else (rest, plane)
        self.arrivals, self.sems = (near_in, far_in), (near_sem, far_sem)
        self.half_rows = full.shape[0] // 2
        self.sizes = [self.half_rows // self.levels[0][0]]
        self.sizes.append(self.sizes[0] // self.levels[1][0])
        self.own = own
        self.data = full.at[self.half_span(self.col)] if own is None else own

    def span(self, start, size):
        return pl.ds(pl.multiple_of(start, 16), size)

    def half_span(self, col):
        return self.span(col * self.half_rows, self.half_rows)

    def level_span(self, level, at):
        base = 0 if level == 0 else self.levels[0][1] * self.sizes[0]
        return self.span(base + at * self.sizes[level], self.sizes[level])

    def out_at(self, span):
        return self.out.at[self.span(self.col * self.half_rows + span.start, span.size)]

    def mates(self, level):
        count, at, row_of = self.levels[level]
        for step in range(1, count):
            mate = lax.rem(at + step, count)
            yield mate, (row_of(mate), self.col)

    def remote(self, src, dst, sems, out_at, in_at, target):
        return pltpu.make_async_remote_copy(
            src, dst, sems.at[0, out_at], sems.at[1, in_at], device_id=target, device_id_type=MESH
        )

    def fetch(self):
        return pltpu.make_async_copy(self.full.at[self.half_span(self.col)], self.own, self.copy_sem)

    def half_copy(self):
        other = self.full.at[self.half_span(1 - self.col)]
        return self.remote(other, self.half_in, self.half_sem, 0, 0, (self.row, 1 - self.col))

    def level_copy(self, level, mate, target):
        at = self.levels[level][1]
        return self.remote(
            self.data.at[self.level_span(level, mate)],
            self.arrivals[level].at[at],
            self.sems[level],
            mate,
            at,
            target,
        )

    def level_arrival(self, level, mate, target):
        slot = self.arrivals[level].at[mate]
        return self.remote(slot, slot, self.sems[level], mate, mate, target)

    def back_copy(self, level, mate, target):
        count, at, _ = self.levels[level]
        mine = self.out_at(self.level_span(level, at))
        return self.remote(mine, mine, self.sems[level], count + mate, count + at, target)

    def back_arrival(self, level, mate, target):
        count = self.levels[level][0]
        theirs = self.out_at(self.level_span(level, mate))
        return self.remote(theirs, theirs, self.sems[level], count + mate, count + mate, target)

    def back_half(self, col):
        part = self.out.at[self.half_span(col)]
        return self.remote(part, part, self.half_sem, 1, 1, (self.row, 1 - self.col))

    def add(self, span, sources):
        block = 64
        base = span.start

        def some(at, carry):
            rows = pl.ds(pl.multiple_of(base + at * block, 16), block)
            total = self.data[rows, :].astype(jnp.float32)
            for source in sources:
                total = total + source(pl.ds(pl.multiple_of(at * block, 16), block)).astype(jnp.float32)
            self.data[rows, :] = total.astype(self.data.dtype)
            return carry

        full = span.size // block
        lax.fori_loop(0, full, some, 0)
        rest = span.size - full * block
        if rest:
            rows = pl.ds(pl.multiple_of(base + full * block, 16), rest)
            total = self.data[rows, :].astype(jnp.float32)
            for source in sources:
                total = total + source(pl.ds(full * block, rest)).astype(jnp.float32)
            self.data[rows, :] = total.astype(self.data.dtype)

    def start_half(self):
        self.half_copy().start()

    def start_level(self, level):
        if level == 0:
            self.half_copy().wait()
            self.add(self.span(0, self.half_rows), [lambda rows: self.half_in[rows, :]])
        else:
            self.gather(0)
        for mate, target in self.mates(level):
            self.level_copy(level, mate, target).start()

    def gather(self, level):
        for mate, target in self.mates(level):
            self.level_copy(level, mate, target).wait_send()
            self.level_arrival(level, mate, target).wait_recv()
        self.add(
            self.level_span(level, self.levels[level][1]),
            [lambda rows, mate=mate: self.arrivals[level][mate, rows, :] for mate, _ in self.mates(level)],
        )

    def start_back(self, level):
        if level == 1:
            self.gather(1)
            span = self.level_span(1, self.levels[1][1])
            copy = pltpu.make_async_copy(self.data.at[span], self.out_at(span), self.copy_sem)
            copy.start()
            copy.wait()
        else:
            for mate, target in self.mates(1):
                self.back_copy(1, mate, target).wait_send()
                self.back_arrival(1, mate, target).wait_recv()
        for mate, target in self.mates(level):
            self.back_copy(level, mate, target).start()

    def start_back_half(self):
        for mate, target in self.mates(0):
            self.back_copy(0, mate, target).wait_send()
            self.back_arrival(0, mate, target).wait_recv()
        self.back_half(self.col).start()

    def finish(self):
        self.back_half(self.col).wait_send()
        self.back_half(1 - self.col).wait_recv()


class Sums:
    def __init__(self, full, own, out, refs):
        self.each = []
        start = 0
        for size, plane_first in sum_pieces(full.shape[0]):
            span = pl.ds(start, size)
            count = 7 if own is None else 8
            mine, refs = list(refs[:count]), refs[count:]
            part = None if own is None else mine.pop(0)
            self.each.append(Sum(full.at[span], part, out.at[span], plane_first, *mine))
            start += size
        self.rest = refs

    def fetch(self):
        for each in self.each:
            each.fetch().start()

    def fetched(self):
        for each in self.each:
            each.fetch().wait()

    def start_half(self):
        for each in self.each:
            each.start_half()

    def start_level(self, level):
        for each in self.each:
            each.start_level(level)

    def start_back(self, level):
        for each in self.each:
            each.start_back(level)

    def start_back_half(self):
        for each in self.each:
            each.start_back_half()

    def finish(self):
        for each in self.each:
            each.finish()


def sum_unit():
    return 2 * lax.axis_size("rows") * 16


def sum_pieces(total):
    unit = sum_unit()
    units = total // unit
    second = units // 3
    pieces = [((units - second) * unit, True)]
    if second:
        pieces.append((second * unit, False))
    return pieces


def sums_scratch(total, lanes, away):
    parts = lax.axis_size("rows") // PLANE
    low, sems = jnp.bfloat16, pltpu.SemaphoreType.DMA
    scratch = []
    for size, plane_first in sum_pieces(total):
        counts = (PLANE, parts) if plane_first else (parts, PLANE)
        half = size // 2
        if away:
            scratch.append(pltpu.VMEM((half, lanes), low))
        scratch += [
            pltpu.VMEM((half, lanes), low),
            pltpu.VMEM((counts[0], half // counts[0], lanes), low),
            pltpu.VMEM((counts[1], half // counts[0] // counts[1], lanes), low),
            sems((2, 2)),
            sems((2, 2 * counts[0])),
            sems((2, 2 * counts[1])),
            sems,
        ]
    return scratch


def sum_rows(rows):
    unit = sum_unit()
    return -(-rows // unit) * unit


def tail_kernel(
    dilated_low,
    first_act,
    dilated_weight,
    reduced,
    one,
    features,
    reduce_weight,
    pre_grad,
    expand_part,
    features_grad,
    expand_out,
    dilated_out,
    reduce_out,
    sums_one,
    near,
    shifted,
    moved,
    act_turned,
    features_turned,
    first_grad,
    reduced_low,
    dilated_data,
    reduce_data,
    slots,
    direct,
    relay,
    edge,
    sems_one,
    *sum_refs,
):
    rows, cols, row, col, me = place()
    low, wide = jnp.bfloat16, jnp.float32
    height = near.shape[1]
    pixels, middle = dilated_low.shape
    channels = features.shape[1]
    width = pixels // height
    count = float(pixels * rows * cols)
    expand_sum = Sums(expand_part, True, expand_out, sum_refs)
    dilated_sum = Sums(dilated_data, None, dilated_out, expand_sum.rest)
    reduce_sum = Sums(reduce_data, None, reduce_out, dilated_sum.rest)
    sums = (expand_sum, dilated_sum, reduce_sum)
    halo = Halo(near, direct, relay, edge)
    greet_all()
    expand_sum.fetch()
    halo.clear()
    for line in range(height):
        near[1, line, EDGE : EDGE + width, :] = dilated_low[line * width : (line + 1) * width, :]
    for data, used in ((dilated_data, 9 * middle), (reduce_data, channels)):
        if data.shape[0] > used:
            data[used:, :] = jnp.zeros((data.shape[0] - used, data.shape[1]), low)
    expand_sum.fetched()
    await_all()
    halo.start()
    expand_sum.start_half()

    def turn_features(block, carry):
        span = pl.ds(pl.multiple_of(block * width, width), width)
        for line in range(height):
            features_turned[span, line * width : (line + 1) * width] = features[
                line * width : (line + 1) * width, span
            ].T
        return carry

    def turn_act(block, carry):
        span = pl.ds(pl.multiple_of(block * width, width), width)
        for line in range(height):
            act_turned[span, line * width : (line + 1) * width] = first_act[
                line * width : (line + 1) * width, span
            ].T
        return carry

    lax.fori_loop(0, middle // width, turn_act, 0)

    def one_way(way):
        shifted[...] = near[way].astype(wide)
        for side in range(3):
            tap = 3 * (2 - way) + side
            rows_of = pl.ds(pl.multiple_of(tap * middle, middle), middle)
            at = EDGE - (side - 1) * MID_RATE
            for line in range(height):
                moved[line * width : (line + 1) * width, :] = shifted[line, at : at + width, :].astype(
                    low
                )
            made = across(moved[...], dilated_weight[tap])
            if isinstance(way, int) and side == 0:
                first_grad[...] = made
            else:
                first_grad[...] += made
            dilated_data[rows_of, :] = jnp.dot(
                act_turned[...], moved[...], preferred_element_type=wide
            ).astype(low)

    halo.wait_own()
    one_way(1)
    halo.pass_first()
    lax.fori_loop(0, channels // width, turn_features, 0)
    halo.pass_rest()
    halo.wait_edges()
    one_way(halo.pair_way)
    halo.wait_relay()
    expand_sum.start_level(0)
    one_way(halo.far_way)
    dilated_sum.start_half()
    expand_sum.start_level(1)
    shift_sum, gain_sum = jnp.zeros((1, middle), wide), jnp.zeros((1, middle), wide)
    for line in range(height):
        span = slice(line * width, (line + 1) * width)
        normed = (reduced[span, :] - one[0:1, :]) * one[1:2, :]
        gated = normed * one[2:3, :] + one[3:4, :]
        sigma = sigmoid(gated)
        up = first_grad[span, :] * (sigma * (1.0 + gated * (1.0 - sigma)))
        first_grad[span, :] = up
        shift_sum = shift_sum + jnp.sum(up, axis=0, keepdims=True)
        gain_sum = gain_sum + jnp.sum(up * normed, axis=0, keepdims=True)
    per = middle // LANES
    put_row(slots, me, 0, shift_sum)
    put_row(slots, me, per, gain_sum)
    share(slots, sems_one)
    dilated_sum.start_level(0)
    shared(slots, sems_one)
    total = jnp.sum(slots[...], axis=0)
    sums_one[...] = total
    shift_mean = take_row(total, 0, middle) / count
    gain_mean = take_row(total, per, middle) / count
    factor = one[2:3, :] * one[1:2, :]
    for line in range(height):
        span = slice(line * width, (line + 1) * width)
        normed = (reduced[span, :] - one[0:1, :]) * one[1:2, :]
        inner = first_grad[span, :] - shift_mean - normed * gain_mean
        reduced_low[span, :] = (inner * factor).astype(low)
    reduce_data[:channels, :] = jnp.dot(
        features_turned[...], reduced_low[...], preferred_element_type=wide
    ).astype(low)
    reduce_sum.start_half()
    expand_sum.start_back(1)
    chunk = 2 * LANES

    def last(block, carry):
        span = pl.ds(pl.multiple_of(block * chunk, chunk), chunk)
        made = across(reduced_low[...], reduce_weight[span, :])
        features_grad[:, span] = (made + pre_grad[:, span].astype(wide)).astype(low)
        return carry

    lax.fori_loop(0, channels // chunk, last, 0)
    reduce_sum.start_level(0)
    expand_sum.start_back(0)
    dilated_sum.start_level(1)
    reduce_sum.start_level(1)
    expand_sum.start_back_half()
    dilated_sum.start_back(1)
    reduce_sum.start_back(1)
    dilated_sum.start_back(0)
    reduce_sum.start_back(0)
    dilated_sum.start_back_half()
    reduce_sum.start_back_half()
    for each in sums:
        each.finish()
    halo.drain()


def tail(height, dilated_low, first_act, dilated_weight, reduced, one, features, reduce_weight, pre_grad,
         expand_part):
    devices = lax.axis_size("rows") * lax.axis_size("cols")
    pixels, middle = dilated_low.shape
    channels = features.shape[1]
    width = pixels // height
    low, wide = jnp.bfloat16, jnp.float32
    shape = jax.ShapeDtypeStruct
    whole = pl.BlockSpec(memory_space=pltpu.VMEM)
    away = pl.BlockSpec(memory_space=pl.ANY)
    sems = pltpu.SemaphoreType.DMA
    per = middle // LANES
    expand_part = jnp.pad(
        expand_part, ((0, sum_rows(expand_part.shape[0]) - expand_part.shape[0]), (0, 0))
    )
    sizes = [sum_rows(expand_part.shape[0]), sum_rows(9 * middle), sum_rows(channels)]
    outs = (
        shape((pixels, channels), low),
        *[shape((size, middle), low) for size in sizes],
        shape((2 * per, LANES), wide),
    )
    scratch = [
        pltpu.VMEM((3, height, width + 2 * EDGE, middle), low),
        pltpu.VMEM((height, width + 2 * EDGE, middle), wide),
        pltpu.VMEM((pixels, middle), low),
        pltpu.VMEM((middle, pixels), low),
        pltpu.VMEM((channels, pixels), low),
        pltpu.VMEM((pixels, middle), wide),
        pltpu.VMEM((pixels, middle), low),
        *[pltpu.VMEM((size, middle), low) for size in sizes[1:]],
        pltpu.VMEM((devices, 2 * per, LANES), wide),
        sems((2, height)),
        sems((2, height)),
        sems((2, 3)),
        sems((2,)),
    ]
    for size, apart in zip(sizes, (True, False, False)):
        scratch += sums_scratch(size, middle, apart)
    return pl.pallas_call(
        functools.partial(tail_kernel),
        out_shape=outs,
        in_specs=[whole] * 8 + [away],
        out_specs=(whole, away, away, away, whole),
        scratch_shapes=scratch,
        compiler_params=pltpu.CompilerParams(
            collective_id=13, has_side_effects=True, vmem_limit_bytes=VMEM_BYTES + (3 << 20)
        ),
        cost_estimate=pl.CostEstimate(
            flops=400 * pixels * middle * middle, bytes_accessed=256 * pixels * channels, transcendentals=0
        ),
        name="tail",
    )(dilated_low, first_act, dilated_weight, reduced, one, features, reduce_weight, pre_grad, expand_part)


def widen_kernel(first, second, expand, dilated, reduce, sep_out, point_out, expand_out, dilated_out, reduce_out):
    wide = jnp.float32
    aspp, middle = point_out.shape[1], expand.shape[2]
    sep_out[0] = first[:, :aspp].astype(wide)
    sep_out[1] = first[:, aspp:].astype(wide)
    sep_out[2] = second[:, :aspp].astype(wide)
    point_out[...] = second[:, aspp:].astype(wide)
    for block in range(expand.shape[0]):
        expand_out[:, block * middle : (block + 1) * middle] = expand[block].astype(wide)
    dilated_out[...] = dilated[...].astype(wide)
    reduce_out[...] = reduce[...].astype(wide)


def widen(early, expand, dilated, reduce, channels, aspp):
    middle = reduce.shape[1]
    wide = jnp.float32
    steps = 16
    rows = channels // steps
    taps = 9 * middle // steps
    lines = middle // steps
    blocks = channels // middle
    shape = jax.ShapeDtypeStruct
    return pl.pallas_call(
        widen_kernel,
        grid=(steps,),
        out_shape=(
            shape((3, channels, aspp), wide),
            shape((channels, aspp), wide),
            shape((middle, channels), wide),
            shape((9 * middle, middle), wide),
            shape((channels, middle), wide),
        ),
        in_specs=[
            pl.BlockSpec((rows, 2 * aspp), lambda step: (step, 0)),
            pl.BlockSpec((rows, 2 * aspp), lambda step: (steps + step, 0)),
            pl.BlockSpec((blocks, lines, middle), lambda step: (0, step, 0)),
            pl.BlockSpec((taps, middle), lambda step: (step, 0)),
            pl.BlockSpec((rows, middle), lambda step: (step, 0)),
        ],
        out_specs=(
            pl.BlockSpec((3, rows, aspp), lambda step: (0, step, 0)),
            pl.BlockSpec((rows, aspp), lambda step: (step, 0)),
            pl.BlockSpec((lines, channels), lambda step: (step, 0)),
            pl.BlockSpec((taps, middle), lambda step: (step, 0)),
            pl.BlockSpec((rows, middle), lambda step: (step, 0)),
        ),
        compiler_params=pltpu.CompilerParams(vmem_limit_bytes=VMEM_BYTES),
        name="widen",
    )(early, early, expand[:channels].reshape(blocks, middle, middle), dilated, reduce)


def on_device(
    features,
    reduce_weight,
    dilated_weight,
    expand_weight,
    mid_gain,
    mid_shift,
    out_gain,
    out_shift,
    aspp_point,
    sep_depth,
    sep_point,
    pool_weight,
    proj_weight,
    aspp_gain,
    aspp_shift,
    head_weight,
    head_bias,
    task_scales,
    crop_ids,
    labels,
    boundary_mask,
    valid_mask,
    geometry_target,
):
    height, width, channels = features.shape
    pixels = height * width
    low = jnp.bfloat16
    aspp_width = proj_weight.shape[1]
    flat = features.reshape(pixels, channels)
    middle = reduce_weight.shape[1]

    (
        reduced, first_act, dilated, second_act, expanded, trunk, one, two, three, count_sums,
        local_sums, crop_part, members,
    ) = front(
        height,
        flat,
        reduce_weight,
        dilated_weight.reshape(3, 3 * middle, middle),
        expand_weight,
        pool_weight,
        mid_gain,
        mid_shift,
        out_gain.reshape(1, channels),
        out_shift.reshape(1, channels),
        crop_ids,
        boundary_mask,
        valid_mask,
    )
    crop_count = count_sums[0, :CROPS]
    lane = jnp.arange(LANES)
    scale_exp = jnp.exp(task_scales)
    task_of = jnp.where(lane < CLASSES, scale_exp[0], jnp.where(lane == CLASSES, scale_exp[1], scale_exp[2]))
    weights = jnp.stack(
        [jnp.where(lane > CLASSES, 2.0, 1.0) * task_of, task_of, jnp.pad(task_scales, (0, LANES - 3))]
    )
    outs = head_weight.shape[1]
    devices = lax.axis_size("rows") * lax.axis_size("cols")
    crop_rows = CROPS * channels // LANES
    piece = -(-crop_rows // devices)
    crop_sums = jnp.pad(local_sums, ((0, piece * devices - crop_rows), (0, 0)))
    crop_sums = jnp.pad(
        crop_sums.reshape(devices, piece, LANES), ((0, 0), (0, -piece % 8), (0, 0))
    )
    branch_low, proj_part, head_part, crop_local, crop_pre, sums_five, sums_four, crop_table, own_low, closing = pyramid(
        height,
        trunk,
        jnp.pad(sep_depth.reshape(27, channels).astype(jnp.float32), ((0, 5), (0, 0))),
        sep_point,
        aspp_point,
        crop_part,
        count_sums,
        members,
        proj_weight,
        aspp_gain,
        aspp_shift,
        head_weight,
        head_bias.reshape(1, outs),
        jnp.pad(weights, ((0, 5), (0, 0))),
        labels,
        boundary_mask,
        valid_mask,
        geometry_target,
        crop_sums,
    )
    crop_table = crop_table[:, :piece].reshape(-1, LANES)[:crop_rows].reshape(-1, CROPS, LANES)
    crop_table = jnp.transpose(crop_table, (1, 0, 2)).reshape(CROPS, channels)
    per = aspp_width // LANES
    proj_shift_grad = sums_five[:per].reshape(1, aspp_width)
    proj_gain_grad = sums_five[per : 2 * per].reshape(1, aspp_width)
    grad_head_bias = sums_five[2 * per + 1, :outs]
    branch_shift_grad = sums_four[: 4 * per].reshape(4, aspp_width)
    branch_gain_grad = sums_four[4 * per :].reshape(4, aspp_width)
    objective, grad_scales = closing[1, 0], closing[0, :3]
    near, early, crop_total = pyramid_weights(
        branch_low.reshape(4, height, width, aspp_width),
        trunk,
        jnp.pad(sep_depth.reshape(27, channels).astype(jnp.float32).T, ((0, 0), (0, LANES - 27))),
        sep_point,
        crop_local,
        proj_part,
        head_part,
    )
    crop_low = (crop_total * gate_slope(crop_pre)).astype(low)
    pooled = (crop_table / crop_count[:, None]).astype(low)
    grad_pool_weight = jnp.einsum("kc,kd->cd", pooled, crop_low, preferred_element_type=jnp.float32)
    pooled_grad = (
        jnp.einsum("kd,cd->kc", crop_low, pool_weight, preferred_element_type=jnp.float32)
        / crop_count[:, None]
    )
    pooled_grad = jnp.pad(pooled_grad, ((0, LANES - CROPS), (0, 0)))
    crop_high = pooled_grad.astype(low)
    crop_rest = (pooled_grad - crop_high.astype(jnp.float32)).astype(low)
    pre_low, expand_part, dilated_low, sums_three, sums_two, early_sum = trunk_back(
        near,
        own_low,
        jnp.pad(sep_depth.reshape(27, channels).astype(jnp.float32).T, ((0, 0), (0, LANES - 27))),
        sep_point,
        aspp_point,
        members,
        crop_high,
        crop_rest,
        expanded,
        flat,
        three,
        dilated,
        two,
        second_act,
        expand_weight,
        early,
    )
    folded = sums_three.reshape(-1, 2 * per, LANES)
    out_shift_grad = folded[:, :per].reshape(1, channels)
    out_gain_grad = folded[:, per:].reshape(1, channels)
    two_shift_grad, two_gain_grad = sums_two.reshape(2, 1, middle)
    grad_features, expand_sum, dilated_sum, reduce_sum, sums_one = tail(
        height,
        dilated_low,
        first_act,
        dilated_weight,
        reduced,
        one,
        flat,
        reduce_weight,
        pre_low,
        expand_part,
    )
    one_shift_grad, one_gain_grad = sums_one.reshape(2, 1, middle)
    grad_features = grad_features.reshape(height, width, channels)
    sep_sum, point_sum, grad_expand_weight, dilated_wide, reduce_wide = widen(
        early_sum, expand_sum, dilated_sum, reduce_sum, channels, aspp_width
    )
    at = 2 * channels
    tables = []
    for size, extent in ((proj_weight.shape[0], aspp_width), (channels, LANES), (aspp_width, LANES)):
        blocks = 2 * aspp_width // extent
        table = early_sum[at : at + size // blocks].reshape(size // blocks, blocks, extent)
        table = table.astype(jnp.float32)
        tables.append(jnp.transpose(table, (1, 0, 2)).reshape(size, extent))
        at += size // blocks
    summed = [
        reduce_wide,
        dilated_wide.reshape(9, middle, middle),
        grad_expand_weight,
        point_sum,
        tables[1][:, :27].T.reshape(3, 9, channels),
        sep_sum,
        tables[0],
        tables[2],
    ]
    grad_mid_gain = jnp.concatenate([one_gain_grad, two_gain_grad], axis=0)
    grad_mid_shift = jnp.concatenate([one_shift_grad, two_shift_grad], axis=0)
    grad_aspp_gain = jnp.concatenate([branch_gain_grad, proj_gain_grad], axis=0)
    grad_aspp_shift = jnp.concatenate([branch_shift_grad, proj_shift_grad], axis=0)
    return (
        objective,
        grad_features,
        summed[0],
        summed[1],
        summed[2],
        grad_mid_gain,
        grad_mid_shift,
        out_gain_grad[0],
        out_shift_grad[0],
        summed[3],
        summed[4],
        summed[5],
        grad_pool_weight,
        summed[6],
        grad_aspp_gain,
        grad_aspp_shift,
        summed[7][:, : head_weight.shape[1]],
        grad_head_bias,
        grad_scales,
    )


def solution(mesh):
    in_specs = (
        P("rows", "cols", None),
        P(),
        P(),
        P(),
        P(),
        P(),
        P(),
        P(),
        P(),
        P(),
        P(),
        P(),
        P(),
        P(),
        P(),
        P(),
        P(),
        P(),
        P("rows", "cols"),
        P("rows", "cols"),
        P("rows", "cols"),
        P("rows", "cols"),
        P(None, "rows", "cols"),
    )
    out_specs = (
        P(),
        P("rows", "cols", None),
        P(),
        P(),
        P(),
        P(),
        P(),
        P(),
        P(),
        P(),
        P(),
        P(),
        P(),
        P(),
        P(),
        P(),
        P(),
        P(),
        P(),
    )
    return jax.shard_map(
        on_device, mesh=mesh, in_specs=in_specs, out_specs=out_specs, check_vma=False
    )
```
